32 devices in a mesh: blk: 4 (over z), rows: 8 (over y, x, core).
Axes of the slice: x: 2, y: 2, z: 4, core: 2. Of those that a mesh axis runs over, the one named last changes fastest.
Arguments:
- tokens: bfloat16 [32, 1280, 256], P('rows', 'blk'), may hold values from -10 to 10
- seg_ids: int32 [32, 1280], P('rows', 'blk'), may hold values from 0 to 2, as said below
- frame_mask: int32 [32, 1280], P('rows', 'blk'), may hold values from 0 to 1, as said below
- cotangent: bfloat16 [32, 1280, 256], P('rows', 'blk'), may hold values from -6 to 6
- g_ff1: float32 [256], replicated, may hold values from 0.5 to 1.5
- w_ff1_in: bfloat16 [256, 1024], replicated, may hold values from -0.375 to 0.375
- w_ff1_out: bfloat16 [1024, 256], replicated, may hold values from -0.375 to 0.375
- g_att: float32 [256], replicated, may hold values from 0.5 to 1.5
- w_query: bfloat16 [256, 256], replicated, may hold values from -0.375 to 0.375
- w_key: bfloat16 [256, 256], replicated, may hold values from -0.375 to 0.375
- w_value: bfloat16 [256, 256], replicated, may hold values from -0.375 to 0.375
- w_output: bfloat16 [256, 256], replicated, may hold values from -1 to 1
- rel_table: float32 [4, 16], replicated, may hold values from -4 to 4
- g_conv: float32 [256], replicated, may hold values from 0.5 to 1.5
- w_pw1: bfloat16 [256, 512], replicated, may hold values from -0.375 to 0.375
- w_depth: bfloat16 [31, 256], replicated, may hold values from -1 to 1
- bn_gain: float32 [256], replicated, may hold values from 0.5 to 1.5
- w_pw2: bfloat16 [256, 256], replicated, may hold values from -0.75 to 0.75
- g_ff2: float32 [256], replicated, may hold values from 0.5 to 1.5
- w_ff2_in: bfloat16 [256, 1024], replicated, may hold values from -0.375 to 0.375
- w_ff2_out: bfloat16 [1024, 256], replicated, may hold values from -0.375 to 0.375
- g_out: float32 [256], replicated, may hold values from 0.5 to 1.5
Outputs:
- output: bfloat16 [32, 1280, 256], P('rows', 'blk')
- tokens_grad: float32 [32, 1280, 256], P('rows', 'blk')
- g_ff1_grad: float32 [256], replicated
- w_ff1_in_grad: float32 [256, 1024], replicated
- w_ff1_out_grad: float32 [1024, 256], replicated
- g_att_grad: float32 [256], replicated
- w_query_grad: float32 [256, 256], replicated
- w_key_grad: float32 [256, 256], replicated
- w_value_grad: float32 [256, 256], replicated
- w_output_grad: float32 [256, 256], replicated
- rel_table_grad: float32 [4, 16], replicated
- g_conv_grad: float32 [256], replicated
- w_pw1_grad: float32 [256, 512], replicated
- w_depth_grad: float32 [31, 256], replicated
- bn_gain_grad: float32 [256], replicated
- w_pw2_grad: float32 [256, 256], replicated
- g_ff2_grad: float32 [256], replicated
- w_ff2_in_grad: float32 [256, 1024], replicated
- w_ff2_out_grad: float32 [1024, 256], replicated
- g_out_grad: float32 [256], replicated
The draws below stay inside these ranges and needn't reach their ends.
Inputs may be any that keep to these rules, and one draw needn't show every extreme that they name: `seg_ids`: in each row the ids are 0, then 1, then 2, each a non-empty run of frames; utterance 1 begins in the row's first block of 320 frames and ends in its last block. `frame_mask`: zeros only in a run at the end of each row, inside utterance 2, which keeps at least one frame with mask 1.
All inputs are finite; a program needn't handle non-finite values.
Results may differ from the reference program's by a relative error of at most 0.019.
Values may be sent and summed in bfloat16 or wider, within the bound.
No kernel may reach another device: no remote copies, remote signals or barrier semaphores. Data moves between devices by JAX's collectives and lax.ppermute only.
A program may use at most 192 MiB of HBM per device.

```python
import jax
import jax.numpy as jnp
from jax import lax

D = 256
H = 4
HD = 64
FF = 1024
KERNEL = 31
NBUCKET = 16
FR_DEV = 320
HALF = 15
FRAMES = 1280
ROWS = 32


def utterance_bounds(key):
    first_key, second_key, padding_key, flag_key, pick_key, near_first_key, near_second_key = jax.random.split(key, 7)
    far_first = jax.random.randint(first_key, (ROWS,), 1, FR_DEV // 2 + 1)
    far_second = jax.random.randint(second_key, (ROWS,), FRAMES - FR_DEV // 2, FRAMES - FR_DEV // 4)
    padding = jax.random.randint(padding_key, (ROWS,), 1, FR_DEV // 4 + 1)
    row_number = jnp.arange(ROWS, dtype=jnp.int32)
    forced_row = jax.random.randint(pick_key, (), 0, ROWS)
    near_rows = (jax.random.randint(flag_key, (ROWS,), 0, 2) == 1) | (row_number == forced_row)
    near_first = FR_DEV - jax.random.randint(near_first_key, (ROWS,), 1, HALF)
    near_second = FRAMES - FR_DEV + jax.random.randint(near_second_key, (ROWS,), 1, min(HALF - 1, FR_DEV // 2) + 1)
    first_end = jnp.where(near_rows, near_first, far_first)
    second_end = jnp.where(near_rows, near_second, far_second)
    return (first_end, second_end, padding)


def draw_seg_ids(key, part):
    first_end, second_end, padding = utterance_bounds(key)
    positions = jnp.arange(FRAMES, dtype=jnp.int32)
    after_first = (positions[None, :] >= first_end[:, None]).astype(jnp.int32)
    after_second = (positions[None, :] >= second_end[:, None]).astype(jnp.int32)
    return after_first + after_second


def draw_frame_mask(key, part):
    first_end, second_end, padding = utterance_bounds(key)
    positions = jnp.arange(FRAMES, dtype=jnp.int32)
    return (positions[None, :] < FRAMES - padding[:, None]).astype(jnp.int32)


def draw_tokens(key, part):
    key = jax.random.fold_in(key, 5)
    noise_key, lean_key = jax.random.split(key)
    ramp = jnp.arange(FRAMES, dtype=jnp.float32) / FRAMES
    noise = jnp.clip(jax.random.normal(noise_key, (ROWS, FRAMES, D), jnp.float32), -4.0, 4.0)
    lean = jnp.clip(jax.random.normal(lean_key, (D,), jnp.float32), -4.0, 4.0)
    slope = 1.5
    return (noise + slope * ramp[None, :, None] * lean[None, None, :]).astype(jnp.bfloat16)


def steps_of(own_key, shape, shards, least, largest):
    level, own = 1.0, jax.random.fold_in(own_key, 6)
    for dim, blocks in shards:
        steps = jnp.exp(jax.random.uniform(jax.random.fold_in(own, dim), (blocks,), jnp.float32, least / len(shards), largest / len(shards)))
        level = level * jnp.repeat(steps, shape[dim] // blocks).reshape([-1 if axis == dim else 1 for axis in range(len(shape))])
    return level


def gaussian(key, dims, scale, reach, cuts=(), held_as=jnp.bfloat16):
    entries = jax.random.normal(key, dims, jnp.float32) * scale
    if len(cuts) > 0:
        entries = steps_of(key, dims, cuts, -0.22, 0.18) * entries
    return jnp.clip(entries, min=-reach, max=reach).astype(held_as)


def setup_inputs(seed: int = 0) -> dict:
    streams_of = jax.random.split(jax.random.key(seed), 23)
    return {
        "tokens": draw_tokens(jax.random.fold_in(streams_of[22], 71), 0),
        "seg_ids": draw_seg_ids(jax.random.fold_in(streams_of[22], 71), 0),
        "frame_mask": draw_frame_mask(jax.random.fold_in(streams_of[22], 71), 0),
        "cotangent": gaussian(streams_of[3], (ROWS, FRAMES, D), 1.0, 6.0, ((0, 8), (1, 4))),
        "g_ff1": jnp.clip(jax.random.uniform(streams_of[4], (D,), jnp.float32, 0.5, 1.5), 0.5, 1.5),
        "w_ff1_in": gaussian(streams_of[5], (D, FF), D ** -0.5, 0.375),
        "w_ff1_out": gaussian(streams_of[6], (FF, D), (FF // 4) ** -0.5, 0.375),
        "g_att": jnp.clip(jax.random.uniform(streams_of[7], (D,), jnp.float32, 0.5, 1.5), 0.5, 1.5),
        "w_query": gaussian(streams_of[8], (D, D), D ** -0.5, 0.375),
        "w_key": gaussian(streams_of[9], (D, D), D ** -0.5, 0.375),
        "w_value": gaussian(streams_of[10], (D, D), D ** -0.5, 0.375),
        "w_output": gaussian(streams_of[11], (D, D), (D // 8) ** -0.5, 1.0),
        "rel_table": gaussian(streams_of[12], (H, NBUCKET), 1.0, 4.0, (), jnp.float32),
        "g_conv": jnp.clip(jax.random.uniform(streams_of[13], (D,), jnp.float32, 0.5, 1.5), 0.5, 1.5),
        "w_pw1": gaussian(streams_of[14], (D, 2 * D), D ** -0.5, 0.375),
        "w_depth": gaussian(streams_of[15], (KERNEL, D), KERNEL ** -0.5, 1.0),
        "bn_gain": jnp.clip(jax.random.uniform(streams_of[16], (D,), jnp.float32, 0.5, 1.5), 0.5, 1.5),
        "w_pw2": gaussian(streams_of[17], (D, D), (D // 4) ** -0.5, 0.75),
        "g_ff2": jnp.clip(jax.random.uniform(streams_of[18], (D,), jnp.float32, 0.5, 1.5), 0.5, 1.5),
        "w_ff2_in": gaussian(streams_of[19], (D, FF), D ** -0.5, 0.375),
        "w_ff2_out": gaussian(streams_of[20], (FF, D), (FF // 4) ** -0.5, 0.375),
        "g_out": jnp.clip(jax.random.uniform(streams_of[21], (D,), jnp.float32, 0.5, 1.5), 0.5, 1.5),
    }


epsilon = 1e-05
masked_score = -1e+30
highest = lax.Precision.HIGHEST

@jax.custom_vjp
def low(v):
    return lax.optimization_barrier(v.astype(jnp.bfloat16)).astype(jnp.float32)

@jax.custom_vjp
def low_back(v):
    return v

def low_keep(v):
    return (low(v), None)

def low_pass(kept, grad):
    return (grad,)

def back_keep(v):
    return (v, None)

def back_low(kept, grad):
    return (low(grad),)
low.defvjp(low_keep, low_pass)
low_back.defvjp(back_keep, back_low)

def layer_norm(values, norm_gain):
    center = lax.optimization_barrier(jnp.mean(values, axis=-1, keepdims=True))
    shifted = values - center
    spread = lax.optimization_barrier(jnp.mean(shifted * shifted, axis=-1, keepdims=True))
    return shifted * lax.rsqrt(spread + epsilon) * norm_gain

def matmul(left_side, right_side):
    return jnp.dot(left_side, right_side, precision=highest, preferred_element_type=jnp.float32)

def feed_forward(values, norm_gain, weight_in, weight_out):
    normed = low(layer_norm(values, norm_gain))
    hidden = low_back(matmul(normed, weight_in))
    return low_back(matmul(low(jax.nn.silu(hidden)), weight_out))

def bucket_index(distance):
    levels = NBUCKET // 2
    magnitude = jnp.abs(distance)
    bucket_level = jnp.zeros(distance.shape, jnp.int32)
    for exponent in range(levels - 1):
        bucket_level = bucket_level + (magnitude >= 4 ** exponent).astype(jnp.int32)
    return bucket_level + levels * (distance > 0).astype(jnp.int32)

def attention_row(values, segment_row, live_row, norm_gain, w_query, w_key, w_value, w_output, rel_table):
    normed = low(layer_norm(values, norm_gain))

    def split_heads(weight):
        return low(low_back(matmul(normed, weight))).reshape(FRAMES, H, HD)
    queries = split_heads(w_query)
    key_heads = split_heads(w_key)
    value_heads = split_heads(w_value)
    position = jnp.arange(FRAMES, dtype=jnp.int32)
    position_bias = jnp.take(rel_table, bucket_index(position[None, :] - position[:, None]), axis=1)
    raw_scores = jnp.einsum('qhd,khd->hqk', queries, key_heads, precision=highest) * HD ** (-0.5) + position_bias
    scores = low_back(raw_scores)
    allowed = (segment_row[:, None] == segment_row[None, :]) & (live_row[None, :] == 1)
    attn_weights = jax.nn.softmax(jnp.where(allowed[None], scores, masked_score), axis=-1)
    mixed_heads = jnp.einsum('hqk,khd->qhd', low(attn_weights), value_heads, precision=highest).reshape(FRAMES, D)
    return low_back(matmul(low(low_back(mixed_heads)), w_output))

def depthwise(gated_units, segment_row, w_depth):
    padded = jnp.pad(gated_units, ((HALF, HALF), (0, 0)))
    segment_pad = jnp.pad(segment_row, (HALF, HALF), constant_values=-1)
    depth_sum = jnp.zeros((FRAMES, D), jnp.float32)
    for kernel_tap in range(KERNEL):
        same_segment = (segment_pad[kernel_tap:kernel_tap + FRAMES] == segment_row).astype(jnp.float32)
        depth_sum = depth_sum + w_depth[kernel_tap] * padded[kernel_tap:kernel_tap + FRAMES] * same_segment[:, None]
    return depth_sum

def first_part(params, tokens_row, segment_row, live_row):
    g_ff1, w_ff1_in, w_ff1_out, g_att, w_query, w_key, w_value, w_output, rel_table, g_conv, w_pw1, w_depth = params
    after_ffn = tokens_row + 0.5 * feed_forward(tokens_row, g_ff1, w_ff1_in, w_ff1_out)
    after_att = after_ffn + attention_row(after_ffn, segment_row, live_row, g_att, w_query, w_key, w_value, w_output, rel_table)
    normed = low(layer_norm(after_att, g_conv))
    gate_pair = low_back(matmul(normed, w_pw1))
    live_frames = live_row.astype(jnp.float32)[:, None]
    gated_units = low(gate_pair[:, :D] * jax.nn.sigmoid(gate_pair[:, D:]) * live_frames)
    return (after_att, low_back(depthwise(gated_units, segment_row, w_depth)))

def last_part(params, after_att, standard):
    bn_gain, w_pw2, g_ff2, w_ff2_in, w_ff2_out, g_out = params
    activation = jax.nn.silu(standard * bn_gain)
    after_conv = after_att + low_back(matmul(low(activation), w_pw2))
    after_ffn = after_conv + 0.5 * feed_forward(after_conv, g_ff2, w_ff2_in, w_ff2_out)
    return layer_norm(after_ffn, g_out)

def forward(tokens, seg_ids, frame_mask, weights):
    first_params = weights[:12]
    last_params = weights[12:]

    def first_row(row_slice):
        return first_part(first_params, row_slice[0], row_slice[1], row_slice[2])
    after_att, depth_out = lax.map(jax.checkpoint(first_row), (tokens, seg_ids, frame_mask))
    live_frames = frame_mask.astype(jnp.float32)[..., None]
    frame_count = jnp.sum(live_frames)
    center = lax.optimization_barrier(jnp.sum(depth_out * live_frames, axis=(0, 1))) / frame_count
    spread = lax.optimization_barrier(jnp.sum(depth_out * depth_out * live_frames, axis=(0, 1))) / frame_count - center * center
    standard = (depth_out - center) * lax.rsqrt(spread + epsilon)

    def last_row(row_slice):
        return last_part(last_params, row_slice[0], row_slice[1])
    return lax.map(jax.checkpoint(last_row), (after_att, standard))

def reference(tokens, seg_ids, frame_mask, cotangent, g_ff1, w_ff1_in, w_ff1_out, g_att, w_query, w_key, w_value, w_output, rel_table, g_conv, w_pw1, w_depth, bn_gain, w_pw2, g_ff2, w_ff2_in, w_ff2_out, g_out):
    weights = tuple((weight_arg.astype(jnp.float32) for weight_arg in (g_ff1, w_ff1_in, w_ff1_out, g_att, w_query, w_key, w_value, w_output, rel_table, g_conv, w_pw1, w_depth, bn_gain, w_pw2, g_ff2, w_ff2_in, w_ff2_out, g_out)))

    def closed(tokens_float, weights_float):
        return forward(tokens_float, seg_ids, frame_mask, weights_float)
    result, pullback = jax.vjp(closed, tokens.astype(jnp.float32), weights)
    token_grad, grads = pullback(cotangent.astype(jnp.float32))
    return (result.astype(jnp.bfloat16), token_grad, grads[0], grads[1], grads[2], grads[3], grads[4], grads[5], grads[6], grads[7], grads[8], grads[9], grads[10], grads[11], grads[12], grads[13], grads[14], grads[15], grads[16], grads[17])
```

```python
import functools
import math

import jax
import jax.numpy as jnp
from jax import lax
from jax.experimental import pallas as pl
from jax.experimental.pallas import tpu as pltpu
from jax.sharding import PartitionSpec as P

H = 4
HD = 64
D = 256
FF = 1024
KERNEL = 31
HALF = KERNEL // 2
NBUCKET = 16

epsilon = 1e-05
masked_score = -1e30

f32 = jnp.float32
bf16 = jnp.bfloat16
LOG2E = math.log2(math.e)
QT = 256
GAP = 16
EXTRA = 16
SAFE_EXPONENT = 60.0
VMEM_LIMIT = 60 * 1024 * 1024


def mm(a, b):
    return lax.dot_general(a, b, (((1,), (0,)), ((), ())), preferred_element_type=f32)


def mm_nt(a, b):
    return lax.dot_general(a, b, (((1,), (1,)), ((), ())), preferred_element_type=f32)


def turned(x):
    return x.astype(f32).T.astype(bf16)


def sigmoid(x):
    return 0.5 + 0.5 * jnp.tanh(0.5 * x)


def norm_hat(v):
    center = jnp.mean(v, axis=-1, keepdims=True)
    shifted = v - center
    spread = jnp.mean(shifted * shifted, axis=-1, keepdims=True)
    inverse = lax.rsqrt(spread + epsilon)
    return shifted * inverse, inverse


def norm_back(upstream, gain, hat, inverse):
    inner = upstream * gain
    inner_mean = jnp.mean(inner, axis=-1, keepdims=True)
    inner_dot = jnp.mean(inner * hat, axis=-1, keepdims=True)
    return inverse * (inner - inner_mean - hat * inner_dot)


def col_sum(x):
    rows, width = x.shape
    return jnp.sum(x.reshape(rows // 8, 8, width), axis=0)


def bucket_ranges():
    levels = NBUCKET // 2
    big = 1 << 30
    edges = [0] + [4**k for k in range(levels - 1)] + [big]
    out = []
    for level in range(levels - 1, 0, -1):
        out.append((level, 1 - edges[level + 1], -edges[level]))
    out.append((0, 0, 0))
    for level in range(1, levels):
        out.append((levels + level, edges[level], edges[level + 1] - 1))
    return out


def tile_buckets(offset):
    low, high = offset * QT - (QT - 1), offset * QT + (QT - 1)
    return [(b, lo) for b, lo, hi in bucket_ranges() if lo <= high and hi >= low]


def mixed_offsets(tiles):
    return [o for o in range(1 - tiles, tiles) if len(tile_buckets(o)) > 1]


def tile_distance(offset):
    row = lax.broadcasted_iota(jnp.int32, (QT, QT), 0)
    col = lax.broadcasted_iota(jnp.int32, (QT, QT), 1)
    return col - row + offset * QT


def frame_index(start, rows, width):
    return (lax.broadcasted_iota(jnp.int32, (rows, width), 0) + start).astype(f32)


def rows_at(start, count, unit):
    return pl.ds(pl.multiple_of(start, unit), count)


def bias_kernel(tiles, table_ref, bias_ref):
    def head(h, carry):
        for k, offset in enumerate(mixed_offsets(tiles)):
            d = tile_distance(offset)
            found = tile_buckets(offset)
            value = jnp.full((QT, QT), table_ref[h, found[0][0]], f32)
            for b, lo in found[1:]:
                value = jnp.where(d >= lo, table_ref[h, b], value)
            bias_ref[h, k] = value * LOG2E
        return carry

    lax.fori_loop(0, H, head, 0)


def place_pieces(me_ref, piece_refs, target_ref, frames):
    for m, piece in enumerate(piece_refs):
        start = (me_ref[0] ^ m) * frames
        target_ref[rows_at(start, frames, 64), :] = piece[0:frames, :]


def take_pieces(me_ref, source_ref, piece_refs, frames):
    for m, piece in enumerate(piece_refs):
        start = (me_ref[0] ^ m) * frames
        piece[...] = source_ref[rows_at(start, frames, 64), :].astype(piece.dtype)


def key_features(start, rows, ends):
    first_end, second_end, live_end = (e[:, :128] for e in ends)
    t = frame_index(start, rows, 128)
    lane = lax.broadcasted_iota(jnp.int32, (rows, 128), 1)
    code = jnp.where(t < first_end, 0, jnp.where(t < second_end, 1, 2))
    code = jnp.where(t < live_end, code, -1)
    barred = jnp.where((lane < 3) & (code != lane), masked_score, 0.0)
    return jnp.where((lane >= 3) & (lane < 6), 1.0, barred).astype(bf16)


def query_features(start, rows, ends):
    first_end, second_end, live_end = (e[:, :128] for e in ends)
    t = frame_index(start, rows, 128)
    lane = lax.broadcasted_iota(jnp.int32, (rows, 128), 1)
    code = jnp.where(t < first_end, 0, jnp.where(t < second_end, 1, 2))
    return jnp.where(code == lane, 1.0, 0.0)


def three_parts(x):
    top = x.astype(bf16).astype(f32)
    middle = (x - top).astype(bf16).astype(f32)
    return top, middle, x - top - middle


def spread_gaps(plain_ref, gap_ref, length, ends):
    first_end, second_end, _ = (e[:, :128] for e in ends)
    total = length + 4 * GAP
    step = GAP * 4

    def chunk(k, carry):
        start = k * step
        g = frame_index(start, step, 128)
        for c in range(2):
            a = plain_ref[c, rows_at(start + 2 * GAP, step, 16), :]
            b = plain_ref[c, rows_at(start + GAP, step, 16), :]
            d = plain_ref[c, rows_at(start, step, 16), :]
            in_first = (g >= GAP) & (g - GAP < first_end)
            in_second = (g - 2 * GAP >= first_end) & (g - 2 * GAP < second_end)
            in_third = (g - 3 * GAP >= second_end) & (g - 3 * GAP < length)
            value = jnp.where(in_first, a, jnp.where(in_second, b, jnp.where(in_third, d, 0.0)))
            gap_ref[c, rows_at(start, step, 16), :] = value
        return carry

    lax.fori_loop(0, total // step, chunk, 0)


def close_gaps(gap_ref, start, rows, ends):
    first_end, second_end, _ = (e[:, :128] for e in ends)
    t = frame_index(start, rows, 128)
    halves = []
    for c in range(2):
        a = gap_ref[c, rows_at(start + GAP, rows, 16), :]
        b = gap_ref[c, rows_at(start + 2 * GAP, rows, 16), :]
        d = gap_ref[c, rows_at(start + 3 * GAP, rows, 16), :]
        halves.append(jnp.where(t < first_end, a, jnp.where(t < second_end, b, d)))
    return jnp.concatenate(halves, axis=1)


CONV_ROWS = 32


def convolve(gap_ref, out_ref, taps_ref, length, mirrored):
    span = length + 2 * GAP

    for c in range(2):

        def chunk(k, carry, c=c):
            start = GAP + k * CONV_ROWS
            total = jnp.zeros((CONV_ROWS, 128), f32)
            for j in range(KERNEL):
                shift = HALF - j if mirrored else j - HALF
                part = gap_ref[c, pl.ds(start + shift, CONV_ROWS), :]
                total = total + part * taps_ref[c, j : j + 1, :]
            out_ref[c, rows_at(start, CONV_ROWS, 16), :] = total
            return carry

        lax.fori_loop(0, span // CONV_ROWS, chunk, 0)


def correlate(grad_ref, unit_ref, out_ref, length):
    span = length + 2 * GAP
    for c in range(2):

        def chunk(k, carry, c=c):
            start = GAP + k * 8
            g = grad_ref[c, rows_at(start, 8, 8), :]
            return tuple(
                total + g * unit_ref[c, pl.ds(start + j - HALF, 8), :] for j, total in enumerate(carry)
            )

        sums = lax.fori_loop(
            0, span // 8, chunk, tuple(jnp.zeros((8, 128), f32) for _ in range(KERNEL))
        )
        for j in range(KERNEL):
            out_ref[j : j + 1, 128 * c : 128 * c + 128] = jnp.sum(sums[j], axis=0, keepdims=True)
    out_ref[KERNEL : KERNEL + 1, :] = jnp.zeros((1, 2 * 128), f32)


def read_ends(ends_ref):
    return ends_ref[0:1, :], ends_ref[1:2, :], ends_ref[2:3, :]


def attend_tile(q2_ref, fq_ref, h, qt, v2_ref, k2_ref, fk_ref, bias_ref, table_ref, tiles, with_max):
    rows = slice(qt * QT, (qt + 1) * QT)
    qa = jnp.concatenate([q2_ref[h, rows, :], fq_ref[rows, :].astype(bf16)], axis=1)
    offsets = mixed_offsets(tiles)

    def scores(kt):
        cols = slice(kt * QT, (kt + 1) * QT)
        ka = jnp.concatenate([k2_ref[h, cols, :], fk_ref[cols, :]], axis=1)
        s = mm_nt(qa, ka)
        o = kt - qt
        if o in offsets:
            return s + bias_ref[h, offsets.index(o)]
        return s + table_ref[h, tile_buckets(o)[0][0]] * LOG2E

    top = None
    if with_max:
        for kt in range(tiles):
            m = jnp.max(scores(kt), axis=1, keepdims=True)
            top = m if top is None else jnp.maximum(top, m)
    total = None
    for kt in range(tiles):
        s = scores(kt)
        if with_max:
            s = s - top
        p = jnp.exp2(s).astype(bf16)
        part = mm(p, v2_ref[h, kt * QT : (kt + 1) * QT, :])
        total = part if total is None else total + part
    return total, top


def kernel_a(
    tiles,
    me_ref,
    table_ref,
    piece0,
    piece1,
    piece2,
    piece3,
    bias_ref,
    g_ff1_ref,
    w_in_ref,
    w_out_ref,
    g_att_ref,
    wq2_ref,
    wk2_ref,
    wv2_ref,
    w_o_ref,
    g_conv_ref,
    w_pw1_ref,
    taps_ref,
    tok_ref,
    ends_ref,
    s1_ref,
    k2_ref,
    v2_ref,
    q2_ref,
    lse_ref,
    mixed_ref,
    s2_ref,
    gap_ref,
    depth_ref,
    sums_ref,
    fq_ref,
    fk_ref,
    fast_ref,
    plain_ref,
    conv_ref,
):
    pieces = (piece0, piece1, piece2, piece3)
    length = tiles * QT
    frames = length // len(pieces)
    place_pieces(me_ref, pieces, tok_ref, frames)
    extra = sum(p[frames : frames + EXTRA, :].astype(f32) for p in pieces)
    first_end = 16.0 * extra[0:1, :] + extra[1:2, :]
    second_end = first_end + 16.0 * extra[2:3, :] + extra[3:4, :]
    live_end = 16.0 * extra[4:5, :] + extra[5:6, :]
    ends_ref[0:1, :] = first_end
    ends_ref[1:2, :] = second_end
    ends_ref[2:3, :] = live_end
    ends_ref[3:8, :] = jnp.zeros((5, D), f32)
    ends = (first_end, second_end, live_end)

    scale = LOG2E * HD**-0.5

    def front(i, carry):
        at = rows_at(i * QT, QT, QT)
        x = tok_ref[at, :].astype(f32)
        hat, _ = norm_hat(x)
        n1 = (hat * g_ff1_ref[...]).astype(bf16)
        hidden = mm(n1, w_in_ref[...])
        act = (hidden * sigmoid(hidden)).astype(bf16)
        s1 = x + 0.5 * mm(act, w_out_ref[...])
        s1_ref[at, :] = s1
        hat, _ = norm_hat(s1)
        n2 = (hat * g_att_ref[...]).astype(bf16)
        lane = lax.broadcasted_iota(jnp.int32, (QT, 128), 1)
        q_top, k_top = carry
        q_all = mm(n2, wq2_ref[...]).astype(bf16).astype(f32) * scale
        k_all = mm(n2, wk2_ref[...]).astype(bf16)
        v_all = mm(n2, wv2_ref[...])
        for h in range(H):
            cols = slice(128 * h, 128 * h + 128)
            q = q_all[:, cols]
            high = q.astype(bf16)
            low = (q - high.astype(f32)).astype(bf16)
            q2_ref[h, at, :] = jnp.where(lane < HD, high.astype(f32), low.astype(f32)).astype(bf16)
            k2_ref[h, at, :] = k_all[:, cols]
            ones = (lane >= HD) & (lane < HD + 3) if h % 2 == 0 else lane < 3
            v2_ref[h, at, :] = jnp.where(ones, 1.0, v_all[:, cols]).astype(bf16)
            q_top = jnp.maximum(q_top, jnp.max(jnp.sum(q * q, axis=1, keepdims=True), axis=0, keepdims=True))
            k = k_all[:, cols].astype(f32)
            k_top = jnp.maximum(k_top, jnp.max(jnp.sum(k * k, axis=1, keepdims=True), axis=0, keepdims=True))
        fq_ref[at, :] = query_features(i * QT, QT, ends)
        fk_ref[at, :] = key_features(i * QT, QT, ends)
        return q_top, k_top

    zero = jnp.zeros((1, 1), f32)
    q_top, k_top = lax.fori_loop(0, tiles, front, (zero, zero))
    bound = jnp.sqrt(q_top * 0.5) * jnp.sqrt(k_top * 0.5)
    fast_ref[0] = jnp.max(jnp.where(bound < SAFE_EXPONENT, 1, 0))

    def attend(with_max):
        def pair(g, carry):
            lane = lax.broadcasted_iota(jnp.int32, (QT, 128), 1)
            for qt in range(tiles):
                rows = slice(qt * QT, (qt + 1) * QT)
                halves = []
                for parity in range(2):
                    h = 2 * g + parity
                    total, top = attend_tile(
                        q2_ref, fq_ref, h, qt, v2_ref, k2_ref, fk_ref, bias_ref, table_ref, tiles, with_max
                    )
                    one = HD if parity == 0 else 0
                    denominator = total[:, one : one + 1]
                    log_total = jnp.log2(denominator)
                    if with_max:
                        log_total = log_total + top
                    halves.append(total / denominator)
                    high, middle, low = three_parts(-log_total)
                    features = fq_ref[rows, :]
                    features = jnp.where(lane == 3, high, features)
                    features = jnp.where(lane == 4, middle, features)
                    features = jnp.where(lane == 5, low, features)
                    lse_ref[h, rows, :] = features.astype(bf16)
                mixed_ref[g, rows, :] = jnp.where(lane < HD, halves[0], halves[1])
            return carry

        lax.fori_loop(0, H // 2, pair, 0)

    @pl.when(fast_ref[0] == 1)
    def _():
        attend(False)

    @pl.when(fast_ref[0] != 1)
    def _():
        attend(True)

    def gate(i, carry):
        at = rows_at(i * QT, QT, QT)
        mixed = jnp.concatenate([mixed_ref[0, at, :], mixed_ref[1, at, :]], axis=1)
        s2 = s1_ref[at, :] + mm(mixed.astype(bf16), w_o_ref[...])
        s2_ref[at, :] = s2
        hat, _ = norm_hat(s2)
        n3 = (hat * g_conv_ref[...]).astype(bf16)
        pair = mm(n3, w_pw1_ref[...])
        live = frame_index(i * QT, QT, D) < live_end
        units = jnp.where(live, pair[:, :D] * sigmoid(pair[:, D:]), 0.0).astype(bf16).astype(f32)
        put = rows_at(i * QT + 3 * GAP, QT, 16)
        plain_ref[0, put, :] = units[:, :128]
        plain_ref[1, put, :] = units[:, 128:]
        return carry

    lax.fori_loop(0, tiles, gate, 0)
    spread_gaps(plain_ref, gap_ref, length, ends)
    convolve(gap_ref, conv_ref, taps_ref, length, False)

    def collect(i, carry):
        total, squares = carry
        at = rows_at(i * QT, QT, QT)
        depth = close_gaps(conv_ref, i * QT, QT, ends)
        depth_ref[at, :] = depth
        kept = jnp.where(frame_index(i * QT, QT, D) < live_end, depth, 0.0)
        return total + col_sum(kept), squares + col_sum(kept * kept)

    empty = jnp.zeros((8, D), f32)
    total, squares = lax.fori_loop(0, tiles, collect, (empty, empty))
    sums_ref[0:1, :] = jnp.sum(total, axis=0, keepdims=True)
    sums_ref[1:2, :] = jnp.sum(squares, axis=0, keepdims=True)
    sums_ref[2:3, :] = live_end
    sums_ref[3:8, :] = jnp.zeros((5, D), f32)


def batch_norm_terms(sums_ref):
    count = sums_ref[2:3, :]
    center = sums_ref[0:1, :] / count
    spread = sums_ref[1:2, :] / count - center * center
    return count, center, lax.rsqrt(spread + epsilon)


def kernel_b(
    tiles,
    me_ref,
    cot0,
    cot1,
    cot2,
    cot3,
    sums_ref,
    depth_ref,
    s2_ref,
    bn_gain_ref,
    w_pw2_ref,
    g_ff2_ref,
    w_in_ref,
    w_out_ref,
    g_out_ref,
    out0,
    out1,
    out2,
    out3,
    grad3_ref,
    bngrad_ref,
    sums2_ref,
    big_ref,
    small_ref,
    cot_ref,
    out_ref,
    dw_in_ref,
    dw_out_ref,
    dw_pw2_ref,
):
    frames = tiles * QT // 4
    place_pieces(me_ref, (cot0, cot1, cot2, cot3), cot_ref, frames)
    dw_in_ref[...] = jnp.zeros_like(dw_in_ref)
    dw_out_ref[...] = jnp.zeros_like(dw_out_ref)
    dw_pw2_ref[...] = jnp.zeros_like(dw_pw2_ref)
    _, center, inverse = batch_norm_terms(sums_ref)
    bn_gain = bn_gain_ref[...]

    def step(i, carry):
        g_out_sum, g_ff2_sum, bn_sum, bn_dot = carry
        at = rows_at(i * QT, QT, QT)
        standard = (depth_ref[at, :] - center) * inverse
        pre = standard * bn_gain
        logistic3 = sigmoid(pre)
        act3 = (pre * logistic3).astype(bf16)
        s3 = s2_ref[at, :] + mm(act3, w_pw2_ref[...])
        hat3, inv3 = norm_hat(s3)
        n4 = (hat3 * g_ff2_ref[...]).astype(bf16)
        hidden = mm(n4, w_in_ref[...])
        logistic = sigmoid(hidden)
        act4 = (hidden * logistic).astype(bf16)
        s4 = s3 + 0.5 * mm(act4, w_out_ref[...])
        hat4, inv4 = norm_hat(s4)
        out_ref[at, :] = (hat4 * g_out_ref[...]).astype(bf16)
        cot = cot_ref[at, :].astype(f32)
        g_out_sum = g_out_sum + col_sum(cot * hat4)
        grad4 = norm_back(cot, g_out_ref[...], hat4, inv4)
        out4 = (0.5 * grad4).astype(bf16)
        dw_out_ref[...] += mm(turned(out4), act4)
        slope = logistic * (1.0 + hidden * (1.0 - logistic))
        hid4 = (mm_nt(out4, w_out_ref[...]) * slope).astype(bf16)
        dw_in_ref[...] += mm(turned(n4), hid4)
        up = mm_nt(hid4, w_in_ref[...])
        g_ff2_sum = g_ff2_sum + col_sum(up * hat3)
        grad3 = grad4 + norm_back(up, g_ff2_ref[...], hat3, inv3)
        grad3_ref[at, :] = grad3
        out3 = grad3.astype(bf16)
        dw_pw2_ref[...] += mm(turned(act3), out3)
        bngrad = mm_nt(out3, w_pw2_ref[...]) * (logistic3 * (1.0 + pre * (1.0 - logistic3)))
        bngrad_ref[at, :] = bngrad
        return g_out_sum, g_ff2_sum, bn_sum + col_sum(bngrad), bn_dot + col_sum(bngrad * standard)

    empty = jnp.zeros((8, D), f32)
    sums = lax.fori_loop(0, tiles, step, (empty,) * 4)
    g_out_sum, g_ff2_sum, bn_sum, bn_dot = (jnp.sum(s, axis=0, keepdims=True) for s in sums)
    sums2_ref[0:1, :] = bn_sum
    sums2_ref[1:2, :] = bn_dot
    sums2_ref[2:8, :] = jnp.zeros((6, D), f32)
    small_ref[0:1, :] = g_ff2_sum
    small_ref[1:2, :] = g_out_sum
    small_ref[2:8, :] = jnp.zeros((6, D), f32)
    big_ref[0:FF, :] = turned_wide(dw_out_ref)
    for c in range(FF // D):
        big_ref[FF + c * D : FF + (c + 1) * D, :] = dw_in_ref[:, c * D : (c + 1) * D].astype(big_ref.dtype)
    big_ref[2 * FF : 2 * FF + D, :] = dw_pw2_ref[...].astype(big_ref.dtype)
    take_pieces(me_ref, out_ref, (out0, out1, out2, out3), frames)


def turned_wide(ref):
    return jnp.concatenate([ref[:, c * D : (c + 1) * D].T for c in range(ref.shape[1] // D)], axis=0).astype(bf16)


def kernel_c(
    tiles,
    me_ref,
    table_ref,
    sums_ref,
    sums2_ref,
    tok_ref,
    ends_ref,
    s1_ref,
    k2_ref,
    v2_ref,
    q2_ref,
    lse_ref,
    mixed_ref,
    s2_ref,
    gap_ref,
    depth_ref,
    grad3_ref,
    bngrad_ref,
    bias_ref,
    g_ff1_ref,
    w_ff1_in_ref,
    w_ff1_out_ref,
    g_att_ref,
    w_q_ref,
    w_k_ref,
    w_v_ref,
    w_o_ref,
    g_conv_ref,
    w_pw1_ref,
    taps_ref,
    bn_gain_ref,
    big_b_ref,
    small_b_ref,
    piece0,
    piece1,
    piece2,
    piece3,
    kept_ref,
    sent_ref,
    big_ref,
    small_ref,
    plain_ref,
    dgap_ref,
    conv_ref,
    grad_ref,
    do_ref,
    dot_ref,
    qt_ref,
    fk_ref,
    dq_ref,
    dkt_ref,
    dvt_ref,
    acc_ref,
    taps_grad_ref,
    dw_in_ref,
    dw_out_ref,
    dw_o_ref,
    dw_pw1_ref,
    dw_q_ref,
    dw_k_ref,
    dw_v_ref,
    out_ref,
):
    length = tiles * QT
    frames = length // 4
    ends = read_ends(ends_ref)
    live_end = ends[2]
    count, center, inverse = batch_norm_terms(sums_ref)
    bn_gain = bn_gain_ref[...]
    e_total = sums2_ref[0:1, :] * bn_gain
    dot_total = sums2_ref[1:2, :]
    for ref in (dw_in_ref, dw_out_ref, dw_o_ref, dw_pw1_ref, dw_q_ref, dw_k_ref, dw_v_ref):
        ref[...] = jnp.zeros_like(ref)


    def batch_back(i, carry):
        at = rows_at(i * QT, QT, QT)
        standard = (depth_ref[at, :] - center) * inverse
        e = bngrad_ref[at, :] * bn_gain
        share = jnp.where(frame_index(i * QT, QT, D) < live_end, 1.0, 0.0) / count
        dg = inverse * (e - share * e_total - share * standard * bn_gain * dot_total)
        dg = dg.astype(bf16).astype(f32)
        put = rows_at(i * QT + 3 * GAP, QT, 16)
        plain_ref[0, put, :] = dg[:, :128]
        plain_ref[1, put, :] = dg[:, 128:]
        return carry

    lax.fori_loop(0, tiles, batch_back, 0)
    spread_gaps(plain_ref, dgap_ref, length, ends)
    convolve(dgap_ref, conv_ref, taps_ref, length, True)
    correlate(dgap_ref, gap_ref, taps_grad_ref, length)

    def gate_back(i, carry):
        g_conv_sum = carry
        at = rows_at(i * QT, QT, QT)
        hat, inv = norm_hat(s2_ref[at, :])
        n3 = (hat * g_conv_ref[...]).astype(bf16)
        pair = mm(n3, w_pw1_ref[...])
        first, logistic = pair[:, :D], sigmoid(pair[:, D:])
        live = frame_index(i * QT, QT, D) < live_end
        ug = jnp.where(live, close_gaps(conv_ref, i * QT, QT, ends), 0.0) * logistic
        pairgrad = jnp.concatenate([ug, ug * first * (1.0 - logistic)], axis=1).astype(bf16)
        dw_pw1_ref[...] += mm(turned(n3), pairgrad)
        up = mm_nt(pairgrad, w_pw1_ref[...])
        g_conv_sum = g_conv_sum + col_sum(up * hat)
        grad2 = grad3_ref[at, :] + norm_back(up, g_conv_ref[...], hat, inv)
        grad_ref[at, :] = grad2
        out2 = grad2.astype(bf16)
        mixed = jnp.concatenate([mixed_ref[0, at, :], mixed_ref[1, at, :]], axis=1)
        dw_o_ref[...] += mm(turned(mixed), out2)
        mixgrad = mm_nt(out2, w_o_ref[...]).astype(bf16)
        dot_ref[:, at] = turned(mixgrad)
        product = mixgrad.astype(f32) * mixed
        lane = lax.broadcasted_iota(jnp.int32, (QT, 128), 1)
        for h in range(H):
            cols = slice(128 * (h // 2), 128 * (h // 2) + 128)
            own = lane < HD if h % 2 == 0 else lane >= HD
            delta = jnp.sum(jnp.where(own, product[:, cols], 0.0), axis=1, keepdims=True)
            high, middle, low = three_parts(-delta)
            base = HD if h % 2 == 0 else 0
            side = jnp.where(lane == base, high, 0.0)
            side = jnp.where(lane == base + 1, middle, side)
            side = jnp.where(lane == base + 2, low, side)
            do_ref[h, at, :] = jnp.where(own, mixgrad[:, cols].astype(f32), side).astype(bf16)
        hat, _ = norm_hat(s1_ref[at, :])
        n2 = (hat * g_att_ref[...]).astype(bf16)
        qt_ref[:, at] = turned(mm(n2, w_q_ref[...]).astype(bf16))
        fk_ref[at, :] = key_features(i * QT, QT, ends)
        return g_conv_sum

    empty = jnp.zeros((8, D), f32)
    g_conv_sum = lax.fori_loop(0, tiles, gate_back, empty)


    offsets = mixed_offsets(tiles)

    def head(h, carry):
        slot = lax.rem(h, 2)
        dkt_ref[rows_at(h * HD, HD, HD), :] = jnp.zeros((HD, length), f32)
        dvt_ref[rows_at(h * HD, HD, HD), :] = jnp.zeros((HD, length), f32)
        flat = {}
        started = set()
        for qt in range(tiles):
            rows = slice(qt * QT, (qt + 1) * QT)
            qa = jnp.concatenate([q2_ref[h, rows, :], lse_ref[h, rows, :]], axis=1)
            do = do_ref[h, rows, :]
            q_turned = qt_ref[rows_at(h * HD, HD, HD), rows]
            do_turned = dot_ref[rows_at(h * HD, HD, HD), rows]
            dq = None
            for kt in range(tiles):
                cols = slice(kt * QT, (kt + 1) * QT)
                ka = jnp.concatenate([k2_ref[h, cols, :], fk_ref[cols, :]], axis=1)
                s = mm_nt(qa, ka)
                o = kt - qt
                if o in offsets:
                    s = s + bias_ref[h, offsets.index(o)]
                else:
                    s = s + table_ref[h, tile_buckets(o)[0][0]] * LOG2E
                p = jnp.exp2(s)
                ds = p * mm_nt(do, v2_ref[h, cols, :])
                if o in offsets:
                    k = offsets.index(o)
                    if k in started:
                        acc_ref[k] += ds
                    else:
                        acc_ref[k] = ds
                        started.add(k)
                else:
                    b = tile_buckets(o)[0][0]
                    flat[b] = flat[b] + col_sum(ds) if b in flat else col_sum(ds)
                p, ds = p.astype(bf16), ds.astype(bf16)
                part = mm(ds, k2_ref[h, cols, :])
                dq = part if dq is None else dq + part
                dkt_ref[rows_at(h * HD, HD, HD), cols] += mm(q_turned, ds)
                dvt_ref[rows_at(h * HD, HD, HD), cols] += mm(do_turned, p)
            dq_ref[h, rows, :] = dq
        table_row = jnp.zeros((1, D), f32)
        lane = lax.broadcasted_iota(jnp.int32, (1, D), 1)
        for k, o in enumerate(offsets):
            d = tile_distance(o)
            value = acc_ref[k]
            found = tile_buckets(o)
            tails = [col_sum(jnp.where(d >= lo, value, 0.0)) for _, lo in found[1:]]
            tails = [col_sum(value)] + tails
            for n, (b, _) in enumerate(found):
                part = tails[n] - tails[n + 1] if n + 1 < len(found) else tails[n]
                flat[b] = flat[b] + part if b in flat else part
        for b, part in flat.items():
            table_row = jnp.where(lane == b, jnp.sum(part), table_row)
        small_ref[pl.ds(h + 4, 1), :] = table_row
        return carry

    small_ref[...] = jnp.zeros_like(small_ref)
    lax.fori_loop(0, H, head, 0)


    def front_back(i, carry):
        g_att_sum, g_ff1_sum = carry
        at = rows_at(i * QT, QT, QT)
        lane = lax.broadcasted_iota(jnp.int32, (QT, 128), 1)
        dq = jnp.concatenate(
            [jnp.where(lane < HD, dq_ref[2 * g, at, :], dq_ref[2 * g + 1, at, :]) for g in range(H // 2)], axis=1
        )
        dq = (dq * HD**-0.5).astype(bf16)
        dk = (dkt_ref[:, at] * HD**-0.5).T.astype(bf16)
        dv = dvt_ref[:, at].T.astype(bf16)
        s1 = s1_ref[at, :]
        hat2, inv2 = norm_hat(s1)
        n2 = turned((hat2 * g_att_ref[...]).astype(bf16))
        dw_q_ref[...] += mm(n2, dq)
        dw_k_ref[...] += mm(n2, dk)
        dw_v_ref[...] += mm(n2, dv)
        attgrad = mm_nt(dq, w_q_ref[...]) + mm_nt(dk, w_k_ref[...]) + mm_nt(dv, w_v_ref[...])
        g_att_sum = g_att_sum + col_sum(attgrad * hat2)
        grad1 = grad_ref[at, :] + norm_back(attgrad, g_att_ref[...], hat2, inv2)
        out1 = (0.5 * grad1).astype(bf16)
        x = tok_ref[at, :].astype(f32)
        hat1, inv1 = norm_hat(x)
        n1 = (hat1 * g_ff1_ref[...]).astype(bf16)
        hidden = mm(n1, w_ff1_in_ref[...])
        logistic = sigmoid(hidden)
        act1 = (hidden * logistic).astype(bf16)
        dw_out_ref[...] += mm(turned(out1), act1)
        slope = logistic * (1.0 + hidden * (1.0 - logistic))
        hid1 = (mm_nt(out1, w_ff1_out_ref[...]) * slope).astype(bf16)
        dw_in_ref[...] += mm(turned(n1), hid1)
        up = mm_nt(hid1, w_ff1_in_ref[...])
        g_ff1_sum = g_ff1_sum + col_sum(up * hat1)
        out_ref[at, :] = grad1 + norm_back(up, g_ff1_ref[...], hat1, inv1)
        return g_att_sum, g_ff1_sum

    g_att_sum, g_ff1_sum = lax.fori_loop(0, tiles, front_back, (empty, empty))
    for k, s in enumerate((g_ff1_sum, g_att_sum, g_conv_sum)):
        small_ref[k : k + 1, :] = jnp.sum(s, axis=0, keepdims=True)
    small_ref[8 : 8 + KERNEL + 1, :] = taps_grad_ref[...]
    big_ref[0:FF, :] = turned_wide(dw_out_ref)
    for c in range(FF // D):
        big_ref[FF + c * D : FF + (c + 1) * D, :] = dw_in_ref[:, c * D : (c + 1) * D].astype(bf16)
    base = 2 * FF
    for k, ref in enumerate((dw_q_ref, dw_k_ref, dw_v_ref, dw_o_ref)):
        big_ref[base + k * D : base + (k + 1) * D, :] = ref[...].astype(bf16)
    base = 2 * FF + 4 * D
    for c in range(2):
        big_ref[base + c * D : base + (c + 1) * D, :] = dw_pw1_ref[:, c * D : (c + 1) * D].astype(bf16)
    base = BIG_C
    big_ref[base : base + BIG_B, :] = big_b_ref[...]
    base = BIG_C + BIG_B
    big_ref[base : base + SMALL_C, :] = small_ref[...].astype(bf16)
    big_ref[base + SMALL_C : base + SMALL_C + SMALL_B, :] = small_b_ref[...].astype(bf16)
    used = base + SMALL_C + SMALL_B
    big_ref[used:, :] = jnp.zeros((big_ref.shape[0] - used, D), bf16)
    half = big_ref.shape[0] // 2
    side = me_ref[1]
    kept_ref[...] = big_ref[rows_at(side * half, half, half), :]
    sent_ref[...] = big_ref[rows_at((1 - side) * half, half, half), :]
    take_pieces(me_ref, out_ref, (piece0, piece1, piece2, piece3), frames)


def swap(x, axis, bit):
    size = lax.axis_size(axis)
    return lax.ppermute(x, axis, [(i, i ^ bit) for i in range(size)])


def doubling_steps():
    steps = []
    for axis in ("rows", "blk"):
        size = lax.axis_size(axis)
        bit = 1
        while bit < size:
            steps.append((axis, bit))
            bit *= 2
    return steps


def sum_everywhere(x):
    for axis, bit in doubling_steps():
        x = x + swap(x, axis, bit)
    return x


def to_pieces(x, me):
    own = lax.dynamic_index_in_dim(x, me, 0, keepdims=False)
    pieces = [own]
    for m in range(1, x.shape[0]):
        pieces.append(swap(lax.dynamic_index_in_dim(x, me ^ m, 0, keepdims=False), "blk", m))
    return pieces


def from_pieces(pieces):
    return [pieces[0]] + [swap(p, "blk", m) for m, p in enumerate(pieces) if m > 0]


def keep_half(x, axis, bit):
    half = x.shape[0] // 2
    side = (lax.axis_index(axis) // bit) % 2
    kept = lax.dynamic_slice_in_dim(x, side * half, half, 0)
    sent = lax.dynamic_slice_in_dim(x, (1 - side) * half, half, 0)
    got = swap(sent.astype(bf16), axis, bit)
    return kept.astype(f32) + got.astype(f32)


def join_half(x, axis, bit):
    side = (lax.axis_index(axis) // bit) % 2
    got = swap(x, axis, bit)
    return jnp.where(side == 0, jnp.concatenate([x, got]), jnp.concatenate([got, x]))


def reduce_gradients(kept, sent, token_grads):
    got = swap(sent, "rows", 1)
    got, token_grads = lax.optimization_barrier((got, token_grads))
    token_grads = from_pieces(token_grads)
    x = kept.astype(f32) + got.astype(f32)
    half = x.shape[0] // 2
    a, b = x[:half], x[half:]
    a_steps = (("rows", 2), ("rows", 4), ("blk", 2), ("blk", 1))
    b_steps = (("rows", 4), ("rows", 2), ("blk", 2), ("blk", 1))
    for k, (sa, sb) in enumerate(zip(a_steps, b_steps)):
        if k == 2:
            a, b, token_grads = lax.optimization_barrier((a, b, token_grads))
        a, b = keep_half(a, *sa), keep_half(b, *sb)
    a, b = a.astype(bf16), b.astype(bf16)
    for sa, sb in zip(a_steps[::-1], b_steps[::-1]):
        a, b = join_half(a, *sa), join_half(b, *sb)
    return (a, b, swap(a, "rows", 1), swap(b, "rows", 1)), token_grads


BIG_B = 2 * FF + D
BIG_C = 2 * FF + 6 * D
SMALL_C = 40
SMALL_B = 8


def kernel_d(
    frames,
    me_ref,
    o0,
    o1,
    o2,
    o3,
    t0,
    t1,
    t2,
    t3,
    own_a,
    own_b,
    other_a,
    other_b,
    output_ref,
    tokens_ref,
    ff1_in,
    ff1_out,
    w_q,
    w_k,
    w_v,
    w_o,
    pw1,
    pw2,
    ff2_in,
    ff2_out,
    small_ref,
    big_ref,
):
    quarter = own_a.shape[0]
    side = me_ref[1]
    for k, (own, other) in enumerate(((own_a, other_a), (own_b, other_b))):
        big_ref[rows_at((2 * side + k) * quarter, quarter, 64), :] = own[...]
        big_ref[rows_at((2 * (1 - side) + k) * quarter, quarter, 64), :] = other[...]
    for m, (o, t) in enumerate(zip((o0, o1, o2, o3), (t0, t1, t2, t3))):
        output_ref[me_ref[0] ^ m] = o[...]
        tokens_ref[me_ref[0] ^ m] = t[...].astype(f32)
    ff1_out[...] = big_ref[0:FF, :].astype(f32)
    for c in range(FF // D):
        ff1_in[:, c * D : (c + 1) * D] = big_ref[FF + c * D : FF + (c + 1) * D, :].astype(f32)
    base = 2 * FF
    for k, ref in enumerate((w_q, w_k, w_v, w_o)):
        ref[...] = big_ref[base + k * D : base + (k + 1) * D, :].astype(f32)
    base = 2 * FF + 4 * D
    for c in range(2):
        pw1[:, c * D : (c + 1) * D] = big_ref[base + c * D : base + (c + 1) * D, :].astype(f32)
    base = BIG_C
    ff2_out[...] = big_ref[base : base + FF, :].astype(f32)
    for c in range(FF // D):
        at = base + FF + c * D
        ff2_in[:, c * D : (c + 1) * D] = big_ref[at : at + D, :].astype(f32)
    pw2[...] = big_ref[base + 2 * FF : base + 2 * FF + D, :].astype(f32)
    small_ref[...] = big_ref[BIG_C + BIG_B : BIG_C + BIG_B + SMALL_C + SMALL_B, :].astype(f32)


def shape_of(shape, dtype):
    return jax.ShapeDtypeStruct(shape, dtype)


def call(body, smem, outs, scratch, name, far_in=(), far_out=(), micros=1):
    def place(far, count):
        return [pl.BlockSpec(memory_space=pl.ANY if k in far else pltpu.VMEM) for k in range(count)]

    def run(*operands):
        specs = [pl.BlockSpec(memory_space=pltpu.SMEM)] * smem + place(far_in, len(operands))[smem:]
        return pl.pallas_call(
            body,
            out_shape=outs,
            in_specs=specs,
            out_specs=place(far_out, len(outs)),
            scratch_shapes=scratch,
            compiler_params=pltpu.CompilerParams(vmem_limit_bytes=VMEM_LIMIT),
            cost_estimate=pl.CostEstimate(flops=micros * 10**9, bytes_accessed=micros * 10**6, transcendentals=0),
            name=name,
        )(*operands)

    return run


def twice(weight):
    heads = weight.reshape(D, H, HD)
    return jnp.concatenate([heads, heads], axis=2).reshape(D, 2 * D)


def one_side(weight):
    heads = weight.reshape(D, H // 2, 2, HD)
    empty = jnp.zeros_like(heads[:, :, 0])
    even = jnp.concatenate([heads[:, :, 0], empty], axis=2)
    odd = jnp.concatenate([empty, heads[:, :, 1]], axis=2)
    return jnp.stack([even, odd], axis=2).reshape(D, 2 * D)


def row_device(
    tokens,
    seg_ids,
    frame_mask,
    cotangent,
    g_ff1,
    w_ff1_in,
    w_ff1_out,
    g_att,
    w_query,
    w_key,
    w_value,
    w_output,
    rel_table,
    g_conv,
    w_pw1,
    w_depth,
    bn_gain,
    w_pw2,
    g_ff2,
    w_ff2_in,
    w_ff2_out,
    g_out,
):
    blocks, frames, _ = tokens.shape
    length = blocks * frames
    tiles = length // QT
    padded_rows = length + 4 * GAP
    n_mixed = len(mixed_offsets(tiles))
    me = lax.axis_index("blk")
    me_ref = jnp.stack([me, lax.axis_index("rows") % 2]).astype(jnp.int32)
    gains = [g.reshape(1, D) for g in (g_ff1, g_att, g_conv, bn_gain, g_ff2, g_out)]
    g_ff1, g_att, g_conv, bn_gain, g_ff2, g_out = gains

    lengths = [
        jnp.sum((seg_ids == 0).astype(jnp.int32), axis=1),
        jnp.sum((seg_ids == 1).astype(jnp.int32), axis=1),
        jnp.sum(frame_mask, axis=1),
    ]
    digits = jnp.stack([part for n in lengths for part in (n // 16, n % 16)], axis=1)
    digits = jnp.pad(digits, ((0, 0), (0, EXTRA - digits.shape[1]))).astype(bf16)
    extra = jnp.broadcast_to(digits[:, :, None], (blocks, EXTRA, D))
    token_pieces = to_pieces(jnp.concatenate([tokens, extra], axis=1), me)
    cotangent, token_pieces = lax.optimization_barrier((cotangent, token_pieces))
    cot_pieces = to_pieces(cotangent, me)

    bias = call(
        functools.partial(bias_kernel, tiles), 1, [shape_of((H, n_mixed, QT, QT), f32)], [], "bias_tiles"
    )(rel_table)[0]
    taps = jnp.pad(w_depth.astype(f32), ((0, 1), (0, 0))).reshape(KERNEL + 1, 2, 128).transpose(1, 0, 2)

    (tok, ends, s1, k2, v2, q2, lse, mixed, s2, gap, depth, sums) = call(
        functools.partial(kernel_a, tiles),
        2,
        [
            shape_of((length, D), bf16),
            shape_of((8, D), f32),
            shape_of((length, D), f32),
            shape_of((H, length, 128), bf16),
            shape_of((H, length, 128), bf16),
            shape_of((H, length, 128), bf16),
            shape_of((H, length, 128), bf16),
            shape_of((H // 2, length, 128), f32),
            shape_of((length, D), f32),
            shape_of((2, padded_rows, 128), f32),
            shape_of((length, D), f32),
            shape_of((8, D), f32),
        ],
        [
            pltpu.VMEM((length, 128), f32),
            pltpu.VMEM((length, 128), bf16),
            pltpu.SMEM((1,), jnp.int32),
            pltpu.VMEM((2, length + 6 * GAP, 128), f32),
            pltpu.VMEM((2, padded_rows, 128), f32),
        ],
        "first_part",
        micros=40,
    )(
        me_ref,
        rel_table,
        *token_pieces,
        bias,
        g_ff1,
        w_ff1_in,
        w_ff1_out,
        g_att,
        twice(w_query),
        twice(w_key),
        one_side(w_value),
        w_output,
        g_conv,
        w_pw1,
        taps,
    )
    sums = sum_everywhere(sums)

    (o0, o1, o2, o3, grad3, bngrad, sums2, big_b, small_b) = call(
        functools.partial(kernel_b, tiles),
        1,
        [shape_of((frames, D), bf16)] * 4
        + [
            shape_of((length, D), f32),
            shape_of((length, D), f32),
            shape_of((8, D), f32),
            shape_of((BIG_B, D), bf16),
            shape_of((SMALL_B, D), f32),
        ],
        [
            pltpu.VMEM((length, D), bf16),
            pltpu.VMEM((length, D), bf16),
            pltpu.VMEM((D, FF), f32),
            pltpu.VMEM((D, FF), f32),
            pltpu.VMEM((D, D), f32),
        ],
        "middle_part",
        micros=15,
    )(me_ref, *cot_pieces, sums, depth, s2, bn_gain, w_pw2, g_ff2, w_ff2_in, w_ff2_out, g_out)
    out_pieces = from_pieces([o0, o1, o2, o3])
    sums2 = sum_everywhere(sums2)

    rows = BIG_C + BIG_B + SMALL_C + SMALL_B
    whole = -(-rows // 1024) * 1024
    (t0, t1, t2, t3, kept, sent) = call(
        functools.partial(kernel_c, tiles),
        2,
        [shape_of((frames, D), bf16)] * 4 + [shape_of((whole // 2, D), bf16)] * 2,
        [
            pltpu.VMEM((whole, D), bf16),
            pltpu.VMEM((SMALL_C, D), f32),
            pltpu.VMEM((2, length + 6 * GAP, 128), f32),
            pltpu.VMEM((2, padded_rows, 128), f32),
            pltpu.VMEM((2, padded_rows, 128), f32),
            pltpu.VMEM((length, D), f32),
            pltpu.VMEM((H, length, 128), bf16),
            pltpu.VMEM((D, length), bf16),
            pltpu.VMEM((D, length), bf16),
            pltpu.VMEM((length, 128), bf16),
            pltpu.VMEM((H, length, 128), f32),
            pltpu.VMEM((D, length), f32),
            pltpu.VMEM((D, length), f32),
            pltpu.VMEM((n_mixed, QT, QT), f32),
            pltpu.VMEM((KERNEL + 1, D), f32),
            pltpu.VMEM((D, FF), f32),
            pltpu.VMEM((D, FF), f32),
            pltpu.VMEM((D, D), f32),
            pltpu.VMEM((D, 2 * D), f32),
            pltpu.VMEM((D, D), f32),
            pltpu.VMEM((D, D), f32),
            pltpu.VMEM((D, D), f32),
            pltpu.VMEM((length, D), f32),
        ],
        "last_part",
        micros=60,
    )(
        me_ref,
        rel_table,
        sums,
        sums2,
        tok,
        ends,
        s1,
        k2,
        v2,
        q2,
        lse,
        mixed,
        s2,
        gap,
        depth,
        grad3,
        bngrad,
        bias,
        g_ff1,
        w_ff1_in,
        w_ff1_out,
        g_att,
        w_query,
        w_key,
        w_value,
        w_output,
        g_conv,
        w_pw1,
        taps,
        bn_gain,
        big_b,
        small_b,
    )
    kept, sent, out_pieces = lax.optimization_barrier((kept, sent, out_pieces))
    reduced, token_grads = reduce_gradients(kept, sent, [t0, t1, t2, t3])

    (output, tokens_grad, ff1_in, ff1_out, w_q, w_k, w_v, w_o, pw1, pw2, ff2_in, ff2_out, small) = call(
        functools.partial(kernel_d, frames),
        1,
        [
            shape_of((blocks, frames, D), bf16),
            shape_of((blocks, frames, D), f32),
            shape_of((D, FF), f32),
            shape_of((FF, D), f32),
            shape_of((D, D), f32),
            shape_of((D, D), f32),
            shape_of((D, D), f32),
            shape_of((D, D), f32),
            shape_of((D, 2 * D), f32),
            shape_of((D, D), f32),
            shape_of((D, FF), f32),
            shape_of((FF, D), f32),
            shape_of((SMALL_C + SMALL_B, D), f32),
        ],
        [pltpu.VMEM((whole, D), bf16)],
        "unpack",
        micros=5,
    )(me_ref, *out_pieces, *token_grads, *reduced)
    return (
        output,
        tokens_grad,
        small[0],
        ff1_in,
        ff1_out,
        small[1],
        w_q,
        w_k,
        w_v,
        w_o,
        small[4:8, :NBUCKET],
        small[2],
        pw1,
        small[8 : 8 + KERNEL],
        sums2[1],
        pw2,
        small[SMALL_C],
        ff2_in,
        ff2_out,
        small[SMALL_C + 1],
    )


def padded(x, sides, width):
    for axis, dim in sides:
        size, length = (lax.axis_size(axis), x.shape[dim])
        up = [(i, (i + 1) % size) for i in range(size - 1)]
        down = [(j, i) for i, j in up]
        last = lax.slice_in_dim(x, length - width, length, axis=dim)
        first = lax.slice_in_dim(x, 0, width, axis=dim)
        before = lax.ppermute(last, axis, up)
        after = lax.ppermute(first, axis, down)
        x = jnp.concatenate([before, x, after], axis=dim)
    return x


def norm_forward(values, norm_gain):
    center = jnp.mean(values, axis=-1, keepdims=True)
    shifted = values - center
    spread = jnp.mean(shifted * shifted, axis=-1, keepdims=True)
    inverse = lax.rsqrt(spread + epsilon)
    scaled = shifted * inverse
    return (scaled * norm_gain, (scaled, inverse))


def norm_backward(upstream, norm_gain, stored):
    scaled, inverse = stored
    gain_grad = jnp.sum(upstream * scaled, axis=(0, 1))
    inner_grad = upstream * norm_gain
    inner_mean = jnp.mean(inner_grad, axis=-1, keepdims=True)
    inner_dot = jnp.mean(inner_grad * scaled, axis=-1, keepdims=True)
    return (inverse * (inner_grad - inner_mean - scaled * inner_dot), gain_grad)


def project(left_side, weight):
    return jnp.einsum("rfd,de->rfe", left_side, weight, preferred_element_type=jnp.float32)


def project_back(upstream, weight):
    return jnp.einsum("rfe,de->rfd", upstream, weight, preferred_element_type=jnp.float32)


def weight_product(left_side, upstream):
    return jnp.einsum("rfd,rfe->de", left_side, upstream, preferred_element_type=jnp.float32)


def silu_slope(values):
    logistic = jax.nn.sigmoid(values)
    return logistic * (1.0 + values * (1.0 - logistic))


def ffn_forward(values, norm_gain, weight_in, weight_out):
    normed, norm_stored = norm_forward(values, norm_gain)
    normed_low = normed.astype(jnp.bfloat16)
    hidden = project(normed_low, weight_in)
    act_low = jax.nn.silu(hidden).astype(jnp.bfloat16)
    return (project(act_low, weight_out), (norm_stored, normed_low, hidden, act_low))


def ffn_backward(stream_grad, norm_gain, weight_in, weight_out, stored):
    norm_stored, normed_low, hidden, act_low = stored
    out_low = (0.5 * stream_grad).astype(jnp.bfloat16)
    out_weight_grad = weight_product(act_low, out_low)
    hidden_low = (project_back(out_low, weight_out) * silu_slope(hidden)).astype(jnp.bfloat16)
    in_weight_grad = weight_product(normed_low, hidden_low)
    input_grad, gain_grad = norm_backward(
        project_back(hidden_low, weight_in), norm_gain, norm_stored
    )
    return (stream_grad + input_grad, (gain_grad, in_weight_grad, out_weight_grad))


def bucket_bias(query_pos, key_pos, rel_table):
    distance = key_pos[None, :] - query_pos[:, None]
    levels = NBUCKET // 2
    magnitude = jnp.abs(distance)
    bucket = levels * (distance > 0).astype(jnp.int32)
    for exponent in range(levels - 1):
        bucket = bucket + (magnitude >= 4**exponent).astype(jnp.int32)
    onehot = (bucket[:, :, None] == jnp.arange(NBUCKET, dtype=jnp.int32)[None, None, :]).astype(
        jnp.float32
    )
    position_bias = jnp.einsum("qkb,hb->hqk", onehot, rel_table, precision=lax.Precision.HIGHEST)
    return (position_bias, onehot)


def block_at(source, block_index, query_heads, segment_float, query_pos, rel_table):
    key_all, value_all, code_all = source
    row_count, frames = segment_float.shape
    key_start = block_index * frames
    key_block = lax.dynamic_slice_in_dim(key_all, key_start, frames, 1).reshape(
        row_count, frames, H, HD
    )
    value_block = lax.dynamic_slice_in_dim(value_all, key_start, frames, 1).reshape(
        row_count, frames, H, HD
    )
    code_block = lax.dynamic_slice_in_dim(code_all, key_start, frames, 1)
    key_pos = key_start + jnp.arange(frames, dtype=jnp.int32)
    position_bias, onehot = bucket_bias(query_pos, key_pos, rel_table)
    raw_scores = (
        jnp.einsum("rqhd,rkhd->rhqk", query_heads, key_block, preferred_element_type=jnp.float32)
        * HD ** (-0.5)
        + position_bias[None]
    )
    allowed = (segment_float[:, :, None] == code_block.astype(jnp.float32)[:, None, :])[:, None]
    return (jnp.where(allowed, raw_scores, masked_score), allowed, onehot, key_block, value_block)


def attend_forward(
    values, segment, code_low, norm_gain, w_query, w_key, w_value, w_output, rel_table
):
    row_count, frames, model_width = values.shape
    normed, norm_stored = norm_forward(values, norm_gain)
    normed_low = normed.astype(jnp.bfloat16)
    query_low = project(normed_low, w_query).astype(jnp.bfloat16)
    key_low = project(normed_low, w_key).astype(jnp.bfloat16)
    value_low = project(normed_low, w_value).astype(jnp.bfloat16)
    gathered = (
        lax.all_gather(key_low, "blk", axis=1, tiled=True),
        lax.all_gather(value_low, "blk", axis=1, tiled=True),
        lax.all_gather(code_low, "blk", axis=1, tiled=True),
    )
    segment_float = segment.astype(jnp.float32)
    query_pos = lax.axis_index("blk") * frames + jnp.arange(frames, dtype=jnp.int32)
    query_heads = query_low.reshape(row_count, frames, H, HD)
    blocks = lax.axis_size("blk")

    def max_step(block_index, loop_state):
        running_max, running_sum = loop_state
        scores, allowed, onehot, key_block, value_block = block_at(
            gathered, block_index, query_heads, segment_float, query_pos, rel_table
        )
        new_max = jnp.maximum(running_max, jnp.max(scores, axis=-1))
        kept_exp = jnp.where(allowed, jnp.exp(scores - new_max[..., None]), 0.0)
        return (new_max, running_sum * jnp.exp(running_max - new_max) + jnp.sum(kept_exp, axis=-1))

    start_max = jnp.full((row_count, H, frames), masked_score, jnp.float32)
    running_max, running_sum = lax.fori_loop(
        0, blocks, max_step, (start_max, jnp.zeros_like(start_max))
    )
    log_total = running_max + jnp.log(running_sum)

    def mix_step(block_index, mixed_sum):
        scores, allowed, onehot, key_block, value_block = block_at(
            gathered, block_index, query_heads, segment_float, query_pos, rel_table
        )
        attn_low = jnp.where(allowed, jnp.exp(scores - log_total[..., None]), 0.0).astype(
            jnp.bfloat16
        )
        return mixed_sum + jnp.einsum(
            "rhqk,rkhd->rqhd", attn_low, value_block, preferred_element_type=jnp.float32
        )

    mixed_heads = lax.fori_loop(
        0, blocks, mix_step, jnp.zeros((row_count, frames, H, HD), jnp.float32)
    )
    mixed_heads = mixed_heads.reshape(row_count, frames, model_width)
    mixed_low = mixed_heads.astype(jnp.bfloat16)
    stored = (
        norm_stored,
        normed_low,
        query_heads,
        key_low,
        value_low,
        code_low,
        gathered,
        log_total,
        mixed_heads,
        mixed_low,
        segment_float,
        query_pos,
    )
    return (project(mixed_low, w_output), stored)


def attend_backward(stream_grad, norm_gain, w_query, w_key, w_value, w_output, rel_table, stored):
    (
        norm_stored,
        normed_low,
        query_heads,
        key_low,
        value_low,
        code_low,
        gathered,
        log_total,
        mixed_heads,
        mixed_low,
        segment_float,
        query_pos,
    ) = stored
    row_count, frames, model_width = stream_grad.shape
    grad_low = stream_grad.astype(jnp.bfloat16)
    w_output_grad = weight_product(mixed_low, grad_low)
    mixed_grad = (
        project_back(grad_low, w_output).astype(jnp.bfloat16).reshape(row_count, frames, H, HD)
    )
    row_delta = jnp.einsum(
        "rqhd,rqhd->rhq",
        mixed_grad.astype(jnp.float32),
        mixed_heads.reshape(row_count, frames, H, HD),
    )
    source = (
        lax.all_gather(key_low, "blk", axis=1, tiled=True),
        lax.all_gather(value_low, "blk", axis=1, tiled=True),
        lax.all_gather(code_low, "blk", axis=1, tiled=True),
    )
    blocks = lax.axis_size("blk")
    scale = HD ** (-0.5)

    def score_grads(block_index):
        scores, allowed, onehot, key_block, value_block = block_at(
            source, block_index, query_heads, segment_float, query_pos, rel_table
        )
        attn_weights = jnp.where(allowed, jnp.exp(scores - log_total[..., None]), 0.0)
        weight_grad = jnp.einsum(
            "rqhd,rkhd->rhqk", mixed_grad, value_block, preferred_element_type=jnp.float32
        )
        score_low = (attn_weights * (weight_grad - row_delta[..., None])).astype(jnp.bfloat16)
        return (attn_weights, score_low, onehot, key_block)

    def grad_step(block_index, loop_state):
        query_grad, key_buffer, value_buffer, table_grad = loop_state
        attn_weights, score_low, onehot, key_block = score_grads(block_index)
        attn_low = attn_weights.astype(jnp.bfloat16)
        query_grad = query_grad + jnp.einsum(
            "rhqk,rkhd->rqhd", score_low, key_block, preferred_element_type=jnp.float32
        )
        key_part = (
            jnp.einsum(
                "rhqk,rqhd->rkhd", score_low, query_heads, preferred_element_type=jnp.float32
            )
            * scale
        )
        value_part = jnp.einsum(
            "rhqk,rqhd->rkhd", attn_low, mixed_grad, preferred_element_type=jnp.float32
        )
        key_start = block_index * frames
        key_buffer = lax.dynamic_update_slice_in_dim(
            key_buffer, key_part.reshape(row_count, frames, model_width), key_start, 1
        )
        value_buffer = lax.dynamic_update_slice_in_dim(
            value_buffer, value_part.reshape(row_count, frames, model_width), key_start, 1
        )
        table_grad = table_grad + jnp.einsum(
            "hqk,qkb->hb",
            jnp.sum(score_low.astype(jnp.float32), axis=0),
            onehot,
            precision=lax.Precision.HIGHEST,
        )
        return (query_grad, key_buffer, value_buffer, table_grad)

    empty_buffer = jnp.zeros((row_count, blocks * frames, model_width), jnp.float32)
    start_state = (
        jnp.zeros((row_count, frames, H, HD), jnp.float32),
        empty_buffer,
        empty_buffer,
        jnp.zeros((H, NBUCKET), jnp.float32),
    )
    query_grad, key_buffer, value_buffer, table_grad = lax.fori_loop(
        0, blocks, grad_step, start_state
    )
    key_total, value_total = (
        lax.psum_scatter(
            key_buffer.astype(jnp.bfloat16), "blk", scatter_dimension=1, tiled=True
        ).astype(jnp.float32),
        lax.psum_scatter(
            value_buffer.astype(jnp.bfloat16), "blk", scatter_dimension=1, tiled=True
        ).astype(jnp.float32),
    )
    query_grad_low = (
        (query_grad * scale).reshape(row_count, frames, model_width).astype(jnp.bfloat16)
    )
    key_grad_low = key_total.astype(jnp.bfloat16)
    value_grad_low = value_total.astype(jnp.bfloat16)
    w_query_grad = weight_product(normed_low, query_grad_low)
    w_key_grad = weight_product(normed_low, key_grad_low)
    w_value_grad = weight_product(normed_low, value_grad_low)
    normed_grad = (
        project_back(query_grad_low, w_query)
        + project_back(key_grad_low, w_key)
        + project_back(value_grad_low, w_value)
    )
    input_grad, gain_grad = norm_backward(normed_grad, norm_gain, norm_stored)
    return (
        stream_grad + input_grad,
        (gain_grad, w_query_grad, w_key_grad, w_value_grad, w_output_grad, table_grad),
    )


def conv_forward(values, segment, live_mask, norm_gain, w_pw1, w_depth, bn_gain, w_pw2):
    row_count, frames, model_width = values.shape
    normed, norm_stored = norm_forward(values, norm_gain)
    normed_low = normed.astype(jnp.bfloat16)
    gate_pair = project(normed_low, w_pw1)
    first_half = gate_pair[..., :model_width]
    logistic = jax.nn.sigmoid(gate_pair[..., model_width:])
    live_frames = live_mask.astype(jnp.float32)[..., None]
    gated_low = (first_half * logistic * live_frames).astype(jnp.bfloat16)
    wide_units, wide_segment = (
        padded(gated_low, (("blk", 1),), KERNEL // 2),
        padded(segment.astype(jnp.bfloat16), (("blk", 1),), KERNEL // 2),
    )
    segment_float = segment.astype(jnp.float32)
    depth_sum = jnp.zeros((row_count, frames, model_width), jnp.float32)
    for kernel_tap in range(KERNEL):
        same_segment = (
            wide_segment[:, kernel_tap : kernel_tap + frames].astype(jnp.float32) == segment_float
        ).astype(jnp.float32)
        depth_sum = (
            depth_sum
            + w_depth[kernel_tap].astype(jnp.float32)
            * wide_units[:, kernel_tap : kernel_tap + frames].astype(jnp.float32)
            * same_segment[..., None]
        )
    norm_totals = lax.psum(
        (
            jnp.sum(depth_sum * live_frames, axis=(0, 1)),
            jnp.sum(depth_sum * depth_sum * live_frames, axis=(0, 1)),
            jnp.sum(live_frames),
        ),
        ("blk", "rows"),
    )
    frame_count = norm_totals[2]
    center = norm_totals[0] / frame_count
    spread = norm_totals[1] / frame_count - center * center
    inverse = lax.rsqrt(spread + epsilon)
    standard = (depth_sum - center) * inverse
    pre_act = standard * bn_gain
    act_low = jax.nn.silu(pre_act).astype(jnp.bfloat16)
    stored = (
        norm_stored,
        normed_low,
        first_half,
        logistic,
        live_frames,
        wide_units,
        wide_segment,
        frame_count,
        inverse,
        standard,
        pre_act,
        act_low,
    )
    return (project(act_low, w_pw2), stored)


def conv_backward(stream_grad, segment, norm_gain, w_pw1, w_depth, bn_gain, w_pw2, stored):
    (
        norm_stored,
        normed_low,
        first_half,
        logistic,
        live_frames,
        wide_units,
        wide_segment,
        frame_count,
        inverse,
        standard,
        pre_act,
        act_low,
    ) = stored
    row_count, frames, model_width = stream_grad.shape
    grad_low = stream_grad.astype(jnp.bfloat16)
    w_pw2_grad = weight_product(act_low, grad_low)
    act_grad = project_back(grad_low, w_pw2) * silu_slope(pre_act)
    hat_grad = act_grad * bn_gain
    grad_sums = lax.psum(
        (jnp.sum(hat_grad, axis=(0, 1)), jnp.sum(act_grad * standard, axis=(0, 1))), ("blk", "rows")
    )
    hat_total, bn_gain_grad = grad_sums
    frame_share = live_frames / frame_count
    depth_low = (
        inverse
        * (hat_grad - frame_share * hat_total - frame_share * standard * bn_gain * bn_gain_grad)
    ).astype(jnp.bfloat16)
    wide_grad = padded(depth_low, (("blk", 1),), KERNEL // 2)
    segment_float = segment.astype(jnp.float32)
    depth_float = depth_low.astype(jnp.float32)
    unit_grad = jnp.zeros((row_count, frames, model_width), jnp.float32)
    tap_grads = []
    for kernel_tap in range(KERNEL):
        forward_same = (
            wide_segment[:, kernel_tap : kernel_tap + frames].astype(jnp.float32) == segment_float
        ).astype(jnp.float32)[..., None]
        tap_grads.append(
            jnp.sum(
                depth_float
                * wide_units[:, kernel_tap : kernel_tap + frames].astype(jnp.float32)
                * forward_same,
                axis=(0, 1),
            )
        )
        mirror = KERNEL - 1 - kernel_tap
        backward_same = (
            wide_segment[:, mirror : mirror + frames].astype(jnp.float32) == segment_float
        ).astype(jnp.float32)[..., None]
        unit_grad = (
            unit_grad
            + w_depth[kernel_tap].astype(jnp.float32)
            * wide_grad[:, mirror : mirror + frames].astype(jnp.float32)
            * backward_same
        )
    unit_grad = unit_grad * live_frames
    pair_low = jnp.concatenate(
        [unit_grad * logistic, unit_grad * first_half * logistic * (1.0 - logistic)], axis=-1
    ).astype(jnp.bfloat16)
    w_pw1_grad = weight_product(normed_low, pair_low)
    input_grad, gain_grad = norm_backward(project_back(pair_low, w_pw1), norm_gain, norm_stored)
    return (
        stream_grad + input_grad,
        (gain_grad, w_pw1_grad, jnp.stack(tap_grads), bn_gain_grad, w_pw2_grad),
    )


def per_device(
    tokens,
    seg_ids,
    frame_mask,
    cotangent,
    g_ff1,
    w_ff1_in,
    w_ff1_out,
    g_att,
    w_query,
    w_key,
    w_value,
    w_output,
    rel_table,
    g_conv,
    w_pw1,
    w_depth,
    bn_gain,
    w_pw2,
    g_ff2,
    w_ff2_in,
    w_ff2_out,
    g_out,
):
    start_stream = tokens.astype(jnp.float32)
    ffn_one, ffn_one_stored = ffn_forward(start_stream, g_ff1, w_ff1_in, w_ff1_out)
    after_ffn = start_stream + 0.5 * ffn_one
    code_low = jnp.where(frame_mask == 1, seg_ids, -1).astype(jnp.bfloat16)
    attended, attend_stored = attend_forward(
        after_ffn, seg_ids, code_low, g_att, w_query, w_key, w_value, w_output, rel_table
    )
    after_att = after_ffn + attended
    conv_out, conv_stored = conv_forward(
        after_att, seg_ids, frame_mask, g_conv, w_pw1, w_depth, bn_gain, w_pw2
    )
    after_conv = after_att + conv_out
    ffn_two, ffn_two_stored = ffn_forward(after_conv, g_ff2, w_ff2_in, w_ff2_out)
    after_two = after_conv + 0.5 * ffn_two
    final_norm, final_stored = norm_forward(after_two, g_out)
    stream_grad, g_out_grad = norm_backward(cotangent.astype(jnp.float32), g_out, final_stored)
    stream_grad, ffn_two_grads = ffn_backward(
        stream_grad, g_ff2, w_ff2_in, w_ff2_out, ffn_two_stored
    )
    stream_grad, conv_grads = conv_backward(
        stream_grad, seg_ids, g_conv, w_pw1, w_depth, bn_gain, w_pw2, conv_stored
    )
    stream_grad, attend_grads = attend_backward(
        stream_grad, g_att, w_query, w_key, w_value, w_output, rel_table, attend_stored
    )
    stream_grad, ffn_one_grads = ffn_backward(
        stream_grad, g_ff1, w_ff1_in, w_ff1_out, ffn_one_stored
    )
    summed = lax.psum(
        (
            ffn_one_grads[0],
            ffn_one_grads[1],
            ffn_one_grads[2],
            attend_grads[0],
            attend_grads[1],
            attend_grads[2],
            attend_grads[3],
            attend_grads[4],
            attend_grads[5],
            conv_grads[0],
            conv_grads[1],
            conv_grads[2],
            conv_grads[4],
            ffn_two_grads[0],
            ffn_two_grads[1],
            ffn_two_grads[2],
            g_out_grad,
        ),
        ("blk", "rows"),
    )
    return (
        final_norm.astype(jnp.bfloat16),
        stream_grad,
        summed[0],
        summed[1],
        summed[2],
        summed[3],
        summed[4],
        summed[5],
        summed[6],
        summed[7],
        summed[8],
        summed[9],
        summed[10],
        summed[11],
        conv_grads[3],
        summed[12],
        summed[13],
        summed[14],
        summed[15],
        summed[16],
    )


def solution(mesh):
    blocks, groups = mesh.shape["blk"], mesh.shape["rows"]

    def device(tokens, *rest):
        rows, frames, _ = tokens.shape
        whole_rows = rows == blocks == 4 and groups == 8 and (rows * frames) % QT == 0
        return (row_device if whole_rows else per_device)(tokens, *rest)

    return jax.shard_map(
        device,
        mesh=mesh,
        in_specs=(
            P("rows", "blk", None),
            P("rows", "blk"),
            P("rows", "blk"),
            P("rows", "blk", None),
        )
        + (P(),) * 18,
        out_specs=(P("rows", "blk", None),) * 2 + (P(),) * 18,
        check_vma=False,
    )
```

```python
import functools
import math

import jax
import jax.numpy as jnp
from jax import lax
from jax.experimental import pallas as pl
from jax.experimental.pallas import tpu as pltpu
from jax.sharding import PartitionSpec as P

H = 4
HD = 64
D = 256
FF = 1024
KERNEL = 31
HALF = KERNEL // 2
NBUCKET = 16

epsilon = 1e-05
masked_score = -1e30

f32 = jnp.float32
bf16 = jnp.bfloat16
LOG2E = math.log2(math.e)
QT = 256
GAP = 16
EXTRA = 16
SAFE_EXPONENT = 60.0
MIB = 1024 * 1024


def mm(a, b):
    return lax.dot_general(a, b, (((1,), (0,)), ((), ())), preferred_element_type=f32)


def mm_nt(a, b):
    return lax.dot_general(a, b, (((1,), (1,)), ((), ())), preferred_element_type=f32)


def turned(x):
    return x.astype(f32).T.astype(bf16)


def sigmoid(x):
    return 0.5 + 0.5 * jnp.tanh(0.5 * x)


def norm_hat(v):
    center = jnp.mean(v, axis=-1, keepdims=True)
    shifted = v - center
    spread = jnp.mean(shifted * shifted, axis=-1, keepdims=True)
    inverse = lax.rsqrt(spread + epsilon)
    return shifted * inverse, inverse


def norm_back(upstream, gain, hat, inverse):
    inner = upstream * gain
    inner_mean = jnp.mean(inner, axis=-1, keepdims=True)
    inner_dot = jnp.mean(inner * hat, axis=-1, keepdims=True)
    return inverse * (inner - inner_mean - hat * inner_dot)


def col_sum(x):
    rows, width = x.shape
    return jnp.sum(x.reshape(rows // 8, 8, width), axis=0)


def bucket_ranges():
    levels = NBUCKET // 2
    big = 1 << 30
    edges = [0] + [4**k for k in range(levels - 1)] + [big]
    out = []
    for level in range(levels - 1, 0, -1):
        out.append((level, 1 - edges[level + 1], -edges[level]))
    out.append((0, 0, 0))
    for level in range(1, levels):
        out.append((levels + level, edges[level], edges[level + 1] - 1))
    return out


def tile_buckets(offset):
    low, high = offset * QT - (QT - 1), offset * QT + (QT - 1)
    return [(b, lo) for b, lo, hi in bucket_ranges() if lo <= high and hi >= low]


def mixed_offsets(tiles):
    return [o for o in range(1 - tiles, tiles) if len(tile_buckets(o)) > 1]


def tile_distance(offset):
    row = lax.broadcasted_iota(jnp.int32, (QT, QT), 0)
    col = lax.broadcasted_iota(jnp.int32, (QT, QT), 1)
    return col - row + offset * QT


def frame_index(start, rows, width):
    return (lax.broadcasted_iota(jnp.int32, (rows, width), 0) + start).astype(f32)


def rows_at(start, count, unit):
    return pl.ds(pl.multiple_of(start, unit), count)


def bias_kernel(tiles, table_ref, bias_ref):
    def head(h, carry):
        for k, offset in enumerate(mixed_offsets(tiles)):
            d = tile_distance(offset)
            found = tile_buckets(offset)
            value = jnp.full((QT, QT), table_ref[h, found[0][0]], f32)
            for b, lo in found[1:]:
                value = jnp.where(d >= lo, table_ref[h, b], value)
            bias_ref[h, k] = value * LOG2E
        return carry

    lax.fori_loop(0, H, head, 0)


def place_pieces(me_ref, piece_refs, target_ref, frames):
    for m, piece in enumerate(piece_refs):
        start = (me_ref[0] ^ m) * frames
        target_ref[rows_at(start, frames, 64), :] = piece[0:frames, :]


def take_pieces(me_ref, source_ref, piece_refs, frames):
    for m, piece in enumerate(piece_refs):
        start = (me_ref[0] ^ m) * frames
        piece[...] = source_ref[rows_at(start, frames, 64), :].astype(piece.dtype)


def key_features(start, rows, ends):
    first_end, second_end, live_end = (e[:, :128] for e in ends)
    t = frame_index(start, rows, 128)
    lane = lax.broadcasted_iota(jnp.int32, (rows, 128), 1)
    code = jnp.where(t < first_end, 0, jnp.where(t < second_end, 1, 2))
    code = jnp.where(t < live_end, code, -1)
    barred = jnp.where((lane < 3) & (code != lane), masked_score, 0.0)
    return jnp.where((lane >= 3) & (lane < 6), 1.0, barred).astype(bf16)


def query_features(start, rows, ends):
    first_end, second_end, live_end = (e[:, :128] for e in ends)
    t = frame_index(start, rows, 128)
    lane = lax.broadcasted_iota(jnp.int32, (rows, 128), 1)
    code = jnp.where(t < first_end, 0, jnp.where(t < second_end, 1, 2))
    return jnp.where(code == lane, 1.0, 0.0)


def three_parts(x):
    top = x.astype(bf16).astype(f32)
    middle = (x - top).astype(bf16).astype(f32)
    return top, middle, x - top - middle


def spread_gaps(plain_ref, gap_ref, length, ends):
    first_end, second_end, _ = (e[:, :128] for e in ends)
    total = length + 4 * GAP
    step = GAP * 4

    def chunk(k, carry):
        start = k * step
        g = frame_index(start, step, 128)
        for c in range(2):
            a = plain_ref[c, rows_at(start + 2 * GAP, step, 16), :]
            b = plain_ref[c, rows_at(start + GAP, step, 16), :]
            d = plain_ref[c, rows_at(start, step, 16), :]
            in_first = (g >= GAP) & (g - GAP < first_end)
            in_second = (g - 2 * GAP >= first_end) & (g - 2 * GAP < second_end)
            in_third = (g - 3 * GAP >= second_end) & (g - 3 * GAP < length)
            value = jnp.where(in_first, a, jnp.where(in_second, b, jnp.where(in_third, d, 0.0)))
            gap_ref[c, rows_at(start, step, 16), :] = value
        return carry

    lax.fori_loop(0, total // step, chunk, 0)


def close_gaps(gap_ref, start, rows, ends):
    first_end, second_end, _ = (e[:, :128] for e in ends)
    t = frame_index(start, rows, 128)
    halves = []
    for c in range(2):
        a = gap_ref[c, rows_at(start + GAP, rows, 16), :]
        b = gap_ref[c, rows_at(start + 2 * GAP, rows, 16), :]
        d = gap_ref[c, rows_at(start + 3 * GAP, rows, 16), :]
        halves.append(jnp.where(t < first_end, a, jnp.where(t < second_end, b, d)))
    return jnp.concatenate(halves, axis=1)


CONV_ROWS = 32
BACK_ROWS = 16


def tapped(part, tap):
    rows = part.shape[0]
    return (part.reshape(rows // 8, 8, 128) * tap[None]).reshape(rows, 128)


def convolve(gap_ref, out_ref, taps_ref, length):
    span = length + 2 * GAP

    for c in range(2):

        def chunk(k, carry, c=c):
            start = GAP + k * CONV_ROWS
            total = jnp.zeros((CONV_ROWS, 128), f32)
            for j in range(KERNEL):
                part = gap_ref[c, pl.ds(start + j - HALF, CONV_ROWS), :]
                total = total + tapped(part, taps_ref[c, j])
            out_ref[c, rows_at(start, CONV_ROWS, 16), :] = total
            return carry

        lax.fori_loop(0, span // CONV_ROWS, chunk, 0)


def convolve_back(dgap_ref, gap_ref, out_ref, taps_ref, taps_grad_ref, length):
    span = length + 2 * GAP
    for c in range(2):

        def chunk(k, carry, c=c):
            start = GAP + k * BACK_ROWS
            units = gap_ref[c, rows_at(start, BACK_ROWS, 16), :]
            total = jnp.zeros((BACK_ROWS, 128), f32)
            sums = []
            for j in range(KERNEL):
                part = dgap_ref[c, pl.ds(start + HALF - j, BACK_ROWS), :]
                total = total + tapped(part, taps_ref[c, j])
                sums.append(carry[j] + col_sum(part * units))
            out_ref[c, rows_at(start, BACK_ROWS, 16), :] = total
            return tuple(sums)

        sums = lax.fori_loop(0, span // BACK_ROWS, chunk, tuple(jnp.zeros((8, 128), f32) for _ in range(KERNEL)))
        for j in range(KERNEL):
            taps_grad_ref[j : j + 1, 128 * c : 128 * c + 128] = jnp.sum(sums[j], axis=0, keepdims=True)
    taps_grad_ref[KERNEL : KERNEL + 1, :] = jnp.zeros((1, 2 * 128), f32)


def add_to(ref, first, value):
    ref[...] = value if first else ref[...] + value


def read_ends(ends_ref):
    return ends_ref[0:1, :], ends_ref[1:2, :], ends_ref[2:3, :]


FRONT = 1280
GATE = 1280


def attend_tile(q2_ref, fq_ref, h, qt, k2_ref, fk_ref, bias_ref, table_ref, tiles):
    rows = slice(qt * QT, (qt + 1) * QT)
    qa = jnp.concatenate([q2_ref[h, rows, :], fq_ref[rows, :]], axis=1)
    ka = jnp.concatenate([k2_ref[h], fk_ref[...]], axis=1)
    offsets = mixed_offsets(tiles)
    s_all = mm_nt(qa, ka)
    parts = []
    for kt in range(tiles):
        s = s_all[:, kt * QT : (kt + 1) * QT]
        o = kt - qt
        if o in offsets:
            s = s + bias_ref[h, offsets.index(o)]
        else:
            s = s + table_ref[h, tile_buckets(o)[0][0]] * LOG2E
        parts.append(jnp.exp2(s).astype(bf16))
    return jnp.concatenate(parts, axis=1)


def attend_tile_below_max(q2_ref, fq_ref, h, rows, start, k2_ref, fk_ref, table_ref, s_ref, tiles):
    qa = jnp.concatenate([q2_ref[h, rows, :], fq_ref[rows, :]], axis=1)
    ka = jnp.concatenate([k2_ref[h], fk_ref[...]], axis=1)
    s_ref[...] = mm_nt(qa, ka)
    ranges = bucket_ranges()

    def add_bias(kt, top):
        cols = rows_at(kt * QT, QT, QT)
        d = tile_distance(0) + (kt * QT - start)
        value = jnp.full((QT, QT), table_ref[h, ranges[0][0]], f32)
        for b, low, _ in ranges[1:]:
            value = jnp.where(d >= low, table_ref[h, b], value)
        s = s_ref[:, cols] + value * LOG2E
        s_ref[:, cols] = s
        return jnp.maximum(top, jnp.max(s, axis=1, keepdims=True))

    top = lax.fori_loop(0, tiles, add_bias, jnp.full((QT, 1), -jnp.inf, f32))
    return jnp.exp2(s_ref[...] - top).astype(bf16)


def kernel_a(
    tiles,
    me_ref,
    table_ref,
    piece0,
    piece1,
    piece2,
    piece3,
    bias_ref,
    g_ff1_ref,
    w_in_ref,
    w_out_ref,
    g_att_ref,
    wq2_ref,
    wk2_ref,
    wv2_ref,
    w_o_ref,
    g_conv_ref,
    w_pw1_ref,
    taps_ref,
    tok_ref,
    ends_ref,
    s1_ref,
    k2_ref,
    v2_ref,
    weights_ref,
    inverse_ref,
    mixed_ref,
    s2_ref,
    gap_ref,
    depth_ref,
    sums_ref,
    q2_ref,
    fq_ref,
    fk_ref,
    fast_ref,
    p_ref,
    s_ref,
    plain_ref,
    conv_ref,
    moved,
):
    pieces = (piece0, piece1, piece2, piece3)
    length = tiles * QT
    frames = length // len(pieces)
    place_pieces(me_ref, pieces, tok_ref, frames)
    extra = sum(p[frames : frames + EXTRA, :].astype(f32) for p in pieces)
    first_end = 16.0 * extra[0:1, :] + extra[1:2, :]
    second_end = first_end + 16.0 * extra[2:3, :] + extra[3:4, :]
    live_end = 16.0 * extra[4:5, :] + extra[5:6, :]
    ends_ref[0:1, :] = first_end
    ends_ref[1:2, :] = second_end
    ends_ref[2:3, :] = live_end
    ends_ref[3:8, :] = jnp.zeros((5, D), f32)
    ends = (first_end, second_end, live_end)

    scale = LOG2E * HD**-0.5

    def front(i, carry):
        at = slice(i * FRONT, (i + 1) * FRONT)
        x = tok_ref[at, :].astype(f32)
        hat, _ = norm_hat(x)
        n1 = (hat * g_ff1_ref[...]).astype(bf16)
        hidden = mm(n1, w_in_ref[...])
        act = (hidden * sigmoid(hidden)).astype(bf16)
        s1 = x + 0.5 * mm(act, w_out_ref[...])
        s1_ref[at, :] = s1
        hat, _ = norm_hat(s1)
        n2 = (hat * g_att_ref[...]).astype(bf16)
        lane = lax.broadcasted_iota(jnp.int32, (FRONT, 128), 1)
        q_top, k_top = carry
        q_all = mm(n2, wq2_ref[...]).astype(bf16).astype(f32) * scale
        k_all = mm(n2, wk2_ref[...]).astype(bf16)
        v_all = mm(n2, wv2_ref[...])
        for h in range(H):
            cols = slice(128 * h, 128 * h + 128)
            q = q_all[:, cols]
            high = q.astype(bf16)
            low = (q - high.astype(f32)).astype(bf16)
            q2_ref[h, at, :] = jnp.where(lane < HD, high.astype(f32), low.astype(f32)).astype(bf16)
            k2_ref[h, at, :] = k_all[:, cols]
            ones = (lane >= HD) & (lane < HD + 3) if h % 2 == 0 else lane < 3
            v2_ref[h, at, :] = jnp.where(ones, 1.0, v_all[:, cols]).astype(bf16)
            q_top = jnp.maximum(q_top, jnp.max(jnp.sum(q * q, axis=1, keepdims=True)))
            k = k_all[:, cols].astype(f32)
            k_top = jnp.maximum(k_top, jnp.max(jnp.sum(k * k, axis=1, keepdims=True)))
        fq_ref[at, :] = query_features(i * FRONT, FRONT, ends).astype(bf16)
        fk_ref[at, :] = key_features(i * FRONT, FRONT, ends)
        return q_top, k_top

    q_top, k_top = jnp.float32(0.0), jnp.float32(0.0)
    for i in range(length // FRONT):
        q_top, k_top = front(i, (q_top, k_top))
    fast_ref[0] = jnp.where(q_top * k_top < 4.0 * SAFE_EXPONENT**2, 1, 0)

    def weights_copy(h, slot):
        return pltpu.make_async_copy(p_ref.at[slot], weights_ref.at[h], moved.at[slot])

    def room(h, slot):
        @pl.when(h > 1)
        def _():
            weights_copy(h - 2, slot).wait()

    def mix(h, slot, rows, p):
        p_ref[slot, rows, :] = p
        total = mm(p, v2_ref[h])
        lane = lax.broadcasted_iota(jnp.int32, (QT, 128), 1)
        first = slot == 0
        denominator = jnp.where(first, total[:, HD : HD + 1], total[:, 0:1])
        inverse = jnp.broadcast_to(1.0 / denominator, (QT, 128))
        mixed = total * inverse
        g = lax.div(h, 2)
        new = jnp.logical_or(first, lane >= HD)
        mixed_ref[g, rows, :] = jnp.where(new, mixed, mixed_ref[g, rows, :])
        inverse_ref[g, rows, :] = jnp.where(new, inverse, inverse_ref[g, rows, :])

    @pl.when(fast_ref[0] == 1)
    def _():
        def head(h, carry):
            slot = lax.rem(h, 2)
            room(h, slot)
            for qt in range(tiles):
                p = attend_tile(q2_ref, fq_ref, h, qt, k2_ref, fk_ref, bias_ref, table_ref, tiles)
                mix(h, slot, slice(qt * QT, (qt + 1) * QT), p)
            weights_copy(h, slot).start()
            return carry

        lax.fori_loop(0, H, head, 0)

    @pl.when(fast_ref[0] != 1)
    def _():
        def head(h, carry):
            slot = lax.rem(h, 2)
            room(h, slot)

            def tile(qt, carry):
                rows = rows_at(qt * QT, QT, QT)
                p = attend_tile_below_max(
                    q2_ref, fq_ref, h, rows, qt * QT, k2_ref, fk_ref, table_ref, s_ref, tiles
                )
                mix(h, slot, rows, p)
                return carry

            lax.fori_loop(0, tiles, tile, 0)
            weights_copy(h, slot).start()
            return carry

        lax.fori_loop(0, H, head, 0)

    def gate(i):
        at = slice(i * GATE, (i + 1) * GATE)
        mixed = jnp.concatenate([mixed_ref[0, at, :], mixed_ref[1, at, :]], axis=1)
        s2 = s1_ref[at, :] + mm(mixed.astype(bf16), w_o_ref[...])
        s2_ref[at, :] = s2
        hat, _ = norm_hat(s2)
        n3 = (hat * g_conv_ref[...]).astype(bf16)
        pair = mm(n3, w_pw1_ref[...])
        live = frame_index(i * GATE, GATE, D) < live_end
        units = jnp.where(live, pair[:, :D] * sigmoid(pair[:, D:]), 0.0).astype(bf16).astype(f32)
        put = slice(i * GATE + 3 * GAP, (i + 1) * GATE + 3 * GAP)
        plain_ref[0, put, :] = units[:, :128]
        plain_ref[1, put, :] = units[:, 128:]

    for i in range(length // GATE):
        gate(i)
    spread_gaps(plain_ref, gap_ref, length, ends)
    convolve(gap_ref, conv_ref, taps_ref, length)

    def collect(i, carry):
        total, squares = carry
        at = rows_at(i * QT, QT, QT)
        depth = close_gaps(conv_ref, i * QT, QT, ends)
        depth_ref[at, :] = depth
        kept = jnp.where(frame_index(i * QT, QT, D) < live_end, depth, 0.0)
        return total + col_sum(kept), squares + col_sum(kept * kept)

    empty = jnp.zeros((8, D), f32)
    total, squares = lax.fori_loop(0, tiles, collect, (empty, empty))
    sums_ref[0:1, :] = jnp.sum(total, axis=0, keepdims=True)
    sums_ref[1:2, :] = jnp.sum(squares, axis=0, keepdims=True)
    sums_ref[2:3, :] = live_end
    sums_ref[3:8, :] = jnp.zeros((5, D), f32)
    for parity in range(2):
        weights_copy(H - 2 + parity, parity).wait()


MIDDLE = 1280


def batch_norm_terms(sums_ref):
    count = sums_ref[2:3, :]
    center = sums_ref[0:1, :] / count
    spread = sums_ref[1:2, :] / count - center * center
    return count, center, lax.rsqrt(spread + epsilon)


def kernel_b(
    tiles,
    me_ref,
    cot0,
    cot1,
    cot2,
    cot3,
    sums_ref,
    depth_ref,
    s2_ref,
    bn_gain_ref,
    w_pw2_ref,
    g_ff2_ref,
    w_in_ref,
    w_out_ref,
    g_out_ref,
    out0,
    out1,
    out2,
    out3,
    grad3_ref,
    bngrad_ref,
    sums2_ref,
    big_ref,
    small_ref,
    cot_ref,
    out_ref,
    dw_in_ref,
    dw_out_ref,
    dw_pw2_ref,
):
    length = tiles * QT
    frames = length // 4
    place_pieces(me_ref, (cot0, cot1, cot2, cot3), cot_ref, frames)
    _, center, inverse = batch_norm_terms(sums_ref)
    bn_gain = bn_gain_ref[...]

    def step(i, carry):
        g_out_sum, g_ff2_sum, bn_sum, bn_dot = carry
        at = slice(i * MIDDLE, (i + 1) * MIDDLE)
        standard = (depth_ref[at, :] - center) * inverse
        pre = standard * bn_gain
        logistic3 = sigmoid(pre)
        act3 = (pre * logistic3).astype(bf16)
        s3 = s2_ref[at, :] + mm(act3, w_pw2_ref[...])
        hat3, inv3 = norm_hat(s3)
        n4 = (hat3 * g_ff2_ref[...]).astype(bf16)
        hidden = mm(n4, w_in_ref[...])
        logistic = sigmoid(hidden)
        act4 = (hidden * logistic).astype(bf16)
        s4 = s3 + 0.5 * mm(act4, w_out_ref[...])
        hat4, inv4 = norm_hat(s4)
        out_ref[at, :] = (hat4 * g_out_ref[...]).astype(bf16)
        cot = cot_ref[at, :].astype(f32)
        g_out_sum = g_out_sum + col_sum(cot * hat4)
        grad4 = norm_back(cot, g_out_ref[...], hat4, inv4)
        out4 = (0.5 * grad4).astype(bf16)
        add_to(dw_out_ref, i == 0, mm(turned(out4), act4))
        slope = logistic * (1.0 + hidden * (1.0 - logistic))
        hid4 = (mm_nt(out4, w_out_ref[...]) * slope).astype(bf16)
        add_to(dw_in_ref, i == 0, mm(turned(n4), hid4))
        up = mm_nt(hid4, w_in_ref[...])
        g_ff2_sum = g_ff2_sum + col_sum(up * hat3)
        grad3 = grad4 + norm_back(up, g_ff2_ref[...], hat3, inv3)
        grad3_ref[at, :] = grad3
        out3 = grad3.astype(bf16)
        add_to(dw_pw2_ref, i == 0, mm(turned(act3), out3))
        bngrad = mm_nt(out3, w_pw2_ref[...]) * (logistic3 * (1.0 + pre * (1.0 - logistic3)))
        bngrad_ref[at, :] = bngrad
        return g_out_sum, g_ff2_sum, bn_sum + col_sum(bngrad), bn_dot + col_sum(bngrad * standard)

    empty = jnp.zeros((8, D), f32)
    sums = (empty,) * 4
    for i in range(length // MIDDLE):
        sums = step(i, sums)
    g_out_sum, g_ff2_sum, bn_sum, bn_dot = (jnp.sum(s, axis=0, keepdims=True) for s in sums)
    sums2_ref[0:1, :] = bn_sum
    sums2_ref[1:2, :] = bn_dot
    sums2_ref[2:8, :] = jnp.zeros((6, D), f32)
    small_ref[0:1, :] = g_ff2_sum
    small_ref[1:2, :] = g_out_sum
    small_ref[2:8, :] = jnp.zeros((6, D), f32)
    big_ref[0:FF, :] = turned_wide(dw_out_ref)
    for c in range(FF // D):
        big_ref[FF + c * D : FF + (c + 1) * D, :] = dw_in_ref[:, c * D : (c + 1) * D].astype(big_ref.dtype)
    big_ref[2 * FF : 2 * FF + D, :] = dw_pw2_ref[...].astype(big_ref.dtype)
    take_pieces(me_ref, out_ref, (out0, out1, out2, out3), frames)


def turned_wide(ref):
    return jnp.concatenate([ref[:, c * D : (c + 1) * D].T for c in range(ref.shape[1] // D)], axis=0).astype(bf16)


BACK = 640
LAST = 256


def kernel_c(
    tiles,
    me_ref,
    sums_ref,
    sums2_ref,
    tok_ref,
    ends_ref,
    s1_ref,
    k2_ref,
    v2_ref,
    weights_ref,
    inverse_ref,
    mixed_ref,
    s2_ref,
    gap_ref,
    depth_ref,
    grad3_ref,
    bngrad_ref,
    g_ff1_ref,
    w_ff1_in_ref,
    w_ff1_out_ref,
    g_att_ref,
    w_q_ref,
    w_k_ref,
    w_v_ref,
    w_o_ref,
    g_conv_ref,
    w_pw1_ref,
    taps_ref,
    bn_gain_ref,
    big_b_ref,
    small_b_ref,
    piece0,
    piece1,
    piece2,
    piece3,
    kept_ref,
    sent_ref,
    big_ref,
    small_ref,
    plain_ref,
    dgap_ref,
    grad_ref,
    do_ref,
    dot_ref,
    qt_ref,
    p_ref,
    dq_ref,
    dkt_ref,
    dvt_ref,
    acc_ref,
    taps_grad_ref,
    dw_in_ref,
    dw_out_ref,
    dw_o_ref,
    dw_pw1_ref,
    dw_q_ref,
    dw_k_ref,
    dw_v_ref,
    arrived,
):
    length = tiles * QT
    frames = length // 4
    ends = read_ends(ends_ref)
    live_end = ends[2]
    count, center, inverse = batch_norm_terms(sums_ref)
    bn_gain = bn_gain_ref[...]
    e_total = sums2_ref[0:1, :] * bn_gain
    dot_total = sums2_ref[1:2, :]

    def weights_copy(h, slot):
        return pltpu.make_async_copy(weights_ref.at[h], p_ref.at[slot], arrived.at[slot])

    weights_copy(0, 0).start()


    def batch_back(i, carry):
        at = rows_at(i * QT, QT, QT)
        standard = (depth_ref[at, :] - center) * inverse
        e = bngrad_ref[at, :] * bn_gain
        share = jnp.where(frame_index(i * QT, QT, D) < live_end, 1.0, 0.0) / count
        dg = inverse * (e - share * e_total - share * standard * bn_gain * dot_total)
        dg = dg.astype(bf16).astype(f32)
        put = rows_at(i * QT + 3 * GAP, QT, 16)
        plain_ref[0, put, :] = dg[:, :128]
        plain_ref[1, put, :] = dg[:, 128:]
        return carry

    lax.fori_loop(0, tiles, batch_back, 0)
    spread_gaps(plain_ref, dgap_ref, length, ends)
    convolve_back(dgap_ref, gap_ref, plain_ref, taps_ref, taps_grad_ref, length)

    def gate_back(i, g_conv_sum):
        at = slice(i * BACK, (i + 1) * BACK)
        hat, inv = norm_hat(s2_ref[at, :])
        n3 = (hat * g_conv_ref[...]).astype(bf16)
        pair = mm(n3, w_pw1_ref[...])
        first, logistic = pair[:, :D], sigmoid(pair[:, D:])
        live = frame_index(i * BACK, BACK, D) < live_end
        ug = jnp.where(live, close_gaps(plain_ref, i * BACK, BACK, ends), 0.0) * logistic
        pairgrad = jnp.concatenate([ug, ug * first * (1.0 - logistic)], axis=1).astype(bf16)
        add_to(dw_pw1_ref, i == 0, mm(turned(n3), pairgrad))
        up = mm_nt(pairgrad, w_pw1_ref[...])
        g_conv_sum = g_conv_sum + col_sum(up * hat)
        grad2 = grad3_ref[at, :] + norm_back(up, g_conv_ref[...], hat, inv)
        grad_ref[at, :] = grad2
        out2 = grad2.astype(bf16)
        mixed = jnp.concatenate([mixed_ref[0, at, :], mixed_ref[1, at, :]], axis=1)
        add_to(dw_o_ref, i == 0, mm(turned(mixed), out2))
        mixgrad = mm_nt(out2, w_o_ref[...]).astype(bf16).astype(f32)
        mixgrad = (mixgrad * jnp.concatenate([inverse_ref[0, at, :], inverse_ref[1, at, :]], axis=1)).astype(bf16)
        dot_ref[:, at] = turned(mixgrad)
        product = mixgrad.astype(f32) * mixed
        lane = lax.broadcasted_iota(jnp.int32, (BACK, 128), 1)
        for h in range(H):
            cols = slice(128 * (h // 2), 128 * (h // 2) + 128)
            own = lane < HD if h % 2 == 0 else lane >= HD
            delta = jnp.sum(jnp.where(own, product[:, cols], 0.0), axis=1, keepdims=True)
            high, middle, low = three_parts(-delta)
            base = HD if h % 2 == 0 else 0
            side = jnp.where(lane == base, high, 0.0)
            side = jnp.where(lane == base + 1, middle, side)
            side = jnp.where(lane == base + 2, low, side)
            do_ref[h, at, :] = jnp.where(own, mixgrad[:, cols].astype(f32), side).astype(bf16)
        hat, _ = norm_hat(s1_ref[at, :])
        n2 = (hat * g_att_ref[...]).astype(bf16)
        qt_ref[:, at] = turned(mm(n2, w_q_ref[...]).astype(bf16))
        return g_conv_sum

    empty = jnp.zeros((8, D), f32)
    g_conv_sum = empty
    for i in range(length // BACK):
        g_conv_sum = gate_back(i, g_conv_sum)


    offsets = mixed_offsets(tiles)

    def head(h, carry):
        slot = lax.rem(h, 2)

        @pl.when(h + 1 < H)
        def _():
            weights_copy(h + 1, 1 - slot).start()

        weights_copy(h, slot).wait()
        flat = {}
        started = set()
        own = rows_at(h * HD, HD, HD)
        dvt_ref[own, :] = mm(dot_ref[own, :], p_ref[slot])
        pair = lax.div(h, 2)
        for qt in range(tiles):
            rows = slice(qt * QT, (qt + 1) * QT)
            d_all = mm_nt(do_ref[h, rows, :], v2_ref[h])
            low = []
            for kt in range(tiles):
                cols = slice(kt * QT, (kt + 1) * QT)
                ds = p_ref[slot, rows, cols].astype(f32) * d_all[:, cols]
                o = kt - qt
                if o in offsets:
                    k = offsets.index(o)
                    acc_ref[k] = acc_ref[k] + ds if k in started else ds
                    started.add(k)
                else:
                    b = tile_buckets(o)[0][0]
                    flat[b] = flat[b] + col_sum(ds) if b in flat else col_sum(ds)
                low.append(ds.astype(bf16))
            low = jnp.concatenate(low, axis=1)
            p_ref[slot, rows, :] = low
            dq = mm(low, k2_ref[h])
            own_half = (lax.broadcasted_iota(jnp.int32, (QT, 128), 1) < HD) == (slot == 0)
            dq_ref[pair, rows, :] = jnp.where(own_half, dq, dq_ref[pair, rows, :])
        dkt_ref[own, :] = mm(qt_ref[own, :], p_ref[slot])
        table_row = jnp.zeros((1, D), f32)
        lane = lax.broadcasted_iota(jnp.int32, (1, D), 1)
        for k, o in enumerate(offsets):
            d = tile_distance(o)
            value = acc_ref[k]
            found = tile_buckets(o)
            tails = [col_sum(jnp.where(d >= lo, value, 0.0)) for _, lo in found[1:]]
            tails = [col_sum(value)] + tails
            for n, (b, _) in enumerate(found):
                part = tails[n] - tails[n + 1] if n + 1 < len(found) else tails[n]
                flat[b] = flat[b] + part if b in flat else part
        for b, part in flat.items():
            table_row = jnp.where(lane == b, jnp.sum(part), table_row)
        small_ref[pl.ds(h + 4, 1), :] = table_row
        return carry

    small_ref[...] = jnp.zeros_like(small_ref)
    lax.fori_loop(0, H, head, 0)


    def front_back(i, carry):
        g_att_sum, g_ff1_sum = carry
        at = slice(i * LAST, (i + 1) * LAST)
        dq = jnp.concatenate([dq_ref[g, at, :] for g in range(H // 2)], axis=1)
        dq = (dq * HD**-0.5).astype(bf16)
        dk = (dkt_ref[:, at] * HD**-0.5).T.astype(bf16)
        dv = dvt_ref[:, at].T.astype(bf16)
        s1 = s1_ref[at, :]
        hat2, inv2 = norm_hat(s1)
        n2 = turned((hat2 * g_att_ref[...]).astype(bf16))
        add_to(dw_q_ref, i == 0, mm(n2, dq))
        add_to(dw_k_ref, i == 0, mm(n2, dk))
        add_to(dw_v_ref, i == 0, mm(n2, dv))
        attgrad = mm_nt(dq, w_q_ref[...]) + mm_nt(dk, w_k_ref[...]) + mm_nt(dv, w_v_ref[...])
        g_att_sum = g_att_sum + col_sum(attgrad * hat2)
        grad1 = grad_ref[at, :] + norm_back(attgrad, g_att_ref[...], hat2, inv2)
        out1 = (0.5 * grad1).astype(bf16)
        x = tok_ref[at, :].astype(f32)
        hat1, inv1 = norm_hat(x)
        n1 = (hat1 * g_ff1_ref[...]).astype(bf16)
        hidden = mm(n1, w_ff1_in_ref[...])
        logistic = sigmoid(hidden)
        act1 = (hidden * logistic).astype(bf16)
        add_to(dw_out_ref, i == 0, mm(turned(out1), act1))
        slope = logistic * (1.0 + hidden * (1.0 - logistic))
        hid1 = (mm_nt(out1, w_ff1_out_ref[...]) * slope).astype(bf16)
        add_to(dw_in_ref, i == 0, mm(turned(n1), hid1))
        up = mm_nt(hid1, w_ff1_in_ref[...])
        g_ff1_sum = g_ff1_sum + col_sum(up * hat1)
        grad_ref[at, :] = grad1 + norm_back(up, g_ff1_ref[...], hat1, inv1)
        return g_att_sum, g_ff1_sum

    g_att_sum, g_ff1_sum = empty, empty
    for i in range(length // LAST):
        g_att_sum, g_ff1_sum = front_back(i, (g_att_sum, g_ff1_sum))
    for k, s in enumerate((g_ff1_sum, g_att_sum, g_conv_sum)):
        small_ref[k : k + 1, :] = jnp.sum(s, axis=0, keepdims=True)
    small_ref[8 : 8 + KERNEL + 1, :] = taps_grad_ref[...]
    big_ref[0:FF, :] = turned_wide(dw_out_ref)
    for c in range(FF // D):
        big_ref[FF + c * D : FF + (c + 1) * D, :] = dw_in_ref[:, c * D : (c + 1) * D].astype(bf16)
    base = 2 * FF
    for k, ref in enumerate((dw_q_ref, dw_k_ref, dw_v_ref, dw_o_ref)):
        big_ref[base + k * D : base + (k + 1) * D, :] = ref[...].astype(bf16)
    base = 2 * FF + 4 * D
    for c in range(2):
        big_ref[base + c * D : base + (c + 1) * D, :] = dw_pw1_ref[:, c * D : (c + 1) * D].astype(bf16)
    base = BIG_C
    big_ref[base : base + BIG_B, :] = big_b_ref[...]
    base = BIG_C + BIG_B
    big_ref[base : base + SMALL_C, :] = small_ref[...].astype(bf16)
    big_ref[base + SMALL_C : base + SMALL_C + SMALL_B, :] = small_b_ref[...].astype(bf16)
    used = base + SMALL_C + SMALL_B
    big_ref[used:, :] = jnp.zeros((big_ref.shape[0] - used, D), bf16)
    half = big_ref.shape[0] // 2
    side = me_ref[1]
    kept_ref[...] = big_ref[rows_at(side * half, half, half), :]
    sent_ref[...] = big_ref[rows_at((1 - side) * half, half, half), :]
    take_pieces(me_ref, grad_ref, (piece0, piece1, piece2, piece3), frames)


def swap(x, axis, bit):
    size = lax.axis_size(axis)
    return lax.ppermute(x, axis, [(i, i ^ bit) for i in range(size)])


def doubling_steps():
    steps = []
    for axis in ("rows", "blk"):
        size = lax.axis_size(axis)
        bit = 1
        while bit < size:
            steps.append((axis, bit))
            bit *= 2
    return steps


def sum_everywhere(x):
    for axis, bit in doubling_steps():
        x = x + swap(x, axis, bit)
    return x


def to_pieces(x, me):
    own = lax.dynamic_index_in_dim(x, me, 0, keepdims=False)
    pieces = [own]
    for m in range(1, x.shape[0]):
        pieces.append(swap(lax.dynamic_index_in_dim(x, me ^ m, 0, keepdims=False), "blk", m))
    return pieces


def from_pieces(pieces):
    return [pieces[0]] + [swap(p, "blk", m) for m, p in enumerate(pieces) if m > 0]


def keep_half(x, axis, bit):
    half = x.shape[0] // 2
    side = (lax.axis_index(axis) // bit) % 2
    kept = lax.dynamic_slice_in_dim(x, side * half, half, 0)
    sent = lax.dynamic_slice_in_dim(x, (1 - side) * half, half, 0)
    got = swap(sent.astype(bf16), axis, bit)
    return kept.astype(f32) + got.astype(f32)


def join_half(x, axis, bit):
    side = (lax.axis_index(axis) // bit) % 2
    got = swap(x, axis, bit)
    return jnp.where(side == 0, jnp.concatenate([x, got]), jnp.concatenate([got, x]))


def reduce_gradients(kept, sent, token_grads):
    got = swap(sent, "rows", 1)
    got, token_grads = lax.optimization_barrier((got, token_grads))
    token_grads = from_pieces(token_grads)
    x = kept.astype(f32) + got.astype(f32)
    half = x.shape[0] // 2
    a, b = x[:half], x[half:]
    a_steps = (("rows", 2), ("rows", 4), ("blk", 1), ("blk", 2))
    b_steps = (("rows", 4), ("rows", 2), ("blk", 1), ("blk", 2))
    for k, (sa, sb) in enumerate(zip(a_steps, b_steps)):
        if k == 2:
            a, b, token_grads = lax.optimization_barrier((a, b, token_grads))
        a, b = keep_half(a, *sa), keep_half(b, *sb)
    a, b = a.astype(bf16), b.astype(bf16)
    for sa, sb in zip(a_steps[::-1], b_steps[::-1]):
        a, b = join_half(a, *sa), join_half(b, *sb)
    return (a, b, swap(a, "rows", 1), swap(b, "rows", 1)), token_grads


BIG_B = 2 * FF + D
BIG_C = 2 * FF + 6 * D
SMALL_C = 40
SMALL_B = 8


def kernel_d(
    frames,
    me_ref,
    o0,
    o1,
    o2,
    o3,
    t0,
    t1,
    t2,
    t3,
    own_a,
    own_b,
    other_a,
    other_b,
    sums2_ref,
    output_ref,
    tokens_ref,
    ff1_in,
    ff1_out,
    w_q,
    w_k,
    w_v,
    w_o,
    pw1,
    pw2,
    ff2_in,
    ff2_out,
    g_ff1,
    g_att,
    g_conv,
    rel,
    taps,
    g_ff2,
    g_out,
    bn_gain,
    big_ref,
):
    quarter = own_a.shape[0]
    side = me_ref[1]
    for k, (own, other) in enumerate(((own_a, other_a), (own_b, other_b))):
        big_ref[rows_at((2 * side + k) * quarter, quarter, 64), :] = own[...]
        big_ref[rows_at((2 * (1 - side) + k) * quarter, quarter, 64), :] = other[...]
    for m, (o, t) in enumerate(zip((o0, o1, o2, o3), (t0, t1, t2, t3))):
        output_ref[me_ref[0] ^ m] = o[...]
        tokens_ref[me_ref[0] ^ m] = t[...].astype(f32)
    ff1_out[...] = big_ref[0:FF, :].astype(f32)
    for c in range(FF // D):
        ff1_in[:, c * D : (c + 1) * D] = big_ref[FF + c * D : FF + (c + 1) * D, :].astype(f32)
    base = 2 * FF
    for k, ref in enumerate((w_q, w_k, w_v, w_o)):
        ref[...] = big_ref[base + k * D : base + (k + 1) * D, :].astype(f32)
    base = 2 * FF + 4 * D
    for c in range(2):
        pw1[:, c * D : (c + 1) * D] = big_ref[base + c * D : base + (c + 1) * D, :].astype(f32)
    base = BIG_C
    ff2_out[...] = big_ref[base : base + FF, :].astype(f32)
    for c in range(FF // D):
        at = base + FF + c * D
        ff2_in[:, c * D : (c + 1) * D] = big_ref[at : at + D, :].astype(f32)
    pw2[...] = big_ref[base + 2 * FF : base + 2 * FF + D, :].astype(f32)
    small = big_ref[BIG_C + BIG_B : BIG_C + BIG_B + SMALL_C + SMALL_B, :].astype(f32)
    g_ff1[...], g_att[...], g_conv[...] = small[0:1], small[1:2], small[2:3]
    rel[...] = small[4:8, :NBUCKET]
    taps[...] = small[8 : 8 + KERNEL]
    g_ff2[...], g_out[...] = small[SMALL_C : SMALL_C + 1], small[SMALL_C + 1 : SMALL_C + 2]
    bn_gain[...] = sums2_ref[1:2, :]


def shape_of(shape, dtype):
    return jax.ShapeDtypeStruct(shape, dtype)


def call(body, smem, outs, scratch, name, far_in=(), far_out=(), micros=1, mib=16):
    def place(far, count):
        return [pl.BlockSpec(memory_space=pl.ANY if k in far else pltpu.VMEM) for k in range(count)]

    def run(*operands):
        specs = [pl.BlockSpec(memory_space=pltpu.SMEM)] * smem + place(far_in, len(operands))[smem:]
        return pl.pallas_call(
            body,
            out_shape=outs,
            in_specs=specs,
            out_specs=place(far_out, len(outs)),
            scratch_shapes=scratch,
            compiler_params=pltpu.CompilerParams(vmem_limit_bytes=mib * MIB),
            cost_estimate=pl.CostEstimate(flops=micros * 10**9, bytes_accessed=micros * 10**6, transcendentals=0),
            name=name,
        )(*operands)

    return run


def twice(weight):
    heads = weight.reshape(D, H, HD)
    return jnp.concatenate([heads, heads], axis=2).reshape(D, 2 * D)


def one_side(weight):
    heads = weight.reshape(D, H // 2, 2, HD)
    empty = jnp.zeros_like(heads[:, :, 0])
    even = jnp.concatenate([heads[:, :, 0], empty], axis=2)
    odd = jnp.concatenate([empty, heads[:, :, 1]], axis=2)
    return jnp.stack([even, odd], axis=2).reshape(D, 2 * D)


MIB_A = 34
MIB_B = 32
MIB_C = 44


def packed_rows():
    rows = BIG_C + BIG_B + SMALL_C + SMALL_B
    return -(-rows // 1024) * 1024


def run_a(tiles, *operands):
    length = tiles * QT
    frames = length // 4
    padded_rows = length + 4 * GAP
    n_mixed = len(mixed_offsets(tiles))
    return call(
        functools.partial(kernel_a, tiles),
        2,
        [
            shape_of((length, D), bf16),
            shape_of((8, D), f32),
            shape_of((length, D), f32),
            shape_of((H, length, 128), bf16),
            shape_of((H, length, 128), bf16),
            shape_of((H, length, length), bf16),
            shape_of((H // 2, length, 128), f32),
            shape_of((H // 2, length, 128), f32),
            shape_of((length, D), f32),
            shape_of((2, padded_rows, 128), f32),
            shape_of((length, D), f32),
            shape_of((8, D), f32),
        ],
        [
            pltpu.VMEM((H, length, 128), bf16),
            pltpu.VMEM((length, 128), bf16),
            pltpu.VMEM((length, 128), bf16),
            pltpu.SMEM((1,), jnp.int32),
            pltpu.VMEM((2, length, length), bf16),
            pltpu.VMEM((QT, length), f32),
            pltpu.VMEM((2, length + 6 * GAP, 128), f32),
            pltpu.VMEM((2, padded_rows, 128), f32),
            pltpu.SemaphoreType.DMA((2,)),
        ],
        "first_part",
        far_out=(5,),
        micros=30,
        mib=MIB_A,
    )(*operands)


def run_b(tiles, *operands):
    length = tiles * QT
    frames = length // 4
    padded_rows = length + 4 * GAP
    n_mixed = len(mixed_offsets(tiles))
    return call(
        functools.partial(kernel_b, tiles),
        1,
        [shape_of((frames, D), bf16)] * 4
        + [
            shape_of((length, D), f32),
            shape_of((length, D), f32),
            shape_of((8, D), f32),
            shape_of((BIG_B, D), bf16),
            shape_of((SMALL_B, D), f32),
        ],
        [
            pltpu.VMEM((length, D), bf16),
            pltpu.VMEM((length, D), bf16),
            pltpu.VMEM((D, FF), f32),
            pltpu.VMEM((D, FF), f32),
            pltpu.VMEM((D, D), f32),
        ],
        "middle_part",
        micros=12,
        mib=MIB_B,
    )(*operands)


def run_c(tiles, *operands):
    length = tiles * QT
    frames = length // 4
    padded_rows = length + 4 * GAP
    n_mixed = len(mixed_offsets(tiles))
    return call(
        functools.partial(kernel_c, tiles),
        1,
        [shape_of((frames, D), bf16)] * 4 + [shape_of((packed_rows() // 2, D), bf16)] * 2,
        [
            pltpu.VMEM((packed_rows(), D), bf16),
            pltpu.VMEM((SMALL_C, D), f32),
            pltpu.VMEM((2, length + 6 * GAP, 128), f32),
            pltpu.VMEM((2, padded_rows, 128), f32),
            pltpu.VMEM((length, D), f32),
            pltpu.VMEM((H, length, 128), bf16),
            pltpu.VMEM((D, length), bf16),
            pltpu.VMEM((D, length), bf16),
            pltpu.VMEM((2, length, length), bf16),
            pltpu.VMEM((H // 2, length, 128), f32),
            pltpu.VMEM((D, length), f32),
            pltpu.VMEM((D, length), f32),
            pltpu.VMEM((n_mixed, QT, QT), f32),
            pltpu.VMEM((KERNEL + 1, D), f32),
            pltpu.VMEM((D, FF), f32),
            pltpu.VMEM((D, FF), f32),
            pltpu.VMEM((D, D), f32),
            pltpu.VMEM((D, 2 * D), f32),
            pltpu.VMEM((D, D), f32),
            pltpu.VMEM((D, D), f32),
            pltpu.VMEM((D, D), f32),
            pltpu.SemaphoreType.DMA((2,)),
        ],
        "last_part",
        far_in=(8,),
        micros=45,
        mib=MIB_C,
    )(*operands)


def row_device(
    tokens,
    seg_ids,
    frame_mask,
    cotangent,
    g_ff1,
    w_ff1_in,
    w_ff1_out,
    g_att,
    w_query,
    w_key,
    w_value,
    w_output,
    rel_table,
    g_conv,
    w_pw1,
    w_depth,
    bn_gain,
    w_pw2,
    g_ff2,
    w_ff2_in,
    w_ff2_out,
    g_out,
):
    blocks, frames, _ = tokens.shape
    length = blocks * frames
    tiles = length // QT
    n_mixed = len(mixed_offsets(tiles))
    me = lax.axis_index("blk")
    me_ref = jnp.stack([me, lax.axis_index("rows") % 2]).astype(jnp.int32)
    gains = [g.reshape(1, D) for g in (g_ff1, g_att, g_conv, bn_gain, g_ff2, g_out)]
    g_ff1, g_att, g_conv, bn_gain, g_ff2, g_out = gains

    lengths = [
        jnp.sum((seg_ids == 0).astype(jnp.int32), axis=1),
        jnp.sum((seg_ids == 1).astype(jnp.int32), axis=1),
        jnp.sum(frame_mask, axis=1),
    ]
    digits = jnp.stack([part for n in lengths for part in (n // 16, n % 16)], axis=1)
    digits = jnp.pad(digits, ((0, 0), (0, EXTRA - digits.shape[1]))).astype(bf16)
    extra = jnp.broadcast_to(digits[:, :, None], (blocks, EXTRA, D))
    token_pieces = to_pieces(jnp.concatenate([tokens, extra], axis=1), me)
    cotangent, token_pieces = lax.optimization_barrier((cotangent, token_pieces))
    cot_pieces = to_pieces(cotangent, me)

    bias = call(
        functools.partial(bias_kernel, tiles), 1, [shape_of((H, n_mixed, QT, QT), f32)], [], "bias_tiles"
    )(rel_table)[0]
    taps = w_depth.astype(f32).reshape(KERNEL, 2, 128).transpose(1, 0, 2)
    taps = jnp.broadcast_to(taps[:, :, None, :], (2, KERNEL, 8, 128))

    (tok, ends, s1, k2, v2, weights, inverse, mixed, s2, gap, depth, sums) = run_a(
        tiles,
        me_ref,
        rel_table,
        *token_pieces,
        bias,
        g_ff1,
        w_ff1_in,
        w_ff1_out,
        g_att,
        twice(w_query),
        twice(w_key),
        one_side(w_value),
        w_output,
        g_conv,
        w_pw1,
        taps,
    )
    sums = sum_everywhere(sums)

    (o0, o1, o2, o3, grad3, bngrad, sums2, big_b, small_b) = run_b(
        tiles, me_ref, *cot_pieces, sums, depth, s2, bn_gain, w_pw2, g_ff2, w_ff2_in, w_ff2_out, g_out
    )
    out_pieces = from_pieces([o0, o1, o2, o3])
    sums2 = sum_everywhere(sums2)

    (t0, t1, t2, t3, kept, sent) = run_c(
        tiles,
        me_ref,
        sums,
        sums2,
        tok,
        ends,
        s1,
        k2,
        v2,
        weights,
        inverse,
        mixed,
        s2,
        gap,
        depth,
        grad3,
        bngrad,
        g_ff1,
        w_ff1_in,
        w_ff1_out,
        g_att,
        w_query,
        w_key,
        w_value,
        w_output,
        g_conv,
        w_pw1,
        taps,
        bn_gain,
        big_b,
        small_b,
    )
    kept, sent, out_pieces = lax.optimization_barrier((kept, sent, out_pieces))
    reduced, token_grads = reduce_gradients(kept, sent, [t0, t1, t2, t3])

    (output, tokens_grad, ff1_in, ff1_out, w_q, w_k, w_v, w_o, pw1, pw2, ff2_in, ff2_out, *small) = call(
        functools.partial(kernel_d, frames),
        1,
        [
            shape_of((blocks, frames, D), bf16),
            shape_of((blocks, frames, D), f32),
            shape_of((D, FF), f32),
            shape_of((FF, D), f32),
            shape_of((D, D), f32),
            shape_of((D, D), f32),
            shape_of((D, D), f32),
            shape_of((D, D), f32),
            shape_of((D, 2 * D), f32),
            shape_of((D, D), f32),
            shape_of((D, FF), f32),
            shape_of((FF, D), f32),
            *[shape_of((1, D), f32)] * 3,
            shape_of((H, NBUCKET), f32),
            shape_of((KERNEL, D), f32),
            *[shape_of((1, D), f32)] * 3,
        ],
        [pltpu.VMEM((packed_rows(), D), bf16)],
        "unpack",
        micros=5,
        mib=32,
    )(me_ref, *out_pieces, *token_grads, *reduced, sums2)
    d_g_ff1, d_g_att, d_g_conv, rel, d_taps, d_g_ff2, d_g_out, d_bn_gain = small
    return (
        output,
        tokens_grad,
        d_g_ff1.reshape(D),
        ff1_in,
        ff1_out,
        d_g_att.reshape(D),
        w_q,
        w_k,
        w_v,
        w_o,
        rel,
        d_g_conv.reshape(D),
        pw1,
        d_taps,
        d_bn_gain.reshape(D),
        pw2,
        d_g_ff2.reshape(D),
        ff2_in,
        ff2_out,
        d_g_out.reshape(D),
    )


def padded(x, sides, width):
    for axis, dim in sides:
        size, length = (lax.axis_size(axis), x.shape[dim])
        up = [(i, (i + 1) % size) for i in range(size - 1)]
        down = [(j, i) for i, j in up]
        last = lax.slice_in_dim(x, length - width, length, axis=dim)
        first = lax.slice_in_dim(x, 0, width, axis=dim)
        before = lax.ppermute(last, axis, up)
        after = lax.ppermute(first, axis, down)
        x = jnp.concatenate([before, x, after], axis=dim)
    return x


def norm_forward(values, norm_gain):
    center = jnp.mean(values, axis=-1, keepdims=True)
    shifted = values - center
    spread = jnp.mean(shifted * shifted, axis=-1, keepdims=True)
    inverse = lax.rsqrt(spread + epsilon)
    scaled = shifted * inverse
    return (scaled * norm_gain, (scaled, inverse))


def norm_backward(upstream, norm_gain, stored):
    scaled, inverse = stored
    gain_grad = jnp.sum(upstream * scaled, axis=(0, 1))
    inner_grad = upstream * norm_gain
    inner_mean = jnp.mean(inner_grad, axis=-1, keepdims=True)
    inner_dot = jnp.mean(inner_grad * scaled, axis=-1, keepdims=True)
    return (inverse * (inner_grad - inner_mean - scaled * inner_dot), gain_grad)


def project(left_side, weight):
    return jnp.einsum("rfd,de->rfe", left_side, weight, preferred_element_type=jnp.float32)


def project_back(upstream, weight):
    return jnp.einsum("rfe,de->rfd", upstream, weight, preferred_element_type=jnp.float32)


def weight_product(left_side, upstream):
    return jnp.einsum("rfd,rfe->de", left_side, upstream, preferred_element_type=jnp.float32)


def silu_slope(values):
    logistic = jax.nn.sigmoid(values)
    return logistic * (1.0 + values * (1.0 - logistic))


def ffn_forward(values, norm_gain, weight_in, weight_out):
    normed, norm_stored = norm_forward(values, norm_gain)
    normed_low = normed.astype(jnp.bfloat16)
    hidden = project(normed_low, weight_in)
    act_low = jax.nn.silu(hidden).astype(jnp.bfloat16)
    return (project(act_low, weight_out), (norm_stored, normed_low, hidden, act_low))


def ffn_backward(stream_grad, norm_gain, weight_in, weight_out, stored):
    norm_stored, normed_low, hidden, act_low = stored
    out_low = (0.5 * stream_grad).astype(jnp.bfloat16)
    out_weight_grad = weight_product(act_low, out_low)
    hidden_low = (project_back(out_low, weight_out) * silu_slope(hidden)).astype(jnp.bfloat16)
    in_weight_grad = weight_product(normed_low, hidden_low)
    input_grad, gain_grad = norm_backward(
        project_back(hidden_low, weight_in), norm_gain, norm_stored
    )
    return (stream_grad + input_grad, (gain_grad, in_weight_grad, out_weight_grad))


def bucket_bias(query_pos, key_pos, rel_table):
    distance = key_pos[None, :] - query_pos[:, None]
    levels = NBUCKET // 2
    magnitude = jnp.abs(distance)
    bucket = levels * (distance > 0).astype(jnp.int32)
    for exponent in range(levels - 1):
        bucket = bucket + (magnitude >= 4**exponent).astype(jnp.int32)
    onehot = (bucket[:, :, None] == jnp.arange(NBUCKET, dtype=jnp.int32)[None, None, :]).astype(
        jnp.float32
    )
    position_bias = jnp.einsum("qkb,hb->hqk", onehot, rel_table, precision=lax.Precision.HIGHEST)
    return (position_bias, onehot)


def block_at(source, block_index, query_heads, segment_float, query_pos, rel_table):
    key_all, value_all, code_all = source
    row_count, frames = segment_float.shape
    key_start = block_index * frames
    key_block = lax.dynamic_slice_in_dim(key_all, key_start, frames, 1).reshape(
        row_count, frames, H, HD
    )
    value_block = lax.dynamic_slice_in_dim(value_all, key_start, frames, 1).reshape(
        row_count, frames, H, HD
    )
    code_block = lax.dynamic_slice_in_dim(code_all, key_start, frames, 1)
    key_pos = key_start + jnp.arange(frames, dtype=jnp.int32)
    position_bias, onehot = bucket_bias(query_pos, key_pos, rel_table)
    raw_scores = (
        jnp.einsum("rqhd,rkhd->rhqk", query_heads, key_block, preferred_element_type=jnp.float32)
        * HD ** (-0.5)
        + position_bias[None]
    )
    allowed = (segment_float[:, :, None] == code_block.astype(jnp.float32)[:, None, :])[:, None]
    return (jnp.where(allowed, raw_scores, masked_score), allowed, onehot, key_block, value_block)


def attend_forward(
    values, segment, code_low, norm_gain, w_query, w_key, w_value, w_output, rel_table
):
    row_count, frames, model_width = values.shape
    normed, norm_stored = norm_forward(values, norm_gain)
    normed_low = normed.astype(jnp.bfloat16)
    query_low = project(normed_low, w_query).astype(jnp.bfloat16)
    key_low = project(normed_low, w_key).astype(jnp.bfloat16)
    value_low = project(normed_low, w_value).astype(jnp.bfloat16)
    gathered = (
        lax.all_gather(key_low, "blk", axis=1, tiled=True),
        lax.all_gather(value_low, "blk", axis=1, tiled=True),
        lax.all_gather(code_low, "blk", axis=1, tiled=True),
    )
    segment_float = segment.astype(jnp.float32)
    query_pos = lax.axis_index("blk") * frames + jnp.arange(frames, dtype=jnp.int32)
    query_heads = query_low.reshape(row_count, frames, H, HD)
    blocks = lax.axis_size("blk")

    def max_step(block_index, loop_state):
        running_max, running_sum = loop_state
        scores, allowed, onehot, key_block, value_block = block_at(
            gathered, block_index, query_heads, segment_float, query_pos, rel_table
        )
        new_max = jnp.maximum(running_max, jnp.max(scores, axis=-1))
        kept_exp = jnp.where(allowed, jnp.exp(scores - new_max[..., None]), 0.0)
        return (new_max, running_sum * jnp.exp(running_max - new_max) + jnp.sum(kept_exp, axis=-1))

    start_max = jnp.full((row_count, H, frames), masked_score, jnp.float32)
    running_max, running_sum = lax.fori_loop(
        0, blocks, max_step, (start_max, jnp.zeros_like(start_max))
    )
    log_total = running_max + jnp.log(running_sum)

    def mix_step(block_index, mixed_sum):
        scores, allowed, onehot, key_block, value_block = block_at(
            gathered, block_index, query_heads, segment_float, query_pos, rel_table
        )
        attn_low = jnp.where(allowed, jnp.exp(scores - log_total[..., None]), 0.0).astype(
            jnp.bfloat16
        )
        return mixed_sum + jnp.einsum(
            "rhqk,rkhd->rqhd", attn_low, value_block, preferred_element_type=jnp.float32
        )

    mixed_heads = lax.fori_loop(
        0, blocks, mix_step, jnp.zeros((row_count, frames, H, HD), jnp.float32)
    )
    mixed_heads = mixed_heads.reshape(row_count, frames, model_width)
    mixed_low = mixed_heads.astype(jnp.bfloat16)
    stored = (
        norm_stored,
        normed_low,
        query_heads,
        key_low,
        value_low,
        code_low,
        gathered,
        log_total,
        mixed_heads,
        mixed_low,
        segment_float,
        query_pos,
    )
    return (project(mixed_low, w_output), stored)


def attend_backward(stream_grad, norm_gain, w_query, w_key, w_value, w_output, rel_table, stored):
    (
        norm_stored,
        normed_low,
        query_heads,
        key_low,
        value_low,
        code_low,
        gathered,
        log_total,
        mixed_heads,
        mixed_low,
        segment_float,
        query_pos,
    ) = stored
    row_count, frames, model_width = stream_grad.shape
    grad_low = stream_grad.astype(jnp.bfloat16)
    w_output_grad = weight_product(mixed_low, grad_low)
    mixed_grad = (
        project_back(grad_low, w_output).astype(jnp.bfloat16).reshape(row_count, frames, H, HD)
    )
    row_delta = jnp.einsum(
        "rqhd,rqhd->rhq",
        mixed_grad.astype(jnp.float32),
        mixed_heads.reshape(row_count, frames, H, HD),
    )
    source = (
        lax.all_gather(key_low, "blk", axis=1, tiled=True),
        lax.all_gather(value_low, "blk", axis=1, tiled=True),
        lax.all_gather(code_low, "blk", axis=1, tiled=True),
    )
    blocks = lax.axis_size("blk")
    scale = HD ** (-0.5)

    def score_grads(block_index):
        scores, allowed, onehot, key_block, value_block = block_at(
            source, block_index, query_heads, segment_float, query_pos, rel_table
        )
        attn_weights = jnp.where(allowed, jnp.exp(scores - log_total[..., None]), 0.0)
        weight_grad = jnp.einsum(
            "rqhd,rkhd->rhqk", mixed_grad, value_block, preferred_element_type=jnp.float32
        )
        score_low = (attn_weights * (weight_grad - row_delta[..., None])).astype(jnp.bfloat16)
        return (attn_weights, score_low, onehot, key_block)

    def grad_step(block_index, loop_state):
        query_grad, key_buffer, value_buffer, table_grad = loop_state
        attn_weights, score_low, onehot, key_block = score_grads(block_index)
        attn_low = attn_weights.astype(jnp.bfloat16)
        query_grad = query_grad + jnp.einsum(
            "rhqk,rkhd->rqhd", score_low, key_block, preferred_element_type=jnp.float32
        )
        key_part = (
            jnp.einsum(
                "rhqk,rqhd->rkhd", score_low, query_heads, preferred_element_type=jnp.float32
            )
            * scale
        )
        value_part = jnp.einsum(
            "rhqk,rqhd->rkhd", attn_low, mixed_grad, preferred_element_type=jnp.float32
        )
        key_start = block_index * frames
        key_buffer = lax.dynamic_update_slice_in_dim(
            key_buffer, key_part.reshape(row_count, frames, model_width), key_start, 1
        )
        value_buffer = lax.dynamic_update_slice_in_dim(
            value_buffer, value_part.reshape(row_count, frames, model_width), key_start, 1
        )
        table_grad = table_grad + jnp.einsum(
            "hqk,qkb->hb",
            jnp.sum(score_low.astype(jnp.float32), axis=0),
            onehot,
            precision=lax.Precision.HIGHEST,
        )
        return (query_grad, key_buffer, value_buffer, table_grad)

    empty_buffer = jnp.zeros((row_count, blocks * frames, model_width), jnp.float32)
    start_state = (
        jnp.zeros((row_count, frames, H, HD), jnp.float32),
        empty_buffer,
        empty_buffer,
        jnp.zeros((H, NBUCKET), jnp.float32),
    )
    query_grad, key_buffer, value_buffer, table_grad = lax.fori_loop(
        0, blocks, grad_step, start_state
    )
    key_total, value_total = (
        lax.psum_scatter(
            key_buffer.astype(jnp.bfloat16), "blk", scatter_dimension=1, tiled=True
        ).astype(jnp.float32),
        lax.psum_scatter(
            value_buffer.astype(jnp.bfloat16), "blk", scatter_dimension=1, tiled=True
        ).astype(jnp.float32),
    )
    query_grad_low = (
        (query_grad * scale).reshape(row_count, frames, model_width).astype(jnp.bfloat16)
    )
    key_grad_low = key_total.astype(jnp.bfloat16)
    value_grad_low = value_total.astype(jnp.bfloat16)
    w_query_grad = weight_product(normed_low, query_grad_low)
    w_key_grad = weight_product(normed_low, key_grad_low)
    w_value_grad = weight_product(normed_low, value_grad_low)
    normed_grad = (
        project_back(query_grad_low, w_query)
        + project_back(key_grad_low, w_key)
        + project_back(value_grad_low, w_value)
    )
    input_grad, gain_grad = norm_backward(normed_grad, norm_gain, norm_stored)
    return (
        stream_grad + input_grad,
        (gain_grad, w_query_grad, w_key_grad, w_value_grad, w_output_grad, table_grad),
    )


def conv_forward(values, segment, live_mask, norm_gain, w_pw1, w_depth, bn_gain, w_pw2):
    row_count, frames, model_width = values.shape
    normed, norm_stored = norm_forward(values, norm_gain)
    normed_low = normed.astype(jnp.bfloat16)
    gate_pair = project(normed_low, w_pw1)
    first_half = gate_pair[..., :model_width]
    logistic = jax.nn.sigmoid(gate_pair[..., model_width:])
    live_frames = live_mask.astype(jnp.float32)[..., None]
    gated_low = (first_half * logistic * live_frames).astype(jnp.bfloat16)
    wide_units, wide_segment = (
        padded(gated_low, (("blk", 1),), KERNEL // 2),
        padded(segment.astype(jnp.bfloat16), (("blk", 1),), KERNEL // 2),
    )
    segment_float = segment.astype(jnp.float32)
    depth_sum = jnp.zeros((row_count, frames, model_width), jnp.float32)
    for kernel_tap in range(KERNEL):
        same_segment = (
            wide_segment[:, kernel_tap : kernel_tap + frames].astype(jnp.float32) == segment_float
        ).astype(jnp.float32)
        depth_sum = (
            depth_sum
            + w_depth[kernel_tap].astype(jnp.float32)
            * wide_units[:, kernel_tap : kernel_tap + frames].astype(jnp.float32)
            * same_segment[..., None]
        )
    norm_totals = lax.psum(
        (
            jnp.sum(depth_sum * live_frames, axis=(0, 1)),
            jnp.sum(depth_sum * depth_sum * live_frames, axis=(0, 1)),
            jnp.sum(live_frames),
        ),
        ("blk", "rows"),
    )
    frame_count = norm_totals[2]
    center = norm_totals[0] / frame_count
    spread = norm_totals[1] / frame_count - center * center
    inverse = lax.rsqrt(spread + epsilon)
    standard = (depth_sum - center) * inverse
    pre_act = standard * bn_gain
    act_low = jax.nn.silu(pre_act).astype(jnp.bfloat16)
    stored = (
        norm_stored,
        normed_low,
        first_half,
        logistic,
        live_frames,
        wide_units,
        wide_segment,
        frame_count,
        inverse,
        standard,
        pre_act,
        act_low,
    )
    return (project(act_low, w_pw2), stored)


def conv_backward(stream_grad, segment, norm_gain, w_pw1, w_depth, bn_gain, w_pw2, stored):
    (
        norm_stored,
        normed_low,
        first_half,
        logistic,
        live_frames,
        wide_units,
        wide_segment,
        frame_count,
        inverse,
        standard,
        pre_act,
        act_low,
    ) = stored
    row_count, frames, model_width = stream_grad.shape
    grad_low = stream_grad.astype(jnp.bfloat16)
    w_pw2_grad = weight_product(act_low, grad_low)
    act_grad = project_back(grad_low, w_pw2) * silu_slope(pre_act)
    hat_grad = act_grad * bn_gain
    grad_sums = lax.psum(
        (jnp.sum(hat_grad, axis=(0, 1)), jnp.sum(act_grad * standard, axis=(0, 1))), ("blk", "rows")
    )
    hat_total, bn_gain_grad = grad_sums
    frame_share = live_frames / frame_count
    depth_low = (
        inverse
        * (hat_grad - frame_share * hat_total - frame_share * standard * bn_gain * bn_gain_grad)
    ).astype(jnp.bfloat16)
    wide_grad = padded(depth_low, (("blk", 1),), KERNEL // 2)
    segment_float = segment.astype(jnp.float32)
    depth_float = depth_low.astype(jnp.float32)
    unit_grad = jnp.zeros((row_count, frames, model_width), jnp.float32)
    tap_grads = []
    for kernel_tap in range(KERNEL):
        forward_same = (
            wide_segment[:, kernel_tap : kernel_tap + frames].astype(jnp.float32) == segment_float
        ).astype(jnp.float32)[..., None]
        tap_grads.append(
            jnp.sum(
                depth_float
                * wide_units[:, kernel_tap : kernel_tap + frames].astype(jnp.float32)
                * forward_same,
                axis=(0, 1),
            )
        )
        mirror = KERNEL - 1 - kernel_tap
        backward_same = (
            wide_segment[:, mirror : mirror + frames].astype(jnp.float32) == segment_float
        ).astype(jnp.float32)[..., None]
        unit_grad = (
            unit_grad
            + w_depth[kernel_tap].astype(jnp.float32)
            * wide_grad[:, mirror : mirror + frames].astype(jnp.float32)
            * backward_same
        )
    unit_grad = unit_grad * live_frames
    pair_low = jnp.concatenate(
        [unit_grad * logistic, unit_grad * first_half * logistic * (1.0 - logistic)], axis=-1
    ).astype(jnp.bfloat16)
    w_pw1_grad = weight_product(normed_low, pair_low)
    input_grad, gain_grad = norm_backward(project_back(pair_low, w_pw1), norm_gain, norm_stored)
    return (
        stream_grad + input_grad,
        (gain_grad, w_pw1_grad, jnp.stack(tap_grads), bn_gain_grad, w_pw2_grad),
    )


def per_device(
    tokens,
    seg_ids,
    frame_mask,
    cotangent,
    g_ff1,
    w_ff1_in,
    w_ff1_out,
    g_att,
    w_query,
    w_key,
    w_value,
    w_output,
    rel_table,
    g_conv,
    w_pw1,
    w_depth,
    bn_gain,
    w_pw2,
    g_ff2,
    w_ff2_in,
    w_ff2_out,
    g_out,
):
    start_stream = tokens.astype(jnp.float32)
    ffn_one, ffn_one_stored = ffn_forward(start_stream, g_ff1, w_ff1_in, w_ff1_out)
    after_ffn = start_stream + 0.5 * ffn_one
    code_low = jnp.where(frame_mask == 1, seg_ids, -1).astype(jnp.bfloat16)
    attended, attend_stored = attend_forward(
        after_ffn, seg_ids, code_low, g_att, w_query, w_key, w_value, w_output, rel_table
    )
    after_att = after_ffn + attended
    conv_out, conv_stored = conv_forward(
        after_att, seg_ids, frame_mask, g_conv, w_pw1, w_depth, bn_gain, w_pw2
    )
    after_conv = after_att + conv_out
    ffn_two, ffn_two_stored = ffn_forward(after_conv, g_ff2, w_ff2_in, w_ff2_out)
    after_two = after_conv + 0.5 * ffn_two
    final_norm, final_stored = norm_forward(after_two, g_out)
    stream_grad, g_out_grad = norm_backward(cotangent.astype(jnp.float32), g_out, final_stored)
    stream_grad, ffn_two_grads = ffn_backward(
        stream_grad, g_ff2, w_ff2_in, w_ff2_out, ffn_two_stored
    )
    stream_grad, conv_grads = conv_backward(
        stream_grad, seg_ids, g_conv, w_pw1, w_depth, bn_gain, w_pw2, conv_stored
    )
    stream_grad, attend_grads = attend_backward(
        stream_grad, g_att, w_query, w_key, w_value, w_output, rel_table, attend_stored
    )
    stream_grad, ffn_one_grads = ffn_backward(
        stream_grad, g_ff1, w_ff1_in, w_ff1_out, ffn_one_stored
    )
    summed = lax.psum(
        (
            ffn_one_grads[0],
            ffn_one_grads[1],
            ffn_one_grads[2],
            attend_grads[0],
            attend_grads[1],
            attend_grads[2],
            attend_grads[3],
            attend_grads[4],
            attend_grads[5],
            conv_grads[0],
            conv_grads[1],
            conv_grads[2],
            conv_grads[4],
            ffn_two_grads[0],
            ffn_two_grads[1],
            ffn_two_grads[2],
            g_out_grad,
        ),
        ("blk", "rows"),
    )
    return (
        final_norm.astype(jnp.bfloat16),
        stream_grad,
        summed[0],
        summed[1],
        summed[2],
        summed[3],
        summed[4],
        summed[5],
        summed[6],
        summed[7],
        summed[8],
        summed[9],
        summed[10],
        summed[11],
        conv_grads[3],
        summed[12],
        summed[13],
        summed[14],
        summed[15],
        summed[16],
    )


def solution(mesh):
    blocks, groups = mesh.shape["blk"], mesh.shape["rows"]

    def device(tokens, *rest):
        rows, frames, _ = tokens.shape
        whole_rows = rows == blocks == 4 and groups == 8 and (rows * frames) % QT == 0
        return (row_device if whole_rows else per_device)(tokens, *rest)

    return jax.shard_map(
        device,
        mesh=mesh,
        in_specs=(
            P("rows", "blk", None),
            P("rows", "blk"),
            P("rows", "blk"),
            P("rows", "blk", None),
        )
        + (P(),) * 18,
        out_specs=(P("rows", "blk", None),) * 2 + (P(),) * 18,
        check_vma=False,
    )
```

```python
import functools
import math

import jax
import jax.numpy as jnp
from jax import lax
from jax.experimental import pallas as pl
from jax.experimental.pallas import tpu as pltpu
from jax.sharding import PartitionSpec as P

H = 4
HD = 64
D = 256
FF = 1024
KERNEL = 31
HALF = KERNEL // 2
NBUCKET = 16

epsilon = 1e-05
masked_score = -1e30

f32 = jnp.float32
bf16 = jnp.bfloat16
LOG2E = math.log2(math.e)
QT = 256
GAP = 16
EXTRA = 16
SAFE_EXPONENT = 60.0
MIB = 1024 * 1024


def mm(a, b):
    return lax.dot_general(a, b, (((1,), (0,)), ((), ())), preferred_element_type=f32)


def mm_nt(a, b):
    return lax.dot_general(a, b, (((1,), (1,)), ((), ())), preferred_element_type=f32)


def turned(x):
    return x.astype(f32).T.astype(bf16)


def sigmoid(x):
    return 0.5 + 0.5 * jnp.tanh(0.5 * x)


def norm_hat(v):
    center = jnp.mean(v, axis=-1, keepdims=True)
    shifted = v - center
    spread = jnp.mean(shifted * shifted, axis=-1, keepdims=True)
    inverse = lax.rsqrt(spread + epsilon)
    return shifted * inverse, inverse


def norm_back(upstream, gain, hat, inverse):
    inner = upstream * gain
    inner_mean = jnp.mean(inner, axis=-1, keepdims=True)
    inner_dot = jnp.mean(inner * hat, axis=-1, keepdims=True)
    return inverse * (inner - inner_mean - hat * inner_dot)


def col_sum(x):
    rows, width = x.shape
    return jnp.sum(x.reshape(rows // 8, 8, width), axis=0)


def bucket_ranges():
    levels = NBUCKET // 2
    big = 1 << 30
    edges = [0] + [4**k for k in range(levels - 1)] + [big]
    out = []
    for level in range(levels - 1, 0, -1):
        out.append((level, 1 - edges[level + 1], -edges[level]))
    out.append((0, 0, 0))
    for level in range(1, levels):
        out.append((levels + level, edges[level], edges[level + 1] - 1))
    return out


def tile_buckets(offset):
    low, high = offset * QT - (QT - 1), offset * QT + (QT - 1)
    return [(b, lo) for b, lo, hi in bucket_ranges() if lo <= high and hi >= low]


def mixed_offsets(tiles):
    return [o for o in range(1 - tiles, tiles) if len(tile_buckets(o)) > 1]


def tile_distance(offset):
    row = lax.broadcasted_iota(jnp.int32, (QT, QT), 0)
    col = lax.broadcasted_iota(jnp.int32, (QT, QT), 1)
    return col - row + offset * QT


def frame_index(start, rows, width):
    return (lax.broadcasted_iota(jnp.int32, (rows, width), 0) + start).astype(f32)


def rows_at(start, count, unit):
    return pl.ds(pl.multiple_of(start, unit), count)


def bias_kernel(tiles, table_ref, bias_ref):
    def head(h, carry):
        for k, offset in enumerate(mixed_offsets(tiles)):
            d = tile_distance(offset)
            found = tile_buckets(offset)
            value = jnp.full((QT, QT), table_ref[h, found[0][0]], f32)
            for b, lo in found[1:]:
                value = jnp.where(d >= lo, table_ref[h, b], value)
            bias_ref[h, k] = value * LOG2E
        return carry

    lax.fori_loop(0, H, head, 0)


def place_pieces(me_ref, piece_refs, target_ref, frames):
    for m, piece in enumerate(piece_refs):
        start = (me_ref[0] ^ m) * frames
        target_ref[rows_at(start, frames, 64), :] = piece[0:frames, :]


def take_pieces(me_ref, source_ref, piece_refs, frames):
    for m, piece in enumerate(piece_refs):
        start = (me_ref[0] ^ m) * frames
        piece[...] = source_ref[rows_at(start, frames, 64), :].astype(piece.dtype)


def key_features(start, rows, ends):
    first_end, second_end, live_end = (e[:, :128] for e in ends)
    t = frame_index(start, rows, 128)
    lane = lax.broadcasted_iota(jnp.int32, (rows, 128), 1)
    code = jnp.where(t < first_end, 0, jnp.where(t < second_end, 1, 2))
    code = jnp.where(t < live_end, code, -1)
    barred = jnp.where((lane < 3) & (code != lane), masked_score, 0.0)
    return jnp.where((lane >= 3) & (lane < 6), 1.0, barred).astype(bf16)


def query_features(start, rows, ends):
    first_end, second_end, live_end = (e[:, :128] for e in ends)
    t = frame_index(start, rows, 128)
    lane = lax.broadcasted_iota(jnp.int32, (rows, 128), 1)
    code = jnp.where(t < first_end, 0, jnp.where(t < second_end, 1, 2))
    return jnp.where(code == lane, 1.0, 0.0)


def three_parts(x):
    top = x.astype(bf16).astype(f32)
    middle = (x - top).astype(bf16).astype(f32)
    return top, middle, x - top - middle


def spread_gaps(plain_ref, gap_ref, length, ends):
    first_end, second_end, _ = (e[:, :128] for e in ends)
    total = length + 4 * GAP
    step = GAP * 4

    def chunk(k, carry):
        start = k * step
        g = frame_index(start, step, 128)
        for c in range(2):
            a = plain_ref[c, rows_at(start + 2 * GAP, step, 16), :]
            b = plain_ref[c, rows_at(start + GAP, step, 16), :]
            d = plain_ref[c, rows_at(start, step, 16), :]
            in_first = (g >= GAP) & (g - GAP < first_end)
            in_second = (g - 2 * GAP >= first_end) & (g - 2 * GAP < second_end)
            in_third = (g - 3 * GAP >= second_end) & (g - 3 * GAP < length)
            value = jnp.where(in_first, a, jnp.where(in_second, b, jnp.where(in_third, d, 0.0)))
            gap_ref[c, rows_at(start, step, 16), :] = value
        return carry

    lax.fori_loop(0, total // step, chunk, 0)


def close_gaps(gap_ref, start, rows, ends):
    first_end, second_end, _ = (e[:, :128] for e in ends)
    t = frame_index(start, rows, 128)
    halves = []
    for c in range(2):
        a = gap_ref[c, rows_at(start + GAP, rows, 16), :]
        b = gap_ref[c, rows_at(start + 2 * GAP, rows, 16), :]
        d = gap_ref[c, rows_at(start + 3 * GAP, rows, 16), :]
        halves.append(jnp.where(t < first_end, a, jnp.where(t < second_end, b, d)))
    return jnp.concatenate(halves, axis=1)


CONV_ROWS = 32
BACK_ROWS = 32


def tapped(part, tap):
    rows = part.shape[0]
    return (part.reshape(rows // 8, 8, 128) * tap[None]).reshape(rows, 128)


def shifted_parts(ref, c, start, rows):
    for r in range(8):
        window = ref[c, pl.ds(start - 16 + r, rows + 24), :]
        for q in range(4):
            shift = 8 * q + r - 16
            if abs(shift) <= HALF:
                yield shift, window[8 * q : 8 * q + rows]


def convolve(gap_ref, out_ref, taps_ref, length):
    span = length + 2 * GAP

    for c in range(2):

        def chunk(k, carry, c=c):
            start = GAP + k * CONV_ROWS
            total = jnp.zeros((CONV_ROWS, 128), f32)
            for shift, part in shifted_parts(gap_ref, c, start, CONV_ROWS):
                total = total + tapped(part, taps_ref[c, shift + HALF])
            out_ref[c, rows_at(start, CONV_ROWS, 16), :] = total
            return carry

        lax.fori_loop(0, span // CONV_ROWS, chunk, 0)


def convolve_back(dgap_ref, gap_ref, out_ref, taps_ref, taps_grad_ref, length):
    span = length + 2 * GAP
    for c in range(2):

        def chunk(k, carry, c=c):
            start = GAP + k * BACK_ROWS
            units = gap_ref[c, rows_at(start, BACK_ROWS, 16), :]
            total = jnp.zeros((BACK_ROWS, 128), f32)
            sums = list(carry)
            for shift, part in shifted_parts(dgap_ref, c, start, BACK_ROWS):
                j = HALF - shift
                total = total + tapped(part, taps_ref[c, j])
                sums[j] = sums[j] + col_sum(part * units)
            out_ref[c, rows_at(start, BACK_ROWS, 16), :] = total
            return tuple(sums)

        sums = lax.fori_loop(0, span // BACK_ROWS, chunk, tuple(jnp.zeros((8, 128), f32) for _ in range(KERNEL)))
        for j in range(KERNEL):
            taps_grad_ref[j : j + 1, 128 * c : 128 * c + 128] = jnp.sum(sums[j], axis=0, keepdims=True)
    taps_grad_ref[KERNEL : KERNEL + 1, :] = jnp.zeros((1, 2 * 128), f32)


def add_to(ref, first, value):
    ref[...] = value if first else ref[...] + value


def read_ends(ends_ref):
    return ends_ref[0:1, :], ends_ref[1:2, :], ends_ref[2:3, :]


FRONT = 1280
GATE = 1280


def attend_tile(q2_ref, fq_ref, h, qt, k2_ref, fk_ref, bias_ref, table_ref, tiles):
    rows = slice(qt * QT, (qt + 1) * QT)
    qa = jnp.concatenate([q2_ref[h, rows, :], fq_ref[rows, :]], axis=1)
    ka = jnp.concatenate([k2_ref[h], fk_ref[...]], axis=1)
    offsets = mixed_offsets(tiles)
    s_all = mm_nt(qa, ka)
    parts = []
    for kt in range(tiles):
        s = s_all[:, kt * QT : (kt + 1) * QT]
        o = kt - qt
        if o in offsets:
            s = s + bias_ref[h, offsets.index(o)]
        else:
            s = s + table_ref[h, tile_buckets(o)[0][0]] * LOG2E
        parts.append(jnp.exp2(s).astype(bf16))
    return jnp.concatenate(parts, axis=1)


def attend_tile_below_max(q2_ref, fq_ref, h, rows, start, k2_ref, fk_ref, table_ref, s_ref, tiles):
    qa = jnp.concatenate([q2_ref[h, rows, :], fq_ref[rows, :]], axis=1)
    ka = jnp.concatenate([k2_ref[h], fk_ref[...]], axis=1)
    s_ref[...] = mm_nt(qa, ka)
    ranges = bucket_ranges()

    def add_bias(kt, top):
        cols = rows_at(kt * QT, QT, QT)
        d = tile_distance(0) + (kt * QT - start)
        value = jnp.full((QT, QT), table_ref[h, ranges[0][0]], f32)
        for b, low, _ in ranges[1:]:
            value = jnp.where(d >= low, table_ref[h, b], value)
        s = s_ref[:, cols] + value * LOG2E
        s_ref[:, cols] = s
        return jnp.maximum(top, jnp.max(s, axis=1, keepdims=True))

    top = lax.fori_loop(0, tiles, add_bias, jnp.full((QT, 1), -jnp.inf, f32))
    return jnp.exp2(s_ref[...] - top).astype(bf16)


def kernel_a(
    tiles,
    me_ref,
    table_ref,
    piece0,
    piece1,
    piece2,
    piece3,
    bias_ref,
    g_ff1_ref,
    w_in_ref,
    w_out_ref,
    g_att_ref,
    wq2_ref,
    wk2_ref,
    wv2_ref,
    w_o_ref,
    g_conv_ref,
    w_pw1_ref,
    taps_ref,
    tok_ref,
    ends_ref,
    s1_ref,
    k2_ref,
    v2_ref,
    weights_ref,
    inverse_ref,
    mixed_ref,
    s2_ref,
    gap_ref,
    depth_ref,
    sums_ref,
    q2_ref,
    fq_ref,
    fk_ref,
    fast_ref,
    p_ref,
    s_ref,
    plain_ref,
    conv_ref,
    moved,
):
    pieces = (piece0, piece1, piece2, piece3)
    length = tiles * QT
    frames = length // len(pieces)
    place_pieces(me_ref, pieces, tok_ref, frames)
    extra = sum(p[frames : frames + EXTRA, :].astype(f32) for p in pieces)
    first_end = 16.0 * extra[0:1, :] + extra[1:2, :]
    second_end = first_end + 16.0 * extra[2:3, :] + extra[3:4, :]
    live_end = 16.0 * extra[4:5, :] + extra[5:6, :]
    ends_ref[0:1, :] = first_end
    ends_ref[1:2, :] = second_end
    ends_ref[2:3, :] = live_end
    ends_ref[3:8, :] = jnp.zeros((5, D), f32)
    ends = (first_end, second_end, live_end)

    scale = LOG2E * HD**-0.5

    def front(i, carry):
        at = slice(i * FRONT, (i + 1) * FRONT)
        x = tok_ref[at, :].astype(f32)
        hat, _ = norm_hat(x)
        n1 = (hat * g_ff1_ref[...]).astype(bf16)
        hidden = mm(n1, w_in_ref[...])
        act = (hidden * sigmoid(hidden)).astype(bf16)
        s1 = x + 0.5 * mm(act, w_out_ref[...])
        s1_ref[at, :] = s1
        hat, _ = norm_hat(s1)
        n2 = (hat * g_att_ref[...]).astype(bf16)
        lane = lax.broadcasted_iota(jnp.int32, (FRONT, 128), 1)
        q_top, k_top = carry
        q_all = mm(n2, wq2_ref[...]).astype(bf16).astype(f32) * scale
        k_all = mm(n2, wk2_ref[...]).astype(bf16)
        v_all = mm(n2, wv2_ref[...])
        for h in range(H):
            cols = slice(128 * h, 128 * h + 128)
            q = q_all[:, cols]
            high = q.astype(bf16)
            low = (q - high.astype(f32)).astype(bf16)
            q2_ref[h, at, :] = jnp.where(lane < HD, high.astype(f32), low.astype(f32)).astype(bf16)
            k2_ref[h, at, :] = k_all[:, cols]
            ones = (lane >= HD) & (lane < HD + 3) if h % 2 == 0 else lane < 3
            v2_ref[h, at, :] = jnp.where(ones, 1.0, v_all[:, cols]).astype(bf16)
            q_top = jnp.maximum(q_top, jnp.max(jnp.sum(q * q, axis=1, keepdims=True)))
            k = k_all[:, cols].astype(f32)
            k_top = jnp.maximum(k_top, jnp.max(jnp.sum(k * k, axis=1, keepdims=True)))
        fq_ref[at, :] = query_features(i * FRONT, FRONT, ends).astype(bf16)
        fk_ref[at, :] = key_features(i * FRONT, FRONT, ends)
        return q_top, k_top

    q_top, k_top = jnp.float32(0.0), jnp.float32(0.0)
    for i in range(length // FRONT):
        q_top, k_top = front(i, (q_top, k_top))
    fast_ref[0] = jnp.where(q_top * k_top < 4.0 * SAFE_EXPONENT**2, 1, 0)

    def weights_copy(h, slot):
        return pltpu.make_async_copy(p_ref.at[slot], weights_ref.at[h], moved.at[slot])

    def room(h, slot):
        @pl.when(h > 1)
        def _():
            weights_copy(h - 2, slot).wait()

    def mix(h, slot, rows, p):
        p_ref[slot, rows, :] = p
        total = mm(p, v2_ref[h])
        lane = lax.broadcasted_iota(jnp.int32, (QT, 128), 1)
        first = slot == 0
        denominator = jnp.where(first, total[:, HD : HD + 1], total[:, 0:1])
        inverse = jnp.broadcast_to(1.0 / denominator, (QT, 128))
        mixed = total * inverse
        g = lax.div(h, 2)
        new = jnp.logical_or(first, lane >= HD)
        mixed_ref[g, rows, :] = jnp.where(new, mixed, mixed_ref[g, rows, :])
        inverse_ref[g, rows, :] = jnp.where(new, inverse, inverse_ref[g, rows, :])

    @pl.when(fast_ref[0] == 1)
    def _():
        def head(h, carry):
            slot = lax.rem(h, 2)
            room(h, slot)
            for qt in range(tiles):
                p = attend_tile(q2_ref, fq_ref, h, qt, k2_ref, fk_ref, bias_ref, table_ref, tiles)
                mix(h, slot, slice(qt * QT, (qt + 1) * QT), p)
            weights_copy(h, slot).start()
            return carry

        lax.fori_loop(0, H, head, 0)

    @pl.when(fast_ref[0] != 1)
    def _():
        def head(h, carry):
            slot = lax.rem(h, 2)
            room(h, slot)

            def tile(qt, carry):
                rows = rows_at(qt * QT, QT, QT)
                p = attend_tile_below_max(
                    q2_ref, fq_ref, h, rows, qt * QT, k2_ref, fk_ref, table_ref, s_ref, tiles
                )
                mix(h, slot, rows, p)
                return carry

            lax.fori_loop(0, tiles, tile, 0)
            weights_copy(h, slot).start()
            return carry

        lax.fori_loop(0, H, head, 0)

    def gate(i):
        at = slice(i * GATE, (i + 1) * GATE)
        mixed = jnp.concatenate([mixed_ref[0, at, :], mixed_ref[1, at, :]], axis=1)
        s2 = s1_ref[at, :] + mm(mixed.astype(bf16), w_o_ref[...])
        s2_ref[at, :] = s2
        hat, _ = norm_hat(s2)
        n3 = (hat * g_conv_ref[...]).astype(bf16)
        pair = mm(n3, w_pw1_ref[...])
        live = frame_index(i * GATE, GATE, D) < live_end
        units = jnp.where(live, pair[:, :D] * sigmoid(pair[:, D:]), 0.0).astype(bf16).astype(f32)
        put = slice(i * GATE + 3 * GAP, (i + 1) * GATE + 3 * GAP)
        plain_ref[0, put, :] = units[:, :128]
        plain_ref[1, put, :] = units[:, 128:]

    for i in range(length // GATE):
        gate(i)
    spread_gaps(plain_ref, gap_ref, length, ends)
    convolve(gap_ref, conv_ref, taps_ref, length)

    def collect(i, carry):
        total, squares = carry
        at = rows_at(i * QT, QT, QT)
        depth = close_gaps(conv_ref, i * QT, QT, ends)
        depth_ref[at, :] = depth
        kept = jnp.where(frame_index(i * QT, QT, D) < live_end, depth, 0.0)
        return total + col_sum(kept), squares + col_sum(kept * kept)

    empty = jnp.zeros((8, D), f32)
    total, squares = lax.fori_loop(0, tiles, collect, (empty, empty))
    sums_ref[0:1, :] = jnp.sum(total, axis=0, keepdims=True)
    sums_ref[1:2, :] = jnp.sum(squares, axis=0, keepdims=True)
    sums_ref[2:3, :] = live_end
    sums_ref[3:8, :] = jnp.zeros((5, D), f32)
    for parity in range(2):
        weights_copy(H - 2 + parity, parity).wait()


MIDDLE = 1280


def batch_norm_terms(sums_ref):
    count = sums_ref[2:3, :]
    center = sums_ref[0:1, :] / count
    spread = sums_ref[1:2, :] / count - center * center
    return count, center, lax.rsqrt(spread + epsilon)


def kernel_b(
    tiles,
    me_ref,
    cot0,
    cot1,
    cot2,
    cot3,
    sums_ref,
    depth_ref,
    s2_ref,
    bn_gain_ref,
    w_pw2_ref,
    g_ff2_ref,
    w_in_ref,
    w_out_ref,
    g_out_ref,
    out0,
    out1,
    out2,
    out3,
    grad3_ref,
    bngrad_ref,
    sums2_ref,
    big_ref,
    small_ref,
    cot_ref,
    out_ref,
    dw_in_ref,
    dw_out_ref,
    dw_pw2_ref,
):
    length = tiles * QT
    frames = length // 4
    place_pieces(me_ref, (cot0, cot1, cot2, cot3), cot_ref, frames)
    _, center, inverse = batch_norm_terms(sums_ref)
    bn_gain = bn_gain_ref[...]

    def step(i, carry):
        g_out_sum, g_ff2_sum, bn_sum, bn_dot = carry
        at = slice(i * MIDDLE, (i + 1) * MIDDLE)
        standard = (depth_ref[at, :] - center) * inverse
        pre = standard * bn_gain
        logistic3 = sigmoid(pre)
        act3 = (pre * logistic3).astype(bf16)
        s3 = s2_ref[at, :] + mm(act3, w_pw2_ref[...])
        hat3, inv3 = norm_hat(s3)
        n4 = (hat3 * g_ff2_ref[...]).astype(bf16)
        hidden = mm(n4, w_in_ref[...])
        logistic = sigmoid(hidden)
        act4 = (hidden * logistic).astype(bf16)
        s4 = s3 + 0.5 * mm(act4, w_out_ref[...])
        hat4, inv4 = norm_hat(s4)
        out_ref[at, :] = (hat4 * g_out_ref[...]).astype(bf16)
        cot = cot_ref[at, :].astype(f32)
        g_out_sum = g_out_sum + col_sum(cot * hat4)
        grad4 = norm_back(cot, g_out_ref[...], hat4, inv4)
        out4 = (0.5 * grad4).astype(bf16)
        add_to(dw_out_ref, i == 0, mm(turned(out4), act4))
        slope = logistic * (1.0 + hidden * (1.0 - logistic))
        hid4 = (mm_nt(out4, w_out_ref[...]) * slope).astype(bf16)
        add_to(dw_in_ref, i == 0, mm(turned(n4), hid4))
        up = mm_nt(hid4, w_in_ref[...])
        g_ff2_sum = g_ff2_sum + col_sum(up * hat3)
        grad3 = grad4 + norm_back(up, g_ff2_ref[...], hat3, inv3)
        grad3_ref[at, :] = grad3
        out3 = grad3.astype(bf16)
        add_to(dw_pw2_ref, i == 0, mm(turned(act3), out3))
        bngrad = mm_nt(out3, w_pw2_ref[...]) * (logistic3 * (1.0 + pre * (1.0 - logistic3)))
        bngrad_ref[at, :] = bngrad
        return g_out_sum, g_ff2_sum, bn_sum + col_sum(bngrad), bn_dot + col_sum(bngrad * standard)

    empty = jnp.zeros((8, D), f32)
    sums = (empty,) * 4
    for i in range(length // MIDDLE):
        sums = step(i, sums)
    g_out_sum, g_ff2_sum, bn_sum, bn_dot = (jnp.sum(s, axis=0, keepdims=True) for s in sums)
    sums2_ref[0:1, :] = bn_sum
    sums2_ref[1:2, :] = bn_dot
    sums2_ref[2:8, :] = jnp.zeros((6, D), f32)
    small_ref[0:1, :] = g_ff2_sum
    small_ref[1:2, :] = g_out_sum
    small_ref[2:8, :] = jnp.zeros((6, D), f32)
    big_ref[0:FF, :] = turned_wide(dw_out_ref)
    for c in range(FF // D):
        big_ref[FF + c * D : FF + (c + 1) * D, :] = dw_in_ref[:, c * D : (c + 1) * D].astype(big_ref.dtype)
    big_ref[2 * FF : 2 * FF + D, :] = dw_pw2_ref[...].astype(big_ref.dtype)
    take_pieces(me_ref, out_ref, (out0, out1, out2, out3), frames)


def turned_wide(ref):
    return jnp.concatenate([ref[:, c * D : (c + 1) * D].T for c in range(ref.shape[1] // D)], axis=0).astype(bf16)


BACK = 640
LAST = 256


def kernel_c(
    tiles,
    me_ref,
    sums_ref,
    sums2_ref,
    ends_ref,
    s1_ref,
    inverse_ref,
    mixed_ref,
    s2_ref,
    gap_ref,
    depth_ref,
    grad3_ref,
    bngrad_ref,
    g_att_ref,
    w_q_ref,
    w_o_ref,
    g_conv_ref,
    w_pw1_ref,
    taps_ref,
    bn_gain_ref,
    grad_ref,
    do_ref,
    dot_ref,
    qt_ref,
    dw_o_ref,
    dw_pw1_ref,
    taps_grad_ref,
    row_ref,
    plain_ref,
    dgap_ref,
):
    length = tiles * QT
    ends = read_ends(ends_ref)
    live_end = ends[2]
    count, center, inverse = batch_norm_terms(sums_ref)
    bn_gain = bn_gain_ref[...]
    e_total = sums2_ref[0:1, :] * bn_gain
    dot_total = sums2_ref[1:2, :]


    def batch_back(i, carry):
        at = rows_at(i * QT, QT, QT)
        standard = (depth_ref[at, :] - center) * inverse
        e = bngrad_ref[at, :] * bn_gain
        share = jnp.where(frame_index(i * QT, QT, D) < live_end, 1.0, 0.0) / count
        dg = inverse * (e - share * e_total - share * standard * bn_gain * dot_total)
        dg = dg.astype(bf16).astype(f32)
        put = rows_at(i * QT + 3 * GAP, QT, 16)
        plain_ref[0, put, :] = dg[:, :128]
        plain_ref[1, put, :] = dg[:, 128:]
        return carry

    lax.fori_loop(0, tiles, batch_back, 0)
    spread_gaps(plain_ref, dgap_ref, length, ends)
    convolve_back(dgap_ref, gap_ref, plain_ref, taps_ref, taps_grad_ref, length)

    def gate_back(i, g_conv_sum):
        at = slice(i * BACK, (i + 1) * BACK)
        hat, inv = norm_hat(s2_ref[at, :])
        n3 = (hat * g_conv_ref[...]).astype(bf16)
        pair = mm(n3, w_pw1_ref[...])
        first, logistic = pair[:, :D], sigmoid(pair[:, D:])
        live = frame_index(i * BACK, BACK, D) < live_end
        ug = jnp.where(live, close_gaps(plain_ref, i * BACK, BACK, ends), 0.0) * logistic
        pairgrad = jnp.concatenate([ug, ug * first * (1.0 - logistic)], axis=1).astype(bf16)
        add_to(dw_pw1_ref, i == 0, mm(turned(n3), pairgrad))
        up = mm_nt(pairgrad, w_pw1_ref[...])
        g_conv_sum = g_conv_sum + col_sum(up * hat)
        grad2 = grad3_ref[at, :] + norm_back(up, g_conv_ref[...], hat, inv)
        grad_ref[at, :] = grad2
        out2 = grad2.astype(bf16)
        mixed = jnp.concatenate([mixed_ref[0, at, :], mixed_ref[1, at, :]], axis=1)
        add_to(dw_o_ref, i == 0, mm(turned(mixed), out2))
        mixgrad = mm_nt(out2, w_o_ref[...]).astype(bf16).astype(f32)
        mixgrad = (mixgrad * jnp.concatenate([inverse_ref[0, at, :], inverse_ref[1, at, :]], axis=1)).astype(bf16)
        dot_ref[:, at] = turned(mixgrad)
        product = mixgrad.astype(f32) * mixed
        lane = lax.broadcasted_iota(jnp.int32, (BACK, 128), 1)
        for h in range(H):
            cols = slice(128 * (h // 2), 128 * (h // 2) + 128)
            own = lane < HD if h % 2 == 0 else lane >= HD
            delta = jnp.sum(jnp.where(own, product[:, cols], 0.0), axis=1, keepdims=True)
            high, middle, low = three_parts(-delta)
            base = HD if h % 2 == 0 else 0
            side = jnp.where(lane == base, high, 0.0)
            side = jnp.where(lane == base + 1, middle, side)
            side = jnp.where(lane == base + 2, low, side)
            do_ref[h, at, :] = jnp.where(own, mixgrad[:, cols].astype(f32), side).astype(bf16)
        hat, _ = norm_hat(s1_ref[at, :])
        n2 = (hat * g_att_ref[...]).astype(bf16)
        qt_ref[:, at] = turned(mm(n2, w_q_ref[...]).astype(bf16))
        return g_conv_sum

    empty = jnp.zeros((8, D), f32)
    g_conv_sum = empty
    for i in range(length // BACK):
        g_conv_sum = gate_back(i, g_conv_sum)
    row_ref[0:1, :] = jnp.sum(g_conv_sum, axis=0, keepdims=True)
    row_ref[1:8, :] = jnp.zeros((7, D), f32)


def kernel_e(
    tiles,
    me_ref,
    tok_ref,
    s1_ref,
    k2_ref,
    v2_ref,
    weights_ref,
    grad_ref,
    do_ref,
    dot_ref,
    qt_ref,
    dw_o_ref,
    dw_pw1_ref,
    taps_grad_ref,
    row_ref,
    out0,
    out1,
    out2,
    out3,
    g_ff1_ref,
    w_ff1_in_ref,
    w_ff1_out_ref,
    g_att_ref,
    w_q_ref,
    w_k_ref,
    w_v_ref,
    big_b_ref,
    small_b_ref,
    output_ref,
    blocks_ref,
    kept_a,
    kept_b,
    sent_a,
    sent_b,
    small_ref,
    p_ref,
    dq_ref,
    dkt_ref,
    dvt_ref,
    acc_ref,
    dw_in_ref,
    dw_out_ref,
    dw_q_ref,
    dw_k_ref,
    dw_v_ref,
    last_ref,
    arrived,
):
    length = tiles * QT
    frames = length // 4

    def weights_copy(h, slot):
        return pltpu.make_async_copy(weights_ref.at[h], p_ref.at[slot], arrived.at[slot])

    weights_copy(0, 0).start()
    for m, piece in enumerate((out0, out1, out2, out3)):
        output_ref[me_ref[0] ^ m] = piece[...]
    empty = jnp.zeros((8, D), f32)


    offsets = mixed_offsets(tiles)

    def head(h, carry):
        slot = lax.rem(h, 2)

        @pl.when(h + 1 < H)
        def _():
            weights_copy(h + 1, 1 - slot).start()

        weights_copy(h, slot).wait()
        flat = {}
        started = set()
        own = rows_at(h * HD, HD, HD)
        dvt_ref[own, :] = mm(dot_ref[own, :], p_ref[slot])
        pair = lax.div(h, 2)
        for qt in range(tiles):
            rows = slice(qt * QT, (qt + 1) * QT)
            d_all = mm_nt(do_ref[h, rows, :], v2_ref[h])
            low = []
            for kt in range(tiles):
                cols = slice(kt * QT, (kt + 1) * QT)
                ds = p_ref[slot, rows, cols].astype(f32) * d_all[:, cols]
                o = kt - qt
                if o in offsets:
                    k = offsets.index(o)
                    acc_ref[k] = acc_ref[k] + ds if k in started else ds
                    started.add(k)
                else:
                    b = tile_buckets(o)[0][0]
                    flat[b] = flat[b] + col_sum(ds) if b in flat else col_sum(ds)
                low.append(ds.astype(bf16))
            low = jnp.concatenate(low, axis=1)
            p_ref[slot, rows, :] = low
            dq = mm(low, k2_ref[h])
            own_half = (lax.broadcasted_iota(jnp.int32, (QT, 128), 1) < HD) == (slot == 0)
            dq_ref[pair, rows, :] = jnp.where(own_half, dq, dq_ref[pair, rows, :])
        dkt_ref[own, :] = mm(qt_ref[own, :], p_ref[slot])
        table_row = jnp.zeros((1, D), f32)
        lane = lax.broadcasted_iota(jnp.int32, (1, D), 1)
        for k, o in enumerate(offsets):
            d = tile_distance(o)
            value = acc_ref[k]
            found = tile_buckets(o)
            tails = [col_sum(jnp.where(d >= lo, value, 0.0)) for _, lo in found[1:]]
            tails = [col_sum(value)] + tails
            for n, (b, _) in enumerate(found):
                part = tails[n] - tails[n + 1] if n + 1 < len(found) else tails[n]
                flat[b] = flat[b] + part if b in flat else part
        for b, part in flat.items():
            table_row = jnp.where(lane == b, jnp.sum(part), table_row)
        small_ref[pl.ds(h + 4, 1), :] = table_row
        return carry

    small_ref[...] = jnp.zeros_like(small_ref)
    lax.fori_loop(0, H, head, 0)


    def front_back(i, carry):
        g_att_sum, g_ff1_sum = carry
        at = slice(i * LAST, (i + 1) * LAST)
        dq = jnp.concatenate([dq_ref[g, at, :] for g in range(H // 2)], axis=1)
        dq = (dq * HD**-0.5).astype(bf16)
        dk = (dkt_ref[:, at] * HD**-0.5).T.astype(bf16)
        dv = dvt_ref[:, at].T.astype(bf16)
        s1 = s1_ref[at, :]
        hat2, inv2 = norm_hat(s1)
        n2 = turned((hat2 * g_att_ref[...]).astype(bf16))
        add_to(dw_q_ref, i == 0, mm(n2, dq))
        add_to(dw_k_ref, i == 0, mm(n2, dk))
        add_to(dw_v_ref, i == 0, mm(n2, dv))
        attgrad = mm_nt(dq, w_q_ref[...]) + mm_nt(dk, w_k_ref[...]) + mm_nt(dv, w_v_ref[...])
        g_att_sum = g_att_sum + col_sum(attgrad * hat2)
        grad1 = grad_ref[at, :] + norm_back(attgrad, g_att_ref[...], hat2, inv2)
        out1 = (0.5 * grad1).astype(bf16)
        x = tok_ref[at, :].astype(f32)
        hat1, inv1 = norm_hat(x)
        n1 = (hat1 * g_ff1_ref[...]).astype(bf16)
        hidden = mm(n1, w_ff1_in_ref[...])
        logistic = sigmoid(hidden)
        act1 = (hidden * logistic).astype(bf16)
        add_to(dw_out_ref, i == 0, mm(turned(out1), act1))
        slope = logistic * (1.0 + hidden * (1.0 - logistic))
        hid1 = (mm_nt(out1, w_ff1_out_ref[...]) * slope).astype(bf16)
        add_to(dw_in_ref, i == 0, mm(turned(n1), hid1))
        up = mm_nt(hid1, w_ff1_in_ref[...])
        g_ff1_sum = g_ff1_sum + col_sum(up * hat1)
        last_ref[at, :] = grad1 + norm_back(up, g_ff1_ref[...], hat1, inv1)
        return g_att_sum, g_ff1_sum

    g_att_sum, g_ff1_sum = empty, empty
    for i in range(length // LAST):
        g_att_sum, g_ff1_sum = front_back(i, (g_att_sum, g_ff1_sum))
    for k, s in enumerate((g_ff1_sum, g_att_sum)):
        small_ref[k : k + 1, :] = jnp.sum(s, axis=0, keepdims=True)
    small_ref[2:3, :] = row_ref[0:1, :]
    small_ref[8 : 8 + KERNEL + 1, :] = taps_grad_ref[...]
    for b in range(length // frames):
        blocks_ref[b] = last_ref[b * frames : (b + 1) * frames, :].astype(bf16)
    quarter = kept_a.shape[0]

    def put(start, value):
        side, first = start // (2 * quarter), start // quarter % 2 == 0
        at = slice(start % quarter, start % quarter + value.shape[0])

        @pl.when(me_ref[1] == side)
        def _():
            (kept_a if first else kept_b)[at, :] = value

        @pl.when(me_ref[1] != side)
        def _():
            (sent_a if first else sent_b)[at, :] = value

    for c in range(FF // D):
        put(c * D, dw_out_ref[:, c * D : (c + 1) * D].T.astype(bf16))
        put(FF + c * D, dw_in_ref[:, c * D : (c + 1) * D].astype(bf16))
    for k, ref in enumerate((dw_q_ref, dw_k_ref, dw_v_ref, dw_o_ref)):
        put(2 * FF + k * D, ref[...].astype(bf16))
    for c in range(2):
        put(2 * FF + (4 + c) * D, dw_pw1_ref[:, c * D : (c + 1) * D].astype(bf16))
    for c in range(BIG_B // D):
        put(BIG_C + c * D, big_b_ref[c * D : (c + 1) * D, :])
    rest = 4 * quarter - BIG_C - BIG_B - SMALL_C - SMALL_B
    small = [small_ref[...], small_b_ref[...], jnp.zeros((rest, D), f32)]
    put(BIG_C + BIG_B, jnp.concatenate(small, axis=0).astype(bf16))


def swap(x, axis, bit):
    size = lax.axis_size(axis)
    return lax.ppermute(x, axis, [(i, i ^ bit) for i in range(size)])


def doubling_steps():
    steps = []
    for axis in ("rows", "blk"):
        size = lax.axis_size(axis)
        bit = 1
        while bit < size:
            steps.append((axis, bit))
            bit *= 2
    return steps


def sum_everywhere(x):
    for axis, bit in doubling_steps():
        x = x + swap(x, axis, bit)
    return x


def to_pieces(x, me):
    own = lax.dynamic_index_in_dim(x, me, 0, keepdims=False)
    pieces = [own]
    for m in range(1, x.shape[0]):
        pieces.append(swap(lax.dynamic_index_in_dim(x, me ^ m, 0, keepdims=False), "blk", m))
    return pieces


def from_pieces(pieces):
    return [pieces[0]] + [swap(p, "blk", m) for m, p in enumerate(pieces) if m > 0]


def cut(terms, start, rows):
    return sum(lax.dynamic_slice_in_dim(t, start, rows, 0).astype(f32) for t in terms).astype(bf16)


def keep_half(terms, axis, bit):
    half = terms[0].shape[0] // 2
    side = (lax.axis_index(axis) // bit) % 2
    got = swap(cut(terms, (1 - side) * half, half), axis, bit)
    return [cut(terms, side * half, half), got]


def join_half(x, axis, bit):
    side = (lax.axis_index(axis) // bit) % 2
    got = swap(x, axis, bit)
    return jnp.where(side == 0, jnp.concatenate([x, got]), jnp.concatenate([got, x]))


def reduce_gradients(kept, sent, token_blocks, me, place):
    a, b = ([k, swap(s, "rows", 1)] for k, s in zip(kept, sent))
    t0, t1, t2, t3 = to_pieces(token_blocks, me)
    a_steps = (("rows", 2), ("rows", 4), ("blk", 1), ("blk", 2))
    b_steps = (("rows", 4), ("rows", 2), ("blk", 1), ("blk", 2))
    for k, (sa, sb) in enumerate(zip(a_steps, b_steps)):
        if k == 1:
            b[1], t1, t3 = lax.optimization_barrier((b[1], t1, t3))
        if k == 3:
            b[1], t2 = lax.optimization_barrier((b[1], t2))
            tokens_grad = place([t0, t1, t2, t3], f32)
        a, b = keep_half(a, *sa), keep_half(b, *sb)
    a, b = cut(a, 0, a[0].shape[0]), cut(b, 0, b[0].shape[0])
    for k, (sa, sb) in enumerate(zip(a_steps[::-1], b_steps[::-1])):
        if k == 2:
            b, tokens_grad = lax.optimization_barrier((b, tokens_grad))
        a, b = join_half(a, *sa), join_half(b, *sb)
    return (a, b, swap(a, "rows", 1), swap(b, "rows", 1)), tokens_grad


BIG_B = 2 * FF + D
BIG_C = 2 * FF + 6 * D
SMALL_C = 40
SMALL_B = 8


def place_kernel(me_ref, p0, p1, p2, p3, target_ref):
    for m, p in enumerate((p0, p1, p2, p3)):
        target_ref[me_ref[0] ^ m] = p[...].astype(target_ref.dtype)


def kernel_d(
    me_ref,
    own_a,
    own_b,
    other_a,
    other_b,
    sums2_ref,
    ff1_in,
    ff1_out,
    w_q,
    w_k,
    w_v,
    w_o,
    pw1,
    pw2,
    ff2_in,
    ff2_out,
    g_ff1,
    g_att,
    g_conv,
    rel,
    taps,
    g_ff2,
    g_out,
    bn_gain,
    big_ref,
):
    quarter = own_a.shape[0]
    side = me_ref[1]
    for k, (own, other) in enumerate(((own_a, other_a), (own_b, other_b))):
        big_ref[rows_at((2 * side + k) * quarter, quarter, 64), :] = own[...]
        big_ref[rows_at((2 * (1 - side) + k) * quarter, quarter, 64), :] = other[...]
    ff1_out[...] = big_ref[0:FF, :].astype(f32)
    for c in range(FF // D):
        ff1_in[:, c * D : (c + 1) * D] = big_ref[FF + c * D : FF + (c + 1) * D, :].astype(f32)
    base = 2 * FF
    for k, ref in enumerate((w_q, w_k, w_v, w_o)):
        ref[...] = big_ref[base + k * D : base + (k + 1) * D, :].astype(f32)
    base = 2 * FF + 4 * D
    for c in range(2):
        pw1[:, c * D : (c + 1) * D] = big_ref[base + c * D : base + (c + 1) * D, :].astype(f32)
    base = BIG_C
    ff2_out[...] = big_ref[base : base + FF, :].astype(f32)
    for c in range(FF // D):
        at = base + FF + c * D
        ff2_in[:, c * D : (c + 1) * D] = big_ref[at : at + D, :].astype(f32)
    pw2[...] = big_ref[base + 2 * FF : base + 2 * FF + D, :].astype(f32)
    small = big_ref[BIG_C + BIG_B : BIG_C + BIG_B + SMALL_C + SMALL_B, :].astype(f32)
    g_ff1[...], g_att[...], g_conv[...] = small[0:1], small[1:2], small[2:3]
    rel[...] = small[4:8, :NBUCKET]
    taps[...] = small[8 : 8 + KERNEL]
    g_ff2[...], g_out[...] = small[SMALL_C : SMALL_C + 1], small[SMALL_C + 1 : SMALL_C + 2]
    bn_gain[...] = sums2_ref[1:2, :]


def shape_of(shape, dtype):
    return jax.ShapeDtypeStruct(shape, dtype)


def call(body, smem, outs, scratch, name, far_in=(), far_out=(), micros=1, mib=16):
    def place(far, count):
        return [pl.BlockSpec(memory_space=pl.ANY if k in far else pltpu.VMEM) for k in range(count)]

    def run(*operands):
        specs = [pl.BlockSpec(memory_space=pltpu.SMEM)] * smem + place(far_in, len(operands))[smem:]
        return pl.pallas_call(
            body,
            out_shape=outs,
            in_specs=specs,
            out_specs=place(far_out, len(outs)),
            scratch_shapes=scratch,
            compiler_params=pltpu.CompilerParams(vmem_limit_bytes=mib * MIB),
            cost_estimate=pl.CostEstimate(flops=micros * 10**9, bytes_accessed=micros * 10**6, transcendentals=0),
            name=name,
        )(*operands)

    return run


def twice(weight):
    heads = weight.reshape(D, H, HD)
    return jnp.concatenate([heads, heads], axis=2).reshape(D, 2 * D)


def one_side(weight):
    heads = weight.reshape(D, H // 2, 2, HD)
    empty = jnp.zeros_like(heads[:, :, 0])
    even = jnp.concatenate([heads[:, :, 0], empty], axis=2)
    odd = jnp.concatenate([empty, heads[:, :, 1]], axis=2)
    return jnp.stack([even, odd], axis=2).reshape(D, 2 * D)


MIB_A = 23
MIB_B = 29
MIB_C = 20
MIB_E = 34


def packed_rows():
    rows = BIG_C + BIG_B + SMALL_C + SMALL_B
    return -(-rows // 1024) * 1024


def run_a(tiles, *operands):
    length = tiles * QT
    frames = length // 4
    padded_rows = length + 4 * GAP
    n_mixed = len(mixed_offsets(tiles))
    return call(
        functools.partial(kernel_a, tiles),
        2,
        [
            shape_of((length, D), bf16),
            shape_of((8, D), f32),
            shape_of((length, D), f32),
            shape_of((H, length, 128), bf16),
            shape_of((H, length, 128), bf16),
            shape_of((H, length, length), bf16),
            shape_of((H // 2, length, 128), f32),
            shape_of((H // 2, length, 128), f32),
            shape_of((length, D), f32),
            shape_of((2, padded_rows, 128), f32),
            shape_of((length, D), f32),
            shape_of((8, D), f32),
        ],
        [
            pltpu.VMEM((H, length, 128), bf16),
            pltpu.VMEM((length, 128), bf16),
            pltpu.VMEM((length, 128), bf16),
            pltpu.SMEM((1,), jnp.int32),
            pltpu.VMEM((2, length, length), bf16),
            pltpu.VMEM((QT, length), f32),
            pltpu.VMEM((2, length + 6 * GAP, 128), f32),
            pltpu.VMEM((2, padded_rows, 128), f32),
            pltpu.SemaphoreType.DMA((2,)),
        ],
        "first_part",
        far_out=(5,),
        micros=30,
        mib=MIB_A,
    )(*operands)


def run_b(tiles, *operands):
    length = tiles * QT
    frames = length // 4
    padded_rows = length + 4 * GAP
    n_mixed = len(mixed_offsets(tiles))
    return call(
        functools.partial(kernel_b, tiles),
        1,
        [shape_of((frames, D), bf16)] * 4
        + [
            shape_of((length, D), f32),
            shape_of((length, D), f32),
            shape_of((8, D), f32),
            shape_of((BIG_B, D), bf16),
            shape_of((SMALL_B, D), f32),
        ],
        [
            pltpu.VMEM((length, D), bf16),
            pltpu.VMEM((length, D), bf16),
            pltpu.VMEM((D, FF), f32),
            pltpu.VMEM((D, FF), f32),
            pltpu.VMEM((D, D), f32),
        ],
        "middle_part",
        micros=12,
        mib=MIB_B,
    )(*operands)


def run_c(tiles, *operands):
    length = tiles * QT
    padded_rows = length + 4 * GAP
    return call(
        functools.partial(kernel_c, tiles),
        1,
        [
            shape_of((length, D), f32),
            shape_of((H, length, 128), bf16),
            shape_of((D, length), bf16),
            shape_of((D, length), bf16),
            shape_of((D, D), f32),
            shape_of((D, 2 * D), f32),
            shape_of((KERNEL + 1, D), f32),
            shape_of((8, D), f32),
        ],
        [
            pltpu.VMEM((2, length + 6 * GAP, 128), f32),
            pltpu.VMEM((2, padded_rows, 128), f32),
        ],
        "third_part",
        micros=16,
        mib=MIB_C,
    )(*operands)


def run_e(tiles, *operands):
    length = tiles * QT
    frames = length // 4
    n_mixed = len(mixed_offsets(tiles))
    return call(
        functools.partial(kernel_e, tiles),
        1,
        [shape_of((4, frames, D), bf16)] * 2
        + [shape_of((packed_rows() // 4, D), bf16)] * 4,
        [
            pltpu.VMEM((SMALL_C, D), f32),
            pltpu.VMEM((2, length, length), bf16),
            pltpu.VMEM((H // 2, length, 128), f32),
            pltpu.VMEM((D, length), f32),
            pltpu.VMEM((D, length), f32),
            pltpu.VMEM((n_mixed, QT, QT), f32),
            pltpu.VMEM((D, FF), f32),
            pltpu.VMEM((D, FF), f32),
            pltpu.VMEM((D, D), f32),
            pltpu.VMEM((D, D), f32),
            pltpu.VMEM((D, D), f32),
            pltpu.VMEM((length, D), f32),
            pltpu.SemaphoreType.DMA((2,)),
        ],
        "last_part",
        far_in=(5,),
        micros=24,
        mib=MIB_E,
    )(*operands)


def row_device(
    tokens,
    seg_ids,
    frame_mask,
    cotangent,
    g_ff1,
    w_ff1_in,
    w_ff1_out,
    g_att,
    w_query,
    w_key,
    w_value,
    w_output,
    rel_table,
    g_conv,
    w_pw1,
    w_depth,
    bn_gain,
    w_pw2,
    g_ff2,
    w_ff2_in,
    w_ff2_out,
    g_out,
):
    blocks, frames, _ = tokens.shape
    length = blocks * frames
    tiles = length // QT
    n_mixed = len(mixed_offsets(tiles))
    me = lax.axis_index("blk")
    me_ref = jnp.stack([me, lax.axis_index("rows") % 2]).astype(jnp.int32)
    gains = [g.reshape(1, D) for g in (g_ff1, g_att, g_conv, bn_gain, g_ff2, g_out)]
    g_ff1, g_att, g_conv, bn_gain, g_ff2, g_out = gains

    found = jnp.stack([seg_ids == 0, seg_ids == 1, frame_mask == 1], axis=1)
    lengths = jnp.sum(found.astype(jnp.int32), axis=2)
    digits = jnp.stack([lengths // 16, lengths % 16], axis=2).reshape(blocks, 6)
    digits = jnp.pad(digits, ((0, 0), (0, EXTRA - digits.shape[1]))).astype(bf16)
    extra = jnp.broadcast_to(digits[:, :, None], (blocks, EXTRA, D))
    token_pieces = to_pieces(jnp.concatenate([tokens, extra], axis=1), me)
    cotangent, token_pieces = lax.optimization_barrier((cotangent, token_pieces))
    cot_pieces = to_pieces(cotangent, me)

    bias = call(
        functools.partial(bias_kernel, tiles), 1, [shape_of((H, n_mixed, QT, QT), f32)], [], "bias_tiles"
    )(rel_table)[0]
    taps = w_depth.astype(f32).reshape(KERNEL, 2, 128).transpose(1, 0, 2)
    taps = jnp.broadcast_to(taps[:, :, None, :], (2, KERNEL, 8, 128))

    (tok, ends, s1, k2, v2, weights, inverse, mixed, s2, gap, depth, sums) = run_a(
        tiles,
        me_ref,
        rel_table,
        *token_pieces,
        bias,
        g_ff1,
        w_ff1_in,
        w_ff1_out,
        g_att,
        twice(w_query),
        twice(w_key),
        one_side(w_value),
        w_output,
        g_conv,
        w_pw1,
        taps,
    )
    sums = sum_everywhere(sums)

    (o0, o1, o2, o3, grad3, bngrad, sums2, big_b, small_b) = run_b(
        tiles, me_ref, *cot_pieces, sums, depth, s2, bn_gain, w_pw2, g_ff2, w_ff2_in, w_ff2_out, g_out
    )
    out_pieces = from_pieces([o0, o1, o2, o3])
    sums2 = sum_everywhere(sums2)

    (grad2, do, dot, qt, dw_o, dw_pw1, taps_grad, row) = run_c(
        tiles,
        me_ref,
        sums,
        sums2,
        ends,
        s1,
        inverse,
        mixed,
        s2,
        gap,
        depth,
        grad3,
        bngrad,
        g_att,
        w_query,
        w_output,
        g_conv,
        w_pw1,
        taps,
        bn_gain,
    )
    (output, token_blocks, *packed) = run_e(
        tiles,
        me_ref,
        tok,
        s1,
        k2,
        v2,
        weights,
        grad2,
        do,
        dot,
        qt,
        dw_o,
        dw_pw1,
        taps_grad,
        row,
        *out_pieces,
        g_ff1,
        w_ff1_in,
        w_ff1_out,
        g_att,
        w_query,
        w_key,
        w_value,
        big_b,
        small_b,
    )

    def place(pieces, dtype):
        return call(place_kernel, 1, [shape_of((blocks, frames, D), dtype)], [], "place", micros=2, mib=8)(me_ref, *pieces)[0]

    reduced, tokens_grad = reduce_gradients(packed[:2], packed[2:], token_blocks, me, place)
    (ff1_in, ff1_out, w_q, w_k, w_v, w_o, pw1, pw2, ff2_in, ff2_out, *small) = call(
        kernel_d,
        1,
        [
            shape_of((D, FF), f32),
            shape_of((FF, D), f32),
            shape_of((D, D), f32),
            shape_of((D, D), f32),
            shape_of((D, D), f32),
            shape_of((D, D), f32),
            shape_of((D, 2 * D), f32),
            shape_of((D, D), f32),
            shape_of((D, FF), f32),
            shape_of((FF, D), f32),
            *[shape_of((1, D), f32)] * 3,
            shape_of((H, NBUCKET), f32),
            shape_of((KERNEL, D), f32),
            *[shape_of((1, D), f32)] * 3,
        ],
        [pltpu.VMEM((packed_rows(), D), bf16)],
        "unpack",
        micros=5,
        mib=13,
    )(me_ref, *reduced, sums2)
    d_g_ff1, d_g_att, d_g_conv, rel, d_taps, d_g_ff2, d_g_out, d_bn_gain = small
    return (
        output,
        tokens_grad,
        d_g_ff1.reshape(D),
        ff1_in,
        ff1_out,
        d_g_att.reshape(D),
        w_q,
        w_k,
        w_v,
        w_o,
        rel,
        d_g_conv.reshape(D),
        pw1,
        d_taps,
        d_bn_gain.reshape(D),
        pw2,
        d_g_ff2.reshape(D),
        ff2_in,
        ff2_out,
        d_g_out.reshape(D),
    )


def padded(x, sides, width):
    for axis, dim in sides:
        size, length = (lax.axis_size(axis), x.shape[dim])
        up = [(i, (i + 1) % size) for i in range(size - 1)]
        down = [(j, i) for i, j in up]
        last = lax.slice_in_dim(x, length - width, length, axis=dim)
        first = lax.slice_in_dim(x, 0, width, axis=dim)
        before = lax.ppermute(last, axis, up)
        after = lax.ppermute(first, axis, down)
        x = jnp.concatenate([before, x, after], axis=dim)
    return x


def norm_forward(values, norm_gain):
    center = jnp.mean(values, axis=-1, keepdims=True)
    shifted = values - center
    spread = jnp.mean(shifted * shifted, axis=-1, keepdims=True)
    inverse = lax.rsqrt(spread + epsilon)
    scaled = shifted * inverse
    return (scaled * norm_gain, (scaled, inverse))


def norm_backward(upstream, norm_gain, stored):
    scaled, inverse = stored
    gain_grad = jnp.sum(upstream * scaled, axis=(0, 1))
    inner_grad = upstream * norm_gain
    inner_mean = jnp.mean(inner_grad, axis=-1, keepdims=True)
    inner_dot = jnp.mean(inner_grad * scaled, axis=-1, keepdims=True)
    return (inverse * (inner_grad - inner_mean - scaled * inner_dot), gain_grad)


def project(left_side, weight):
    return jnp.einsum("rfd,de->rfe", left_side, weight, preferred_element_type=jnp.float32)


def project_back(upstream, weight):
    return jnp.einsum("rfe,de->rfd", upstream, weight, preferred_element_type=jnp.float32)


def weight_product(left_side, upstream):
    return jnp.einsum("rfd,rfe->de", left_side, upstream, preferred_element_type=jnp.float32)


def silu_slope(values):
    logistic = jax.nn.sigmoid(values)
    return logistic * (1.0 + values * (1.0 - logistic))


def ffn_forward(values, norm_gain, weight_in, weight_out):
    normed, norm_stored = norm_forward(values, norm_gain)
    normed_low = normed.astype(jnp.bfloat16)
    hidden = project(normed_low, weight_in)
    act_low = jax.nn.silu(hidden).astype(jnp.bfloat16)
    return (project(act_low, weight_out), (norm_stored, normed_low, hidden, act_low))


def ffn_backward(stream_grad, norm_gain, weight_in, weight_out, stored):
    norm_stored, normed_low, hidden, act_low = stored
    out_low = (0.5 * stream_grad).astype(jnp.bfloat16)
    out_weight_grad = weight_product(act_low, out_low)
    hidden_low = (project_back(out_low, weight_out) * silu_slope(hidden)).astype(jnp.bfloat16)
    in_weight_grad = weight_product(normed_low, hidden_low)
    input_grad, gain_grad = norm_backward(
        project_back(hidden_low, weight_in), norm_gain, norm_stored
    )
    return (stream_grad + input_grad, (gain_grad, in_weight_grad, out_weight_grad))


def bucket_bias(query_pos, key_pos, rel_table):
    distance = key_pos[None, :] - query_pos[:, None]
    levels = NBUCKET // 2
    magnitude = jnp.abs(distance)
    bucket = levels * (distance > 0).astype(jnp.int32)
    for exponent in range(levels - 1):
        bucket = bucket + (magnitude >= 4**exponent).astype(jnp.int32)
    onehot = (bucket[:, :, None] == jnp.arange(NBUCKET, dtype=jnp.int32)[None, None, :]).astype(
        jnp.float32
    )
    position_bias = jnp.einsum("qkb,hb->hqk", onehot, rel_table, precision=lax.Precision.HIGHEST)
    return (position_bias, onehot)


def block_at(source, block_index, query_heads, segment_float, query_pos, rel_table):
    key_all, value_all, code_all = source
    row_count, frames = segment_float.shape
    key_start = block_index * frames
    key_block = lax.dynamic_slice_in_dim(key_all, key_start, frames, 1).reshape(
        row_count, frames, H, HD
    )
    value_block = lax.dynamic_slice_in_dim(value_all, key_start, frames, 1).reshape(
        row_count, frames, H, HD
    )
    code_block = lax.dynamic_slice_in_dim(code_all, key_start, frames, 1)
    key_pos = key_start + jnp.arange(frames, dtype=jnp.int32)
    position_bias, onehot = bucket_bias(query_pos, key_pos, rel_table)
    raw_scores = (
        jnp.einsum("rqhd,rkhd->rhqk", query_heads, key_block, preferred_element_type=jnp.float32)
        * HD ** (-0.5)
        + position_bias[None]
    )
    allowed = (segment_float[:, :, None] == code_block.astype(jnp.float32)[:, None, :])[:, None]
    return (jnp.where(allowed, raw_scores, masked_score), allowed, onehot, key_block, value_block)


def attend_forward(
    values, segment, code_low, norm_gain, w_query, w_key, w_value, w_output, rel_table
):
    row_count, frames, model_width = values.shape
    normed, norm_stored = norm_forward(values, norm_gain)
    normed_low = normed.astype(jnp.bfloat16)
    query_low = project(normed_low, w_query).astype(jnp.bfloat16)
    key_low = project(normed_low, w_key).astype(jnp.bfloat16)
    value_low = project(normed_low, w_value).astype(jnp.bfloat16)
    gathered = (
        lax.all_gather(key_low, "blk", axis=1, tiled=True),
        lax.all_gather(value_low, "blk", axis=1, tiled=True),
        lax.all_gather(code_low, "blk", axis=1, tiled=True),
    )
    segment_float = segment.astype(jnp.float32)
    query_pos = lax.axis_index("blk") * frames + jnp.arange(frames, dtype=jnp.int32)
    query_heads = query_low.reshape(row_count, frames, H, HD)
    blocks = lax.axis_size("blk")

    def max_step(block_index, loop_state):
        running_max, running_sum = loop_state
        scores, allowed, onehot, key_block, value_block = block_at(
            gathered, block_index, query_heads, segment_float, query_pos, rel_table
        )
        new_max = jnp.maximum(running_max, jnp.max(scores, axis=-1))
        kept_exp = jnp.where(allowed, jnp.exp(scores - new_max[..., None]), 0.0)
        return (new_max, running_sum * jnp.exp(running_max - new_max) + jnp.sum(kept_exp, axis=-1))

    start_max = jnp.full((row_count, H, frames), masked_score, jnp.float32)
    running_max, running_sum = lax.fori_loop(
        0, blocks, max_step, (start_max, jnp.zeros_like(start_max))
    )
    log_total = running_max + jnp.log(running_sum)

    def mix_step(block_index, mixed_sum):
        scores, allowed, onehot, key_block, value_block = block_at(
            gathered, block_index, query_heads, segment_float, query_pos, rel_table
        )
        attn_low = jnp.where(allowed, jnp.exp(scores - log_total[..., None]), 0.0).astype(
            jnp.bfloat16
        )
        return mixed_sum + jnp.einsum(
            "rhqk,rkhd->rqhd", attn_low, value_block, preferred_element_type=jnp.float32
        )

    mixed_heads = lax.fori_loop(
        0, blocks, mix_step, jnp.zeros((row_count, frames, H, HD), jnp.float32)
    )
    mixed_heads = mixed_heads.reshape(row_count, frames, model_width)
    mixed_low = mixed_heads.astype(jnp.bfloat16)
    stored = (
        norm_stored,
        normed_low,
        query_heads,
        key_low,
        value_low,
        code_low,
        gathered,
        log_total,
        mixed_heads,
        mixed_low,
        segment_float,
        query_pos,
    )
    return (project(mixed_low, w_output), stored)


def attend_backward(stream_grad, norm_gain, w_query, w_key, w_value, w_output, rel_table, stored):
    (
        norm_stored,
        normed_low,
        query_heads,
        key_low,
        value_low,
        code_low,
        gathered,
        log_total,
        mixed_heads,
        mixed_low,
        segment_float,
        query_pos,
    ) = stored
    row_count, frames, model_width = stream_grad.shape
    grad_low = stream_grad.astype(jnp.bfloat16)
    w_output_grad = weight_product(mixed_low, grad_low)
    mixed_grad = (
        project_back(grad_low, w_output).astype(jnp.bfloat16).reshape(row_count, frames, H, HD)
    )
    row_delta = jnp.einsum(
        "rqhd,rqhd->rhq",
        mixed_grad.astype(jnp.float32),
        mixed_heads.reshape(row_count, frames, H, HD),
    )
    source = (
        lax.all_gather(key_low, "blk", axis=1, tiled=True),
        lax.all_gather(value_low, "blk", axis=1, tiled=True),
        lax.all_gather(code_low, "blk", axis=1, tiled=True),
    )
    blocks = lax.axis_size("blk")
    scale = HD ** (-0.5)

    def score_grads(block_index):
        scores, allowed, onehot, key_block, value_block = block_at(
            source, block_index, query_heads, segment_float, query_pos, rel_table
        )
        attn_weights = jnp.where(allowed, jnp.exp(scores - log_total[..., None]), 0.0)
        weight_grad = jnp.einsum(
            "rqhd,rkhd->rhqk", mixed_grad, value_block, preferred_element_type=jnp.float32
        )
        score_low = (attn_weights * (weight_grad - row_delta[..., None])).astype(jnp.bfloat16)
        return (attn_weights, score_low, onehot, key_block)

    def grad_step(block_index, loop_state):
        query_grad, key_buffer, value_buffer, table_grad = loop_state
        attn_weights, score_low, onehot, key_block = score_grads(block_index)
        attn_low = attn_weights.astype(jnp.bfloat16)
        query_grad = query_grad + jnp.einsum(
            "rhqk,rkhd->rqhd", score_low, key_block, preferred_element_type=jnp.float32
        )
        key_part = (
            jnp.einsum(
                "rhqk,rqhd->rkhd", score_low, query_heads, preferred_element_type=jnp.float32
            )
            * scale
        )
        value_part = jnp.einsum(
            "rhqk,rqhd->rkhd", attn_low, mixed_grad, preferred_element_type=jnp.float32
        )
        key_start = block_index * frames
        key_buffer = lax.dynamic_update_slice_in_dim(
            key_buffer, key_part.reshape(row_count, frames, model_width), key_start, 1
        )
        value_buffer = lax.dynamic_update_slice_in_dim(
            value_buffer, value_part.reshape(row_count, frames, model_width), key_start, 1
        )
        table_grad = table_grad + jnp.einsum(
            "hqk,qkb->hb",
            jnp.sum(score_low.astype(jnp.float32), axis=0),
            onehot,
            precision=lax.Precision.HIGHEST,
        )
        return (query_grad, key_buffer, value_buffer, table_grad)

    empty_buffer = jnp.zeros((row_count, blocks * frames, model_width), jnp.float32)
    start_state = (
        jnp.zeros((row_count, frames, H, HD), jnp.float32),
        empty_buffer,
        empty_buffer,
        jnp.zeros((H, NBUCKET), jnp.float32),
    )
    query_grad, key_buffer, value_buffer, table_grad = lax.fori_loop(
        0, blocks, grad_step, start_state
    )
    key_total, value_total = (
        lax.psum_scatter(
            key_buffer.astype(jnp.bfloat16), "blk", scatter_dimension=1, tiled=True
        ).astype(jnp.float32),
        lax.psum_scatter(
            value_buffer.astype(jnp.bfloat16), "blk", scatter_dimension=1, tiled=True
        ).astype(jnp.float32),
    )
    query_grad_low = (
        (query_grad * scale).reshape(row_count, frames, model_width).astype(jnp.bfloat16)
    )
    key_grad_low = key_total.astype(jnp.bfloat16)
    value_grad_low = value_total.astype(jnp.bfloat16)
    w_query_grad = weight_product(normed_low, query_grad_low)
    w_key_grad = weight_product(normed_low, key_grad_low)
    w_value_grad = weight_product(normed_low, value_grad_low)
    normed_grad = (
        project_back(query_grad_low, w_query)
        + project_back(key_grad_low, w_key)
        + project_back(value_grad_low, w_value)
    )
    input_grad, gain_grad = norm_backward(normed_grad, norm_gain, norm_stored)
    return (
        stream_grad + input_grad,
        (gain_grad, w_query_grad, w_key_grad, w_value_grad, w_output_grad, table_grad),
    )


def conv_forward(values, segment, live_mask, norm_gain, w_pw1, w_depth, bn_gain, w_pw2):
    row_count, frames, model_width = values.shape
    normed, norm_stored = norm_forward(values, norm_gain)
    normed_low = normed.astype(jnp.bfloat16)
    gate_pair = project(normed_low, w_pw1)
    first_half = gate_pair[..., :model_width]
    logistic = jax.nn.sigmoid(gate_pair[..., model_width:])
    live_frames = live_mask.astype(jnp.float32)[..., None]
    gated_low = (first_half * logistic * live_frames).astype(jnp.bfloat16)
    wide_units, wide_segment = (
        padded(gated_low, (("blk", 1),), KERNEL // 2),
        padded(segment.astype(jnp.bfloat16), (("blk", 1),), KERNEL // 2),
    )
    segment_float = segment.astype(jnp.float32)
    depth_sum = jnp.zeros((row_count, frames, model_width), jnp.float32)
    for kernel_tap in range(KERNEL):
        same_segment = (
            wide_segment[:, kernel_tap : kernel_tap + frames].astype(jnp.float32) == segment_float
        ).astype(jnp.float32)
        depth_sum = (
            depth_sum
            + w_depth[kernel_tap].astype(jnp.float32)
            * wide_units[:, kernel_tap : kernel_tap + frames].astype(jnp.float32)
            * same_segment[..., None]
        )
    norm_totals = lax.psum(
        (
            jnp.sum(depth_sum * live_frames, axis=(0, 1)),
            jnp.sum(depth_sum * depth_sum * live_frames, axis=(0, 1)),
            jnp.sum(live_frames),
        ),
        ("blk", "rows"),
    )
    frame_count = norm_totals[2]
    center = norm_totals[0] / frame_count
    spread = norm_totals[1] / frame_count - center * center
    inverse = lax.rsqrt(spread + epsilon)
    standard = (depth_sum - center) * inverse
    pre_act = standard * bn_gain
    act_low = jax.nn.silu(pre_act).astype(jnp.bfloat16)
    stored = (
        norm_stored,
        normed_low,
        first_half,
        logistic,
        live_frames,
        wide_units,
        wide_segment,
        frame_count,
        inverse,
        standard,
        pre_act,
        act_low,
    )
    return (project(act_low, w_pw2), stored)


def conv_backward(stream_grad, segment, norm_gain, w_pw1, w_depth, bn_gain, w_pw2, stored):
    (
        norm_stored,
        normed_low,
        first_half,
        logistic,
        live_frames,
        wide_units,
        wide_segment,
        frame_count,
        inverse,
        standard,
        pre_act,
        act_low,
    ) = stored
    row_count, frames, model_width = stream_grad.shape
    grad_low = stream_grad.astype(jnp.bfloat16)
    w_pw2_grad = weight_product(act_low, grad_low)
    act_grad = project_back(grad_low, w_pw2) * silu_slope(pre_act)
    hat_grad = act_grad * bn_gain
    grad_sums = lax.psum(
        (jnp.sum(hat_grad, axis=(0, 1)), jnp.sum(act_grad * standard, axis=(0, 1))), ("blk", "rows")
    )
    hat_total, bn_gain_grad = grad_sums
    frame_share = live_frames / frame_count
    depth_low = (
        inverse
        * (hat_grad - frame_share * hat_total - frame_share * standard * bn_gain * bn_gain_grad)
    ).astype(jnp.bfloat16)
    wide_grad = padded(depth_low, (("blk", 1),), KERNEL // 2)
    segment_float = segment.astype(jnp.float32)
    depth_float = depth_low.astype(jnp.float32)
    unit_grad = jnp.zeros((row_count, frames, model_width), jnp.float32)
    tap_grads = []
    for kernel_tap in range(KERNEL):
        forward_same = (
            wide_segment[:, kernel_tap : kernel_tap + frames].astype(jnp.float32) == segment_float
        ).astype(jnp.float32)[..., None]
        tap_grads.append(
            jnp.sum(
                depth_float
                * wide_units[:, kernel_tap : kernel_tap + frames].astype(jnp.float32)
                * forward_same,
                axis=(0, 1),
            )
        )
        mirror = KERNEL - 1 - kernel_tap
        backward_same = (
            wide_segment[:, mirror : mirror + frames].astype(jnp.float32) == segment_float
        ).astype(jnp.float32)[..., None]
        unit_grad = (
            unit_grad
            + w_depth[kernel_tap].astype(jnp.float32)
            * wide_grad[:, mirror : mirror + frames].astype(jnp.float32)
            * backward_same
        )
    unit_grad = unit_grad * live_frames
    pair_low = jnp.concatenate(
        [unit_grad * logistic, unit_grad * first_half * logistic * (1.0 - logistic)], axis=-1
    ).astype(jnp.bfloat16)
    w_pw1_grad = weight_product(normed_low, pair_low)
    input_grad, gain_grad = norm_backward(project_back(pair_low, w_pw1), norm_gain, norm_stored)
    return (
        stream_grad + input_grad,
        (gain_grad, w_pw1_grad, jnp.stack(tap_grads), bn_gain_grad, w_pw2_grad),
    )


def per_device(
    tokens,
    seg_ids,
    frame_mask,
    cotangent,
    g_ff1,
    w_ff1_in,
    w_ff1_out,
    g_att,
    w_query,
    w_key,
    w_value,
    w_output,
    rel_table,
    g_conv,
    w_pw1,
    w_depth,
    bn_gain,
    w_pw2,
    g_ff2,
    w_ff2_in,
    w_ff2_out,
    g_out,
):
    start_stream = tokens.astype(jnp.float32)
    ffn_one, ffn_one_stored = ffn_forward(start_stream, g_ff1, w_ff1_in, w_ff1_out)
    after_ffn = start_stream + 0.5 * ffn_one
    code_low = jnp.where(frame_mask == 1, seg_ids, -1).astype(jnp.bfloat16)
    attended, attend_stored = attend_forward(
        after_ffn, seg_ids, code_low, g_att, w_query, w_key, w_value, w_output, rel_table
    )
    after_att = after_ffn + attended
    conv_out, conv_stored = conv_forward(
        after_att, seg_ids, frame_mask, g_conv, w_pw1, w_depth, bn_gain, w_pw2
    )
    after_conv = after_att + conv_out
    ffn_two, ffn_two_stored = ffn_forward(after_conv, g_ff2, w_ff2_in, w_ff2_out)
    after_two = after_conv + 0.5 * ffn_two
    final_norm, final_stored = norm_forward(after_two, g_out)
    stream_grad, g_out_grad = norm_backward(cotangent.astype(jnp.float32), g_out, final_stored)
    stream_grad, ffn_two_grads = ffn_backward(
        stream_grad, g_ff2, w_ff2_in, w_ff2_out, ffn_two_stored
    )
    stream_grad, conv_grads = conv_backward(
        stream_grad, seg_ids, g_conv, w_pw1, w_depth, bn_gain, w_pw2, conv_stored
    )
    stream_grad, attend_grads = attend_backward(
        stream_grad, g_att, w_query, w_key, w_value, w_output, rel_table, attend_stored
    )
    stream_grad, ffn_one_grads = ffn_backward(
        stream_grad, g_ff1, w_ff1_in, w_ff1_out, ffn_one_stored
    )
    summed = lax.psum(
        (
            ffn_one_grads[0],
            ffn_one_grads[1],
            ffn_one_grads[2],
            attend_grads[0],
            attend_grads[1],
            attend_grads[2],
            attend_grads[3],
            attend_grads[4],
            attend_grads[5],
            conv_grads[0],
            conv_grads[1],
            conv_grads[2],
            conv_grads[4],
            ffn_two_grads[0],
            ffn_two_grads[1],
            ffn_two_grads[2],
            g_out_grad,
        ),
        ("blk", "rows"),
    )
    return (
        final_norm.astype(jnp.bfloat16),
        stream_grad,
        summed[0],
        summed[1],
        summed[2],
        summed[3],
        summed[4],
        summed[5],
        summed[6],
        summed[7],
        summed[8],
        summed[9],
        summed[10],
        summed[11],
        conv_grads[3],
        summed[12],
        summed[13],
        summed[14],
        summed[15],
        summed[16],
    )


def solution(mesh):
    blocks, groups = mesh.shape["blk"], mesh.shape["rows"]

    def device(tokens, *rest):
        rows, frames, _ = tokens.shape
        whole_rows = rows == blocks == 4 and groups == 8 and (rows * frames) % QT == 0
        return (row_device if whole_rows else per_device)(tokens, *rest)

    return jax.shard_map(
        device,
        mesh=mesh,
        in_specs=(
            P("rows", "blk", None),
            P("rows", "blk"),
            P("rows", "blk"),
            P("rows", "blk", None),
        )
        + (P(),) * 18,
        out_specs=(P("rows", "blk", None),) * 2 + (P(),) * 18,
        check_vma=False,
    )
```

```python
import functools
import math

import jax
import jax.numpy as jnp
from jax import lax
from jax.experimental import pallas as pl
from jax.experimental.pallas import tpu as pltpu
from jax.sharding import PartitionSpec as P

H = 4
HD = 64
D = 256
FF = 1024
KERNEL = 31
HALF = KERNEL // 2
NBUCKET = 16

epsilon = 1e-05
masked_score = -1e30

f32 = jnp.float32
bf16 = jnp.bfloat16
LOG2E = math.log2(math.e)
QT = 256
GAP = 16
EXTRA = 16
SAFE_EXPONENT = 60.0
MIB = 1024 * 1024


def mm(a, b):
    return lax.dot_general(a, b, (((1,), (0,)), ((), ())), preferred_element_type=f32)


def mm_nt(a, b):
    return lax.dot_general(a, b, (((1,), (1,)), ((), ())), preferred_element_type=f32)


def turned(x):
    return x.astype(f32).T.astype(bf16)


def sigmoid(x):
    return 0.5 + 0.5 * jnp.tanh(0.5 * x)


def norm_hat(v):
    center = jnp.mean(v, axis=-1, keepdims=True)
    shifted = v - center
    spread = jnp.mean(shifted * shifted, axis=-1, keepdims=True)
    inverse = lax.rsqrt(spread + epsilon)
    return shifted * inverse, inverse


def norm_back(upstream, gain, hat, inverse):
    inner = upstream * gain
    inner_mean = jnp.mean(inner, axis=-1, keepdims=True)
    inner_dot = jnp.mean(inner * hat, axis=-1, keepdims=True)
    return inverse * (inner - inner_mean - hat * inner_dot)


def col_sum(x):
    rows, width = x.shape
    return jnp.sum(x.reshape(rows // 8, 8, width), axis=0)


def bucket_ranges():
    levels = NBUCKET // 2
    big = 1 << 30
    edges = [0] + [4**k for k in range(levels - 1)] + [big]
    out = []
    for level in range(levels - 1, 0, -1):
        out.append((level, 1 - edges[level + 1], -edges[level]))
    out.append((0, 0, 0))
    for level in range(1, levels):
        out.append((levels + level, edges[level], edges[level + 1] - 1))
    return out


def tile_buckets(offset):
    low, high = offset * QT - (QT - 1), offset * QT + (QT - 1)
    return [(b, lo) for b, lo, hi in bucket_ranges() if lo <= high and hi >= low]


def mixed_offsets(tiles):
    return [o for o in range(1 - tiles, tiles) if len(tile_buckets(o)) > 1]


def tile_distance(offset):
    row = lax.broadcasted_iota(jnp.int32, (QT, QT), 0)
    col = lax.broadcasted_iota(jnp.int32, (QT, QT), 1)
    return col - row + offset * QT


def frame_index(start, rows, width):
    return (lax.broadcasted_iota(jnp.int32, (rows, width), 0) + start).astype(f32)


def rows_at(start, count, unit):
    return pl.ds(pl.multiple_of(start, unit), count)


def bias_kernel(tiles, table_ref, bias_ref):
    def head(h, carry):
        for k, offset in enumerate(mixed_offsets(tiles)):
            d = tile_distance(offset)
            found = tile_buckets(offset)
            value = jnp.full((QT, QT), table_ref[h, found[0][0]], f32)
            for b, lo in found[1:]:
                value = jnp.where(d >= lo, table_ref[h, b], value)
            bias_ref[h, k] = value * LOG2E
        return carry

    lax.fori_loop(0, H, head, 0)


def place_pieces(me_ref, piece_refs, target_ref, frames):
    for m, piece in enumerate(piece_refs):
        start = (me_ref[0] ^ m) * frames
        target_ref[rows_at(start, frames, 64), :] = piece[0:frames, :]


def take_pieces(me_ref, source_ref, piece_refs, frames):
    for m, piece in enumerate(piece_refs):
        start = (me_ref[0] ^ m) * frames
        piece[...] = source_ref[rows_at(start, frames, 64), :].astype(piece.dtype)


def key_features(start, rows, ends):
    first_end, second_end, live_end = (e[:, :128] for e in ends)
    t = frame_index(start, rows, 128)
    lane = lax.broadcasted_iota(jnp.int32, (rows, 128), 1)
    code = jnp.where(t < first_end, 0, jnp.where(t < second_end, 1, 2))
    code = jnp.where(t < live_end, code, -1)
    barred = jnp.where((lane < 3) & (code != lane), masked_score, 0.0)
    return jnp.where((lane >= 3) & (lane < 6), 1.0, barred).astype(bf16)


def query_features(start, rows, ends):
    first_end, second_end, live_end = (e[:, :128] for e in ends)
    t = frame_index(start, rows, 128)
    lane = lax.broadcasted_iota(jnp.int32, (rows, 128), 1)
    code = jnp.where(t < first_end, 0, jnp.where(t < second_end, 1, 2))
    return jnp.where(code == lane, 1.0, 0.0)


def three_parts(x):
    top = x.astype(bf16).astype(f32)
    middle = (x - top).astype(bf16).astype(f32)
    return top, middle, x - top - middle


def spread_gaps(plain_ref, gap_ref, length, ends):
    first_end, second_end, _ = (e[:, :128] for e in ends)
    total = length + 4 * GAP
    step = GAP * 4

    def chunk(k, carry):
        start = k * step
        g = frame_index(start, step, 128)
        for c in range(2):
            a = plain_ref[c, rows_at(start + 2 * GAP, step, 16), :]
            b = plain_ref[c, rows_at(start + GAP, step, 16), :]
            d = plain_ref[c, rows_at(start, step, 16), :]
            in_first = (g >= GAP) & (g - GAP < first_end)
            in_second = (g - 2 * GAP >= first_end) & (g - 2 * GAP < second_end)
            in_third = (g - 3 * GAP >= second_end) & (g - 3 * GAP < length)
            value = jnp.where(in_first, a, jnp.where(in_second, b, jnp.where(in_third, d, 0.0)))
            gap_ref[c, rows_at(start, step, 16), :] = value
        return carry

    lax.fori_loop(0, total // step, chunk, 0)


def close_gaps(gap_ref, start, rows, ends):
    first_end, second_end, _ = (e[:, :128] for e in ends)
    t = frame_index(start, rows, 128)
    halves = []
    for c in range(2):
        a = gap_ref[c, rows_at(start + GAP, rows, 16), :]
        b = gap_ref[c, rows_at(start + 2 * GAP, rows, 16), :]
        d = gap_ref[c, rows_at(start + 3 * GAP, rows, 16), :]
        halves.append(jnp.where(t < first_end, a, jnp.where(t < second_end, b, d)))
    return jnp.concatenate(halves, axis=1)


CONV_ROWS = 32
BACK_ROWS = 32


def tapped(part, tap):
    rows = part.shape[0]
    return (part.reshape(rows // 8, 8, 128) * tap[None]).reshape(rows, 128)


def shifted_parts(ref, c, start, rows):
    for r in range(8):
        window = ref[c, pl.ds(start - 16 + r, rows + 24), :]
        for q in range(4):
            shift = 8 * q + r - 16
            if abs(shift) <= HALF:
                yield shift, window[8 * q : 8 * q + rows]


def convolve(gap_ref, out_ref, taps_ref, length):
    span = length + 2 * GAP

    for c in range(2):

        def chunk(k, carry, c=c):
            start = GAP + k * CONV_ROWS
            total = jnp.zeros((CONV_ROWS, 128), f32)
            for shift, part in shifted_parts(gap_ref, c, start, CONV_ROWS):
                total = total + tapped(part, taps_ref[c, shift + HALF])
            out_ref[c, rows_at(start, CONV_ROWS, 16), :] = total
            return carry

        lax.fori_loop(0, span // CONV_ROWS, chunk, 0, unroll=2)


def convolve_back(dgap_ref, gap_ref, out_ref, taps_ref, taps_grad_ref, length):
    span = length + 2 * GAP
    for c in range(2):

        def chunk(k, carry, c=c):
            start = GAP + k * BACK_ROWS
            units = gap_ref[c, rows_at(start, BACK_ROWS, 16), :]
            total = jnp.zeros((BACK_ROWS, 128), f32)
            sums = list(carry)
            for shift, part in shifted_parts(dgap_ref, c, start, BACK_ROWS):
                j = HALF - shift
                total = total + tapped(part, taps_ref[c, j])
                sums[j] = sums[j] + col_sum(part * units)
            out_ref[c, rows_at(start, BACK_ROWS, 16), :] = total
            return tuple(sums)

        sums = lax.fori_loop(0, span // BACK_ROWS, chunk, tuple(jnp.zeros((8, 128), f32) for _ in range(KERNEL)), unroll=2)
        for j in range(KERNEL):
            taps_grad_ref[j : j + 1, 128 * c : 128 * c + 128] = jnp.sum(sums[j], axis=0, keepdims=True)
    taps_grad_ref[KERNEL : KERNEL + 1, :] = jnp.zeros((1, 2 * 128), f32)


def add_to(ref, first, value):
    ref[...] = value if first else ref[...] + value


def read_ends(ends_ref):
    return ends_ref[0:1, :], ends_ref[1:2, :], ends_ref[2:3, :]


FRONT = 1280
GATE = 1280


def attend_tile(q2_ref, fq_ref, h, qt, k2_ref, fk_ref, bias_ref, table_ref, tiles):
    rows = slice(qt * QT, (qt + 1) * QT)
    qa = jnp.concatenate([q2_ref[h, rows, :], fq_ref[rows, :]], axis=1)
    ka = jnp.concatenate([k2_ref[h], fk_ref[...]], axis=1)
    offsets = mixed_offsets(tiles)
    s_all = mm_nt(qa, ka)
    parts = []
    for kt in range(tiles):
        s = s_all[:, kt * QT : (kt + 1) * QT]
        o = kt - qt
        if o in offsets:
            s = s + bias_ref[h, offsets.index(o)]
        else:
            s = s + table_ref[h, tile_buckets(o)[0][0]] * LOG2E
        parts.append(jnp.exp2(s).astype(bf16))
    return jnp.concatenate(parts, axis=1)


def attend_tile_below_max(q2_ref, fq_ref, h, rows, start, k2_ref, fk_ref, table_ref, s_ref, tiles):
    qa = jnp.concatenate([q2_ref[h, rows, :], fq_ref[rows, :]], axis=1)
    ka = jnp.concatenate([k2_ref[h], fk_ref[...]], axis=1)
    s_ref[...] = mm_nt(qa, ka)
    ranges = bucket_ranges()

    def add_bias(kt, top):
        cols = rows_at(kt * QT, QT, QT)
        d = tile_distance(0) + (kt * QT - start)
        value = jnp.full((QT, QT), table_ref[h, ranges[0][0]], f32)
        for b, low, _ in ranges[1:]:
            value = jnp.where(d >= low, table_ref[h, b], value)
        s = s_ref[:, cols] + value * LOG2E
        s_ref[:, cols] = s
        return jnp.maximum(top, jnp.max(s, axis=1, keepdims=True))

    top = lax.fori_loop(0, tiles, add_bias, jnp.full((QT, 1), -jnp.inf, f32))
    return jnp.exp2(s_ref[...] - top).astype(bf16)


def kernel_a(
    tiles,
    me_ref,
    table_ref,
    piece0,
    piece1,
    piece2,
    piece3,
    bias_ref,
    g_ff1_ref,
    w_in_ref,
    w_out_ref,
    g_att_ref,
    wq2_ref,
    wk2_ref,
    wv2_ref,
    w_o_ref,
    g_conv_ref,
    w_pw1_ref,
    taps_ref,
    tok_ref,
    ends_ref,
    s1_ref,
    k2_ref,
    v2_ref,
    weights_ref,
    inverse_ref,
    mixed_ref,
    s2_ref,
    gap_ref,
    depth_ref,
    sums_ref,
    q2_ref,
    fq_ref,
    fk_ref,
    fast_ref,
    p_ref,
    s_ref,
    plain_ref,
    conv_ref,
    moved,
):
    pieces = (piece0, piece1, piece2, piece3)
    length = tiles * QT
    frames = length // len(pieces)
    place_pieces(me_ref, pieces, tok_ref, frames)
    extra = sum(p[frames : frames + EXTRA, :].astype(f32) for p in pieces)
    first_end = 16.0 * extra[0:1, :] + extra[1:2, :]
    second_end = first_end + 16.0 * extra[2:3, :] + extra[3:4, :]
    live_end = 16.0 * extra[4:5, :] + extra[5:6, :]
    ends_ref[0:1, :] = first_end
    ends_ref[1:2, :] = second_end
    ends_ref[2:3, :] = live_end
    ends_ref[3:8, :] = jnp.zeros((5, D), f32)
    ends = (first_end, second_end, live_end)

    scale = LOG2E * HD**-0.5

    def front(i, carry):
        at = slice(i * FRONT, (i + 1) * FRONT)
        x = tok_ref[at, :].astype(f32)
        hat, _ = norm_hat(x)
        n1 = (hat * g_ff1_ref[...]).astype(bf16)
        hidden = mm(n1, w_in_ref[...])
        act = (hidden * sigmoid(hidden)).astype(bf16)
        s1 = x + 0.5 * mm(act, w_out_ref[...])
        s1_ref[at, :] = s1
        hat, _ = norm_hat(s1)
        n2 = (hat * g_att_ref[...]).astype(bf16)
        lane = lax.broadcasted_iota(jnp.int32, (FRONT, 128), 1)
        q_top, k_top = carry
        q_all = mm(n2, wq2_ref[...]).astype(bf16).astype(f32) * scale
        k_all = mm(n2, wk2_ref[...]).astype(bf16)
        v_all = mm(n2, wv2_ref[...])
        for h in range(H):
            cols = slice(128 * h, 128 * h + 128)
            q = q_all[:, cols]
            high = q.astype(bf16)
            low = (q - high.astype(f32)).astype(bf16)
            q2_ref[h, at, :] = jnp.where(lane < HD, high.astype(f32), low.astype(f32)).astype(bf16)
            k2_ref[h, at, :] = k_all[:, cols]
            ones = (lane >= HD) & (lane < HD + 3) if h % 2 == 0 else lane < 3
            v2_ref[h, at, :] = jnp.where(ones, 1.0, v_all[:, cols]).astype(bf16)
            q_top = jnp.maximum(q_top, jnp.max(jnp.sum(q * q, axis=1, keepdims=True)))
            k = k_all[:, cols].astype(f32)
            k_top = jnp.maximum(k_top, jnp.max(jnp.sum(k * k, axis=1, keepdims=True)))
        fq_ref[at, :] = query_features(i * FRONT, FRONT, ends).astype(bf16)
        fk_ref[at, :] = key_features(i * FRONT, FRONT, ends)
        return q_top, k_top

    q_top, k_top = jnp.float32(0.0), jnp.float32(0.0)
    for i in range(length // FRONT):
        q_top, k_top = front(i, (q_top, k_top))
    fast_ref[0] = jnp.where(q_top * k_top < 4.0 * SAFE_EXPONENT**2, 1, 0)

    def weights_copy(h, slot):
        return pltpu.make_async_copy(p_ref.at[slot], weights_ref.at[h], moved.at[slot])

    def room(h, slot):
        @pl.when(h > 1)
        def _():
            weights_copy(h - 2, slot).wait()

    def mix(h, slot, rows, p):
        p_ref[slot, rows, :] = p
        total = mm(p, v2_ref[h])
        lane = lax.broadcasted_iota(jnp.int32, (QT, 128), 1)
        first = slot == 0
        denominator = jnp.where(first, total[:, HD : HD + 1], total[:, 0:1])
        inverse = jnp.broadcast_to(1.0 / denominator, (QT, 128))
        mixed = total * inverse
        g = lax.div(h, 2)
        new = jnp.logical_or(first, lane >= HD)
        mixed_ref[g, rows, :] = jnp.where(new, mixed, mixed_ref[g, rows, :])
        inverse_ref[g, rows, :] = jnp.where(new, inverse, inverse_ref[g, rows, :])

    @pl.when(fast_ref[0] == 1)
    def _():
        def head(h, carry):
            slot = lax.rem(h, 2)
            room(h, slot)
            for qt in range(tiles):
                p = attend_tile(q2_ref, fq_ref, h, qt, k2_ref, fk_ref, bias_ref, table_ref, tiles)
                mix(h, slot, slice(qt * QT, (qt + 1) * QT), p)
            weights_copy(h, slot).start()
            return carry

        lax.fori_loop(0, H, head, 0)

    @pl.when(fast_ref[0] != 1)
    def _():
        def head(h, carry):
            slot = lax.rem(h, 2)
            room(h, slot)

            def tile(qt, carry):
                rows = rows_at(qt * QT, QT, QT)
                p = attend_tile_below_max(
                    q2_ref, fq_ref, h, rows, qt * QT, k2_ref, fk_ref, table_ref, s_ref, tiles
                )
                mix(h, slot, rows, p)
                return carry

            lax.fori_loop(0, tiles, tile, 0)
            weights_copy(h, slot).start()
            return carry

        lax.fori_loop(0, H, head, 0)

    def gate(i):
        at = slice(i * GATE, (i + 1) * GATE)
        mixed = jnp.concatenate([mixed_ref[0, at, :], mixed_ref[1, at, :]], axis=1)
        s2 = s1_ref[at, :] + mm(mixed.astype(bf16), w_o_ref[...])
        s2_ref[at, :] = s2
        hat, _ = norm_hat(s2)
        n3 = (hat * g_conv_ref[...]).astype(bf16)
        pair = mm(n3, w_pw1_ref[...])
        live = frame_index(i * GATE, GATE, D) < live_end
        units = jnp.where(live, pair[:, :D] * sigmoid(pair[:, D:]), 0.0).astype(bf16).astype(f32)
        put = slice(i * GATE + 3 * GAP, (i + 1) * GATE + 3 * GAP)
        plain_ref[0, put, :] = units[:, :128]
        plain_ref[1, put, :] = units[:, 128:]

    for i in range(length // GATE):
        gate(i)
    spread_gaps(plain_ref, gap_ref, length, ends)
    convolve(gap_ref, conv_ref, taps_ref, length)

    def collect(i, carry):
        total, squares = carry
        at = rows_at(i * QT, QT, QT)
        depth = close_gaps(conv_ref, i * QT, QT, ends)
        depth_ref[at, :] = depth
        kept = jnp.where(frame_index(i * QT, QT, D) < live_end, depth, 0.0)
        return total + col_sum(kept), squares + col_sum(kept * kept)

    empty = jnp.zeros((8, D), f32)
    total, squares = lax.fori_loop(0, tiles, collect, (empty, empty))
    sums_ref[0:1, :] = jnp.sum(total, axis=0, keepdims=True)
    sums_ref[1:2, :] = jnp.sum(squares, axis=0, keepdims=True)
    sums_ref[2:3, :] = live_end
    sums_ref[3:8, :] = jnp.zeros((5, D), f32)
    for parity in range(2):
        weights_copy(H - 2 + parity, parity).wait()


MIDDLE = 1280


def batch_norm_terms(sums_ref):
    count = sums_ref[2:3, :]
    center = sums_ref[0:1, :] / count
    spread = sums_ref[1:2, :] / count - center * center
    return count, center, lax.rsqrt(spread + epsilon)


def kernel_b(
    tiles,
    me_ref,
    cot0,
    cot1,
    cot2,
    cot3,
    sums_ref,
    depth_ref,
    s2_ref,
    bn_gain_ref,
    w_pw2_ref,
    g_ff2_ref,
    w_in_ref,
    w_out_ref,
    g_out_ref,
    out0,
    out1,
    out2,
    out3,
    grad3_ref,
    bngrad_ref,
    sums2_ref,
    big_ref,
    small_ref,
    cot_ref,
    out_ref,
    dw_in_ref,
    dw_out_ref,
    dw_pw2_ref,
):
    length = tiles * QT
    frames = length // 4
    place_pieces(me_ref, (cot0, cot1, cot2, cot3), cot_ref, frames)
    _, center, inverse = batch_norm_terms(sums_ref)
    bn_gain = bn_gain_ref[...]

    def step(i, carry):
        g_out_sum, g_ff2_sum, bn_sum, bn_dot = carry
        at = slice(i * MIDDLE, (i + 1) * MIDDLE)
        standard = (depth_ref[at, :] - center) * inverse
        pre = standard * bn_gain
        logistic3 = sigmoid(pre)
        act3 = (pre * logistic3).astype(bf16)
        s3 = s2_ref[at, :] + mm(act3, w_pw2_ref[...])
        hat3, inv3 = norm_hat(s3)
        n4 = (hat3 * g_ff2_ref[...]).astype(bf16)
        hidden = mm(n4, w_in_ref[...])
        logistic = sigmoid(hidden)
        act4 = (hidden * logistic).astype(bf16)
        s4 = s3 + 0.5 * mm(act4, w_out_ref[...])
        hat4, inv4 = norm_hat(s4)
        out_ref[at, :] = (hat4 * g_out_ref[...]).astype(bf16)
        cot = cot_ref[at, :].astype(f32)
        g_out_sum = g_out_sum + col_sum(cot * hat4)
        grad4 = norm_back(cot, g_out_ref[...], hat4, inv4)
        out4 = (0.5 * grad4).astype(bf16)
        add_to(dw_out_ref, i == 0, mm(turned(out4), act4))
        slope = logistic * (1.0 + hidden * (1.0 - logistic))
        hid4 = (mm_nt(out4, w_out_ref[...]) * slope).astype(bf16)
        add_to(dw_in_ref, i == 0, mm(turned(n4), hid4))
        up = mm_nt(hid4, w_in_ref[...])
        g_ff2_sum = g_ff2_sum + col_sum(up * hat3)
        grad3 = grad4 + norm_back(up, g_ff2_ref[...], hat3, inv3)
        grad3_ref[at, :] = grad3
        out3 = grad3.astype(bf16)
        add_to(dw_pw2_ref, i == 0, mm(turned(act3), out3))
        bngrad = mm_nt(out3, w_pw2_ref[...]) * (logistic3 * (1.0 + pre * (1.0 - logistic3)))
        bngrad_ref[at, :] = bngrad
        return g_out_sum, g_ff2_sum, bn_sum + col_sum(bngrad), bn_dot + col_sum(bngrad * standard)

    empty = jnp.zeros((8, D), f32)
    sums = (empty,) * 4
    for i in range(length // MIDDLE):
        sums = step(i, sums)
    g_out_sum, g_ff2_sum, bn_sum, bn_dot = (jnp.sum(s, axis=0, keepdims=True) for s in sums)
    sums2_ref[0:1, :] = bn_sum
    sums2_ref[1:2, :] = bn_dot
    sums2_ref[2:8, :] = jnp.zeros((6, D), f32)
    small_ref[0:1, :] = g_ff2_sum
    small_ref[1:2, :] = g_out_sum
    small_ref[2:8, :] = jnp.zeros((6, D), f32)
    big_ref[0:FF, :] = turned_wide(dw_out_ref)
    for c in range(FF // D):
        big_ref[FF + c * D : FF + (c + 1) * D, :] = dw_in_ref[:, c * D : (c + 1) * D].astype(big_ref.dtype)
    big_ref[2 * FF : 2 * FF + D, :] = dw_pw2_ref[...].astype(big_ref.dtype)
    take_pieces(me_ref, out_ref, (out0, out1, out2, out3), frames)


def turned_wide(ref):
    return jnp.concatenate([ref[:, c * D : (c + 1) * D].T for c in range(ref.shape[1] // D)], axis=0).astype(bf16)


BACK = 640
LAST = 256


def kernel_c(
    tiles,
    me_ref,
    sums_ref,
    sums2_ref,
    ends_ref,
    s1_ref,
    inverse_ref,
    mixed_ref,
    s2_ref,
    gap_ref,
    depth_ref,
    grad3_ref,
    bngrad_ref,
    g_att_ref,
    w_q_ref,
    w_o_ref,
    g_conv_ref,
    w_pw1_ref,
    taps_ref,
    bn_gain_ref,
    grad_ref,
    do_ref,
    dot_ref,
    qt_ref,
    dw_o_ref,
    dw_pw1_ref,
    taps_grad_ref,
    row_ref,
    plain_ref,
    dgap_ref,
):
    length = tiles * QT
    ends = read_ends(ends_ref)
    live_end = ends[2]
    count, center, inverse = batch_norm_terms(sums_ref)
    bn_gain = bn_gain_ref[...]
    e_total = sums2_ref[0:1, :] * bn_gain
    dot_total = sums2_ref[1:2, :]


    def batch_back(i, carry):
        at = rows_at(i * QT, QT, QT)
        standard = (depth_ref[at, :] - center) * inverse
        e = bngrad_ref[at, :] * bn_gain
        share = jnp.where(frame_index(i * QT, QT, D) < live_end, 1.0, 0.0) / count
        dg = inverse * (e - share * e_total - share * standard * bn_gain * dot_total)
        dg = dg.astype(bf16).astype(f32)
        put = rows_at(i * QT + 3 * GAP, QT, 16)
        plain_ref[0, put, :] = dg[:, :128]
        plain_ref[1, put, :] = dg[:, 128:]
        return carry

    lax.fori_loop(0, tiles, batch_back, 0)
    spread_gaps(plain_ref, dgap_ref, length, ends)
    convolve_back(dgap_ref, gap_ref, plain_ref, taps_ref, taps_grad_ref, length)

    def gate_back(i, g_conv_sum):
        at = slice(i * BACK, (i + 1) * BACK)
        hat, inv = norm_hat(s2_ref[at, :])
        n3 = (hat * g_conv_ref[...]).astype(bf16)
        pair = mm(n3, w_pw1_ref[...])
        first, logistic = pair[:, :D], sigmoid(pair[:, D:])
        live = frame_index(i * BACK, BACK, D) < live_end
        ug = jnp.where(live, close_gaps(plain_ref, i * BACK, BACK, ends), 0.0) * logistic
        pairgrad = jnp.concatenate([ug, ug * first * (1.0 - logistic)], axis=1).astype(bf16)
        add_to(dw_pw1_ref, i == 0, mm(turned(n3), pairgrad))
        up = mm_nt(pairgrad, w_pw1_ref[...])
        g_conv_sum = g_conv_sum + col_sum(up * hat)
        grad2 = grad3_ref[at, :] + norm_back(up, g_conv_ref[...], hat, inv)
        grad_ref[at, :] = grad2
        out2 = grad2.astype(bf16)
        mixed = jnp.concatenate([mixed_ref[0, at, :], mixed_ref[1, at, :]], axis=1)
        add_to(dw_o_ref, i == 0, mm(turned(mixed), out2))
        mixgrad = mm_nt(out2, w_o_ref[...]).astype(bf16).astype(f32)
        mixgrad = (mixgrad * jnp.concatenate([inverse_ref[0, at, :], inverse_ref[1, at, :]], axis=1)).astype(bf16)
        dot_ref[:, at] = turned(mixgrad)
        product = mixgrad.astype(f32) * mixed
        lane = lax.broadcasted_iota(jnp.int32, (BACK, 128), 1)
        for h in range(H):
            cols = slice(128 * (h // 2), 128 * (h // 2) + 128)
            own = lane < HD if h % 2 == 0 else lane >= HD
            delta = jnp.sum(jnp.where(own, product[:, cols], 0.0), axis=1, keepdims=True)
            high, middle, low = three_parts(-delta)
            base = HD if h % 2 == 0 else 0
            side = jnp.where(lane == base, high, 0.0)
            side = jnp.where(lane == base + 1, middle, side)
            side = jnp.where(lane == base + 2, low, side)
            do_ref[h, at, :] = jnp.where(own, mixgrad[:, cols].astype(f32), side).astype(bf16)
        hat, _ = norm_hat(s1_ref[at, :])
        n2 = (hat * g_att_ref[...]).astype(bf16)
        qt_ref[:, at] = turned(mm(n2, w_q_ref[...]).astype(bf16))
        return g_conv_sum

    empty = jnp.zeros((8, D), f32)
    g_conv_sum = empty
    for i in range(length // BACK):
        g_conv_sum = gate_back(i, g_conv_sum)
    row_ref[0:1, :] = jnp.sum(g_conv_sum, axis=0, keepdims=True)
    row_ref[1:8, :] = jnp.zeros((7, D), f32)


def kernel_e(
    tiles,
    me_ref,
    tok_ref,
    s1_ref,
    k2_ref,
    v2_ref,
    weights_ref,
    grad_ref,
    do_ref,
    dot_ref,
    qt_ref,
    dw_o_ref,
    dw_pw1_ref,
    taps_grad_ref,
    row_ref,
    out0,
    out1,
    out2,
    out3,
    g_ff1_ref,
    w_ff1_in_ref,
    w_ff1_out_ref,
    g_att_ref,
    w_q_ref,
    w_k_ref,
    w_v_ref,
    big_b_ref,
    small_b_ref,
    output_ref,
    blocks_ref,
    kept_a,
    kept_b,
    sent_a,
    sent_b,
    small_ref,
    p_ref,
    dq_ref,
    dkt_ref,
    dvt_ref,
    acc_ref,
    dw_in_ref,
    dw_out_ref,
    dw_q_ref,
    dw_k_ref,
    dw_v_ref,
    last_ref,
    arrived,
):
    length = tiles * QT
    frames = length // 4

    def weights_copy(h, slot):
        return pltpu.make_async_copy(weights_ref.at[h], p_ref.at[slot], arrived.at[slot])

    weights_copy(0, 0).start()
    for m, piece in enumerate((out0, out1, out2, out3)):
        output_ref[me_ref[0] ^ m] = piece[...]
    empty = jnp.zeros((8, D), f32)


    offsets = mixed_offsets(tiles)

    def head(h, carry):
        slot = lax.rem(h, 2)

        @pl.when(h + 1 < H)
        def _():
            weights_copy(h + 1, 1 - slot).start()

        weights_copy(h, slot).wait()
        flat = {}
        started = set()
        own = rows_at(h * HD, HD, HD)
        dvt_ref[own, :] = mm(dot_ref[own, :], p_ref[slot])
        pair = lax.div(h, 2)
        for qt in range(tiles):
            rows = slice(qt * QT, (qt + 1) * QT)
            d_all = mm_nt(do_ref[h, rows, :], v2_ref[h])
            low = []
            for kt in range(tiles):
                cols = slice(kt * QT, (kt + 1) * QT)
                ds = p_ref[slot, rows, cols].astype(f32) * d_all[:, cols]
                o = kt - qt
                if o in offsets:
                    k = offsets.index(o)
                    acc_ref[k] = acc_ref[k] + ds if k in started else ds
                    started.add(k)
                else:
                    b = tile_buckets(o)[0][0]
                    flat[b] = flat[b] + col_sum(ds) if b in flat else col_sum(ds)
                low.append(ds.astype(bf16))
            low = jnp.concatenate(low, axis=1)
            p_ref[slot, rows, :] = low
            dq = mm(low, k2_ref[h])
            own_half = (lax.broadcasted_iota(jnp.int32, (QT, 128), 1) < HD) == (slot == 0)
            dq_ref[pair, rows, :] = jnp.where(own_half, dq, dq_ref[pair, rows, :])
        dkt_ref[own, :] = mm(qt_ref[own, :], p_ref[slot])
        table_row = jnp.zeros((1, D), f32)
        lane = lax.broadcasted_iota(jnp.int32, (1, D), 1)
        for k, o in enumerate(offsets):
            d = tile_distance(o)
            value = acc_ref[k]
            found = tile_buckets(o)
            tails = [col_sum(jnp.where(d >= lo, value, 0.0)) for _, lo in found[1:]]
            tails = [col_sum(value)] + tails
            for n, (b, _) in enumerate(found):
                part = tails[n] - tails[n + 1] if n + 1 < len(found) else tails[n]
                flat[b] = flat[b] + part if b in flat else part
        for b, part in flat.items():
            table_row = jnp.where(lane == b, jnp.sum(part), table_row)
        small_ref[pl.ds(h + 4, 1), :] = table_row
        return carry

    small_ref[...] = jnp.zeros_like(small_ref)
    lax.fori_loop(0, H, head, 0)


    def front_back(i, carry):
        g_att_sum, g_ff1_sum = carry
        at = slice(i * LAST, (i + 1) * LAST)
        dq = jnp.concatenate([dq_ref[g, at, :] for g in range(H // 2)], axis=1)
        dq = (dq * HD**-0.5).astype(bf16)
        dk = (dkt_ref[:, at] * HD**-0.5).T.astype(bf16)
        dv = dvt_ref[:, at].T.astype(bf16)
        s1 = s1_ref[at, :]
        hat2, inv2 = norm_hat(s1)
        n2 = turned((hat2 * g_att_ref[...]).astype(bf16))
        add_to(dw_q_ref, i == 0, mm(n2, dq))
        add_to(dw_k_ref, i == 0, mm(n2, dk))
        add_to(dw_v_ref, i == 0, mm(n2, dv))
        attgrad = mm_nt(dq, w_q_ref[...]) + mm_nt(dk, w_k_ref[...]) + mm_nt(dv, w_v_ref[...])
        g_att_sum = g_att_sum + col_sum(attgrad * hat2)
        grad1 = grad_ref[at, :] + norm_back(attgrad, g_att_ref[...], hat2, inv2)
        out1 = (0.5 * grad1).astype(bf16)
        x = tok_ref[at, :].astype(f32)
        hat1, inv1 = norm_hat(x)
        n1 = (hat1 * g_ff1_ref[...]).astype(bf16)
        hidden = mm(n1, w_ff1_in_ref[...])
        logistic = sigmoid(hidden)
        act1 = (hidden * logistic).astype(bf16)
        add_to(dw_out_ref, i == 0, mm(turned(out1), act1))
        slope = logistic * (1.0 + hidden * (1.0 - logistic))
        hid1 = (mm_nt(out1, w_ff1_out_ref[...]) * slope).astype(bf16)
        add_to(dw_in_ref, i == 0, mm(turned(n1), hid1))
        up = mm_nt(hid1, w_ff1_in_ref[...])
        g_ff1_sum = g_ff1_sum + col_sum(up * hat1)
        last_ref[at, :] = grad1 + norm_back(up, g_ff1_ref[...], hat1, inv1)
        return g_att_sum, g_ff1_sum

    g_att_sum, g_ff1_sum = empty, empty
    for i in range(length // LAST):
        g_att_sum, g_ff1_sum = front_back(i, (g_att_sum, g_ff1_sum))
    for k, s in enumerate((g_ff1_sum, g_att_sum)):
        small_ref[k : k + 1, :] = jnp.sum(s, axis=0, keepdims=True)
    small_ref[2:3, :] = row_ref[0:1, :]
    small_ref[8 : 8 + KERNEL + 1, :] = taps_grad_ref[...]
    for b in range(length // frames):
        blocks_ref[b] = last_ref[b * frames : (b + 1) * frames, :].astype(bf16)
    quarter = kept_a.shape[0]

    def put(start, value):
        side, first = start // (2 * quarter), start // quarter % 2 == 0
        at = slice(start % quarter, start % quarter + value.shape[0])

        @pl.when(me_ref[1] == side)
        def _():
            (kept_a if first else kept_b)[at, :] = value

        @pl.when(me_ref[1] != side)
        def _():
            (sent_a if first else sent_b)[at, :] = value

    for c in range(FF // D):
        put(c * D, dw_out_ref[:, c * D : (c + 1) * D].T.astype(bf16))
        put(FF + c * D, dw_in_ref[:, c * D : (c + 1) * D].astype(bf16))
    for k, ref in enumerate((dw_q_ref, dw_k_ref, dw_v_ref, dw_o_ref)):
        put(2 * FF + k * D, ref[...].astype(bf16))
    for c in range(2):
        put(2 * FF + (4 + c) * D, dw_pw1_ref[:, c * D : (c + 1) * D].astype(bf16))
    for c in range(BIG_B // D):
        put(BIG_C + c * D, big_b_ref[c * D : (c + 1) * D, :])
    rest = 4 * quarter - BIG_C - BIG_B - SMALL_C - SMALL_B
    small = [small_ref[...], small_b_ref[...], jnp.zeros((rest, D), f32)]
    put(BIG_C + BIG_B, jnp.concatenate(small, axis=0).astype(bf16))


def swap(x, axis, bit):
    size = lax.axis_size(axis)
    return lax.ppermute(x, axis, [(i, i ^ bit) for i in range(size)])


def doubling_steps():
    steps = []
    for axis in ("rows", "blk"):
        size = lax.axis_size(axis)
        bit = 1
        while bit < size:
            steps.append((axis, bit))
            bit *= 2
    return steps


def sum_everywhere(x):
    for axis, bit in doubling_steps():
        x = x + swap(x, axis, bit)
    return x


def to_pieces(x, me):
    own = lax.dynamic_index_in_dim(x, me, 0, keepdims=False)
    pieces = [own]
    for m in range(1, x.shape[0]):
        pieces.append(swap(lax.dynamic_index_in_dim(x, me ^ m, 0, keepdims=False), "blk", m))
    return pieces


def from_pieces(pieces):
    return [pieces[0]] + [swap(p, "blk", m) for m, p in enumerate(pieces) if m > 0]


def cut(terms, start, rows):
    return sum(lax.dynamic_slice_in_dim(t, start, rows, 0).astype(f32) for t in terms).astype(bf16)


def keep_half(terms, axis, bit):
    half = terms[0].shape[0] // 2
    side = (lax.axis_index(axis) // bit) % 2
    got = swap(cut(terms, (1 - side) * half, half), axis, bit)
    return [cut(terms, side * half, half), got]


def join_half(x, axis, bit):
    side = (lax.axis_index(axis) // bit) % 2
    got = swap(x, axis, bit)
    return jnp.where(side == 0, jnp.concatenate([x, got]), jnp.concatenate([got, x]))


def halve_kernel(me_ref, kept_a, kept_b, got_a, got_b, send_a, send_b, keep_a, keep_b):
    half = send_a.shape[0]
    parts = ((kept_a, got_a, send_a, keep_a, me_ref[2]), (kept_b, got_b, send_b, keep_b, me_ref[3]))
    for kept, got, send, keep, side in parts:
        for target, place in ((send, 1 - side), (keep, side)):
            at = rows_at(place * half, half, 64)
            target[...] = (kept[at, :].astype(f32) + got[at, :].astype(f32)).astype(bf16)


def reduce_gradients(kept, sent, token_blocks, me, me_ref, place):
    got_a, got_b = (swap(s, "rows", 1) for s in sent)
    t0, t1, t2, t3 = to_pieces(token_blocks, me)
    rows = kept[0].shape[0] // 2
    send_a, send_b, keep_a, keep_b = call(
        halve_kernel, 1, [shape_of((rows, D), bf16)] * 4, [], "halves", micros=1, mib=8
    )(me_ref, *kept, got_a, got_b)
    a, b = [keep_a, swap(send_a, "rows", 2)], [keep_b, swap(send_b, "rows", 4)]
    a_steps = (("rows", 2), ("rows", 4), ("blk", 1), ("blk", 2))
    b_steps = (("rows", 4), ("rows", 2), ("blk", 1), ("blk", 2))
    for k, (sa, sb) in enumerate(zip(a_steps, b_steps)):
        if k == 0:
            continue
        if k == 1:
            b[1], t1, t3 = lax.optimization_barrier((b[1], t1, t3))
        if k == 3:
            b[1], t2 = lax.optimization_barrier((b[1], t2))
            tokens_grad = place([t0, t1, t2, t3], f32)
        a, b = keep_half(a, *sa), keep_half(b, *sb)
    a, b = cut(a, 0, a[0].shape[0]), cut(b, 0, b[0].shape[0])
    for k, (sa, sb) in enumerate(zip(a_steps[::-1], b_steps[::-1])):
        if k == 2:
            b, tokens_grad = lax.optimization_barrier((b, tokens_grad))
        a, b = join_half(a, *sa), join_half(b, *sb)
    return (a, b, swap(a, "rows", 1), swap(b, "rows", 1)), tokens_grad


BIG_B = 2 * FF + D
BIG_C = 2 * FF + 6 * D
SMALL_C = 40
SMALL_B = 8


def place_kernel(me_ref, p0, p1, p2, p3, target_ref):
    for m, p in enumerate((p0, p1, p2, p3)):
        target_ref[me_ref[0] ^ m] = p[...].astype(target_ref.dtype)


def kernel_d(
    me_ref,
    own_a,
    own_b,
    other_a,
    other_b,
    sums2_ref,
    ff1_in,
    ff1_out,
    w_q,
    w_k,
    w_v,
    w_o,
    pw1,
    pw2,
    ff2_in,
    ff2_out,
    g_ff1,
    g_att,
    g_conv,
    rel,
    taps,
    g_ff2,
    g_out,
    bn_gain,
    big_ref,
):
    quarter = own_a.shape[0]
    side = me_ref[1]
    for k, (own, other) in enumerate(((own_a, other_a), (own_b, other_b))):
        big_ref[rows_at((2 * side + k) * quarter, quarter, 64), :] = own[...]
        big_ref[rows_at((2 * (1 - side) + k) * quarter, quarter, 64), :] = other[...]
    ff1_out[...] = big_ref[0:FF, :].astype(f32)
    for c in range(FF // D):
        ff1_in[:, c * D : (c + 1) * D] = big_ref[FF + c * D : FF + (c + 1) * D, :].astype(f32)
    base = 2 * FF
    for k, ref in enumerate((w_q, w_k, w_v, w_o)):
        ref[...] = big_ref[base + k * D : base + (k + 1) * D, :].astype(f32)
    base = 2 * FF + 4 * D
    for c in range(2):
        pw1[:, c * D : (c + 1) * D] = big_ref[base + c * D : base + (c + 1) * D, :].astype(f32)
    base = BIG_C
    ff2_out[...] = big_ref[base : base + FF, :].astype(f32)
    for c in range(FF // D):
        at = base + FF + c * D
        ff2_in[:, c * D : (c + 1) * D] = big_ref[at : at + D, :].astype(f32)
    pw2[...] = big_ref[base + 2 * FF : base + 2 * FF + D, :].astype(f32)
    small = big_ref[BIG_C + BIG_B : BIG_C + BIG_B + SMALL_C + SMALL_B, :].astype(f32)
    g_ff1[...], g_att[...], g_conv[...] = small[0:1], small[1:2], small[2:3]
    rel[...] = small[4:8, :NBUCKET]
    taps[...] = small[8 : 8 + KERNEL]
    g_ff2[...], g_out[...] = small[SMALL_C : SMALL_C + 1], small[SMALL_C + 1 : SMALL_C + 2]
    bn_gain[...] = sums2_ref[1:2, :]


def shape_of(shape, dtype):
    return jax.ShapeDtypeStruct(shape, dtype)


def call(body, smem, outs, scratch, name, far_in=(), far_out=(), micros=1, mib=16):
    def place(far, count):
        return [pl.BlockSpec(memory_space=pl.ANY if k in far else pltpu.VMEM) for k in range(count)]

    def run(*operands):
        specs = [pl.BlockSpec(memory_space=pltpu.SMEM)] * smem + place(far_in, len(operands))[smem:]
        return pl.pallas_call(
            body,
            out_shape=outs,
            in_specs=specs,
            out_specs=place(far_out, len(outs)),
            scratch_shapes=scratch,
            compiler_params=pltpu.CompilerParams(vmem_limit_bytes=mib * MIB),
            cost_estimate=pl.CostEstimate(flops=micros * 10**9, bytes_accessed=micros * 10**6, transcendentals=0),
            name=name,
        )(*operands)

    return run


def twice(weight):
    heads = weight.reshape(D, H, HD)
    return jnp.concatenate([heads, heads], axis=2).reshape(D, 2 * D)


def one_side(weight):
    heads = weight.reshape(D, H // 2, 2, HD)
    empty = jnp.zeros_like(heads[:, :, 0])
    even = jnp.concatenate([heads[:, :, 0], empty], axis=2)
    odd = jnp.concatenate([empty, heads[:, :, 1]], axis=2)
    return jnp.stack([even, odd], axis=2).reshape(D, 2 * D)


MIB_A = 23
MIB_B = 29
MIB_C = 20
MIB_E = 34


def packed_rows():
    rows = BIG_C + BIG_B + SMALL_C + SMALL_B
    return -(-rows // 1024) * 1024


def run_a(tiles, *operands):
    length = tiles * QT
    frames = length // 4
    padded_rows = length + 4 * GAP
    n_mixed = len(mixed_offsets(tiles))
    return call(
        functools.partial(kernel_a, tiles),
        2,
        [
            shape_of((length, D), bf16),
            shape_of((8, D), f32),
            shape_of((length, D), f32),
            shape_of((H, length, 128), bf16),
            shape_of((H, length, 128), bf16),
            shape_of((H, length, length), bf16),
            shape_of((H // 2, length, 128), f32),
            shape_of((H // 2, length, 128), f32),
            shape_of((length, D), f32),
            shape_of((2, padded_rows, 128), f32),
            shape_of((length, D), f32),
            shape_of((8, D), f32),
        ],
        [
            pltpu.VMEM((H, length, 128), bf16),
            pltpu.VMEM((length, 128), bf16),
            pltpu.VMEM((length, 128), bf16),
            pltpu.SMEM((1,), jnp.int32),
            pltpu.VMEM((2, length, length), bf16),
            pltpu.VMEM((QT, length), f32),
            pltpu.VMEM((2, length + 6 * GAP, 128), f32),
            pltpu.VMEM((2, padded_rows, 128), f32),
            pltpu.SemaphoreType.DMA((2,)),
        ],
        "first_part",
        far_out=(5,),
        micros=30,
        mib=MIB_A,
    )(*operands)


def run_b(tiles, *operands):
    length = tiles * QT
    frames = length // 4
    padded_rows = length + 4 * GAP
    n_mixed = len(mixed_offsets(tiles))
    return call(
        functools.partial(kernel_b, tiles),
        1,
        [shape_of((frames, D), bf16)] * 4
        + [
            shape_of((length, D), f32),
            shape_of((length, D), f32),
            shape_of((8, D), f32),
            shape_of((BIG_B, D), bf16),
            shape_of((SMALL_B, D), f32),
        ],
        [
            pltpu.VMEM((length, D), bf16),
            pltpu.VMEM((length, D), bf16),
            pltpu.VMEM((D, FF), f32),
            pltpu.VMEM((D, FF), f32),
            pltpu.VMEM((D, D), f32),
        ],
        "middle_part",
        micros=12,
        mib=MIB_B,
    )(*operands)


def run_c(tiles, *operands):
    length = tiles * QT
    padded_rows = length + 4 * GAP
    return call(
        functools.partial(kernel_c, tiles),
        1,
        [
            shape_of((length, D), f32),
            shape_of((H, length, 128), bf16),
            shape_of((D, length), bf16),
            shape_of((D, length), bf16),
            shape_of((D, D), f32),
            shape_of((D, 2 * D), f32),
            shape_of((KERNEL + 1, D), f32),
            shape_of((8, D), f32),
        ],
        [
            pltpu.VMEM((2, length + 6 * GAP, 128), f32),
            pltpu.VMEM((2, padded_rows, 128), f32),
        ],
        "third_part",
        micros=16,
        mib=MIB_C,
    )(*operands)


def run_e(tiles, *operands):
    length = tiles * QT
    frames = length // 4
    n_mixed = len(mixed_offsets(tiles))
    return call(
        functools.partial(kernel_e, tiles),
        1,
        [shape_of((4, frames, D), bf16)] * 2
        + [shape_of((packed_rows() // 4, D), bf16)] * 4,
        [
            pltpu.VMEM((SMALL_C, D), f32),
            pltpu.VMEM((2, length, length), bf16),
            pltpu.VMEM((H // 2, length, 128), f32),
            pltpu.VMEM((D, length), f32),
            pltpu.VMEM((D, length), f32),
            pltpu.VMEM((n_mixed, QT, QT), f32),
            pltpu.VMEM((D, FF), f32),
            pltpu.VMEM((D, FF), f32),
            pltpu.VMEM((D, D), f32),
            pltpu.VMEM((D, D), f32),
            pltpu.VMEM((D, D), f32),
            pltpu.VMEM((length, D), f32),
            pltpu.SemaphoreType.DMA((2,)),
        ],
        "last_part",
        far_in=(5,),
        micros=24,
        mib=MIB_E,
    )(*operands)


def row_device(
    tokens,
    seg_ids,
    frame_mask,
    cotangent,
    g_ff1,
    w_ff1_in,
    w_ff1_out,
    g_att,
    w_query,
    w_key,
    w_value,
    w_output,
    rel_table,
    g_conv,
    w_pw1,
    w_depth,
    bn_gain,
    w_pw2,
    g_ff2,
    w_ff2_in,
    w_ff2_out,
    g_out,
):
    blocks, frames, _ = tokens.shape
    length = blocks * frames
    tiles = length // QT
    n_mixed = len(mixed_offsets(tiles))
    me = lax.axis_index("blk")
    group = lax.axis_index("rows")
    me_ref = jnp.stack([me, group % 2, group // 2 % 2, group // 4 % 2]).astype(jnp.int32)
    gains = [g.reshape(1, D) for g in (g_ff1, g_att, g_conv, bn_gain, g_ff2, g_out)]
    g_ff1, g_att, g_conv, bn_gain, g_ff2, g_out = gains

    found = jnp.stack([seg_ids == 0, seg_ids == 1, frame_mask == 1], axis=1)
    lengths = jnp.sum(found.astype(jnp.int32), axis=2)
    digits = jnp.stack([lengths // 16, lengths % 16], axis=2).reshape(blocks, 6)
    digits = jnp.pad(digits, ((0, 0), (0, EXTRA - digits.shape[1]))).astype(bf16)
    extra = jnp.broadcast_to(digits[:, :, None], (blocks, EXTRA, D))
    token_pieces = to_pieces(jnp.concatenate([tokens, extra], axis=1), me)
    cotangent, token_pieces = lax.optimization_barrier((cotangent, token_pieces))
    cot_pieces = to_pieces(cotangent, me)

    bias = call(
        functools.partial(bias_kernel, tiles), 1, [shape_of((H, n_mixed, QT, QT), f32)], [], "bias_tiles"
    )(rel_table)[0]
    taps = w_depth.astype(f32).reshape(KERNEL, 2, 128).transpose(1, 0, 2)
    taps = jnp.broadcast_to(taps[:, :, None, :], (2, KERNEL, 8, 128))

    (tok, ends, s1, k2, v2, weights, inverse, mixed, s2, gap, depth, sums) = run_a(
        tiles,
        me_ref,
        rel_table,
        *token_pieces,
        bias,
        g_ff1,
        w_ff1_in,
        w_ff1_out,
        g_att,
        twice(w_query),
        twice(w_key),
        one_side(w_value),
        w_output,
        g_conv,
        w_pw1,
        taps,
    )
    sums = sum_everywhere(sums)

    (o0, o1, o2, o3, grad3, bngrad, sums2, big_b, small_b) = run_b(
        tiles, me_ref, *cot_pieces, sums, depth, s2, bn_gain, w_pw2, g_ff2, w_ff2_in, w_ff2_out, g_out
    )
    out_pieces = from_pieces([o0, o1, o2, o3])
    sums2 = sum_everywhere(sums2)

    (grad2, do, dot, qt, dw_o, dw_pw1, taps_grad, row) = run_c(
        tiles,
        me_ref,
        sums,
        sums2,
        ends,
        s1,
        inverse,
        mixed,
        s2,
        gap,
        depth,
        grad3,
        bngrad,
        g_att,
        w_query,
        w_output,
        g_conv,
        w_pw1,
        taps,
        bn_gain,
    )
    (output, token_blocks, *packed) = run_e(
        tiles,
        me_ref,
        tok,
        s1,
        k2,
        v2,
        weights,
        grad2,
        do,
        dot,
        qt,
        dw_o,
        dw_pw1,
        taps_grad,
        row,
        *out_pieces,
        g_ff1,
        w_ff1_in,
        w_ff1_out,
        g_att,
        w_query,
        w_key,
        w_value,
        big_b,
        small_b,
    )

    def place(pieces, dtype):
        return call(place_kernel, 1, [shape_of((blocks, frames, D), dtype)], [], "place", micros=2, mib=8)(me_ref, *pieces)[0]

    reduced, tokens_grad = reduce_gradients(packed[:2], packed[2:], token_blocks, me, me_ref, place)
    (ff1_in, ff1_out, w_q, w_k, w_v, w_o, pw1, pw2, ff2_in, ff2_out, *small) = call(
        kernel_d,
        1,
        [
            shape_of((D, FF), f32),
            shape_of((FF, D), f32),
            shape_of((D, D), f32),
            shape_of((D, D), f32),
            shape_of((D, D), f32),
            shape_of((D, D), f32),
            shape_of((D, 2 * D), f32),
            shape_of((D, D), f32),
            shape_of((D, FF), f32),
            shape_of((FF, D), f32),
            *[shape_of((1, D), f32)] * 3,
            shape_of((H, NBUCKET), f32),
            shape_of((KERNEL, D), f32),
            *[shape_of((1, D), f32)] * 3,
        ],
        [pltpu.VMEM((packed_rows(), D), bf16)],
        "unpack",
        micros=5,
        mib=13,
    )(me_ref, *reduced, sums2)
    d_g_ff1, d_g_att, d_g_conv, rel, d_taps, d_g_ff2, d_g_out, d_bn_gain = small
    return (
        output,
        tokens_grad,
        d_g_ff1.reshape(D),
        ff1_in,
        ff1_out,
        d_g_att.reshape(D),
        w_q,
        w_k,
        w_v,
        w_o,
        rel,
        d_g_conv.reshape(D),
        pw1,
        d_taps,
        d_bn_gain.reshape(D),
        pw2,
        d_g_ff2.reshape(D),
        ff2_in,
        ff2_out,
        d_g_out.reshape(D),
    )


def padded(x, sides, width):
    for axis, dim in sides:
        size, length = (lax.axis_size(axis), x.shape[dim])
        up = [(i, (i + 1) % size) for i in range(size - 1)]
        down = [(j, i) for i, j in up]
        last = lax.slice_in_dim(x, length - width, length, axis=dim)
        first = lax.slice_in_dim(x, 0, width, axis=dim)
        before = lax.ppermute(last, axis, up)
        after = lax.ppermute(first, axis, down)
        x = jnp.concatenate([before, x, after], axis=dim)
    return x


def norm_forward(values, norm_gain):
    center = jnp.mean(values, axis=-1, keepdims=True)
    shifted = values - center
    spread = jnp.mean(shifted * shifted, axis=-1, keepdims=True)
    inverse = lax.rsqrt(spread + epsilon)
    scaled = shifted * inverse
    return (scaled * norm_gain, (scaled, inverse))


def norm_backward(upstream, norm_gain, stored):
    scaled, inverse = stored
    gain_grad = jnp.sum(upstream * scaled, axis=(0, 1))
    inner_grad = upstream * norm_gain
    inner_mean = jnp.mean(inner_grad, axis=-1, keepdims=True)
    inner_dot = jnp.mean(inner_grad * scaled, axis=-1, keepdims=True)
    return (inverse * (inner_grad - inner_mean - scaled * inner_dot), gain_grad)


def project(left_side, weight):
    return jnp.einsum("rfd,de->rfe", left_side, weight, preferred_element_type=jnp.float32)


def project_back(upstream, weight):
    return jnp.einsum("rfe,de->rfd", upstream, weight, preferred_element_type=jnp.float32)


def weight_product(left_side, upstream):
    return jnp.einsum("rfd,rfe->de", left_side, upstream, preferred_element_type=jnp.float32)


def silu_slope(values):
    logistic = jax.nn.sigmoid(values)
    return logistic * (1.0 + values * (1.0 - logistic))


def ffn_forward(values, norm_gain, weight_in, weight_out):
    normed, norm_stored = norm_forward(values, norm_gain)
    normed_low = normed.astype(jnp.bfloat16)
    hidden = project(normed_low, weight_in)
    act_low = jax.nn.silu(hidden).astype(jnp.bfloat16)
    return (project(act_low, weight_out), (norm_stored, normed_low, hidden, act_low))


def ffn_backward(stream_grad, norm_gain, weight_in, weight_out, stored):
    norm_stored, normed_low, hidden, act_low = stored
    out_low = (0.5 * stream_grad).astype(jnp.bfloat16)
    out_weight_grad = weight_product(act_low, out_low)
    hidden_low = (project_back(out_low, weight_out) * silu_slope(hidden)).astype(jnp.bfloat16)
    in_weight_grad = weight_product(normed_low, hidden_low)
    input_grad, gain_grad = norm_backward(
        project_back(hidden_low, weight_in), norm_gain, norm_stored
    )
    return (stream_grad + input_grad, (gain_grad, in_weight_grad, out_weight_grad))


def bucket_bias(query_pos, key_pos, rel_table):
    distance = key_pos[None, :] - query_pos[:, None]
    levels = NBUCKET // 2
    magnitude = jnp.abs(distance)
    bucket = levels * (distance > 0).astype(jnp.int32)
    for exponent in range(levels - 1):
        bucket = bucket + (magnitude >= 4**exponent).astype(jnp.int32)
    onehot = (bucket[:, :, None] == jnp.arange(NBUCKET, dtype=jnp.int32)[None, None, :]).astype(
        jnp.float32
    )
    position_bias = jnp.einsum("qkb,hb->hqk", onehot, rel_table, precision=lax.Precision.HIGHEST)
    return (position_bias, onehot)


def block_at(source, block_index, query_heads, segment_float, query_pos, rel_table):
    key_all, value_all, code_all = source
    row_count, frames = segment_float.shape
    key_start = block_index * frames
    key_block = lax.dynamic_slice_in_dim(key_all, key_start, frames, 1).reshape(
        row_count, frames, H, HD
    )
    value_block = lax.dynamic_slice_in_dim(value_all, key_start, frames, 1).reshape(
        row_count, frames, H, HD
    )
    code_block = lax.dynamic_slice_in_dim(code_all, key_start, frames, 1)
    key_pos = key_start + jnp.arange(frames, dtype=jnp.int32)
    position_bias, onehot = bucket_bias(query_pos, key_pos, rel_table)
    raw_scores = (
        jnp.einsum("rqhd,rkhd->rhqk", query_heads, key_block, preferred_element_type=jnp.float32)
        * HD ** (-0.5)
        + position_bias[None]
    )
    allowed = (segment_float[:, :, None] == code_block.astype(jnp.float32)[:, None, :])[:, None]
    return (jnp.where(allowed, raw_scores, masked_score), allowed, onehot, key_block, value_block)


def attend_forward(
    values, segment, code_low, norm_gain, w_query, w_key, w_value, w_output, rel_table
):
    row_count, frames, model_width = values.shape
    normed, norm_stored = norm_forward(values, norm_gain)
    normed_low = normed.astype(jnp.bfloat16)
    query_low = project(normed_low, w_query).astype(jnp.bfloat16)
    key_low = project(normed_low, w_key).astype(jnp.bfloat16)
    value_low = project(normed_low, w_value).astype(jnp.bfloat16)
    gathered = (
        lax.all_gather(key_low, "blk", axis=1, tiled=True),
        lax.all_gather(value_low, "blk", axis=1, tiled=True),
        lax.all_gather(code_low, "blk", axis=1, tiled=True),
    )
    segment_float = segment.astype(jnp.float32)
    query_pos = lax.axis_index("blk") * frames + jnp.arange(frames, dtype=jnp.int32)
    query_heads = query_low.reshape(row_count, frames, H, HD)
    blocks = lax.axis_size("blk")

    def max_step(block_index, loop_state):
        running_max, running_sum = loop_state
        scores, allowed, onehot, key_block, value_block = block_at(
            gathered, block_index, query_heads, segment_float, query_pos, rel_table
        )
        new_max = jnp.maximum(running_max, jnp.max(scores, axis=-1))
        kept_exp = jnp.where(allowed, jnp.exp(scores - new_max[..., None]), 0.0)
        return (new_max, running_sum * jnp.exp(running_max - new_max) + jnp.sum(kept_exp, axis=-1))

    start_max = jnp.full((row_count, H, frames), masked_score, jnp.float32)
    running_max, running_sum = lax.fori_loop(
        0, blocks, max_step, (start_max, jnp.zeros_like(start_max))
    )
    log_total = running_max + jnp.log(running_sum)

    def mix_step(block_index, mixed_sum):
        scores, allowed, onehot, key_block, value_block = block_at(
            gathered, block_index, query_heads, segment_float, query_pos, rel_table
        )
        attn_low = jnp.where(allowed, jnp.exp(scores - log_total[..., None]), 0.0).astype(
            jnp.bfloat16
        )
        return mixed_sum + jnp.einsum(
            "rhqk,rkhd->rqhd", attn_low, value_block, preferred_element_type=jnp.float32
        )

    mixed_heads = lax.fori_loop(
        0, blocks, mix_step, jnp.zeros((row_count, frames, H, HD), jnp.float32)
    )
    mixed_heads = mixed_heads.reshape(row_count, frames, model_width)
    mixed_low = mixed_heads.astype(jnp.bfloat16)
    stored = (
        norm_stored,
        normed_low,
        query_heads,
        key_low,
        value_low,
        code_low,
        gathered,
        log_total,
        mixed_heads,
        mixed_low,
        segment_float,
        query_pos,
    )
    return (project(mixed_low, w_output), stored)


def attend_backward(stream_grad, norm_gain, w_query, w_key, w_value, w_output, rel_table, stored):
    (
        norm_stored,
        normed_low,
        query_heads,
        key_low,
        value_low,
        code_low,
        gathered,
        log_total,
        mixed_heads,
        mixed_low,
        segment_float,
        query_pos,
    ) = stored
    row_count, frames, model_width = stream_grad.shape
    grad_low = stream_grad.astype(jnp.bfloat16)
    w_output_grad = weight_product(mixed_low, grad_low)
    mixed_grad = (
        project_back(grad_low, w_output).astype(jnp.bfloat16).reshape(row_count, frames, H, HD)
    )
    row_delta = jnp.einsum(
        "rqhd,rqhd->rhq",
        mixed_grad.astype(jnp.float32),
        mixed_heads.reshape(row_count, frames, H, HD),
    )
    source = (
        lax.all_gather(key_low, "blk", axis=1, tiled=True),
        lax.all_gather(value_low, "blk", axis=1, tiled=True),
        lax.all_gather(code_low, "blk", axis=1, tiled=True),
    )
    blocks = lax.axis_size("blk")
    scale = HD ** (-0.5)

    def score_grads(block_index):
        scores, allowed, onehot, key_block, value_block = block_at(
            source, block_index, query_heads, segment_float, query_pos, rel_table
        )
        attn_weights = jnp.where(allowed, jnp.exp(scores - log_total[..., None]), 0.0)
        weight_grad = jnp.einsum(
            "rqhd,rkhd->rhqk", mixed_grad, value_block, preferred_element_type=jnp.float32
        )
        score_low = (attn_weights * (weight_grad - row_delta[..., None])).astype(jnp.bfloat16)
        return (attn_weights, score_low, onehot, key_block)

    def grad_step(block_index, loop_state):
        query_grad, key_buffer, value_buffer, table_grad = loop_state
        attn_weights, score_low, onehot, key_block = score_grads(block_index)
        attn_low = attn_weights.astype(jnp.bfloat16)
        query_grad = query_grad + jnp.einsum(
            "rhqk,rkhd->rqhd", score_low, key_block, preferred_element_type=jnp.float32
        )
        key_part = (
            jnp.einsum(
                "rhqk,rqhd->rkhd", score_low, query_heads, preferred_element_type=jnp.float32
            )
            * scale
        )
        value_part = jnp.einsum(
            "rhqk,rqhd->rkhd", attn_low, mixed_grad, preferred_element_type=jnp.float32
        )
        key_start = block_index * frames
        key_buffer = lax.dynamic_update_slice_in_dim(
            key_buffer, key_part.reshape(row_count, frames, model_width), key_start, 1
        )
        value_buffer = lax.dynamic_update_slice_in_dim(
            value_buffer, value_part.reshape(row_count, frames, model_width), key_start, 1
        )
        table_grad = table_grad + jnp.einsum(
            "hqk,qkb->hb",
            jnp.sum(score_low.astype(jnp.float32), axis=0),
            onehot,
            precision=lax.Precision.HIGHEST,
        )
        return (query_grad, key_buffer, value_buffer, table_grad)

    empty_buffer = jnp.zeros((row_count, blocks * frames, model_width), jnp.float32)
    start_state = (
        jnp.zeros((row_count, frames, H, HD), jnp.float32),
        empty_buffer,
        empty_buffer,
        jnp.zeros((H, NBUCKET), jnp.float32),
    )
    query_grad, key_buffer, value_buffer, table_grad = lax.fori_loop(
        0, blocks, grad_step, start_state
    )
    key_total, value_total = (
        lax.psum_scatter(
            key_buffer.astype(jnp.bfloat16), "blk", scatter_dimension=1, tiled=True
        ).astype(jnp.float32),
        lax.psum_scatter(
            value_buffer.astype(jnp.bfloat16), "blk", scatter_dimension=1, tiled=True
        ).astype(jnp.float32),
    )
    query_grad_low = (
        (query_grad * scale).reshape(row_count, frames, model_width).astype(jnp.bfloat16)
    )
    key_grad_low = key_total.astype(jnp.bfloat16)
    value_grad_low = value_total.astype(jnp.bfloat16)
    w_query_grad = weight_product(normed_low, query_grad_low)
    w_key_grad = weight_product(normed_low, key_grad_low)
    w_value_grad = weight_product(normed_low, value_grad_low)
    normed_grad = (
        project_back(query_grad_low, w_query)
        + project_back(key_grad_low, w_key)
        + project_back(value_grad_low, w_value)
    )
    input_grad, gain_grad = norm_backward(normed_grad, norm_gain, norm_stored)
    return (
        stream_grad + input_grad,
        (gain_grad, w_query_grad, w_key_grad, w_value_grad, w_output_grad, table_grad),
    )


def conv_forward(values, segment, live_mask, norm_gain, w_pw1, w_depth, bn_gain, w_pw2):
    row_count, frames, model_width = values.shape
    normed, norm_stored = norm_forward(values, norm_gain)
    normed_low = normed.astype(jnp.bfloat16)
    gate_pair = project(normed_low, w_pw1)
    first_half = gate_pair[..., :model_width]
    logistic = jax.nn.sigmoid(gate_pair[..., model_width:])
    live_frames = live_mask.astype(jnp.float32)[..., None]
    gated_low = (first_half * logistic * live_frames).astype(jnp.bfloat16)
    wide_units, wide_segment = (
        padded(gated_low, (("blk", 1),), KERNEL // 2),
        padded(segment.astype(jnp.bfloat16), (("blk", 1),), KERNEL // 2),
    )
    segment_float = segment.astype(jnp.float32)
    depth_sum = jnp.zeros((row_count, frames, model_width), jnp.float32)
    for kernel_tap in range(KERNEL):
        same_segment = (
            wide_segment[:, kernel_tap : kernel_tap + frames].astype(jnp.float32) == segment_float
        ).astype(jnp.float32)
        depth_sum = (
            depth_sum
            + w_depth[kernel_tap].astype(jnp.float32)
            * wide_units[:, kernel_tap : kernel_tap + frames].astype(jnp.float32)
            * same_segment[..., None]
        )
    norm_totals = lax.psum(
        (
            jnp.sum(depth_sum * live_frames, axis=(0, 1)),
            jnp.sum(depth_sum * depth_sum * live_frames, axis=(0, 1)),
            jnp.sum(live_frames),
        ),
        ("blk", "rows"),
    )
    frame_count = norm_totals[2]
    center = norm_totals[0] / frame_count
    spread = norm_totals[1] / frame_count - center * center
    inverse = lax.rsqrt(spread + epsilon)
    standard = (depth_sum - center) * inverse
    pre_act = standard * bn_gain
    act_low = jax.nn.silu(pre_act).astype(jnp.bfloat16)
    stored = (
        norm_stored,
        normed_low,
        first_half,
        logistic,
        live_frames,
        wide_units,
        wide_segment,
        frame_count,
        inverse,
        standard,
        pre_act,
        act_low,
    )
    return (project(act_low, w_pw2), stored)


def conv_backward(stream_grad, segment, norm_gain, w_pw1, w_depth, bn_gain, w_pw2, stored):
    (
        norm_stored,
        normed_low,
        first_half,
        logistic,
        live_frames,
        wide_units,
        wide_segment,
        frame_count,
        inverse,
        standard,
        pre_act,
        act_low,
    ) = stored
    row_count, frames, model_width = stream_grad.shape
    grad_low = stream_grad.astype(jnp.bfloat16)
    w_pw2_grad = weight_product(act_low, grad_low)
    act_grad = project_back(grad_low, w_pw2) * silu_slope(pre_act)
    hat_grad = act_grad * bn_gain
    grad_sums = lax.psum(
        (jnp.sum(hat_grad, axis=(0, 1)), jnp.sum(act_grad * standard, axis=(0, 1))), ("blk", "rows")
    )
    hat_total, bn_gain_grad = grad_sums
    frame_share = live_frames / frame_count
    depth_low = (
        inverse
        * (hat_grad - frame_share * hat_total - frame_share * standard * bn_gain * bn_gain_grad)
    ).astype(jnp.bfloat16)
    wide_grad = padded(depth_low, (("blk", 1),), KERNEL // 2)
    segment_float = segment.astype(jnp.float32)
    depth_float = depth_low.astype(jnp.float32)
    unit_grad = jnp.zeros((row_count, frames, model_width), jnp.float32)
    tap_grads = []
    for kernel_tap in range(KERNEL):
        forward_same = (
            wide_segment[:, kernel_tap : kernel_tap + frames].astype(jnp.float32) == segment_float
        ).astype(jnp.float32)[..., None]
        tap_grads.append(
            jnp.sum(
                depth_float
                * wide_units[:, kernel_tap : kernel_tap + frames].astype(jnp.float32)
                * forward_same,
                axis=(0, 1),
            )
        )
        mirror = KERNEL - 1 - kernel_tap
        backward_same = (
            wide_segment[:, mirror : mirror + frames].astype(jnp.float32) == segment_float
        ).astype(jnp.float32)[..., None]
        unit_grad = (
            unit_grad
            + w_depth[kernel_tap].astype(jnp.float32)
            * wide_grad[:, mirror : mirror + frames].astype(jnp.float32)
            * backward_same
        )
    unit_grad = unit_grad * live_frames
    pair_low = jnp.concatenate(
        [unit_grad * logistic, unit_grad * first_half * logistic * (1.0 - logistic)], axis=-1
    ).astype(jnp.bfloat16)
    w_pw1_grad = weight_product(normed_low, pair_low)
    input_grad, gain_grad = norm_backward(project_back(pair_low, w_pw1), norm_gain, norm_stored)
    return (
        stream_grad + input_grad,
        (gain_grad, w_pw1_grad, jnp.stack(tap_grads), bn_gain_grad, w_pw2_grad),
    )


def per_device(
    tokens,
    seg_ids,
    frame_mask,
    cotangent,
    g_ff1,
    w_ff1_in,
    w_ff1_out,
    g_att,
    w_query,
    w_key,
    w_value,
    w_output,
    rel_table,
    g_conv,
    w_pw1,
    w_depth,
    bn_gain,
    w_pw2,
    g_ff2,
    w_ff2_in,
    w_ff2_out,
    g_out,
):
    start_stream = tokens.astype(jnp.float32)
    ffn_one, ffn_one_stored = ffn_forward(start_stream, g_ff1, w_ff1_in, w_ff1_out)
    after_ffn = start_stream + 0.5 * ffn_one
    code_low = jnp.where(frame_mask == 1, seg_ids, -1).astype(jnp.bfloat16)
    attended, attend_stored = attend_forward(
        after_ffn, seg_ids, code_low, g_att, w_query, w_key, w_value, w_output, rel_table
    )
    after_att = after_ffn + attended
    conv_out, conv_stored = conv_forward(
        after_att, seg_ids, frame_mask, g_conv, w_pw1, w_depth, bn_gain, w_pw2
    )
    after_conv = after_att + conv_out
    ffn_two, ffn_two_stored = ffn_forward(after_conv, g_ff2, w_ff2_in, w_ff2_out)
    after_two = after_conv + 0.5 * ffn_two
    final_norm, final_stored = norm_forward(after_two, g_out)
    stream_grad, g_out_grad = norm_backward(cotangent.astype(jnp.float32), g_out, final_stored)
    stream_grad, ffn_two_grads = ffn_backward(
        stream_grad, g_ff2, w_ff2_in, w_ff2_out, ffn_two_stored
    )
    stream_grad, conv_grads = conv_backward(
        stream_grad, seg_ids, g_conv, w_pw1, w_depth, bn_gain, w_pw2, conv_stored
    )
    stream_grad, attend_grads = attend_backward(
        stream_grad, g_att, w_query, w_key, w_value, w_output, rel_table, attend_stored
    )
    stream_grad, ffn_one_grads = ffn_backward(
        stream_grad, g_ff1, w_ff1_in, w_ff1_out, ffn_one_stored
    )
    summed = lax.psum(
        (
            ffn_one_grads[0],
            ffn_one_grads[1],
            ffn_one_grads[2],
            attend_grads[0],
            attend_grads[1],
            attend_grads[2],
            attend_grads[3],
            attend_grads[4],
            attend_grads[5],
            conv_grads[0],
            conv_grads[1],
            conv_grads[2],
            conv_grads[4],
            ffn_two_grads[0],
            ffn_two_grads[1],
            ffn_two_grads[2],
            g_out_grad,
        ),
        ("blk", "rows"),
    )
    return (
        final_norm.astype(jnp.bfloat16),
        stream_grad,
        summed[0],
        summed[1],
        summed[2],
        summed[3],
        summed[4],
        summed[5],
        summed[6],
        summed[7],
        summed[8],
        summed[9],
        summed[10],
        summed[11],
        conv_grads[3],
        summed[12],
        summed[13],
        summed[14],
        summed[15],
        summed[16],
    )


def solution(mesh):
    blocks, groups = mesh.shape["blk"], mesh.shape["rows"]

    def device(tokens, *rest):
        rows, frames, _ = tokens.shape
        whole_rows = rows == blocks == 4 and groups == 8 and (rows * frames) % QT == 0
        return (row_device if whole_rows else per_device)(tokens, *rest)

    return jax.shard_map(
        device,
        mesh=mesh,
        in_specs=(
            P("rows", "blk", None),
            P("rows", "blk"),
            P("rows", "blk"),
            P("rows", "blk", None),
        )
        + (P(),) * 18,
        out_specs=(P("rows", "blk", None),) * 2 + (P(),) * 18,
        check_vma=False,
    )
```

```python
import functools
import math

import jax
import jax.numpy as jnp
from jax import lax
from jax.experimental import pallas as pl
from jax.experimental.pallas import tpu as pltpu
from jax.sharding import PartitionSpec as P

H = 4
HD = 64
D = 256
FF = 1024
KERNEL = 31
HALF = KERNEL // 2
NBUCKET = 16

epsilon = 1e-05
masked_score = -1e30

f32 = jnp.float32
bf16 = jnp.bfloat16
LOG2E = math.log2(math.e)
QT = 256
GAP = 16
EXTRA = 16
SAFE_EXPONENT = 60.0
MIB = 1024 * 1024


def mm(a, b):
    return lax.dot_general(a, b, (((1,), (0,)), ((), ())), preferred_element_type=f32)


def mm_nt(a, b):
    return lax.dot_general(a, b, (((1,), (1,)), ((), ())), preferred_element_type=f32)


def turned(x):
    return x.astype(f32).T.astype(bf16)


def sigmoid(x):
    return 0.5 + 0.5 * jnp.tanh(0.5 * x)


def norm_hat(v):
    center = jnp.mean(v, axis=-1, keepdims=True)
    shifted = v - center
    spread = jnp.mean(shifted * shifted, axis=-1, keepdims=True)
    inverse = lax.rsqrt(spread + epsilon)
    return shifted * inverse, inverse


def norm_back(upstream, gain, hat, inverse):
    inner = upstream * gain
    inner_mean = jnp.mean(inner, axis=-1, keepdims=True)
    inner_dot = jnp.mean(inner * hat, axis=-1, keepdims=True)
    return inverse * (inner - inner_mean - hat * inner_dot)


def col_sum(x):
    rows, width = x.shape
    return jnp.sum(x.reshape(rows // 8, 8, width), axis=0)


def bucket_ranges():
    levels = NBUCKET // 2
    big = 1 << 30
    edges = [0] + [4**k for k in range(levels - 1)] + [big]
    out = []
    for level in range(levels - 1, 0, -1):
        out.append((level, 1 - edges[level + 1], -edges[level]))
    out.append((0, 0, 0))
    for level in range(1, levels):
        out.append((levels + level, edges[level], edges[level + 1] - 1))
    return out


def tile_buckets(offset):
    low, high = offset * QT - (QT - 1), offset * QT + (QT - 1)
    return [(b, lo) for b, lo, hi in bucket_ranges() if lo <= high and hi >= low]


def mixed_offsets(tiles):
    return [o for o in range(1 - tiles, tiles) if len(tile_buckets(o)) > 1]


def tile_distance(offset):
    row = lax.broadcasted_iota(jnp.int32, (QT, QT), 0)
    col = lax.broadcasted_iota(jnp.int32, (QT, QT), 1)
    return col - row + offset * QT


def frame_index(start, rows, width):
    return (lax.broadcasted_iota(jnp.int32, (rows, width), 0) + start).astype(f32)


def rows_at(start, count, unit):
    return pl.ds(pl.multiple_of(start, unit), count)


def bias_kernel(tiles, table_ref, bias_ref):
    def head(h, carry):
        for k, offset in enumerate(mixed_offsets(tiles)):
            d = tile_distance(offset)
            found = tile_buckets(offset)
            value = jnp.full((QT, QT), table_ref[h, found[0][0]], f32)
            for b, lo in found[1:]:
                value = jnp.where(d >= lo, table_ref[h, b], value)
            bias_ref[h, k] = value * LOG2E
        return carry

    lax.fori_loop(0, H, head, 0)


def place_pieces(me_ref, piece_refs, target_ref, frames):
    for m, piece in enumerate(piece_refs):
        start = (me_ref[0] ^ m) * frames
        target_ref[rows_at(start, frames, 64), :] = piece[0:frames, :]


def take_pieces(me_ref, source_ref, piece_refs, frames):
    for m, piece in enumerate(piece_refs):
        start = (me_ref[0] ^ m) * frames
        piece[...] = source_ref[rows_at(start, frames, 64), :].astype(piece.dtype)


def key_features(start, rows, ends):
    first_end, second_end, live_end = (e[:, :128] for e in ends)
    t = frame_index(start, rows, 128)
    lane = lax.broadcasted_iota(jnp.int32, (rows, 128), 1)
    code = jnp.where(t < first_end, 0, jnp.where(t < second_end, 1, 2))
    code = jnp.where(t < live_end, code, -1)
    barred = jnp.where((lane < 3) & (code != lane), masked_score, 0.0)
    return jnp.where((lane >= 3) & (lane < 6), 1.0, barred).astype(bf16)


def query_features(start, rows, ends):
    first_end, second_end, live_end = (e[:, :128] for e in ends)
    t = frame_index(start, rows, 128)
    lane = lax.broadcasted_iota(jnp.int32, (rows, 128), 1)
    code = jnp.where(t < first_end, 0, jnp.where(t < second_end, 1, 2))
    return jnp.where(code == lane, 1.0, 0.0)


def three_parts(x):
    top = x.astype(bf16).astype(f32)
    middle = (x - top).astype(bf16).astype(f32)
    return top, middle, x - top - middle


def spread_gaps(plain_ref, gap_ref, length, ends):
    first_end, second_end, _ = (e[:, :128] for e in ends)
    total = length + 4 * GAP
    step = GAP * 4

    def chunk(k, carry):
        start = k * step
        g = frame_index(start, step, 128)
        for c in range(2):
            a = plain_ref[c, rows_at(start + 2 * GAP, step, 16), :]
            b = plain_ref[c, rows_at(start + GAP, step, 16), :]
            d = plain_ref[c, rows_at(start, step, 16), :]
            in_first = (g >= GAP) & (g - GAP < first_end)
            in_second = (g - 2 * GAP >= first_end) & (g - 2 * GAP < second_end)
            in_third = (g - 3 * GAP >= second_end) & (g - 3 * GAP < length)
            value = jnp.where(in_first, a, jnp.where(in_second, b, jnp.where(in_third, d, 0.0)))
            gap_ref[c, rows_at(start, step, 16), :] = value
        return carry

    lax.fori_loop(0, total // step, chunk, 0)


def close_gaps(gap_ref, start, rows, ends):
    first_end, second_end, _ = (e[:, :128] for e in ends)
    t = frame_index(start, rows, 128)
    halves = []
    for c in range(2):
        a = gap_ref[c, rows_at(start + GAP, rows, 16), :]
        b = gap_ref[c, rows_at(start + 2 * GAP, rows, 16), :]
        d = gap_ref[c, rows_at(start + 3 * GAP, rows, 16), :]
        halves.append(jnp.where(t < first_end, a, jnp.where(t < second_end, b, d)))
    return jnp.concatenate(halves, axis=1)


CONV_ROWS = 32
BACK_ROWS = 32


def tapped(part, tap):
    rows = part.shape[0]
    return (part.reshape(rows // 8, 8, 128) * tap[None]).reshape(rows, 128)


def shifted_parts(ref, c, start, rows):
    for r in range(8):
        window = ref[c, pl.ds(start - 16 + r, rows + 24), :]
        for q in range(4):
            shift = 8 * q + r - 16
            if abs(shift) <= HALF:
                yield shift, window[8 * q : 8 * q + rows]


def convolve(gap_ref, out_ref, taps_ref, length):
    span = length + 2 * GAP

    for c in range(2):

        def chunk(k, carry, c=c):
            start = GAP + k * CONV_ROWS
            total = jnp.zeros((CONV_ROWS, 128), f32)
            for shift, part in shifted_parts(gap_ref, c, start, CONV_ROWS):
                total = total + tapped(part, taps_ref[c, shift + HALF])
            out_ref[c, rows_at(start, CONV_ROWS, 16), :] = total
            return carry

        lax.fori_loop(0, span // CONV_ROWS, chunk, 0, unroll=2)


def convolve_back(dgap_ref, gap_ref, out_ref, taps_ref, taps_grad_ref, length):
    span = length + 2 * GAP
    for c in range(2):

        def chunk(k, carry, c=c):
            start = GAP + k * BACK_ROWS
            units = gap_ref[c, rows_at(start, BACK_ROWS, 16), :]
            total = jnp.zeros((BACK_ROWS, 128), f32)
            sums = list(carry)
            for shift, part in shifted_parts(dgap_ref, c, start, BACK_ROWS):
                j = HALF - shift
                total = total + tapped(part, taps_ref[c, j])
                sums[j] = sums[j] + col_sum(part * units)
            out_ref[c, rows_at(start, BACK_ROWS, 16), :] = total
            return tuple(sums)

        sums = lax.fori_loop(0, span // BACK_ROWS, chunk, tuple(jnp.zeros((8, 128), f32) for _ in range(KERNEL)), unroll=2)
        for j in range(KERNEL):
            taps_grad_ref[j : j + 1, 128 * c : 128 * c + 128] = jnp.sum(sums[j], axis=0, keepdims=True)
    taps_grad_ref[KERNEL : KERNEL + 1, :] = jnp.zeros((1, 2 * 128), f32)


def add_to(ref, first, value):
    ref[...] = value if first else ref[...] + value


def read_ends(ends_ref):
    return ends_ref[0:1, :], ends_ref[1:2, :], ends_ref[2:3, :]


GATE = 1280


def front_frames(tokens, weights, targets, at):
    g_ff1_ref, w_in_ref, w_out_ref, g_att_ref, wq2_ref, wk2_ref, wv2_ref = weights
    s1_ref, q2_ref, k2_ref, v2_ref = targets
    x = tokens.astype(f32)
    hat, _ = norm_hat(x)
    n1 = (hat * g_ff1_ref[...]).astype(bf16)
    hidden = mm(n1, w_in_ref[...])
    act = (hidden * sigmoid(hidden)).astype(bf16)
    s1 = x + 0.5 * mm(act, w_out_ref[...])
    s1_ref[at, :] = s1
    hat, _ = norm_hat(s1)
    n2 = (hat * g_att_ref[...]).astype(bf16)
    lane = lax.broadcasted_iota(jnp.int32, (x.shape[0], 128), 1)
    q_all = mm(n2, wq2_ref[...]).astype(bf16).astype(f32) * (LOG2E * HD**-0.5)
    k_all = mm(n2, wk2_ref[...]).astype(bf16)
    v_all = mm(n2, wv2_ref[...])
    q_top, k_top = jnp.float32(0.0), jnp.float32(0.0)
    for h in range(H):
        cols = slice(128 * h, 128 * h + 128)
        q = q_all[:, cols]
        high = q.astype(bf16)
        low = (q - high.astype(f32)).astype(bf16)
        q2_ref[h, at, :] = jnp.where(lane < HD, high.astype(f32), low.astype(f32)).astype(bf16)
        k2_ref[h, at, :] = k_all[:, cols]
        ones = (lane >= HD) & (lane < HD + 3) if h % 2 == 0 else lane < 3
        v2_ref[h, at, :] = jnp.where(ones, 1.0, v_all[:, cols]).astype(bf16)
        q_top = jnp.maximum(q_top, jnp.max(jnp.sum(q * q, axis=1, keepdims=True)))
        k = k_all[:, cols].astype(f32)
        k_top = jnp.maximum(k_top, jnp.max(jnp.sum(k * k, axis=1, keepdims=True)))
    return q_top, k_top


def front_kernel(
    me_ref,
    piece0,
    piece1,
    g_ff1_ref,
    w_in_ref,
    w_out_ref,
    g_att_ref,
    wq2_ref,
    wk2_ref,
    wv2_ref,
    s1_ref,
    q2_ref,
    k2_ref,
    v2_ref,
    tops_ref,
    tok_ref,
):
    frames = tok_ref.shape[0] // 2
    for m, piece in enumerate((piece0, piece1)):
        tok_ref[rows_at(((me_ref[0] & 1) ^ m) * frames, frames, 64), :] = piece[0:frames, :]
    weights = (g_ff1_ref, w_in_ref, w_out_ref, g_att_ref, wq2_ref, wk2_ref, wv2_ref)
    tops = front_frames(tok_ref[...], weights, (s1_ref, q2_ref, k2_ref, v2_ref), slice(0, 2 * frames))
    tops_ref[0:1, :] = jnp.full((1, 128), tops[0])
    tops_ref[1:2, :] = jnp.full((1, 128), tops[1])
    tops_ref[2:8, :] = jnp.zeros((6, 128), f32)


def attend_tile(q2_ref, fq_ref, h, qt, k2_ref, fk_ref, bias_ref, table_ref, tiles):
    rows = slice(qt * QT, (qt + 1) * QT)
    qa = jnp.concatenate([q2_ref[h, rows, :], fq_ref[rows, :]], axis=1)
    ka = jnp.concatenate([k2_ref[h], fk_ref[...]], axis=1)
    offsets = mixed_offsets(tiles)
    s_all = mm_nt(qa, ka)
    parts = []
    for kt in range(tiles):
        s = s_all[:, kt * QT : (kt + 1) * QT]
        o = kt - qt
        if o in offsets:
            s = s + bias_ref[h, offsets.index(o)]
        else:
            s = s + table_ref[h, tile_buckets(o)[0][0]] * LOG2E
        parts.append(jnp.exp2(s).astype(bf16))
    return jnp.concatenate(parts, axis=1)


def attend_tile_below_max(q2_ref, fq_ref, h, rows, start, k2_ref, fk_ref, table_ref, s_ref, tiles):
    qa = jnp.concatenate([q2_ref[h, rows, :], fq_ref[rows, :]], axis=1)
    ka = jnp.concatenate([k2_ref[h], fk_ref[...]], axis=1)
    s_ref[...] = mm_nt(qa, ka)
    ranges = bucket_ranges()

    def add_bias(kt, top):
        cols = rows_at(kt * QT, QT, QT)
        d = tile_distance(0) + (kt * QT - start)
        value = jnp.full((QT, QT), table_ref[h, ranges[0][0]], f32)
        for b, low, _ in ranges[1:]:
            value = jnp.where(d >= low, table_ref[h, b], value)
        s = s_ref[:, cols] + value * LOG2E
        s_ref[:, cols] = s
        return jnp.maximum(top, jnp.max(s, axis=1, keepdims=True))

    top = lax.fori_loop(0, tiles, add_bias, jnp.full((QT, 1), -jnp.inf, f32))
    return jnp.exp2(s_ref[...] - top).astype(bf16)


def kernel_a(
    tiles,
    me_ref,
    table_ref,
    piece0,
    piece1,
    piece2,
    piece3,
    s1_near,
    q2_near,
    k2_near,
    v2_near,
    tops_near,
    bias_ref,
    g_ff1_ref,
    w_in_ref,
    w_out_ref,
    g_att_ref,
    wq2_ref,
    wk2_ref,
    wv2_ref,
    w_o_ref,
    g_conv_ref,
    w_pw1_ref,
    taps_ref,
    tok_ref,
    ends_ref,
    s1_ref,
    k2_ref,
    v2_ref,
    weights_ref,
    inverse_ref,
    mixed_ref,
    s2_ref,
    gap_ref,
    depth_ref,
    sums_ref,
    q2_ref,
    fq_ref,
    fk_ref,
    fast_ref,
    p_ref,
    s_ref,
    plain_ref,
    conv_ref,
    moved,
):
    pieces = (piece0, piece1, piece2, piece3)
    length = tiles * QT
    frames = length // len(pieces)
    place_pieces(me_ref, pieces, tok_ref, frames)
    extra = sum(p[frames : frames + EXTRA, :].astype(f32) for p in pieces)
    first_end = 16.0 * extra[0:1, :] + extra[1:2, :]
    second_end = first_end + 16.0 * extra[2:3, :] + extra[3:4, :]
    live_end = 16.0 * extra[4:5, :] + extra[5:6, :]
    ends_ref[0:1, :] = first_end
    ends_ref[1:2, :] = second_end
    ends_ref[2:3, :] = live_end
    ends_ref[3:8, :] = jnp.zeros((5, D), f32)
    ends = (first_end, second_end, live_end)

    near, far = rows_at((me_ref[0] >> 1) * 2 * frames, 2 * frames, 64), rows_at((1 - (me_ref[0] >> 1)) * 2 * frames, 2 * frames, 64)
    s1_ref[near, :] = s1_near[...]
    for h in range(H):
        q2_ref[h, near, :], k2_ref[h, near, :], v2_ref[h, near, :] = q2_near[h], k2_near[h], v2_near[h]
    weights = (g_ff1_ref, w_in_ref, w_out_ref, g_att_ref, wq2_ref, wk2_ref, wv2_ref)
    q_top, k_top = front_frames(tok_ref[far, :], weights, (s1_ref, q2_ref, k2_ref, v2_ref), far)
    q_top = jnp.maximum(q_top, jnp.max(tops_near[0:1, :]))
    k_top = jnp.maximum(k_top, jnp.max(tops_near[1:2, :]))
    for i in range(2):
        at = slice(i * 2 * frames, (i + 1) * 2 * frames)
        fq_ref[at, :] = query_features(i * 2 * frames, 2 * frames, ends).astype(bf16)
        fk_ref[at, :] = key_features(i * 2 * frames, 2 * frames, ends)
    fast_ref[0] = jnp.where(q_top * k_top < 4.0 * SAFE_EXPONENT**2, 1, 0)

    def weights_copy(h, slot):
        return pltpu.make_async_copy(p_ref.at[slot], weights_ref.at[h], moved.at[slot])

    def room(h, slot):
        @pl.when(h > 1)
        def _():
            weights_copy(h - 2, slot).wait()

    def mix(h, slot, rows, p):
        p_ref[slot, rows, :] = p
        total = mm(p, v2_ref[h])
        lane = lax.broadcasted_iota(jnp.int32, (QT, 128), 1)
        first = slot == 0
        denominator = jnp.where(first, total[:, HD : HD + 1], total[:, 0:1])
        inverse = jnp.broadcast_to(1.0 / denominator, (QT, 128))
        mixed = total * inverse
        g = lax.div(h, 2)
        new = jnp.logical_or(first, lane >= HD)
        mixed_ref[g, rows, :] = jnp.where(new, mixed, mixed_ref[g, rows, :])
        inverse_ref[g, rows, :] = jnp.where(new, inverse, inverse_ref[g, rows, :])

    @pl.when(fast_ref[0] == 1)
    def _():
        def head(h, carry):
            slot = lax.rem(h, 2)
            room(h, slot)
            for qt in range(tiles):
                p = attend_tile(q2_ref, fq_ref, h, qt, k2_ref, fk_ref, bias_ref, table_ref, tiles)
                mix(h, slot, slice(qt * QT, (qt + 1) * QT), p)
            weights_copy(h, slot).start()
            return carry

        lax.fori_loop(0, H, head, 0)

    @pl.when(fast_ref[0] != 1)
    def _():
        def head(h, carry):
            slot = lax.rem(h, 2)
            room(h, slot)

            def tile(qt, carry):
                rows = rows_at(qt * QT, QT, QT)
                p = attend_tile_below_max(
                    q2_ref, fq_ref, h, rows, qt * QT, k2_ref, fk_ref, table_ref, s_ref, tiles
                )
                mix(h, slot, rows, p)
                return carry

            lax.fori_loop(0, tiles, tile, 0)
            weights_copy(h, slot).start()
            return carry

        lax.fori_loop(0, H, head, 0)

    def gate(i):
        at = slice(i * GATE, (i + 1) * GATE)
        mixed = jnp.concatenate([mixed_ref[0, at, :], mixed_ref[1, at, :]], axis=1)
        s2 = s1_ref[at, :] + mm(mixed.astype(bf16), w_o_ref[...])
        s2_ref[at, :] = s2
        hat, _ = norm_hat(s2)
        n3 = (hat * g_conv_ref[...]).astype(bf16)
        pair = mm(n3, w_pw1_ref[...])
        live = frame_index(i * GATE, GATE, D) < live_end
        units = jnp.where(live, pair[:, :D] * sigmoid(pair[:, D:]), 0.0).astype(bf16).astype(f32)
        put = slice(i * GATE + 3 * GAP, (i + 1) * GATE + 3 * GAP)
        plain_ref[0, put, :] = units[:, :128]
        plain_ref[1, put, :] = units[:, 128:]

    for i in range(length // GATE):
        gate(i)
    spread_gaps(plain_ref, gap_ref, length, ends)
    convolve(gap_ref, conv_ref, taps_ref, length)

    def collect(i, carry):
        total, squares = carry
        at = rows_at(i * QT, QT, QT)
        depth = close_gaps(conv_ref, i * QT, QT, ends)
        depth_ref[at, :] = depth
        kept = jnp.where(frame_index(i * QT, QT, D) < live_end, depth, 0.0)
        return total + col_sum(kept), squares + col_sum(kept * kept)

    empty = jnp.zeros((8, D), f32)
    total, squares = lax.fori_loop(0, tiles, collect, (empty, empty))
    sums_ref[0:1, :] = jnp.sum(total, axis=0, keepdims=True)
    sums_ref[1:2, :] = jnp.sum(squares, axis=0, keepdims=True)
    sums_ref[2:3, :] = live_end
    sums_ref[3:8, :] = jnp.zeros((5, D), f32)
    for parity in range(2):
        weights_copy(H - 2 + parity, parity).wait()


MIDDLE = 1280


def batch_norm_terms(sums_ref):
    count = sums_ref[2:3, :]
    center = sums_ref[0:1, :] / count
    spread = sums_ref[1:2, :] / count - center * center
    return count, center, lax.rsqrt(spread + epsilon)


def kernel_b(
    tiles,
    me_ref,
    cot0,
    cot1,
    cot2,
    cot3,
    sums_ref,
    depth_ref,
    s2_ref,
    bn_gain_ref,
    w_pw2_ref,
    g_ff2_ref,
    w_in_ref,
    w_out_ref,
    g_out_ref,
    out0,
    out1,
    out2,
    out3,
    grad3_ref,
    bngrad_ref,
    sums2_ref,
    big_ref,
    small_ref,
    cot_ref,
    out_ref,
    dw_in_ref,
    dw_out_ref,
    dw_pw2_ref,
):
    length = tiles * QT
    frames = length // 4
    place_pieces(me_ref, (cot0, cot1, cot2, cot3), cot_ref, frames)
    _, center, inverse = batch_norm_terms(sums_ref)
    bn_gain = bn_gain_ref[...]

    def step(i, carry):
        g_out_sum, g_ff2_sum, bn_sum, bn_dot = carry
        at = slice(i * MIDDLE, (i + 1) * MIDDLE)
        standard = (depth_ref[at, :] - center) * inverse
        pre = standard * bn_gain
        logistic3 = sigmoid(pre)
        act3 = (pre * logistic3).astype(bf16)
        s3 = s2_ref[at, :] + mm(act3, w_pw2_ref[...])
        hat3, inv3 = norm_hat(s3)
        n4 = (hat3 * g_ff2_ref[...]).astype(bf16)
        hidden = mm(n4, w_in_ref[...])
        logistic = sigmoid(hidden)
        act4 = (hidden * logistic).astype(bf16)
        s4 = s3 + 0.5 * mm(act4, w_out_ref[...])
        hat4, inv4 = norm_hat(s4)
        out_ref[at, :] = (hat4 * g_out_ref[...]).astype(bf16)
        cot = cot_ref[at, :].astype(f32)
        g_out_sum = g_out_sum + col_sum(cot * hat4)
        grad4 = norm_back(cot, g_out_ref[...], hat4, inv4)
        out4 = (0.5 * grad4).astype(bf16)
        add_to(dw_out_ref, i == 0, mm(turned(out4), act4))
        slope = logistic * (1.0 + hidden * (1.0 - logistic))
        hid4 = (mm_nt(out4, w_out_ref[...]) * slope).astype(bf16)
        add_to(dw_in_ref, i == 0, mm(turned(n4), hid4))
        up = mm_nt(hid4, w_in_ref[...])
        g_ff2_sum = g_ff2_sum + col_sum(up * hat3)
        grad3 = grad4 + norm_back(up, g_ff2_ref[...], hat3, inv3)
        grad3_ref[at, :] = grad3
        out3 = grad3.astype(bf16)
        add_to(dw_pw2_ref, i == 0, mm(turned(act3), out3))
        bngrad = mm_nt(out3, w_pw2_ref[...]) * (logistic3 * (1.0 + pre * (1.0 - logistic3)))
        bngrad_ref[at, :] = bngrad
        return g_out_sum, g_ff2_sum, bn_sum + col_sum(bngrad), bn_dot + col_sum(bngrad * standard)

    empty = jnp.zeros((8, D), f32)
    sums = (empty,) * 4
    for i in range(length // MIDDLE):
        sums = step(i, sums)
    g_out_sum, g_ff2_sum, bn_sum, bn_dot = (jnp.sum(s, axis=0, keepdims=True) for s in sums)
    sums2_ref[0:1, :] = bn_sum
    sums2_ref[1:2, :] = bn_dot
    sums2_ref[2:8, :] = jnp.zeros((6, D), f32)
    small_ref[0:1, :] = g_ff2_sum
    small_ref[1:2, :] = g_out_sum
    small_ref[2:8, :] = jnp.zeros((6, D), f32)
    big_ref[0:FF, :] = turned_wide(dw_out_ref)
    for c in range(FF // D):
        big_ref[FF + c * D : FF + (c + 1) * D, :] = dw_in_ref[:, c * D : (c + 1) * D].astype(big_ref.dtype)
    big_ref[2 * FF : 2 * FF + D, :] = dw_pw2_ref[...].astype(big_ref.dtype)
    take_pieces(me_ref, out_ref, (out0, out1, out2, out3), frames)


def turned_wide(ref):
    return jnp.concatenate([ref[:, c * D : (c + 1) * D].T for c in range(ref.shape[1] // D)], axis=0).astype(bf16)


BACK = 640
LAST = 256


def kernel_c(
    tiles,
    me_ref,
    sums_ref,
    sums2_ref,
    ends_ref,
    s1_ref,
    inverse_ref,
    mixed_ref,
    s2_ref,
    gap_ref,
    depth_ref,
    grad3_ref,
    bngrad_ref,
    g_att_ref,
    w_q_ref,
    w_o_ref,
    g_conv_ref,
    w_pw1_ref,
    taps_ref,
    bn_gain_ref,
    grad_ref,
    do_ref,
    dot_ref,
    qt_ref,
    dw_o_ref,
    dw_pw1_ref,
    taps_grad_ref,
    row_ref,
    plain_ref,
    dgap_ref,
):
    length = tiles * QT
    ends = read_ends(ends_ref)
    live_end = ends[2]
    count, center, inverse = batch_norm_terms(sums_ref)
    bn_gain = bn_gain_ref[...]
    e_total = sums2_ref[0:1, :] * bn_gain
    dot_total = sums2_ref[1:2, :]


    def batch_back(i, carry):
        at = rows_at(i * QT, QT, QT)
        standard = (depth_ref[at, :] - center) * inverse
        e = bngrad_ref[at, :] * bn_gain
        share = jnp.where(frame_index(i * QT, QT, D) < live_end, 1.0, 0.0) / count
        dg = inverse * (e - share * e_total - share * standard * bn_gain * dot_total)
        dg = dg.astype(bf16).astype(f32)
        put = rows_at(i * QT + 3 * GAP, QT, 16)
        plain_ref[0, put, :] = dg[:, :128]
        plain_ref[1, put, :] = dg[:, 128:]
        return carry

    lax.fori_loop(0, tiles, batch_back, 0)
    spread_gaps(plain_ref, dgap_ref, length, ends)
    convolve_back(dgap_ref, gap_ref, plain_ref, taps_ref, taps_grad_ref, length)

    def gate_back(i, g_conv_sum):
        at = slice(i * BACK, (i + 1) * BACK)
        hat, inv = norm_hat(s2_ref[at, :])
        n3 = (hat * g_conv_ref[...]).astype(bf16)
        pair = mm(n3, w_pw1_ref[...])
        first, logistic = pair[:, :D], sigmoid(pair[:, D:])
        live = frame_index(i * BACK, BACK, D) < live_end
        ug = jnp.where(live, close_gaps(plain_ref, i * BACK, BACK, ends), 0.0) * logistic
        pairgrad = jnp.concatenate([ug, ug * first * (1.0 - logistic)], axis=1).astype(bf16)
        add_to(dw_pw1_ref, i == 0, mm(turned(n3), pairgrad))
        up = mm_nt(pairgrad, w_pw1_ref[...])
        g_conv_sum = g_conv_sum + col_sum(up * hat)
        grad2 = grad3_ref[at, :] + norm_back(up, g_conv_ref[...], hat, inv)
        grad_ref[at, :] = grad2
        out2 = grad2.astype(bf16)
        mixed = jnp.concatenate([mixed_ref[0, at, :], mixed_ref[1, at, :]], axis=1)
        add_to(dw_o_ref, i == 0, mm(turned(mixed), out2))
        mixgrad = mm_nt(out2, w_o_ref[...]).astype(bf16).astype(f32)
        mixgrad = (mixgrad * jnp.concatenate([inverse_ref[0, at, :], inverse_ref[1, at, :]], axis=1)).astype(bf16)
        dot_ref[:, at] = turned(mixgrad)
        product = mixgrad.astype(f32) * mixed
        lane = lax.broadcasted_iota(jnp.int32, (BACK, 128), 1)
        for h in range(H):
            cols = slice(128 * (h // 2), 128 * (h // 2) + 128)
            own = lane < HD if h % 2 == 0 else lane >= HD
            delta = jnp.sum(jnp.where(own, product[:, cols], 0.0), axis=1, keepdims=True)
            high, middle, low = three_parts(-delta)
            base = HD if h % 2 == 0 else 0
            side = jnp.where(lane == base, high, 0.0)
            side = jnp.where(lane == base + 1, middle, side)
            side = jnp.where(lane == base + 2, low, side)
            do_ref[h, at, :] = jnp.where(own, mixgrad[:, cols].astype(f32), side).astype(bf16)
        hat, _ = norm_hat(s1_ref[at, :])
        n2 = (hat * g_att_ref[...]).astype(bf16)
        qt_ref[:, at] = turned(mm(n2, w_q_ref[...]).astype(bf16))
        return g_conv_sum

    empty = jnp.zeros((8, D), f32)
    g_conv_sum = empty
    for i in range(length // BACK):
        g_conv_sum = gate_back(i, g_conv_sum)
    row_ref[0:1, :] = jnp.sum(g_conv_sum, axis=0, keepdims=True)
    row_ref[1:8, :] = jnp.zeros((7, D), f32)


def kernel_e(
    tiles,
    me_ref,
    tok_ref,
    s1_ref,
    k2_ref,
    v2_ref,
    weights_ref,
    grad_ref,
    do_ref,
    dot_ref,
    qt_ref,
    dw_o_ref,
    dw_pw1_ref,
    taps_grad_ref,
    row_ref,
    out0,
    out1,
    out2,
    out3,
    g_ff1_ref,
    w_ff1_in_ref,
    w_ff1_out_ref,
    g_att_ref,
    w_q_ref,
    w_k_ref,
    w_v_ref,
    big_b_ref,
    small_b_ref,
    output_ref,
    blocks_ref,
    kept_a,
    kept_b,
    sent_a,
    sent_b,
    small_ref,
    p_ref,
    dq_ref,
    dkt_ref,
    dvt_ref,
    acc_ref,
    dw_in_ref,
    dw_out_ref,
    dw_q_ref,
    dw_k_ref,
    dw_v_ref,
    last_ref,
    arrived,
):
    length = tiles * QT
    frames = length // 4

    def weights_copy(h, slot):
        return pltpu.make_async_copy(weights_ref.at[h], p_ref.at[slot], arrived.at[slot])

    weights_copy(0, 0).start()
    for m, piece in enumerate((out0, out1, out2, out3)):
        output_ref[me_ref[0] ^ m] = piece[...]
    empty = jnp.zeros((8, D), f32)


    offsets = mixed_offsets(tiles)

    def head(h, carry):
        slot = lax.rem(h, 2)

        @pl.when(h + 1 < H)
        def _():
            weights_copy(h + 1, 1 - slot).start()

        weights_copy(h, slot).wait()
        flat = {}
        started = set()
        own = rows_at(h * HD, HD, HD)
        dvt_ref[own, :] = mm(dot_ref[own, :], p_ref[slot])
        pair = lax.div(h, 2)
        for qt in range(tiles):
            rows = slice(qt * QT, (qt + 1) * QT)
            d_all = mm_nt(do_ref[h, rows, :], v2_ref[h])
            low = []
            for kt in range(tiles):
                cols = slice(kt * QT, (kt + 1) * QT)
                ds = p_ref[slot, rows, cols].astype(f32) * d_all[:, cols]
                o = kt - qt
                if o in offsets:
                    k = offsets.index(o)
                    acc_ref[k] = acc_ref[k] + ds if k in started else ds
                    started.add(k)
                else:
                    b = tile_buckets(o)[0][0]
                    flat[b] = flat[b] + col_sum(ds) if b in flat else col_sum(ds)
                low.append(ds.astype(bf16))
            low = jnp.concatenate(low, axis=1)
            p_ref[slot, rows, :] = low
            dq = mm(low, k2_ref[h])
            own_half = (lax.broadcasted_iota(jnp.int32, (QT, 128), 1) < HD) == (slot == 0)
            dq_ref[pair, rows, :] = jnp.where(own_half, dq, dq_ref[pair, rows, :])
        dkt_ref[own, :] = mm(qt_ref[own, :], p_ref[slot])
        table_row = jnp.zeros((1, D), f32)
        lane = lax.broadcasted_iota(jnp.int32, (1, D), 1)
        for k, o in enumerate(offsets):
            d = tile_distance(o)
            value = acc_ref[k]
            found = tile_buckets(o)
            tails = [col_sum(jnp.where(d >= lo, value, 0.0)) for _, lo in found[1:]]
            tails = [col_sum(value)] + tails
            for n, (b, _) in enumerate(found):
                part = tails[n] - tails[n + 1] if n + 1 < len(found) else tails[n]
                flat[b] = flat[b] + part if b in flat else part
        for b, part in flat.items():
            table_row = jnp.where(lane == b, jnp.sum(part), table_row)
        small_ref[pl.ds(h + 4, 1), :] = table_row
        return carry

    small_ref[...] = jnp.zeros_like(small_ref)
    lax.fori_loop(0, H, head, 0)


    def front_back(i, carry):
        g_att_sum, g_ff1_sum = carry
        at = slice(i * LAST, (i + 1) * LAST)
        dq = jnp.concatenate([dq_ref[g, at, :] for g in range(H // 2)], axis=1)
        dq = (dq * HD**-0.5).astype(bf16)
        dk = (dkt_ref[:, at] * HD**-0.5).T.astype(bf16)
        dv = dvt_ref[:, at].T.astype(bf16)
        s1 = s1_ref[at, :]
        hat2, inv2 = norm_hat(s1)
        n2 = turned((hat2 * g_att_ref[...]).astype(bf16))
        add_to(dw_q_ref, i == 0, mm(n2, dq))
        add_to(dw_k_ref, i == 0, mm(n2, dk))
        add_to(dw_v_ref, i == 0, mm(n2, dv))
        attgrad = mm_nt(dq, w_q_ref[...]) + mm_nt(dk, w_k_ref[...]) + mm_nt(dv, w_v_ref[...])
        g_att_sum = g_att_sum + col_sum(attgrad * hat2)
        grad1 = grad_ref[at, :] + norm_back(attgrad, g_att_ref[...], hat2, inv2)
        out1 = (0.5 * grad1).astype(bf16)
        x = tok_ref[at, :].astype(f32)
        hat1, inv1 = norm_hat(x)
        n1 = (hat1 * g_ff1_ref[...]).astype(bf16)
        hidden = mm(n1, w_ff1_in_ref[...])
        logistic = sigmoid(hidden)
        act1 = (hidden * logistic).astype(bf16)
        add_to(dw_out_ref, i == 0, mm(turned(out1), act1))
        slope = logistic * (1.0 + hidden * (1.0 - logistic))
        hid1 = (mm_nt(out1, w_ff1_out_ref[...]) * slope).astype(bf16)
        add_to(dw_in_ref, i == 0, mm(turned(n1), hid1))
        up = mm_nt(hid1, w_ff1_in_ref[...])
        g_ff1_sum = g_ff1_sum + col_sum(up * hat1)
        last_ref[at, :] = grad1 + norm_back(up, g_ff1_ref[...], hat1, inv1)
        return g_att_sum, g_ff1_sum

    g_att_sum, g_ff1_sum = empty, empty
    for i in range(length // LAST):
        g_att_sum, g_ff1_sum = front_back(i, (g_att_sum, g_ff1_sum))
    for k, s in enumerate((g_ff1_sum, g_att_sum)):
        small_ref[k : k + 1, :] = jnp.sum(s, axis=0, keepdims=True)
    small_ref[2:3, :] = row_ref[0:1, :]
    small_ref[8 : 8 + KERNEL + 1, :] = taps_grad_ref[...]
    for b in range(length // frames):
        blocks_ref[b] = last_ref[b * frames : (b + 1) * frames, :].astype(bf16)
    quarter = kept_a.shape[0]

    def put(start, value):
        side, first = start // (2 * quarter), start // quarter % 2 == 0
        at = slice(start % quarter, start % quarter + value.shape[0])

        @pl.when(me_ref[1] == side)
        def _():
            (kept_a if first else kept_b)[at, :] = value

        @pl.when(me_ref[1] != side)
        def _():
            (sent_a if first else sent_b)[at, :] = value

    for c in range(FF // D):
        put(c * D, dw_out_ref[:, c * D : (c + 1) * D].T.astype(bf16))
        put(FF + c * D, dw_in_ref[:, c * D : (c + 1) * D].astype(bf16))
    for k, ref in enumerate((dw_q_ref, dw_k_ref, dw_v_ref, dw_o_ref)):
        put(2 * FF + k * D, ref[...].astype(bf16))
    for c in range(2):
        put(2 * FF + (4 + c) * D, dw_pw1_ref[:, c * D : (c + 1) * D].astype(bf16))
    for c in range(BIG_B // D):
        put(BIG_C + c * D, big_b_ref[c * D : (c + 1) * D, :])
    rest = 4 * quarter - BIG_C - BIG_B - SMALL_C - SMALL_B
    small = [small_ref[...], small_b_ref[...], jnp.zeros((rest, D), f32)]
    put(BIG_C + BIG_B, jnp.concatenate(small, axis=0).astype(bf16))


def swap(x, axis, bit):
    size = lax.axis_size(axis)
    return lax.ppermute(x, axis, [(i, i ^ bit) for i in range(size)])


def doubling_steps():
    steps = []
    for axis in ("rows", "blk"):
        size = lax.axis_size(axis)
        bit = 1
        while bit < size:
            steps.append((axis, bit))
            bit *= 2
    return steps


def sum_everywhere(x):
    for axis, bit in doubling_steps():
        x = x + swap(x, axis, bit)
    return x


def to_pieces(x, me):
    own = lax.dynamic_index_in_dim(x, me, 0, keepdims=False)
    pieces = [own]
    for m in range(1, x.shape[0]):
        pieces.append(swap(lax.dynamic_index_in_dim(x, me ^ m, 0, keepdims=False), "blk", m))
    return pieces


def from_pieces(pieces):
    return [pieces[0]] + [swap(p, "blk", m) for m, p in enumerate(pieces) if m > 0]


def cut(terms, start, rows):
    return sum(lax.dynamic_slice_in_dim(t, start, rows, 0).astype(f32) for t in terms).astype(bf16)


def keep_half(terms, axis, bit):
    half = terms[0].shape[0] // 2
    side = (lax.axis_index(axis) // bit) % 2
    got = swap(cut(terms, (1 - side) * half, half), axis, bit)
    return [cut(terms, side * half, half), got]


def join_half(x, axis, bit):
    side = (lax.axis_index(axis) // bit) % 2
    got = swap(x, axis, bit)
    return jnp.where(side == 0, jnp.concatenate([x, got]), jnp.concatenate([got, x]))


def halve_kernel(me_ref, kept_a, kept_b, got_a, got_b, send_a, send_b, keep_a, keep_b):
    half = send_a.shape[0]
    parts = ((kept_a, got_a, send_a, keep_a, me_ref[2]), (kept_b, got_b, send_b, keep_b, me_ref[3]))
    for kept, got, send, keep, side in parts:
        for target, place in ((send, 1 - side), (keep, side)):
            at = rows_at(place * half, half, 64)
            target[...] = (kept[at, :].astype(f32) + got[at, :].astype(f32)).astype(bf16)


def reduce_gradients(kept, sent, token_blocks, me, me_ref, place):
    got_a, got_b = (swap(s, "rows", 1) for s in sent)
    t0, t1, t2, t3 = to_pieces(token_blocks, me)
    rows = kept[0].shape[0] // 2
    send_a, send_b, keep_a, keep_b = call(
        halve_kernel, 1, [shape_of((rows, D), bf16)] * 4, [], "halves", micros=1, mib=8
    )(me_ref, *kept, got_a, got_b)
    a, b = [keep_a, swap(send_a, "rows", 2)], [keep_b, swap(send_b, "rows", 4)]
    a_steps = (("rows", 2), ("rows", 4), ("blk", 1), ("blk", 2))
    b_steps = (("rows", 4), ("rows", 2), ("blk", 1), ("blk", 2))
    for k, (sa, sb) in enumerate(zip(a_steps, b_steps)):
        if k == 0:
            continue
        if k == 1:
            b[1], t1, t3 = lax.optimization_barrier((b[1], t1, t3))
        if k == 3:
            b[1], t2 = lax.optimization_barrier((b[1], t2))
            tokens_grad = place([t0, t1, t2, t3], f32)
        a, b = keep_half(a, *sa), keep_half(b, *sb)
    a, b = cut(a, 0, a[0].shape[0]), cut(b, 0, b[0].shape[0])
    for k, (sa, sb) in enumerate(zip(a_steps[::-1], b_steps[::-1])):
        if k == 2:
            b, tokens_grad = lax.optimization_barrier((b, tokens_grad))
        a, b = join_half(a, *sa), join_half(b, *sb)
    return (a, b, swap(a, "rows", 1), swap(b, "rows", 1)), tokens_grad


BIG_B = 2 * FF + D
BIG_C = 2 * FF + 6 * D
SMALL_C = 40
SMALL_B = 8


def place_kernel(me_ref, p0, p1, p2, p3, target_ref):
    for m, p in enumerate((p0, p1, p2, p3)):
        target_ref[me_ref[0] ^ m] = p[...].astype(target_ref.dtype)


def kernel_d(
    me_ref,
    own_a,
    own_b,
    other_a,
    other_b,
    sums2_ref,
    ff1_in,
    ff1_out,
    w_q,
    w_k,
    w_v,
    w_o,
    pw1,
    pw2,
    ff2_in,
    ff2_out,
    g_ff1,
    g_att,
    g_conv,
    rel,
    taps,
    g_ff2,
    g_out,
    bn_gain,
    big_ref,
):
    quarter = own_a.shape[0]
    side = me_ref[1]
    for k, (own, other) in enumerate(((own_a, other_a), (own_b, other_b))):
        big_ref[rows_at((2 * side + k) * quarter, quarter, 64), :] = own[...]
        big_ref[rows_at((2 * (1 - side) + k) * quarter, quarter, 64), :] = other[...]
    ff1_out[...] = big_ref[0:FF, :].astype(f32)
    for c in range(FF // D):
        ff1_in[:, c * D : (c + 1) * D] = big_ref[FF + c * D : FF + (c + 1) * D, :].astype(f32)
    base = 2 * FF
    for k, ref in enumerate((w_q, w_k, w_v, w_o)):
        ref[...] = big_ref[base + k * D : base + (k + 1) * D, :].astype(f32)
    base = 2 * FF + 4 * D
    for c in range(2):
        pw1[:, c * D : (c + 1) * D] = big_ref[base + c * D : base + (c + 1) * D, :].astype(f32)
    base = BIG_C
    ff2_out[...] = big_ref[base : base + FF, :].astype(f32)
    for c in range(FF // D):
        at = base + FF + c * D
        ff2_in[:, c * D : (c + 1) * D] = big_ref[at : at + D, :].astype(f32)
    pw2[...] = big_ref[base + 2 * FF : base + 2 * FF + D, :].astype(f32)
    small = big_ref[BIG_C + BIG_B : BIG_C + BIG_B + SMALL_C + SMALL_B, :].astype(f32)
    g_ff1[...], g_att[...], g_conv[...] = small[0:1], small[1:2], small[2:3]
    rel[...] = small[4:8, :NBUCKET]
    taps[...] = small[8 : 8 + KERNEL]
    g_ff2[...], g_out[...] = small[SMALL_C : SMALL_C + 1], small[SMALL_C + 1 : SMALL_C + 2]
    bn_gain[...] = sums2_ref[1:2, :]


def shape_of(shape, dtype):
    return jax.ShapeDtypeStruct(shape, dtype)


def call(body, smem, outs, scratch, name, far_in=(), far_out=(), micros=1, mib=16):
    def place(far, count):
        return [pl.BlockSpec(memory_space=pl.ANY if k in far else pltpu.VMEM) for k in range(count)]

    def run(*operands):
        specs = [pl.BlockSpec(memory_space=pltpu.SMEM)] * smem + place(far_in, len(operands))[smem:]
        return pl.pallas_call(
            body,
            out_shape=outs,
            in_specs=specs,
            out_specs=place(far_out, len(outs)),
            scratch_shapes=scratch,
            compiler_params=pltpu.CompilerParams(vmem_limit_bytes=mib * MIB),
            cost_estimate=pl.CostEstimate(flops=micros * 10**9, bytes_accessed=micros * 10**6, transcendentals=0),
            name=name,
        )(*operands)

    return run


def twice(weight):
    heads = weight.reshape(D, H, HD)
    return jnp.concatenate([heads, heads], axis=2).reshape(D, 2 * D)


def one_side(weight):
    heads = weight.reshape(D, H // 2, 2, HD)
    empty = jnp.zeros_like(heads[:, :, 0])
    even = jnp.concatenate([heads[:, :, 0], empty], axis=2)
    odd = jnp.concatenate([empty, heads[:, :, 1]], axis=2)
    return jnp.stack([even, odd], axis=2).reshape(D, 2 * D)


MIB_A = 24
MIB_B = 29
MIB_C = 20
MIB_E = 34


def packed_rows():
    rows = BIG_C + BIG_B + SMALL_C + SMALL_B
    return -(-rows // 1024) * 1024


def run_a(tiles, *operands):
    length = tiles * QT
    frames = length // 4
    padded_rows = length + 4 * GAP
    n_mixed = len(mixed_offsets(tiles))
    return call(
        functools.partial(kernel_a, tiles),
        2,
        [
            shape_of((length, D), bf16),
            shape_of((8, D), f32),
            shape_of((length, D), f32),
            shape_of((H, length, 128), bf16),
            shape_of((H, length, 128), bf16),
            shape_of((H, length, length), bf16),
            shape_of((H // 2, length, 128), f32),
            shape_of((H // 2, length, 128), f32),
            shape_of((length, D), f32),
            shape_of((2, padded_rows, 128), f32),
            shape_of((length, D), f32),
            shape_of((8, D), f32),
        ],
        [
            pltpu.VMEM((H, length, 128), bf16),
            pltpu.VMEM((length, 128), bf16),
            pltpu.VMEM((length, 128), bf16),
            pltpu.SMEM((1,), jnp.int32),
            pltpu.VMEM((2, length, length), bf16),
            pltpu.VMEM((QT, length), f32),
            pltpu.VMEM((2, length + 6 * GAP, 128), f32),
            pltpu.VMEM((2, padded_rows, 128), f32),
            pltpu.SemaphoreType.DMA((2,)),
        ],
        "first_part",
        far_out=(5,),
        micros=30,
        mib=MIB_A,
    )(*operands)


def run_b(tiles, *operands):
    length = tiles * QT
    frames = length // 4
    padded_rows = length + 4 * GAP
    n_mixed = len(mixed_offsets(tiles))
    return call(
        functools.partial(kernel_b, tiles),
        1,
        [shape_of((frames, D), bf16)] * 4
        + [
            shape_of((length, D), f32),
            shape_of((length, D), f32),
            shape_of((8, D), f32),
            shape_of((BIG_B, D), bf16),
            shape_of((SMALL_B, D), f32),
        ],
        [
            pltpu.VMEM((length, D), bf16),
            pltpu.VMEM((length, D), bf16),
            pltpu.VMEM((D, FF), f32),
            pltpu.VMEM((D, FF), f32),
            pltpu.VMEM((D, D), f32),
        ],
        "middle_part",
        micros=12,
        mib=MIB_B,
    )(*operands)


def run_c(tiles, *operands):
    length = tiles * QT
    padded_rows = length + 4 * GAP
    return call(
        functools.partial(kernel_c, tiles),
        1,
        [
            shape_of((length, D), f32),
            shape_of((H, length, 128), bf16),
            shape_of((D, length), bf16),
            shape_of((D, length), bf16),
            shape_of((D, D), f32),
            shape_of((D, 2 * D), f32),
            shape_of((KERNEL + 1, D), f32),
            shape_of((8, D), f32),
        ],
        [
            pltpu.VMEM((2, length + 6 * GAP, 128), f32),
            pltpu.VMEM((2, padded_rows, 128), f32),
        ],
        "third_part",
        micros=16,
        mib=MIB_C,
    )(*operands)


def run_e(tiles, *operands):
    length = tiles * QT
    frames = length // 4
    n_mixed = len(mixed_offsets(tiles))
    return call(
        functools.partial(kernel_e, tiles),
        1,
        [shape_of((4, frames, D), bf16)] * 2
        + [shape_of((packed_rows() // 4, D), bf16)] * 4,
        [
            pltpu.VMEM((SMALL_C, D), f32),
            pltpu.VMEM((2, length, length), bf16),
            pltpu.VMEM((H // 2, length, 128), f32),
            pltpu.VMEM((D, length), f32),
            pltpu.VMEM((D, length), f32),
            pltpu.VMEM((n_mixed, QT, QT), f32),
            pltpu.VMEM((D, FF), f32),
            pltpu.VMEM((D, FF), f32),
            pltpu.VMEM((D, D), f32),
            pltpu.VMEM((D, D), f32),
            pltpu.VMEM((D, D), f32),
            pltpu.VMEM((length, D), f32),
            pltpu.SemaphoreType.DMA((2,)),
        ],
        "last_part",
        far_in=(5,),
        micros=24,
        mib=MIB_E,
    )(*operands)


def row_device(
    tokens,
    seg_ids,
    frame_mask,
    cotangent,
    g_ff1,
    w_ff1_in,
    w_ff1_out,
    g_att,
    w_query,
    w_key,
    w_value,
    w_output,
    rel_table,
    g_conv,
    w_pw1,
    w_depth,
    bn_gain,
    w_pw2,
    g_ff2,
    w_ff2_in,
    w_ff2_out,
    g_out,
):
    blocks, frames, _ = tokens.shape
    length = blocks * frames
    tiles = length // QT
    n_mixed = len(mixed_offsets(tiles))
    me = lax.axis_index("blk")
    group = lax.axis_index("rows")
    me_ref = jnp.stack([me, group % 2, group // 2 % 2, group // 4 % 2]).astype(jnp.int32)
    gains = [g.reshape(1, D) for g in (g_ff1, g_att, g_conv, bn_gain, g_ff2, g_out)]
    g_ff1, g_att, g_conv, bn_gain, g_ff2, g_out = gains

    found = jnp.stack([seg_ids == 0, seg_ids == 1, frame_mask == 1], axis=1)
    lengths = jnp.sum(found.astype(jnp.int32), axis=2)
    digits = jnp.stack([lengths // 16, lengths % 16], axis=2).reshape(blocks, 6)
    digits = jnp.pad(digits, ((0, 0), (0, EXTRA - digits.shape[1]))).astype(bf16)
    extra = jnp.broadcast_to(digits[:, :, None], (blocks, EXTRA, D))
    token_pieces = to_pieces(jnp.concatenate([tokens, extra], axis=1), me)
    bias = call(
        functools.partial(bias_kernel, tiles), 1, [shape_of((H, n_mixed, QT, QT), f32)], [], "bias_tiles"
    )(rel_table)[0]
    taps = w_depth.astype(f32).reshape(KERNEL, 2, 128).transpose(1, 0, 2)
    taps = jnp.broadcast_to(taps[:, :, None, :], (2, KERNEL, 8, 128))

    projections = (twice(w_query), twice(w_key), one_side(w_value))
    *near, = call(
        front_kernel,
        1,
        [
            shape_of((2 * frames, D), f32),
            shape_of((H, 2 * frames, 128), bf16),
            shape_of((H, 2 * frames, 128), bf16),
            shape_of((H, 2 * frames, 128), bf16),
            shape_of((8, 128), f32),
        ],
        [pltpu.VMEM((2 * frames, D), bf16)],
        "front",
        micros=3,
        mib=MIB_A,
    )(me_ref, *token_pieces[:2], g_ff1, w_ff1_in, w_ff1_out, g_att, *projections)
    cotangent, near[4], *late = lax.optimization_barrier((cotangent, near[4], *token_pieces[2:]))
    token_pieces[2:] = late
    cot_pieces = to_pieces(cotangent, me)
    (tok, ends, s1, k2, v2, weights, inverse, mixed, s2, gap, depth, sums) = run_a(
        tiles,
        me_ref,
        rel_table,
        *token_pieces,
        *near,
        bias,
        g_ff1,
        w_ff1_in,
        w_ff1_out,
        g_att,
        *projections,
        w_output,
        g_conv,
        w_pw1,
        taps,
    )
    sums = sum_everywhere(sums)

    (o0, o1, o2, o3, grad3, bngrad, sums2, big_b, small_b) = run_b(
        tiles, me_ref, *cot_pieces, sums, depth, s2, bn_gain, w_pw2, g_ff2, w_ff2_in, w_ff2_out, g_out
    )
    out_pieces = from_pieces([o0, o1, o2, o3])
    sums2 = sum_everywhere(sums2)

    (grad2, do, dot, qt, dw_o, dw_pw1, taps_grad, row) = run_c(
        tiles,
        me_ref,
        sums,
        sums2,
        ends,
        s1,
        inverse,
        mixed,
        s2,
        gap,
        depth,
        grad3,
        bngrad,
        g_att,
        w_query,
        w_output,
        g_conv,
        w_pw1,
        taps,
        bn_gain,
    )
    (output, token_blocks, *packed) = run_e(
        tiles,
        me_ref,
        tok,
        s1,
        k2,
        v2,
        weights,
        grad2,
        do,
        dot,
        qt,
        dw_o,
        dw_pw1,
        taps_grad,
        row,
        *out_pieces,
        g_ff1,
        w_ff1_in,
        w_ff1_out,
        g_att,
        w_query,
        w_key,
        w_value,
        big_b,
        small_b,
    )

    def place(pieces, dtype):
        return call(place_kernel, 1, [shape_of((blocks, frames, D), dtype)], [], "place", micros=2, mib=8)(me_ref, *pieces)[0]

    reduced, tokens_grad = reduce_gradients(packed[:2], packed[2:], token_blocks, me, me_ref, place)
    (ff1_in, ff1_out, w_q, w_k, w_v, w_o, pw1, pw2, ff2_in, ff2_out, *small) = call(
        kernel_d,
        1,
        [
            shape_of((D, FF), f32),
            shape_of((FF, D), f32),
            shape_of((D, D), f32),
            shape_of((D, D), f32),
            shape_of((D, D), f32),
            shape_of((D, D), f32),
            shape_of((D, 2 * D), f32),
            shape_of((D, D), f32),
            shape_of((D, FF), f32),
            shape_of((FF, D), f32),
            *[shape_of((1, D), f32)] * 3,
            shape_of((H, NBUCKET), f32),
            shape_of((KERNEL, D), f32),
            *[shape_of((1, D), f32)] * 3,
        ],
        [pltpu.VMEM((packed_rows(), D), bf16)],
        "unpack",
        micros=5,
        mib=13,
    )(me_ref, *reduced, sums2)
    d_g_ff1, d_g_att, d_g_conv, rel, d_taps, d_g_ff2, d_g_out, d_bn_gain = small
    return (
        output,
        tokens_grad,
        d_g_ff1.reshape(D),
        ff1_in,
        ff1_out,
        d_g_att.reshape(D),
        w_q,
        w_k,
        w_v,
        w_o,
        rel,
        d_g_conv.reshape(D),
        pw1,
        d_taps,
        d_bn_gain.reshape(D),
        pw2,
        d_g_ff2.reshape(D),
        ff2_in,
        ff2_out,
        d_g_out.reshape(D),
    )


def padded(x, sides, width):
    for axis, dim in sides:
        size, length = (lax.axis_size(axis), x.shape[dim])
        up = [(i, (i + 1) % size) for i in range(size - 1)]
        down = [(j, i) for i, j in up]
        last = lax.slice_in_dim(x, length - width, length, axis=dim)
        first = lax.slice_in_dim(x, 0, width, axis=dim)
        before = lax.ppermute(last, axis, up)
        after = lax.ppermute(first, axis, down)
        x = jnp.concatenate([before, x, after], axis=dim)
    return x


def norm_forward(values, norm_gain):
    center = jnp.mean(values, axis=-1, keepdims=True)
    shifted = values - center
    spread = jnp.mean(shifted * shifted, axis=-1, keepdims=True)
    inverse = lax.rsqrt(spread + epsilon)
    scaled = shifted * inverse
    return (scaled * norm_gain, (scaled, inverse))


def norm_backward(upstream, norm_gain, stored):
    scaled, inverse = stored
    gain_grad = jnp.sum(upstream * scaled, axis=(0, 1))
    inner_grad = upstream * norm_gain
    inner_mean = jnp.mean(inner_grad, axis=-1, keepdims=True)
    inner_dot = jnp.mean(inner_grad * scaled, axis=-1, keepdims=True)
    return (inverse * (inner_grad - inner_mean - scaled * inner_dot), gain_grad)


def project(left_side, weight):
    return jnp.einsum("rfd,de->rfe", left_side, weight, preferred_element_type=jnp.float32)


def project_back(upstream, weight):
    return jnp.einsum("rfe,de->rfd", upstream, weight, preferred_element_type=jnp.float32)


def weight_product(left_side, upstream):
    return jnp.einsum("rfd,rfe->de", left_side, upstream, preferred_element_type=jnp.float32)


def silu_slope(values):
    logistic = jax.nn.sigmoid(values)
    return logistic * (1.0 + values * (1.0 - logistic))


def ffn_forward(values, norm_gain, weight_in, weight_out):
    normed, norm_stored = norm_forward(values, norm_gain)
    normed_low = normed.astype(jnp.bfloat16)
    hidden = project(normed_low, weight_in)
    act_low = jax.nn.silu(hidden).astype(jnp.bfloat16)
    return (project(act_low, weight_out), (norm_stored, normed_low, hidden, act_low))


def ffn_backward(stream_grad, norm_gain, weight_in, weight_out, stored):
    norm_stored, normed_low, hidden, act_low = stored
    out_low = (0.5 * stream_grad).astype(jnp.bfloat16)
    out_weight_grad = weight_product(act_low, out_low)
    hidden_low = (project_back(out_low, weight_out) * silu_slope(hidden)).astype(jnp.bfloat16)
    in_weight_grad = weight_product(normed_low, hidden_low)
    input_grad, gain_grad = norm_backward(
        project_back(hidden_low, weight_in), norm_gain, norm_stored
    )
    return (stream_grad + input_grad, (gain_grad, in_weight_grad, out_weight_grad))


def bucket_bias(query_pos, key_pos, rel_table):
    distance = key_pos[None, :] - query_pos[:, None]
    levels = NBUCKET // 2
    magnitude = jnp.abs(distance)
    bucket = levels * (distance > 0).astype(jnp.int32)
    for exponent in range(levels - 1):
        bucket = bucket + (magnitude >= 4**exponent).astype(jnp.int32)
    onehot = (bucket[:, :, None] == jnp.arange(NBUCKET, dtype=jnp.int32)[None, None, :]).astype(
        jnp.float32
    )
    position_bias = jnp.einsum("qkb,hb->hqk", onehot, rel_table, precision=lax.Precision.HIGHEST)
    return (position_bias, onehot)


def block_at(source, block_index, query_heads, segment_float, query_pos, rel_table):
    key_all, value_all, code_all = source
    row_count, frames = segment_float.shape
    key_start = block_index * frames
    key_block = lax.dynamic_slice_in_dim(key_all, key_start, frames, 1).reshape(
        row_count, frames, H, HD
    )
    value_block = lax.dynamic_slice_in_dim(value_all, key_start, frames, 1).reshape(
        row_count, frames, H, HD
    )
    code_block = lax.dynamic_slice_in_dim(code_all, key_start, frames, 1)
    key_pos = key_start + jnp.arange(frames, dtype=jnp.int32)
    position_bias, onehot = bucket_bias(query_pos, key_pos, rel_table)
    raw_scores = (
        jnp.einsum("rqhd,rkhd->rhqk", query_heads, key_block, preferred_element_type=jnp.float32)
        * HD ** (-0.5)
        + position_bias[None]
    )
    allowed = (segment_float[:, :, None] == code_block.astype(jnp.float32)[:, None, :])[:, None]
    return (jnp.where(allowed, raw_scores, masked_score), allowed, onehot, key_block, value_block)


def attend_forward(
    values, segment, code_low, norm_gain, w_query, w_key, w_value, w_output, rel_table
):
    row_count, frames, model_width = values.shape
    normed, norm_stored = norm_forward(values, norm_gain)
    normed_low = normed.astype(jnp.bfloat16)
    query_low = project(normed_low, w_query).astype(jnp.bfloat16)
    key_low = project(normed_low, w_key).astype(jnp.bfloat16)
    value_low = project(normed_low, w_value).astype(jnp.bfloat16)
    gathered = (
        lax.all_gather(key_low, "blk", axis=1, tiled=True),
        lax.all_gather(value_low, "blk", axis=1, tiled=True),
        lax.all_gather(code_low, "blk", axis=1, tiled=True),
    )
    segment_float = segment.astype(jnp.float32)
    query_pos = lax.axis_index("blk") * frames + jnp.arange(frames, dtype=jnp.int32)
    query_heads = query_low.reshape(row_count, frames, H, HD)
    blocks = lax.axis_size("blk")

    def max_step(block_index, loop_state):
        running_max, running_sum = loop_state
        scores, allowed, onehot, key_block, value_block = block_at(
            gathered, block_index, query_heads, segment_float, query_pos, rel_table
        )
        new_max = jnp.maximum(running_max, jnp.max(scores, axis=-1))
        kept_exp = jnp.where(allowed, jnp.exp(scores - new_max[..., None]), 0.0)
        return (new_max, running_sum * jnp.exp(running_max - new_max) + jnp.sum(kept_exp, axis=-1))

    start_max = jnp.full((row_count, H, frames), masked_score, jnp.float32)
    running_max, running_sum = lax.fori_loop(
        0, blocks, max_step, (start_max, jnp.zeros_like(start_max))
    )
    log_total = running_max + jnp.log(running_sum)

    def mix_step(block_index, mixed_sum):
        scores, allowed, onehot, key_block, value_block = block_at(
            gathered, block_index, query_heads, segment_float, query_pos, rel_table
        )
        attn_low = jnp.where(allowed, jnp.exp(scores - log_total[..., None]), 0.0).astype(
            jnp.bfloat16
        )
        return mixed_sum + jnp.einsum(
            "rhqk,rkhd->rqhd", attn_low, value_block, preferred_element_type=jnp.float32
        )

    mixed_heads = lax.fori_loop(
        0, blocks, mix_step, jnp.zeros((row_count, frames, H, HD), jnp.float32)
    )
    mixed_heads = mixed_heads.reshape(row_count, frames, model_width)
    mixed_low = mixed_heads.astype(jnp.bfloat16)
    stored = (
        norm_stored,
        normed_low,
        query_heads,
        key_low,
        value_low,
        code_low,
        gathered,
        log_total,
        mixed_heads,
        mixed_low,
        segment_float,
        query_pos,
    )
    return (project(mixed_low, w_output), stored)


def attend_backward(stream_grad, norm_gain, w_query, w_key, w_value, w_output, rel_table, stored):
    (
        norm_stored,
        normed_low,
        query_heads,
        key_low,
        value_low,
        code_low,
        gathered,
        log_total,
        mixed_heads,
        mixed_low,
        segment_float,
        query_pos,
    ) = stored
    row_count, frames, model_width = stream_grad.shape
    grad_low = stream_grad.astype(jnp.bfloat16)
    w_output_grad = weight_product(mixed_low, grad_low)
    mixed_grad = (
        project_back(grad_low, w_output).astype(jnp.bfloat16).reshape(row_count, frames, H, HD)
    )
    row_delta = jnp.einsum(
        "rqhd,rqhd->rhq",
        mixed_grad.astype(jnp.float32),
        mixed_heads.reshape(row_count, frames, H, HD),
    )
    source = (
        lax.all_gather(key_low, "blk", axis=1, tiled=True),
        lax.all_gather(value_low, "blk", axis=1, tiled=True),
        lax.all_gather(code_low, "blk", axis=1, tiled=True),
    )
    blocks = lax.axis_size("blk")
    scale = HD ** (-0.5)

    def score_grads(block_index):
        scores, allowed, onehot, key_block, value_block = block_at(
            source, block_index, query_heads, segment_float, query_pos, rel_table
        )
        attn_weights = jnp.where(allowed, jnp.exp(scores - log_total[..., None]), 0.0)
        weight_grad = jnp.einsum(
            "rqhd,rkhd->rhqk", mixed_grad, value_block, preferred_element_type=jnp.float32
        )
        score_low = (attn_weights * (weight_grad - row_delta[..., None])).astype(jnp.bfloat16)
        return (attn_weights, score_low, onehot, key_block)

    def grad_step(block_index, loop_state):
        query_grad, key_buffer, value_buffer, table_grad = loop_state
        attn_weights, score_low, onehot, key_block = score_grads(block_index)
        attn_low = attn_weights.astype(jnp.bfloat16)
        query_grad = query_grad + jnp.einsum(
            "rhqk,rkhd->rqhd", score_low, key_block, preferred_element_type=jnp.float32
        )
        key_part = (
            jnp.einsum(
                "rhqk,rqhd->rkhd", score_low, query_heads, preferred_element_type=jnp.float32
            )
            * scale
        )
        value_part = jnp.einsum(
            "rhqk,rqhd->rkhd", attn_low, mixed_grad, preferred_element_type=jnp.float32
        )
        key_start = block_index * frames
        key_buffer = lax.dynamic_update_slice_in_dim(
            key_buffer, key_part.reshape(row_count, frames, model_width), key_start, 1
        )
        value_buffer = lax.dynamic_update_slice_in_dim(
            value_buffer, value_part.reshape(row_count, frames, model_width), key_start, 1
        )
        table_grad = table_grad + jnp.einsum(
            "hqk,qkb->hb",
            jnp.sum(score_low.astype(jnp.float32), axis=0),
            onehot,
            precision=lax.Precision.HIGHEST,
        )
        return (query_grad, key_buffer, value_buffer, table_grad)

    empty_buffer = jnp.zeros((row_count, blocks * frames, model_width), jnp.float32)
    start_state = (
        jnp.zeros((row_count, frames, H, HD), jnp.float32),
        empty_buffer,
        empty_buffer,
        jnp.zeros((H, NBUCKET), jnp.float32),
    )
    query_grad, key_buffer, value_buffer, table_grad = lax.fori_loop(
        0, blocks, grad_step, start_state
    )
    key_total, value_total = (
        lax.psum_scatter(
            key_buffer.astype(jnp.bfloat16), "blk", scatter_dimension=1, tiled=True
        ).astype(jnp.float32),
        lax.psum_scatter(
            value_buffer.astype(jnp.bfloat16), "blk", scatter_dimension=1, tiled=True
        ).astype(jnp.float32),
    )
    query_grad_low = (
        (query_grad * scale).reshape(row_count, frames, model_width).astype(jnp.bfloat16)
    )
    key_grad_low = key_total.astype(jnp.bfloat16)
    value_grad_low = value_total.astype(jnp.bfloat16)
    w_query_grad = weight_product(normed_low, query_grad_low)
    w_key_grad = weight_product(normed_low, key_grad_low)
    w_value_grad = weight_product(normed_low, value_grad_low)
    normed_grad = (
        project_back(query_grad_low, w_query)
        + project_back(key_grad_low, w_key)
        + project_back(value_grad_low, w_value)
    )
    input_grad, gain_grad = norm_backward(normed_grad, norm_gain, norm_stored)
    return (
        stream_grad + input_grad,
        (gain_grad, w_query_grad, w_key_grad, w_value_grad, w_output_grad, table_grad),
    )


def conv_forward(values, segment, live_mask, norm_gain, w_pw1, w_depth, bn_gain, w_pw2):
    row_count, frames, model_width = values.shape
    normed, norm_stored = norm_forward(values, norm_gain)
    normed_low = normed.astype(jnp.bfloat16)
    gate_pair = project(normed_low, w_pw1)
    first_half = gate_pair[..., :model_width]
    logistic = jax.nn.sigmoid(gate_pair[..., model_width:])
    live_frames = live_mask.astype(jnp.float32)[..., None]
    gated_low = (first_half * logistic * live_frames).astype(jnp.bfloat16)
    wide_units, wide_segment = (
        padded(gated_low, (("blk", 1),), KERNEL // 2),
        padded(segment.astype(jnp.bfloat16), (("blk", 1),), KERNEL // 2),
    )
    segment_float = segment.astype(jnp.float32)
    depth_sum = jnp.zeros((row_count, frames, model_width), jnp.float32)
    for kernel_tap in range(KERNEL):
        same_segment = (
            wide_segment[:, kernel_tap : kernel_tap + frames].astype(jnp.float32) == segment_float
        ).astype(jnp.float32)
        depth_sum = (
            depth_sum
            + w_depth[kernel_tap].astype(jnp.float32)
            * wide_units[:, kernel_tap : kernel_tap + frames].astype(jnp.float32)
            * same_segment[..., None]
        )
    norm_totals = lax.psum(
        (
            jnp.sum(depth_sum * live_frames, axis=(0, 1)),
            jnp.sum(depth_sum * depth_sum * live_frames, axis=(0, 1)),
            jnp.sum(live_frames),
        ),
        ("blk", "rows"),
    )
    frame_count = norm_totals[2]
    center = norm_totals[0] / frame_count
    spread = norm_totals[1] / frame_count - center * center
    inverse = lax.rsqrt(spread + epsilon)
    standard = (depth_sum - center) * inverse
    pre_act = standard * bn_gain
    act_low = jax.nn.silu(pre_act).astype(jnp.bfloat16)
    stored = (
        norm_stored,
        normed_low,
        first_half,
        logistic,
        live_frames,
        wide_units,
        wide_segment,
        frame_count,
        inverse,
        standard,
        pre_act,
        act_low,
    )
    return (project(act_low, w_pw2), stored)


def conv_backward(stream_grad, segment, norm_gain, w_pw1, w_depth, bn_gain, w_pw2, stored):
    (
        norm_stored,
        normed_low,
        first_half,
        logistic,
        live_frames,
        wide_units,
        wide_segment,
        frame_count,
        inverse,
        standard,
        pre_act,
        act_low,
    ) = stored
    row_count, frames, model_width = stream_grad.shape
    grad_low = stream_grad.astype(jnp.bfloat16)
    w_pw2_grad = weight_product(act_low, grad_low)
    act_grad = project_back(grad_low, w_pw2) * silu_slope(pre_act)
    hat_grad = act_grad * bn_gain
    grad_sums = lax.psum(
        (jnp.sum(hat_grad, axis=(0, 1)), jnp.sum(act_grad * standard, axis=(0, 1))), ("blk", "rows")
    )
    hat_total, bn_gain_grad = grad_sums
    frame_share = live_frames / frame_count
    depth_low = (
        inverse
        * (hat_grad - frame_share * hat_total - frame_share * standard * bn_gain * bn_gain_grad)
    ).astype(jnp.bfloat16)
    wide_grad = padded(depth_low, (("blk", 1),), KERNEL // 2)
    segment_float = segment.astype(jnp.float32)
    depth_float = depth_low.astype(jnp.float32)
    unit_grad = jnp.zeros((row_count, frames, model_width), jnp.float32)
    tap_grads = []
    for kernel_tap in range(KERNEL):
        forward_same = (
            wide_segment[:, kernel_tap : kernel_tap + frames].astype(jnp.float32) == segment_float
        ).astype(jnp.float32)[..., None]
        tap_grads.append(
            jnp.sum(
                depth_float
                * wide_units[:, kernel_tap : kernel_tap + frames].astype(jnp.float32)
                * forward_same,
                axis=(0, 1),
            )
        )
        mirror = KERNEL - 1 - kernel_tap
        backward_same = (
            wide_segment[:, mirror : mirror + frames].astype(jnp.float32) == segment_float
        ).astype(jnp.float32)[..., None]
        unit_grad = (
            unit_grad
            + w_depth[kernel_tap].astype(jnp.float32)
            * wide_grad[:, mirror : mirror + frames].astype(jnp.float32)
            * backward_same
        )
    unit_grad = unit_grad * live_frames
    pair_low = jnp.concatenate(
        [unit_grad * logistic, unit_grad * first_half * logistic * (1.0 - logistic)], axis=-1
    ).astype(jnp.bfloat16)
    w_pw1_grad = weight_product(normed_low, pair_low)
    input_grad, gain_grad = norm_backward(project_back(pair_low, w_pw1), norm_gain, norm_stored)
    return (
        stream_grad + input_grad,
        (gain_grad, w_pw1_grad, jnp.stack(tap_grads), bn_gain_grad, w_pw2_grad),
    )


def per_device(
    tokens,
    seg_ids,
    frame_mask,
    cotangent,
    g_ff1,
    w_ff1_in,
    w_ff1_out,
    g_att,
    w_query,
    w_key,
    w_value,
    w_output,
    rel_table,
    g_conv,
    w_pw1,
    w_depth,
    bn_gain,
    w_pw2,
    g_ff2,
    w_ff2_in,
    w_ff2_out,
    g_out,
):
    start_stream = tokens.astype(jnp.float32)
    ffn_one, ffn_one_stored = ffn_forward(start_stream, g_ff1, w_ff1_in, w_ff1_out)
    after_ffn = start_stream + 0.5 * ffn_one
    code_low = jnp.where(frame_mask == 1, seg_ids, -1).astype(jnp.bfloat16)
    attended, attend_stored = attend_forward(
        after_ffn, seg_ids, code_low, g_att, w_query, w_key, w_value, w_output, rel_table
    )
    after_att = after_ffn + attended
    conv_out, conv_stored = conv_forward(
        after_att, seg_ids, frame_mask, g_conv, w_pw1, w_depth, bn_gain, w_pw2
    )
    after_conv = after_att + conv_out
    ffn_two, ffn_two_stored = ffn_forward(after_conv, g_ff2, w_ff2_in, w_ff2_out)
    after_two = after_conv + 0.5 * ffn_two
    final_norm, final_stored = norm_forward(after_two, g_out)
    stream_grad, g_out_grad = norm_backward(cotangent.astype(jnp.float32), g_out, final_stored)
    stream_grad, ffn_two_grads = ffn_backward(
        stream_grad, g_ff2, w_ff2_in, w_ff2_out, ffn_two_stored
    )
    stream_grad, conv_grads = conv_backward(
        stream_grad, seg_ids, g_conv, w_pw1, w_depth, bn_gain, w_pw2, conv_stored
    )
    stream_grad, attend_grads = attend_backward(
        stream_grad, g_att, w_query, w_key, w_value, w_output, rel_table, attend_stored
    )
    stream_grad, ffn_one_grads = ffn_backward(
        stream_grad, g_ff1, w_ff1_in, w_ff1_out, ffn_one_stored
    )
    summed = lax.psum(
        (
            ffn_one_grads[0],
            ffn_one_grads[1],
            ffn_one_grads[2],
            attend_grads[0],
            attend_grads[1],
            attend_grads[2],
            attend_grads[3],
            attend_grads[4],
            attend_grads[5],
            conv_grads[0],
            conv_grads[1],
            conv_grads[2],
            conv_grads[4],
            ffn_two_grads[0],
            ffn_two_grads[1],
            ffn_two_grads[2],
            g_out_grad,
        ),
        ("blk", "rows"),
    )
    return (
        final_norm.astype(jnp.bfloat16),
        stream_grad,
        summed[0],
        summed[1],
        summed[2],
        summed[3],
        summed[4],
        summed[5],
        summed[6],
        summed[7],
        summed[8],
        summed[9],
        summed[10],
        summed[11],
        conv_grads[3],
        summed[12],
        summed[13],
        summed[14],
        summed[15],
        summed[16],
    )


def solution(mesh):
    blocks, groups = mesh.shape["blk"], mesh.shape["rows"]

    def device(tokens, *rest):
        rows, frames, _ = tokens.shape
        whole_rows = rows == blocks == 4 and groups == 8 and (rows * frames) % QT == 0
        return (row_device if whole_rows else per_device)(tokens, *rest)

    return jax.shard_map(
        device,
        mesh=mesh,
        in_specs=(
            P("rows", "blk", None),
            P("rows", "blk"),
            P("rows", "blk"),
            P("rows", "blk", None),
        )
        + (P(),) * 18,
        out_specs=(P("rows", "blk", None),) * 2 + (P(),) * 18,
        check_vma=False,
    )
```

```python
import functools
import math

import jax
import jax.numpy as jnp
from jax import lax
from jax.experimental import pallas as pl
from jax.experimental.pallas import tpu as pltpu
from jax.sharding import PartitionSpec as P

H = 4
HD = 64
D = 256
FF = 1024
KERNEL = 31
HALF = KERNEL // 2
NBUCKET = 16

epsilon = 1e-05
masked_score = -1e30

f32 = jnp.float32
bf16 = jnp.bfloat16
LOG2E = math.log2(math.e)
QT = 256
GAP = 16
EXTRA = 16
SAFE_EXPONENT = 60.0
MIB = 1024 * 1024


def mm(a, b):
    return lax.dot_general(a, b, (((1,), (0,)), ((), ())), preferred_element_type=f32)


def mm_nt(a, b):
    return lax.dot_general(a, b, (((1,), (1,)), ((), ())), preferred_element_type=f32)


def turned(x):
    return x.astype(f32).T.astype(bf16)


def sigmoid(x):
    return 0.5 + 0.5 * jnp.tanh(0.5 * x)


def norm_hat(v):
    center = jnp.mean(v, axis=-1, keepdims=True)
    shifted = v - center
    spread = jnp.mean(shifted * shifted, axis=-1, keepdims=True)
    inverse = lax.rsqrt(spread + epsilon)
    return shifted * inverse, inverse


def norm_back(upstream, gain, hat, inverse):
    inner = upstream * gain
    inner_mean = jnp.mean(inner, axis=-1, keepdims=True)
    inner_dot = jnp.mean(inner * hat, axis=-1, keepdims=True)
    return inverse * (inner - inner_mean - hat * inner_dot)


def col_sum(x):
    rows, width = x.shape
    return jnp.sum(x.reshape(rows // 8, 8, width), axis=0)


def bucket_ranges():
    levels = NBUCKET // 2
    big = 1 << 30
    edges = [0] + [4**k for k in range(levels - 1)] + [big]
    out = []
    for level in range(levels - 1, 0, -1):
        out.append((level, 1 - edges[level + 1], -edges[level]))
    out.append((0, 0, 0))
    for level in range(1, levels):
        out.append((levels + level, edges[level], edges[level + 1] - 1))
    return out


def tile_buckets(offset):
    low, high = offset * QT - (QT - 1), offset * QT + (QT - 1)
    return [(b, lo) for b, lo, hi in bucket_ranges() if lo <= high and hi >= low]


def mixed_offsets(tiles):
    return [o for o in range(1 - tiles, tiles) if len(tile_buckets(o)) > 1]


def tile_distance(offset):
    row = lax.broadcasted_iota(jnp.int32, (QT, QT), 0)
    col = lax.broadcasted_iota(jnp.int32, (QT, QT), 1)
    return col - row + offset * QT


def frame_index(start, rows, width):
    return (lax.broadcasted_iota(jnp.int32, (rows, width), 0) + start).astype(f32)


def rows_at(start, count, unit):
    return pl.ds(pl.multiple_of(start, unit), count)


def bias_kernel(tiles, table_ref, bias_ref):
    def head(h, carry):
        for k, offset in enumerate(mixed_offsets(tiles)):
            d = tile_distance(offset)
            found = tile_buckets(offset)
            value = jnp.full((QT, QT), table_ref[h, found[0][0]], f32)
            for b, lo in found[1:]:
                value = jnp.where(d >= lo, table_ref[h, b], value)
            bias_ref[h, k] = value * LOG2E
        return carry

    lax.fori_loop(0, H, head, 0)


def place_pieces(me_ref, piece_refs, target_ref, frames):
    for m, piece in enumerate(piece_refs):
        start = (me_ref[0] ^ m) * frames
        target_ref[rows_at(start, frames, 64), :] = piece[0:frames, :]


def take_pieces(me_ref, source_ref, piece_refs, frames):
    for m, piece in enumerate(piece_refs):
        start = (me_ref[0] ^ m) * frames
        piece[...] = source_ref[rows_at(start, frames, 64), :].astype(piece.dtype)


def key_features(start, rows, ends):
    first_end, second_end, live_end = (e[:, :128] for e in ends)
    t = frame_index(start, rows, 128)
    lane = lax.broadcasted_iota(jnp.int32, (rows, 128), 1)
    code = jnp.where(t < first_end, 0, jnp.where(t < second_end, 1, 2))
    code = jnp.where(t < live_end, code, -1)
    barred = jnp.where((lane < 3) & (code != lane), masked_score, 0.0)
    return jnp.where((lane >= 3) & (lane < 6), 1.0, barred).astype(bf16)


def query_features(start, rows, ends):
    first_end, second_end, live_end = (e[:, :128] for e in ends)
    t = frame_index(start, rows, 128)
    lane = lax.broadcasted_iota(jnp.int32, (rows, 128), 1)
    code = jnp.where(t < first_end, 0, jnp.where(t < second_end, 1, 2))
    return jnp.where(code == lane, 1.0, 0.0)


def three_parts(x):
    top = x.astype(bf16).astype(f32)
    middle = (x - top).astype(bf16).astype(f32)
    return top, middle, x - top - middle


def spread_gaps(plain_ref, gap_ref, length, ends):
    first_end, second_end, _ = (e[:, :128] for e in ends)
    total = length + 4 * GAP
    step = GAP * 4

    def chunk(k, carry):
        start = k * step
        g = frame_index(start, step, 128)
        for c in range(2):
            a = plain_ref[c, rows_at(start + 2 * GAP, step, 16), :]
            b = plain_ref[c, rows_at(start + GAP, step, 16), :]
            d = plain_ref[c, rows_at(start, step, 16), :]
            in_first = (g >= GAP) & (g - GAP < first_end)
            in_second = (g - 2 * GAP >= first_end) & (g - 2 * GAP < second_end)
            in_third = (g - 3 * GAP >= second_end) & (g - 3 * GAP < length)
            value = jnp.where(in_first, a, jnp.where(in_second, b, jnp.where(in_third, d, 0.0)))
            gap_ref[c, rows_at(start, step, 16), :] = value
        return carry

    lax.fori_loop(0, total // step, chunk, 0)


def close_gaps(gap_ref, start, rows, ends):
    first_end, second_end, _ = (e[:, :128] for e in ends)
    t = frame_index(start, rows, 128)
    halves = []
    for c in range(2):
        a = gap_ref[c, rows_at(start + GAP, rows, 16), :]
        b = gap_ref[c, rows_at(start + 2 * GAP, rows, 16), :]
        d = gap_ref[c, rows_at(start + 3 * GAP, rows, 16), :]
        halves.append(jnp.where(t < first_end, a, jnp.where(t < second_end, b, d)))
    return jnp.concatenate(halves, axis=1)


CONV_ROWS = 32
BACK_ROWS = 32


def tapped(part, tap):
    rows = part.shape[0]
    return (part.reshape(rows // 8, 8, 128) * tap[None]).reshape(rows, 128)


def shifted_parts(ref, c, start, rows):
    for r in range(8):
        window = ref[c, pl.ds(start - 16 + r, rows + 24), :]
        for q in range(4):
            shift = 8 * q + r - 16
            if abs(shift) <= HALF:
                yield shift, window[8 * q : 8 * q + rows]


def convolve(gap_ref, out_ref, taps_ref, length):
    span = length + 2 * GAP

    for c in range(2):

        def chunk(k, carry, c=c):
            start = GAP + k * CONV_ROWS
            total = jnp.zeros((CONV_ROWS, 128), f32)
            for shift, part in shifted_parts(gap_ref, c, start, CONV_ROWS):
                total = total + tapped(part, taps_ref[c, shift + HALF])
            out_ref[c, rows_at(start, CONV_ROWS, 16), :] = total
            return carry

        lax.fori_loop(0, span // CONV_ROWS, chunk, 0, unroll=2)


def convolve_back(dgap_ref, gap_ref, out_ref, taps_ref, taps_grad_ref, length):
    span = length + 2 * GAP
    for c in range(2):

        def chunk(k, carry, c=c):
            start = GAP + k * BACK_ROWS
            units = gap_ref[c, rows_at(start, BACK_ROWS, 16), :]
            total = jnp.zeros((BACK_ROWS, 128), f32)
            sums = list(carry)
            for shift, part in shifted_parts(dgap_ref, c, start, BACK_ROWS):
                j = HALF - shift
                total = total + tapped(part, taps_ref[c, j])
                sums[j] = sums[j] + col_sum(part * units)
            out_ref[c, rows_at(start, BACK_ROWS, 16), :] = total
            return tuple(sums)

        sums = lax.fori_loop(0, span // BACK_ROWS, chunk, tuple(jnp.zeros((8, 128), f32) for _ in range(KERNEL)), unroll=2)
        for j in range(KERNEL):
            taps_grad_ref[j : j + 1, 128 * c : 128 * c + 128] = jnp.sum(sums[j], axis=0, keepdims=True)
    taps_grad_ref[KERNEL : KERNEL + 1, :] = jnp.zeros((1, 2 * 128), f32)


def add_to(ref, first, value):
    ref[...] = value if first else ref[...] + value


def read_ends(ends_ref):
    return ends_ref[0:1, :], ends_ref[1:2, :], ends_ref[2:3, :]


GATE = 1280


def front_frames(tokens, weights, targets, at):
    g_ff1_ref, w_in_ref, w_out_ref, g_att_ref, wq2_ref, wk2_ref, wv2_ref = weights
    s1_ref, q2_ref, k2_ref, v2_ref = targets
    x = tokens.astype(f32)
    hat, _ = norm_hat(x)
    n1 = (hat * g_ff1_ref[...]).astype(bf16)
    hidden = mm(n1, w_in_ref[...])
    act = (hidden * sigmoid(hidden)).astype(bf16)
    s1 = x + 0.5 * mm(act, w_out_ref[...])
    s1_ref[at, :] = s1
    hat, _ = norm_hat(s1)
    n2 = (hat * g_att_ref[...]).astype(bf16)
    lane = lax.broadcasted_iota(jnp.int32, (x.shape[0], 128), 1)
    q_all = mm(n2, wq2_ref[...]).astype(bf16).astype(f32) * (LOG2E * HD**-0.5)
    k_all = mm(n2, wk2_ref[...]).astype(bf16)
    v_all = mm(n2, wv2_ref[...])
    q_top, k_top = jnp.float32(0.0), jnp.float32(0.0)
    for h in range(H):
        cols = slice(128 * h, 128 * h + 128)
        q = q_all[:, cols]
        high = q.astype(bf16)
        low = (q - high.astype(f32)).astype(bf16)
        q2_ref[h, at, :] = jnp.where(lane < HD, high.astype(f32), low.astype(f32)).astype(bf16)
        k2_ref[h, at, :] = k_all[:, cols]
        ones = (lane >= HD) & (lane < HD + 3) if h % 2 == 0 else lane < 3
        v2_ref[h, at, :] = jnp.where(ones, 1.0, v_all[:, cols]).astype(bf16)
        q_top = jnp.maximum(q_top, jnp.max(jnp.sum(q * q, axis=1, keepdims=True)))
        k = k_all[:, cols].astype(f32)
        k_top = jnp.maximum(k_top, jnp.max(jnp.sum(k * k, axis=1, keepdims=True)))
    return q_top, k_top


def front_kernel(
    me_ref,
    piece0,
    piece1,
    g_ff1_ref,
    w_in_ref,
    w_out_ref,
    g_att_ref,
    wq2_ref,
    wk2_ref,
    wv2_ref,
    s1_ref,
    q2_ref,
    k2_ref,
    v2_ref,
    tops_ref,
    tok_ref,
):
    frames = tok_ref.shape[0] // 2
    for m, piece in enumerate((piece0, piece1)):
        tok_ref[rows_at(((me_ref[0] & 1) ^ m) * frames, frames, 64), :] = piece[0:frames, :]
    weights = (g_ff1_ref, w_in_ref, w_out_ref, g_att_ref, wq2_ref, wk2_ref, wv2_ref)
    tops = front_frames(tok_ref[...], weights, (s1_ref, q2_ref, k2_ref, v2_ref), slice(0, 2 * frames))
    tops_ref[0:1, :] = jnp.full((1, 128), tops[0])
    tops_ref[1:2, :] = jnp.full((1, 128), tops[1])
    tops_ref[2:8, :] = jnp.zeros((6, 128), f32)


def attend_tile(q2_ref, fq_ref, h, qt, k2_ref, fk_ref, bias_ref, table_ref, tiles):
    rows = slice(qt * QT, (qt + 1) * QT)
    qa = jnp.concatenate([q2_ref[h, rows, :], fq_ref[rows, :]], axis=1)
    ka = jnp.concatenate([k2_ref[h], fk_ref[...]], axis=1)
    offsets = mixed_offsets(tiles)
    s_all = mm_nt(qa, ka)
    parts = []
    for kt in range(tiles):
        s = s_all[:, kt * QT : (kt + 1) * QT]
        o = kt - qt
        if o in offsets:
            s = s + bias_ref[h, offsets.index(o)]
        else:
            s = s + table_ref[h, tile_buckets(o)[0][0]] * LOG2E
        parts.append(jnp.exp2(s).astype(bf16))
    return jnp.concatenate(parts, axis=1)


def attend_tile_below_max(q2_ref, fq_ref, h, rows, start, k2_ref, fk_ref, table_ref, s_ref, tiles):
    qa = jnp.concatenate([q2_ref[h, rows, :], fq_ref[rows, :]], axis=1)
    ka = jnp.concatenate([k2_ref[h], fk_ref[...]], axis=1)
    s_ref[...] = mm_nt(qa, ka)
    ranges = bucket_ranges()

    def add_bias(kt, top):
        cols = rows_at(kt * QT, QT, QT)
        d = tile_distance(0) + (kt * QT - start)
        value = jnp.full((QT, QT), table_ref[h, ranges[0][0]], f32)
        for b, low, _ in ranges[1:]:
            value = jnp.where(d >= low, table_ref[h, b], value)
        s = s_ref[:, cols] + value * LOG2E
        s_ref[:, cols] = s
        return jnp.maximum(top, jnp.max(s, axis=1, keepdims=True))

    top = lax.fori_loop(0, tiles, add_bias, jnp.full((QT, 1), -jnp.inf, f32))
    return jnp.exp2(s_ref[...] - top).astype(bf16)


def kernel_a(
    tiles,
    me_ref,
    table_ref,
    piece0,
    piece1,
    piece2,
    piece3,
    s1_near,
    q2_near,
    k2_near,
    v2_near,
    tops_near,
    bias_ref,
    g_ff1_ref,
    w_in_ref,
    w_out_ref,
    g_att_ref,
    wq2_ref,
    wk2_ref,
    wv2_ref,
    w_o_ref,
    g_conv_ref,
    w_pw1_ref,
    taps_ref,
    tok_ref,
    ends_ref,
    s1_ref,
    k2_ref,
    v2_ref,
    weights_ref,
    inverse_ref,
    mixed_ref,
    s2_ref,
    gap_ref,
    depth_ref,
    sums_ref,
    q2_ref,
    fq_ref,
    fk_ref,
    fast_ref,
    p_ref,
    s_ref,
    plain_ref,
    conv_ref,
    moved,
):
    pieces = (piece0, piece1, piece2, piece3)
    length = tiles * QT
    frames = length // len(pieces)
    place_pieces(me_ref, pieces, tok_ref, frames)
    extra = sum(p[frames : frames + EXTRA, :].astype(f32) for p in pieces)
    first_end = 16.0 * extra[0:1, :] + extra[1:2, :]
    second_end = first_end + 16.0 * extra[2:3, :] + extra[3:4, :]
    live_end = 16.0 * extra[4:5, :] + extra[5:6, :]
    ends_ref[0:1, :] = first_end
    ends_ref[1:2, :] = second_end
    ends_ref[2:3, :] = live_end
    ends_ref[3:8, :] = jnp.zeros((5, D), f32)
    ends = (first_end, second_end, live_end)

    near, far = rows_at((me_ref[0] >> 1) * 2 * frames, 2 * frames, 64), rows_at((1 - (me_ref[0] >> 1)) * 2 * frames, 2 * frames, 64)
    s1_ref[near, :] = s1_near[...]
    for h in range(H):
        q2_ref[h, near, :], k2_ref[h, near, :], v2_ref[h, near, :] = q2_near[h], k2_near[h], v2_near[h]
    weights = (g_ff1_ref, w_in_ref, w_out_ref, g_att_ref, wq2_ref, wk2_ref, wv2_ref)
    q_top, k_top = front_frames(tok_ref[far, :], weights, (s1_ref, q2_ref, k2_ref, v2_ref), far)
    q_top = jnp.maximum(q_top, jnp.max(tops_near[0:1, :]))
    k_top = jnp.maximum(k_top, jnp.max(tops_near[1:2, :]))
    for i in range(2):
        at = slice(i * 2 * frames, (i + 1) * 2 * frames)
        fq_ref[at, :] = query_features(i * 2 * frames, 2 * frames, ends).astype(bf16)
        fk_ref[at, :] = key_features(i * 2 * frames, 2 * frames, ends)
    fast_ref[0] = jnp.where(q_top * k_top < 4.0 * SAFE_EXPONENT**2, 1, 0)

    def weights_copy(h, slot):
        return pltpu.make_async_copy(p_ref.at[slot], weights_ref.at[h], moved.at[slot])

    def room(h, slot):
        @pl.when(h > 1)
        def _():
            weights_copy(h - 2, slot).wait()

    def mix(h, slot, rows, p):
        p_ref[slot, rows, :] = p
        total = mm(p, v2_ref[h])
        lane = lax.broadcasted_iota(jnp.int32, (QT, 128), 1)
        first = slot == 0
        denominator = jnp.where(first, total[:, HD : HD + 1], total[:, 0:1])
        inverse = jnp.broadcast_to(1.0 / denominator, (QT, 128))
        mixed = total * inverse
        g = lax.div(h, 2)
        new = jnp.logical_or(first, lane >= HD)
        mixed_ref[g, rows, :] = jnp.where(new, mixed, mixed_ref[g, rows, :])
        inverse_ref[g, rows, :] = jnp.where(new, inverse, inverse_ref[g, rows, :])

    @pl.when(fast_ref[0] == 1)
    def _():
        def head(h, carry):
            slot = lax.rem(h, 2)
            room(h, slot)
            for qt in range(tiles):
                p = attend_tile(q2_ref, fq_ref, h, qt, k2_ref, fk_ref, bias_ref, table_ref, tiles)
                mix(h, slot, slice(qt * QT, (qt + 1) * QT), p)
            weights_copy(h, slot).start()
            return carry

        lax.fori_loop(0, H, head, 0)

    @pl.when(fast_ref[0] != 1)
    def _():
        def head(h, carry):
            slot = lax.rem(h, 2)
            room(h, slot)

            def tile(qt, carry):
                rows = rows_at(qt * QT, QT, QT)
                p = attend_tile_below_max(
                    q2_ref, fq_ref, h, rows, qt * QT, k2_ref, fk_ref, table_ref, s_ref, tiles
                )
                mix(h, slot, rows, p)
                return carry

            lax.fori_loop(0, tiles, tile, 0)
            weights_copy(h, slot).start()
            return carry

        lax.fori_loop(0, H, head, 0)

    def gate(i):
        at = slice(i * GATE, (i + 1) * GATE)
        mixed = jnp.concatenate([mixed_ref[0, at, :], mixed_ref[1, at, :]], axis=1)
        s2 = s1_ref[at, :] + mm(mixed.astype(bf16), w_o_ref[...])
        s2_ref[at, :] = s2
        hat, _ = norm_hat(s2)
        n3 = (hat * g_conv_ref[...]).astype(bf16)
        pair = mm(n3, w_pw1_ref[...])
        live = frame_index(i * GATE, GATE, D) < live_end
        units = jnp.where(live, pair[:, :D] * sigmoid(pair[:, D:]), 0.0).astype(bf16).astype(f32)
        put = slice(i * GATE + 3 * GAP, (i + 1) * GATE + 3 * GAP)
        plain_ref[0, put, :] = units[:, :128]
        plain_ref[1, put, :] = units[:, 128:]

    for i in range(length // GATE):
        gate(i)
    spread_gaps(plain_ref, gap_ref, length, ends)
    convolve(gap_ref, conv_ref, taps_ref, length)

    def collect(i, carry):
        total, squares = carry
        at = rows_at(i * QT, QT, QT)
        depth = close_gaps(conv_ref, i * QT, QT, ends)
        depth_ref[at, :] = depth
        kept = jnp.where(frame_index(i * QT, QT, D) < live_end, depth, 0.0)
        return total + col_sum(kept), squares + col_sum(kept * kept)

    empty = jnp.zeros((8, D), f32)
    total, squares = lax.fori_loop(0, tiles, collect, (empty, empty))
    sums_ref[0:1, :] = jnp.sum(total, axis=0, keepdims=True)
    sums_ref[1:2, :] = jnp.sum(squares, axis=0, keepdims=True)
    sums_ref[2:3, :] = live_end
    sums_ref[3:8, :] = jnp.zeros((5, D), f32)
    for parity in range(2):
        weights_copy(H - 2 + parity, parity).wait()


MIDDLE = 1280


def batch_norm_terms(sums_ref):
    count = sums_ref[2:3, :]
    center = sums_ref[0:1, :] / count
    spread = sums_ref[1:2, :] / count - center * center
    return count, center, lax.rsqrt(spread + epsilon)


def kernel_b(
    tiles,
    me_ref,
    cot0,
    cot1,
    cot2,
    cot3,
    sums_ref,
    depth_ref,
    s2_ref,
    bn_gain_ref,
    w_pw2_ref,
    g_ff2_ref,
    w_in_ref,
    w_out_ref,
    g_out_ref,
    out0,
    out1,
    out2,
    out3,
    grad3_ref,
    bngrad_ref,
    sums2_ref,
    big_ref,
    small_ref,
    cot_ref,
    out_ref,
    dw_in_ref,
    dw_out_ref,
    dw_pw2_ref,
):
    length = tiles * QT
    frames = length // 4
    place_pieces(me_ref, (cot0, cot1, cot2, cot3), cot_ref, frames)
    _, center, inverse = batch_norm_terms(sums_ref)
    bn_gain = bn_gain_ref[...]

    def step(i, carry):
        g_out_sum, g_ff2_sum, bn_sum, bn_dot = carry
        at = slice(i * MIDDLE, (i + 1) * MIDDLE)
        standard = (depth_ref[at, :] - center) * inverse
        pre = standard * bn_gain
        logistic3 = sigmoid(pre)
        act3 = (pre * logistic3).astype(bf16)
        s3 = s2_ref[at, :] + mm(act3, w_pw2_ref[...])
        hat3, inv3 = norm_hat(s3)
        n4 = (hat3 * g_ff2_ref[...]).astype(bf16)
        hidden = mm(n4, w_in_ref[...])
        logistic = sigmoid(hidden)
        act4 = (hidden * logistic).astype(bf16)
        s4 = s3 + 0.5 * mm(act4, w_out_ref[...])
        hat4, inv4 = norm_hat(s4)
        out_ref[at, :] = (hat4 * g_out_ref[...]).astype(bf16)
        cot = cot_ref[at, :].astype(f32)
        g_out_sum = g_out_sum + col_sum(cot * hat4)
        grad4 = norm_back(cot, g_out_ref[...], hat4, inv4)
        out4 = (0.5 * grad4).astype(bf16)
        add_to(dw_out_ref, i == 0, mm(turned(out4), act4))
        slope = logistic * (1.0 + hidden * (1.0 - logistic))
        hid4 = (mm_nt(out4, w_out_ref[...]) * slope).astype(bf16)
        add_to(dw_in_ref, i == 0, mm(turned(n4), hid4))
        up = mm_nt(hid4, w_in_ref[...])
        g_ff2_sum = g_ff2_sum + col_sum(up * hat3)
        grad3 = grad4 + norm_back(up, g_ff2_ref[...], hat3, inv3)
        grad3_ref[at, :] = grad3
        out3 = grad3.astype(bf16)
        add_to(dw_pw2_ref, i == 0, mm(turned(act3), out3))
        bngrad = mm_nt(out3, w_pw2_ref[...]) * (logistic3 * (1.0 + pre * (1.0 - logistic3)))
        bngrad_ref[at, :] = bngrad
        return g_out_sum, g_ff2_sum, bn_sum + col_sum(bngrad), bn_dot + col_sum(bngrad * standard)

    empty = jnp.zeros((8, D), f32)
    sums = (empty,) * 4
    for i in range(length // MIDDLE):
        sums = step(i, sums)
    g_out_sum, g_ff2_sum, bn_sum, bn_dot = (jnp.sum(s, axis=0, keepdims=True) for s in sums)
    sums2_ref[0:1, :] = bn_sum
    sums2_ref[1:2, :] = bn_dot
    sums2_ref[2:8, :] = jnp.zeros((6, D), f32)
    small_ref[0:1, :] = g_ff2_sum
    small_ref[1:2, :] = g_out_sum
    small_ref[2:8, :] = jnp.zeros((6, D), f32)
    big_ref[0:FF, :] = turned_wide(dw_out_ref)
    for c in range(FF // D):
        big_ref[FF + c * D : FF + (c + 1) * D, :] = dw_in_ref[:, c * D : (c + 1) * D].astype(big_ref.dtype)
    big_ref[2 * FF : 2 * FF + D, :] = dw_pw2_ref[...].astype(big_ref.dtype)
    take_pieces(me_ref, out_ref, (out0, out1, out2, out3), frames)


def turned_wide(ref):
    return jnp.concatenate([ref[:, c * D : (c + 1) * D].T for c in range(ref.shape[1] // D)], axis=0).astype(bf16)


BACK = 640
LAST = 256


def kernel_c(
    tiles,
    me_ref,
    sums_ref,
    sums2_ref,
    ends_ref,
    s1_ref,
    inverse_ref,
    mixed_ref,
    s2_ref,
    gap_ref,
    depth_ref,
    grad3_ref,
    bngrad_ref,
    g_att_ref,
    w_q_ref,
    w_o_ref,
    g_conv_ref,
    w_pw1_ref,
    taps_ref,
    bn_gain_ref,
    grad_ref,
    do_ref,
    dot_ref,
    qt_ref,
    dw_o_ref,
    dw_pw1_ref,
    taps_grad_ref,
    row_ref,
    plain_ref,
    dgap_ref,
):
    length = tiles * QT
    ends = read_ends(ends_ref)
    live_end = ends[2]
    count, center, inverse = batch_norm_terms(sums_ref)
    bn_gain = bn_gain_ref[...]
    e_total = sums2_ref[0:1, :] * bn_gain
    dot_total = sums2_ref[1:2, :]


    def batch_back(i, carry):
        at = rows_at(i * QT, QT, QT)
        standard = (depth_ref[at, :] - center) * inverse
        e = bngrad_ref[at, :] * bn_gain
        share = jnp.where(frame_index(i * QT, QT, D) < live_end, 1.0, 0.0) / count
        dg = inverse * (e - share * e_total - share * standard * bn_gain * dot_total)
        dg = dg.astype(bf16).astype(f32)
        put = rows_at(i * QT + 3 * GAP, QT, 16)
        plain_ref[0, put, :] = dg[:, :128]
        plain_ref[1, put, :] = dg[:, 128:]
        return carry

    lax.fori_loop(0, tiles, batch_back, 0)
    spread_gaps(plain_ref, dgap_ref, length, ends)
    convolve_back(dgap_ref, gap_ref, plain_ref, taps_ref, taps_grad_ref, length)

    def gate_back(i, g_conv_sum):
        at = slice(i * BACK, (i + 1) * BACK)
        hat, inv = norm_hat(s2_ref[at, :])
        n3 = (hat * g_conv_ref[...]).astype(bf16)
        pair = mm(n3, w_pw1_ref[...])
        first, logistic = pair[:, :D], sigmoid(pair[:, D:])
        live = frame_index(i * BACK, BACK, D) < live_end
        ug = jnp.where(live, close_gaps(plain_ref, i * BACK, BACK, ends), 0.0) * logistic
        pairgrad = jnp.concatenate([ug, ug * first * (1.0 - logistic)], axis=1).astype(bf16)
        add_to(dw_pw1_ref, i == 0, mm(turned(n3), pairgrad))
        up = mm_nt(pairgrad, w_pw1_ref[...])
        g_conv_sum = g_conv_sum + col_sum(up * hat)
        grad2 = grad3_ref[at, :] + norm_back(up, g_conv_ref[...], hat, inv)
        grad_ref[at, :] = grad2
        out2 = grad2.astype(bf16)
        mixed = jnp.concatenate([mixed_ref[0, at, :], mixed_ref[1, at, :]], axis=1)
        add_to(dw_o_ref, i == 0, mm(turned(mixed), out2))
        mixgrad = mm_nt(out2, w_o_ref[...]).astype(bf16).astype(f32)
        mixgrad = (mixgrad * jnp.concatenate([inverse_ref[0, at, :], inverse_ref[1, at, :]], axis=1)).astype(bf16)
        dot_ref[:, at] = turned(mixgrad)
        product = mixgrad.astype(f32) * mixed
        lane = lax.broadcasted_iota(jnp.int32, (BACK, 128), 1)
        for h in range(H):
            cols = slice(128 * (h // 2), 128 * (h // 2) + 128)
            own = lane < HD if h % 2 == 0 else lane >= HD
            delta = jnp.sum(jnp.where(own, product[:, cols], 0.0), axis=1, keepdims=True)
            high, middle, low = three_parts(-delta)
            base = HD if h % 2 == 0 else 0
            side = jnp.where(lane == base, high, 0.0)
            side = jnp.where(lane == base + 1, middle, side)
            side = jnp.where(lane == base + 2, low, side)
            do_ref[h, at, :] = jnp.where(own, mixgrad[:, cols].astype(f32), side).astype(bf16)
        hat, _ = norm_hat(s1_ref[at, :])
        n2 = (hat * g_att_ref[...]).astype(bf16)
        qt_ref[:, at] = turned(mm(n2, w_q_ref[...]).astype(bf16))
        return g_conv_sum

    empty = jnp.zeros((8, D), f32)
    g_conv_sum = empty
    for i in range(length // BACK):
        g_conv_sum = gate_back(i, g_conv_sum)
    row_ref[0:1, :] = jnp.sum(g_conv_sum, axis=0, keepdims=True)
    row_ref[1:8, :] = jnp.zeros((7, D), f32)


def kernel_e(
    tiles,
    me_ref,
    tok_ref,
    s1_ref,
    k2_ref,
    v2_ref,
    weights_ref,
    grad_ref,
    do_ref,
    dot_ref,
    qt_ref,
    dw_o_ref,
    dw_pw1_ref,
    taps_grad_ref,
    row_ref,
    out0,
    out1,
    out2,
    out3,
    g_ff1_ref,
    w_ff1_in_ref,
    w_ff1_out_ref,
    g_att_ref,
    w_q_ref,
    w_k_ref,
    w_v_ref,
    big_b_ref,
    small_b_ref,
    output_ref,
    blocks_ref,
    kept_a,
    kept_b,
    sent_a,
    sent_b,
    small_ref,
    p_ref,
    dq_ref,
    dkt_ref,
    dvt_ref,
    acc_ref,
    dw_in_ref,
    dw_out_ref,
    dw_q_ref,
    dw_k_ref,
    dw_v_ref,
    last_ref,
    arrived,
):
    length = tiles * QT
    frames = length // 4

    def weights_copy(h, slot):
        return pltpu.make_async_copy(weights_ref.at[h], p_ref.at[slot], arrived.at[slot])

    weights_copy(0, 0).start()
    for m, piece in enumerate((out0, out1, out2, out3)):
        output_ref[me_ref[0] ^ m] = piece[...]
    empty = jnp.zeros((8, D), f32)


    offsets = mixed_offsets(tiles)

    def head(h, carry):
        slot = lax.rem(h, 2)

        @pl.when(h + 1 < H)
        def _():
            weights_copy(h + 1, 1 - slot).start()

        weights_copy(h, slot).wait()
        flat = {}
        started = set()
        own = rows_at(h * HD, HD, HD)
        dvt_ref[own, :] = mm(dot_ref[own, :], p_ref[slot])
        pair = lax.div(h, 2)
        for qt in range(tiles):
            rows = slice(qt * QT, (qt + 1) * QT)
            d_all = mm_nt(do_ref[h, rows, :], v2_ref[h])
            low = []
            for kt in range(tiles):
                cols = slice(kt * QT, (kt + 1) * QT)
                ds = p_ref[slot, rows, cols].astype(f32) * d_all[:, cols]
                o = kt - qt
                if o in offsets:
                    k = offsets.index(o)
                    acc_ref[k] = acc_ref[k] + ds if k in started else ds
                    started.add(k)
                else:
                    b = tile_buckets(o)[0][0]
                    flat[b] = flat[b] + col_sum(ds) if b in flat else col_sum(ds)
                low.append(ds.astype(bf16))
            low = jnp.concatenate(low, axis=1)
            p_ref[slot, rows, :] = low
            dq = mm(low, k2_ref[h])
            own_half = (lax.broadcasted_iota(jnp.int32, (QT, 128), 1) < HD) == (slot == 0)
            dq_ref[pair, rows, :] = jnp.where(own_half, dq, dq_ref[pair, rows, :])
        dkt_ref[own, :] = mm(qt_ref[own, :], p_ref[slot])
        table_row = jnp.zeros((1, D), f32)
        lane = lax.broadcasted_iota(jnp.int32, (1, D), 1)
        for k, o in enumerate(offsets):
            d = tile_distance(o)
            value = acc_ref[k]
            found = tile_buckets(o)
            tails = [col_sum(jnp.where(d >= lo, value, 0.0)) for _, lo in found[1:]]
            tails = [col_sum(value)] + tails
            for n, (b, _) in enumerate(found):
                part = tails[n] - tails[n + 1] if n + 1 < len(found) else tails[n]
                flat[b] = flat[b] + part if b in flat else part
        for b, part in flat.items():
            table_row = jnp.where(lane == b, jnp.sum(part), table_row)
        small_ref[pl.ds(h + 4, 1), :] = table_row
        return carry

    small_ref[...] = jnp.zeros_like(small_ref)
    lax.fori_loop(0, H, head, 0)


    def front_back(i, carry):
        g_att_sum, g_ff1_sum = carry
        at = slice(i * LAST, (i + 1) * LAST)
        dq = jnp.concatenate([dq_ref[g, at, :] for g in range(H // 2)], axis=1)
        dq = (dq * HD**-0.5).astype(bf16)
        dk = (dkt_ref[:, at] * HD**-0.5).T.astype(bf16)
        dv = dvt_ref[:, at].T.astype(bf16)
        s1 = s1_ref[at, :]
        hat2, inv2 = norm_hat(s1)
        n2 = turned((hat2 * g_att_ref[...]).astype(bf16))
        add_to(dw_q_ref, i == 0, mm(n2, dq))
        add_to(dw_k_ref, i == 0, mm(n2, dk))
        add_to(dw_v_ref, i == 0, mm(n2, dv))
        attgrad = mm_nt(dq, w_q_ref[...]) + mm_nt(dk, w_k_ref[...]) + mm_nt(dv, w_v_ref[...])
        g_att_sum = g_att_sum + col_sum(attgrad * hat2)
        grad1 = grad_ref[at, :] + norm_back(attgrad, g_att_ref[...], hat2, inv2)
        out1 = (0.5 * grad1).astype(bf16)
        x = tok_ref[at, :].astype(f32)
        hat1, inv1 = norm_hat(x)
        n1 = (hat1 * g_ff1_ref[...]).astype(bf16)
        hidden = mm(n1, w_ff1_in_ref[...])
        logistic = sigmoid(hidden)
        act1 = (hidden * logistic).astype(bf16)
        add_to(dw_out_ref, i == 0, mm(turned(out1), act1))
        slope = logistic * (1.0 + hidden * (1.0 - logistic))
        hid1 = (mm_nt(out1, w_ff1_out_ref[...]) * slope).astype(bf16)
        add_to(dw_in_ref, i == 0, mm(turned(n1), hid1))
        up = mm_nt(hid1, w_ff1_in_ref[...])
        g_ff1_sum = g_ff1_sum + col_sum(up * hat1)
        last_ref[at, :] = grad1 + norm_back(up, g_ff1_ref[...], hat1, inv1)
        return g_att_sum, g_ff1_sum

    g_att_sum, g_ff1_sum = empty, empty
    for i in range(length // LAST):
        g_att_sum, g_ff1_sum = front_back(i, (g_att_sum, g_ff1_sum))
    for k, s in enumerate((g_ff1_sum, g_att_sum)):
        small_ref[k : k + 1, :] = jnp.sum(s, axis=0, keepdims=True)
    small_ref[2:3, :] = row_ref[0:1, :]
    small_ref[8 : 8 + KERNEL + 1, :] = taps_grad_ref[...]
    for b in range(length // frames):
        blocks_ref[b] = last_ref[b * frames : (b + 1) * frames, :].astype(bf16)
    quarter = kept_a.shape[0]

    def put(start, value):
        side, first = start // (2 * quarter), start // quarter % 2 == 0
        at = slice(start % quarter, start % quarter + value.shape[0])

        @pl.when(me_ref[1] == side)
        def _():
            (kept_a if first else kept_b)[at, :] = value

        @pl.when(me_ref[1] != side)
        def _():
            (sent_a if first else sent_b)[at, :] = value

    for c in range(FF // D):
        put(c * D, dw_out_ref[:, c * D : (c + 1) * D].T.astype(bf16))
        put(FF + c * D, dw_in_ref[:, c * D : (c + 1) * D].astype(bf16))
    for k, ref in enumerate((dw_q_ref, dw_k_ref, dw_v_ref, dw_o_ref)):
        put(2 * FF + k * D, ref[...].astype(bf16))
    for c in range(2):
        put(2 * FF + (4 + c) * D, dw_pw1_ref[:, c * D : (c + 1) * D].astype(bf16))
    for c in range(BIG_B // D):
        put(BIG_C + c * D, big_b_ref[c * D : (c + 1) * D, :])
    rest = 4 * quarter - BIG_C - BIG_B - SMALL_C - SMALL_B
    small = [small_ref[...], small_b_ref[...], jnp.zeros((rest, D), f32)]
    put(BIG_C + BIG_B, jnp.concatenate(small, axis=0).astype(bf16))


def swap(x, axis, bit):
    size = lax.axis_size(axis)
    return lax.ppermute(x, axis, [(i, i ^ bit) for i in range(size)])


def doubling_steps():
    steps = []
    for axis in ("rows", "blk"):
        size = lax.axis_size(axis)
        bit = 1
        while bit < size:
            steps.append((axis, bit))
            bit *= 2
    return steps


def sum_everywhere(x):
    for axis, bit in doubling_steps():
        x = x + swap(x, axis, bit)
    return x


def to_pieces(x, me):
    own = lax.dynamic_index_in_dim(x, me, 0, keepdims=False)
    pieces = [own]
    for m in range(1, x.shape[0]):
        pieces.append(swap(lax.dynamic_index_in_dim(x, me ^ m, 0, keepdims=False), "blk", m))
    return pieces


def from_pieces(pieces):
    return [pieces[0]] + [swap(p, "blk", m) for m, p in enumerate(pieces) if m > 0]


def cut(terms, start, rows):
    return sum(lax.dynamic_slice_in_dim(t, start, rows, 0).astype(f32) for t in terms).astype(bf16)


def keep_half(terms, axis, bit):
    half = terms[0].shape[0] // 2
    side = (lax.axis_index(axis) // bit) % 2
    got = swap(cut(terms, (1 - side) * half, half), axis, bit)
    return [cut(terms, side * half, half), got]


def join_half(x, axis, bit):
    side = (lax.axis_index(axis) // bit) % 2
    got = swap(x, axis, bit)
    return jnp.where(side == 0, jnp.concatenate([x, got]), jnp.concatenate([got, x]))


def halve_kernel(me_ref, kept_a, kept_b, got_a, got_b, send_a, send_b, keep_a, keep_b):
    half = send_a.shape[0]
    parts = ((kept_a, got_a, send_a, keep_a, me_ref[2]), (kept_b, got_b, send_b, keep_b, me_ref[3]))
    for kept, got, send, keep, side in parts:
        for target, place in ((send, 1 - side), (keep, side)):
            at = rows_at(place * half, half, 64)
            target[...] = (kept[at, :].astype(f32) + got[at, :].astype(f32)).astype(bf16)


def reduce_gradients(kept, sent, token_blocks, me, me_ref, place):
    got_a, got_b = (swap(s, "rows", 1) for s in sent)
    t0, t1, t2, t3 = to_pieces(token_blocks, me)
    rows = kept[0].shape[0] // 2
    send_a, send_b, keep_a, keep_b = call(
        halve_kernel, 1, [shape_of((rows, D), bf16)] * 4, [], "halves", micros=1, mib=8
    )(me_ref, *kept, got_a, got_b)
    a, b = [keep_a, swap(send_a, "rows", 2)], [keep_b, swap(send_b, "rows", 4)]
    a_steps = (("rows", 2), ("rows", 4), ("blk", 1), ("blk", 2))
    b_steps = (("rows", 4), ("rows", 2), ("blk", 1), ("blk", 2))
    for k, (sa, sb) in enumerate(zip(a_steps, b_steps)):
        if k == 0:
            continue
        if k == 1:
            b[1], t1, t3 = lax.optimization_barrier((b[1], t1, t3))
        if k == 3:
            b[1], t2 = lax.optimization_barrier((b[1], t2))
            tokens_grad = place([t0, t1, t2, t3], f32)
        a, b = keep_half(a, *sa), keep_half(b, *sb)
    a, b = cut(a, 0, a[0].shape[0]), cut(b, 0, b[0].shape[0])
    for k, (sa, sb) in enumerate(zip(a_steps[::-1], b_steps[::-1])):
        if k == 1:
            b, tokens_grad = lax.optimization_barrier((b, tokens_grad))
        a, b = join_half(a, *sa), join_half(b, *sb)
    return (a, b, swap(a, "rows", 1), swap(b, "rows", 1)), tokens_grad


BIG_B = 2 * FF + D
BIG_C = 2 * FF + 6 * D
SMALL_C = 40
SMALL_B = 8


def place_kernel(me_ref, p0, p1, p2, p3, target_ref):
    for m, p in enumerate((p0, p1, p2, p3)):
        target_ref[me_ref[0] ^ m] = p[...].astype(target_ref.dtype)


def kernel_d(
    me_ref,
    own_a,
    own_b,
    other_a,
    other_b,
    sums2_ref,
    ff1_in,
    ff1_out,
    w_q,
    w_k,
    w_v,
    w_o,
    pw1,
    pw2,
    ff2_in,
    ff2_out,
    g_ff1,
    g_att,
    g_conv,
    rel,
    taps,
    g_ff2,
    g_out,
    bn_gain,
    big_ref,
):
    quarter = own_a.shape[0]
    side = me_ref[1]
    for k, (own, other) in enumerate(((own_a, other_a), (own_b, other_b))):
        big_ref[rows_at((2 * side + k) * quarter, quarter, 64), :] = own[...]
        big_ref[rows_at((2 * (1 - side) + k) * quarter, quarter, 64), :] = other[...]
    ff1_out[...] = big_ref[0:FF, :].astype(f32)
    for c in range(FF // D):
        ff1_in[:, c * D : (c + 1) * D] = big_ref[FF + c * D : FF + (c + 1) * D, :].astype(f32)
    base = 2 * FF
    for k, ref in enumerate((w_q, w_k, w_v, w_o)):
        ref[...] = big_ref[base + k * D : base + (k + 1) * D, :].astype(f32)
    base = 2 * FF + 4 * D
    for c in range(2):
        pw1[:, c * D : (c + 1) * D] = big_ref[base + c * D : base + (c + 1) * D, :].astype(f32)
    base = BIG_C
    ff2_out[...] = big_ref[base : base + FF, :].astype(f32)
    for c in range(FF // D):
        at = base + FF + c * D
        ff2_in[:, c * D : (c + 1) * D] = big_ref[at : at + D, :].astype(f32)
    pw2[...] = big_ref[base + 2 * FF : base + 2 * FF + D, :].astype(f32)
    small = big_ref[BIG_C + BIG_B : BIG_C + BIG_B + SMALL_C + SMALL_B, :].astype(f32)
    g_ff1[...], g_att[...], g_conv[...] = small[0:1], small[1:2], small[2:3]
    rel[...] = small[4:8, :NBUCKET]
    taps[...] = small[8 : 8 + KERNEL]
    g_ff2[...], g_out[...] = small[SMALL_C : SMALL_C + 1], small[SMALL_C + 1 : SMALL_C + 2]
    bn_gain[...] = sums2_ref[1:2, :]


def shape_of(shape, dtype):
    return jax.ShapeDtypeStruct(shape, dtype)


def call(body, smem, outs, scratch, name, far_in=(), far_out=(), micros=1, mib=16):
    def place(far, count):
        return [pl.BlockSpec(memory_space=pl.ANY if k in far else pltpu.VMEM) for k in range(count)]

    def run(*operands):
        specs = [pl.BlockSpec(memory_space=pltpu.SMEM)] * smem + place(far_in, len(operands))[smem:]
        return pl.pallas_call(
            body,
            out_shape=outs,
            in_specs=specs,
            out_specs=place(far_out, len(outs)),
            scratch_shapes=scratch,
            compiler_params=pltpu.CompilerParams(vmem_limit_bytes=mib * MIB),
            cost_estimate=pl.CostEstimate(flops=micros * 10**9, bytes_accessed=micros * 10**6, transcendentals=0),
            name=name,
        )(*operands)

    return run


def twice(weight):
    heads = weight.reshape(D, H, HD)
    return jnp.concatenate([heads, heads], axis=2).reshape(D, 2 * D)


def one_side(weight):
    heads = weight.reshape(D, H // 2, 2, HD)
    empty = jnp.zeros_like(heads[:, :, 0])
    even = jnp.concatenate([heads[:, :, 0], empty], axis=2)
    odd = jnp.concatenate([empty, heads[:, :, 1]], axis=2)
    return jnp.stack([even, odd], axis=2).reshape(D, 2 * D)


MIB_A = 24
MIB_B = 29
MIB_C = 20
MIB_E = 34


def packed_rows():
    rows = BIG_C + BIG_B + SMALL_C + SMALL_B
    return -(-rows // 1024) * 1024


def run_a(tiles, *operands):
    length = tiles * QT
    frames = length // 4
    padded_rows = length + 4 * GAP
    n_mixed = len(mixed_offsets(tiles))
    return call(
        functools.partial(kernel_a, tiles),
        2,
        [
            shape_of((length, D), bf16),
            shape_of((8, D), f32),
            shape_of((length, D), f32),
            shape_of((H, length, 128), bf16),
            shape_of((H, length, 128), bf16),
            shape_of((H, length, length), bf16),
            shape_of((H // 2, length, 128), f32),
            shape_of((H // 2, length, 128), f32),
            shape_of((length, D), f32),
            shape_of((2, padded_rows, 128), f32),
            shape_of((length, D), f32),
            shape_of((8, D), f32),
        ],
        [
            pltpu.VMEM((H, length, 128), bf16),
            pltpu.VMEM((length, 128), bf16),
            pltpu.VMEM((length, 128), bf16),
            pltpu.SMEM((1,), jnp.int32),
            pltpu.VMEM((2, length, length), bf16),
            pltpu.VMEM((QT, length), f32),
            pltpu.VMEM((2, length + 6 * GAP, 128), f32),
            pltpu.VMEM((2, padded_rows, 128), f32),
            pltpu.SemaphoreType.DMA((2,)),
        ],
        "first_part",
        far_out=(5,),
        micros=30,
        mib=MIB_A,
    )(*operands)


def run_b(tiles, *operands):
    length = tiles * QT
    frames = length // 4
    padded_rows = length + 4 * GAP
    n_mixed = len(mixed_offsets(tiles))
    return call(
        functools.partial(kernel_b, tiles),
        1,
        [shape_of((frames, D), bf16)] * 4
        + [
            shape_of((length, D), f32),
            shape_of((length, D), f32),
            shape_of((8, D), f32),
            shape_of((BIG_B, D), bf16),
            shape_of((SMALL_B, D), f32),
        ],
        [
            pltpu.VMEM((length, D), bf16),
            pltpu.VMEM((length, D), bf16),
            pltpu.VMEM((D, FF), f32),
            pltpu.VMEM((D, FF), f32),
            pltpu.VMEM((D, D), f32),
        ],
        "middle_part",
        micros=12,
        mib=MIB_B,
    )(*operands)


def run_c(tiles, *operands):
    length = tiles * QT
    padded_rows = length + 4 * GAP
    return call(
        functools.partial(kernel_c, tiles),
        1,
        [
            shape_of((length, D), f32),
            shape_of((H, length, 128), bf16),
            shape_of((D, length), bf16),
            shape_of((D, length), bf16),
            shape_of((D, D), f32),
            shape_of((D, 2 * D), f32),
            shape_of((KERNEL + 1, D), f32),
            shape_of((8, D), f32),
        ],
        [
            pltpu.VMEM((2, length + 6 * GAP, 128), f32),
            pltpu.VMEM((2, padded_rows, 128), f32),
        ],
        "third_part",
        micros=16,
        mib=MIB_C,
    )(*operands)


def run_e(tiles, *operands):
    length = tiles * QT
    frames = length // 4
    n_mixed = len(mixed_offsets(tiles))
    return call(
        functools.partial(kernel_e, tiles),
        1,
        [shape_of((4, frames, D), bf16)] * 2
        + [shape_of((packed_rows() // 4, D), bf16)] * 4,
        [
            pltpu.VMEM((SMALL_C, D), f32),
            pltpu.VMEM((2, length, length), bf16),
            pltpu.VMEM((H // 2, length, 128), f32),
            pltpu.VMEM((D, length), f32),
            pltpu.VMEM((D, length), f32),
            pltpu.VMEM((n_mixed, QT, QT), f32),
            pltpu.VMEM((D, FF), f32),
            pltpu.VMEM((D, FF), f32),
            pltpu.VMEM((D, D), f32),
            pltpu.VMEM((D, D), f32),
            pltpu.VMEM((D, D), f32),
            pltpu.VMEM((length, D), f32),
            pltpu.SemaphoreType.DMA((2,)),
        ],
        "last_part",
        far_in=(5,),
        micros=24,
        mib=MIB_E,
    )(*operands)


def row_device(
    tokens,
    seg_ids,
    frame_mask,
    cotangent,
    g_ff1,
    w_ff1_in,
    w_ff1_out,
    g_att,
    w_query,
    w_key,
    w_value,
    w_output,
    rel_table,
    g_conv,
    w_pw1,
    w_depth,
    bn_gain,
    w_pw2,
    g_ff2,
    w_ff2_in,
    w_ff2_out,
    g_out,
):
    blocks, frames, _ = tokens.shape
    length = blocks * frames
    tiles = length // QT
    n_mixed = len(mixed_offsets(tiles))
    me = lax.axis_index("blk")
    group = lax.axis_index("rows")
    me_ref = jnp.stack([me, group % 2, group // 2 % 2, group // 4 % 2]).astype(jnp.int32)
    gains = [g.reshape(1, D) for g in (g_ff1, g_att, g_conv, bn_gain, g_ff2, g_out)]
    g_ff1, g_att, g_conv, bn_gain, g_ff2, g_out = gains

    found = jnp.stack([seg_ids == 0, seg_ids == 1, frame_mask == 1], axis=1)
    lengths = jnp.sum(found.astype(jnp.int32), axis=2)
    digits = jnp.stack([lengths // 16, lengths % 16], axis=2).reshape(blocks, 6)
    digits = jnp.pad(digits, ((0, 0), (0, EXTRA - digits.shape[1]))).astype(bf16)
    extra = jnp.broadcast_to(digits[:, :, None], (blocks, EXTRA, D))
    token_pieces = to_pieces(jnp.concatenate([tokens, extra], axis=1), me)
    bias = call(
        functools.partial(bias_kernel, tiles), 1, [shape_of((H, n_mixed, QT, QT), f32)], [], "bias_tiles"
    )(rel_table)[0]
    taps = w_depth.astype(f32).reshape(KERNEL, 2, 128).transpose(1, 0, 2)
    taps = jnp.broadcast_to(taps[:, :, None, :], (2, KERNEL, 8, 128))

    projections = (twice(w_query), twice(w_key), one_side(w_value))
    *near, = call(
        front_kernel,
        1,
        [
            shape_of((2 * frames, D), f32),
            shape_of((H, 2 * frames, 128), bf16),
            shape_of((H, 2 * frames, 128), bf16),
            shape_of((H, 2 * frames, 128), bf16),
            shape_of((8, 128), f32),
        ],
        [pltpu.VMEM((2 * frames, D), bf16)],
        "front",
        micros=3,
        mib=MIB_A,
    )(me_ref, *token_pieces[:2], g_ff1, w_ff1_in, w_ff1_out, g_att, *projections)
    cotangent, near[4], *late = lax.optimization_barrier((cotangent, near[4], *token_pieces[2:]))
    token_pieces[2:] = late
    far = [swap(lax.dynamic_index_in_dim(cotangent, me ^ m, 0, keepdims=False), "blk", m) for m in (2, 3, 1)]
    cot_pieces = [lax.dynamic_index_in_dim(cotangent, me, 0, keepdims=False), far[2], far[0], far[1]]
    (tok, ends, s1, k2, v2, weights, inverse, mixed, s2, gap, depth, sums) = run_a(
        tiles,
        me_ref,
        rel_table,
        *token_pieces,
        *near,
        bias,
        g_ff1,
        w_ff1_in,
        w_ff1_out,
        g_att,
        *projections,
        w_output,
        g_conv,
        w_pw1,
        taps,
    )
    sums = sum_everywhere(sums)

    (o0, o1, o2, o3, grad3, bngrad, sums2, big_b, small_b) = run_b(
        tiles, me_ref, *cot_pieces, sums, depth, s2, bn_gain, w_pw2, g_ff2, w_ff2_in, w_ff2_out, g_out
    )
    out_pieces = from_pieces([o0, o1, o2, o3])
    sums2 = sum_everywhere(sums2)

    (grad2, do, dot, qt, dw_o, dw_pw1, taps_grad, row) = run_c(
        tiles,
        me_ref,
        sums,
        sums2,
        ends,
        s1,
        inverse,
        mixed,
        s2,
        gap,
        depth,
        grad3,
        bngrad,
        g_att,
        w_query,
        w_output,
        g_conv,
        w_pw1,
        taps,
        bn_gain,
    )
    (output, token_blocks, *packed) = run_e(
        tiles,
        me_ref,
        tok,
        s1,
        k2,
        v2,
        weights,
        grad2,
        do,
        dot,
        qt,
        dw_o,
        dw_pw1,
        taps_grad,
        row,
        *out_pieces,
        g_ff1,
        w_ff1_in,
        w_ff1_out,
        g_att,
        w_query,
        w_key,
        w_value,
        big_b,
        small_b,
    )

    def place(pieces, dtype):
        return call(place_kernel, 1, [shape_of((blocks, frames, D), dtype)], [], "place", micros=2, mib=8)(me_ref, *pieces)[0]

    reduced, tokens_grad = reduce_gradients(packed[:2], packed[2:], token_blocks, me, me_ref, place)
    (ff1_in, ff1_out, w_q, w_k, w_v, w_o, pw1, pw2, ff2_in, ff2_out, *small) = call(
        kernel_d,
        1,
        [
            shape_of((D, FF), f32),
            shape_of((FF, D), f32),
            shape_of((D, D), f32),
            shape_of((D, D), f32),
            shape_of((D, D), f32),
            shape_of((D, D), f32),
            shape_of((D, 2 * D), f32),
            shape_of((D, D), f32),
            shape_of((D, FF), f32),
            shape_of((FF, D), f32),
            *[shape_of((1, D), f32)] * 3,
            shape_of((H, NBUCKET), f32),
            shape_of((KERNEL, D), f32),
            *[shape_of((1, D), f32)] * 3,
        ],
        [pltpu.VMEM((packed_rows(), D), bf16)],
        "unpack",
        micros=5,
        mib=13,
    )(me_ref, *reduced, sums2)
    d_g_ff1, d_g_att, d_g_conv, rel, d_taps, d_g_ff2, d_g_out, d_bn_gain = small
    return (
        output,
        tokens_grad,
        d_g_ff1.reshape(D),
        ff1_in,
        ff1_out,
        d_g_att.reshape(D),
        w_q,
        w_k,
        w_v,
        w_o,
        rel,
        d_g_conv.reshape(D),
        pw1,
        d_taps,
        d_bn_gain.reshape(D),
        pw2,
        d_g_ff2.reshape(D),
        ff2_in,
        ff2_out,
        d_g_out.reshape(D),
    )


def padded(x, sides, width):
    for axis, dim in sides:
        size, length = (lax.axis_size(axis), x.shape[dim])
        up = [(i, (i + 1) % size) for i in range(size - 1)]
        down = [(j, i) for i, j in up]
        last = lax.slice_in_dim(x, length - width, length, axis=dim)
        first = lax.slice_in_dim(x, 0, width, axis=dim)
        before = lax.ppermute(last, axis, up)
        after = lax.ppermute(first, axis, down)
        x = jnp.concatenate([before, x, after], axis=dim)
    return x


def norm_forward(values, norm_gain):
    center = jnp.mean(values, axis=-1, keepdims=True)
    shifted = values - center
    spread = jnp.mean(shifted * shifted, axis=-1, keepdims=True)
    inverse = lax.rsqrt(spread + epsilon)
    scaled = shifted * inverse
    return (scaled * norm_gain, (scaled, inverse))


def norm_backward(upstream, norm_gain, stored):
    scaled, inverse = stored
    gain_grad = jnp.sum(upstream * scaled, axis=(0, 1))
    inner_grad = upstream * norm_gain
    inner_mean = jnp.mean(inner_grad, axis=-1, keepdims=True)
    inner_dot = jnp.mean(inner_grad * scaled, axis=-1, keepdims=True)
    return (inverse * (inner_grad - inner_mean - scaled * inner_dot), gain_grad)


def project(left_side, weight):
    return jnp.einsum("rfd,de->rfe", left_side, weight, preferred_element_type=jnp.float32)


def project_back(upstream, weight):
    return jnp.einsum("rfe,de->rfd", upstream, weight, preferred_element_type=jnp.float32)


def weight_product(left_side, upstream):
    return jnp.einsum("rfd,rfe->de", left_side, upstream, preferred_element_type=jnp.float32)


def silu_slope(values):
    logistic = jax.nn.sigmoid(values)
    return logistic * (1.0 + values * (1.0 - logistic))


def ffn_forward(values, norm_gain, weight_in, weight_out):
    normed, norm_stored = norm_forward(values, norm_gain)
    normed_low = normed.astype(jnp.bfloat16)
    hidden = project(normed_low, weight_in)
    act_low = jax.nn.silu(hidden).astype(jnp.bfloat16)
    return (project(act_low, weight_out), (norm_stored, normed_low, hidden, act_low))


def ffn_backward(stream_grad, norm_gain, weight_in, weight_out, stored):
    norm_stored, normed_low, hidden, act_low = stored
    out_low = (0.5 * stream_grad).astype(jnp.bfloat16)
    out_weight_grad = weight_product(act_low, out_low)
    hidden_low = (project_back(out_low, weight_out) * silu_slope(hidden)).astype(jnp.bfloat16)
    in_weight_grad = weight_product(normed_low, hidden_low)
    input_grad, gain_grad = norm_backward(
        project_back(hidden_low, weight_in), norm_gain, norm_stored
    )
    return (stream_grad + input_grad, (gain_grad, in_weight_grad, out_weight_grad))


def bucket_bias(query_pos, key_pos, rel_table):
    distance = key_pos[None, :] - query_pos[:, None]
    levels = NBUCKET // 2
    magnitude = jnp.abs(distance)
    bucket = levels * (distance > 0).astype(jnp.int32)
    for exponent in range(levels - 1):
        bucket = bucket + (magnitude >= 4**exponent).astype(jnp.int32)
    onehot = (bucket[:, :, None] == jnp.arange(NBUCKET, dtype=jnp.int32)[None, None, :]).astype(
        jnp.float32
    )
    position_bias = jnp.einsum("qkb,hb->hqk", onehot, rel_table, precision=lax.Precision.HIGHEST)
    return (position_bias, onehot)


def block_at(source, block_index, query_heads, segment_float, query_pos, rel_table):
    key_all, value_all, code_all = source
    row_count, frames = segment_float.shape
    key_start = block_index * frames
    key_block = lax.dynamic_slice_in_dim(key_all, key_start, frames, 1).reshape(
        row_count, frames, H, HD
    )
    value_block = lax.dynamic_slice_in_dim(value_all, key_start, frames, 1).reshape(
        row_count, frames, H, HD
    )
    code_block = lax.dynamic_slice_in_dim(code_all, key_start, frames, 1)
    key_pos = key_start + jnp.arange(frames, dtype=jnp.int32)
    position_bias, onehot = bucket_bias(query_pos, key_pos, rel_table)
    raw_scores = (
        jnp.einsum("rqhd,rkhd->rhqk", query_heads, key_block, preferred_element_type=jnp.float32)
        * HD ** (-0.5)
        + position_bias[None]
    )
    allowed = (segment_float[:, :, None] == code_block.astype(jnp.float32)[:, None, :])[:, None]
    return (jnp.where(allowed, raw_scores, masked_score), allowed, onehot, key_block, value_block)


def attend_forward(
    values, segment, code_low, norm_gain, w_query, w_key, w_value, w_output, rel_table
):
    row_count, frames, model_width = values.shape
    normed, norm_stored = norm_forward(values, norm_gain)
    normed_low = normed.astype(jnp.bfloat16)
    query_low = project(normed_low, w_query).astype(jnp.bfloat16)
    key_low = project(normed_low, w_key).astype(jnp.bfloat16)
    value_low = project(normed_low, w_value).astype(jnp.bfloat16)
    gathered = (
        lax.all_gather(key_low, "blk", axis=1, tiled=True),
        lax.all_gather(value_low, "blk", axis=1, tiled=True),
        lax.all_gather(code_low, "blk", axis=1, tiled=True),
    )
    segment_float = segment.astype(jnp.float32)
    query_pos = lax.axis_index("blk") * frames + jnp.arange(frames, dtype=jnp.int32)
    query_heads = query_low.reshape(row_count, frames, H, HD)
    blocks = lax.axis_size("blk")

    def max_step(block_index, loop_state):
        running_max, running_sum = loop_state
        scores, allowed, onehot, key_block, value_block = block_at(
            gathered, block_index, query_heads, segment_float, query_pos, rel_table
        )
        new_max = jnp.maximum(running_max, jnp.max(scores, axis=-1))
        kept_exp = jnp.where(allowed, jnp.exp(scores - new_max[..., None]), 0.0)
        return (new_max, running_sum * jnp.exp(running_max - new_max) + jnp.sum(kept_exp, axis=-1))

    start_max = jnp.full((row_count, H, frames), masked_score, jnp.float32)
    running_max, running_sum = lax.fori_loop(
        0, blocks, max_step, (start_max, jnp.zeros_like(start_max))
    )
    log_total = running_max + jnp.log(running_sum)

    def mix_step(block_index, mixed_sum):
        scores, allowed, onehot, key_block, value_block = block_at(
            gathered, block_index, query_heads, segment_float, query_pos, rel_table
        )
        attn_low = jnp.where(allowed, jnp.exp(scores - log_total[..., None]), 0.0).astype(
            jnp.bfloat16
        )
        return mixed_sum + jnp.einsum(
            "rhqk,rkhd->rqhd", attn_low, value_block, preferred_element_type=jnp.float32
        )

    mixed_heads = lax.fori_loop(
        0, blocks, mix_step, jnp.zeros((row_count, frames, H, HD), jnp.float32)
    )
    mixed_heads = mixed_heads.reshape(row_count, frames, model_width)
    mixed_low = mixed_heads.astype(jnp.bfloat16)
    stored = (
        norm_stored,
        normed_low,
        query_heads,
        key_low,
        value_low,
        code_low,
        gathered,
        log_total,
        mixed_heads,
        mixed_low,
        segment_float,
        query_pos,
    )
    return (project(mixed_low, w_output), stored)


def attend_backward(stream_grad, norm_gain, w_query, w_key, w_value, w_output, rel_table, stored):
    (
        norm_stored,
        normed_low,
        query_heads,
        key_low,
        value_low,
        code_low,
        gathered,
        log_total,
        mixed_heads,
        mixed_low,
        segment_float,
        query_pos,
    ) = stored
    row_count, frames, model_width = stream_grad.shape
    grad_low = stream_grad.astype(jnp.bfloat16)
    w_output_grad = weight_product(mixed_low, grad_low)
    mixed_grad = (
        project_back(grad_low, w_output).astype(jnp.bfloat16).reshape(row_count, frames, H, HD)
    )
    row_delta = jnp.einsum(
        "rqhd,rqhd->rhq",
        mixed_grad.astype(jnp.float32),
        mixed_heads.reshape(row_count, frames, H, HD),
    )
    source = (
        lax.all_gather(key_low, "blk", axis=1, tiled=True),
        lax.all_gather(value_low, "blk", axis=1, tiled=True),
        lax.all_gather(code_low, "blk", axis=1, tiled=True),
    )
    blocks = lax.axis_size("blk")
    scale = HD ** (-0.5)

    def score_grads(block_index):
        scores, allowed, onehot, key_block, value_block = block_at(
            source, block_index, query_heads, segment_float, query_pos, rel_table
        )
        attn_weights = jnp.where(allowed, jnp.exp(scores - log_total[..., None]), 0.0)
        weight_grad = jnp.einsum(
            "rqhd,rkhd->rhqk", mixed_grad, value_block, preferred_element_type=jnp.float32
        )
        score_low = (attn_weights * (weight_grad - row_delta[..., None])).astype(jnp.bfloat16)
        return (attn_weights, score_low, onehot, key_block)

    def grad_step(block_index, loop_state):
        query_grad, key_buffer, value_buffer, table_grad = loop_state
        attn_weights, score_low, onehot, key_block = score_grads(block_index)
        attn_low = attn_weights.astype(jnp.bfloat16)
        query_grad = query_grad + jnp.einsum(
            "rhqk,rkhd->rqhd", score_low, key_block, preferred_element_type=jnp.float32
        )
        key_part = (
            jnp.einsum(
                "rhqk,rqhd->rkhd", score_low, query_heads, preferred_element_type=jnp.float32
            )
            * scale
        )
        value_part = jnp.einsum(
            "rhqk,rqhd->rkhd", attn_low, mixed_grad, preferred_element_type=jnp.float32
        )
        key_start = block_index * frames
        key_buffer = lax.dynamic_update_slice_in_dim(
            key_buffer, key_part.reshape(row_count, frames, model_width), key_start, 1
        )
        value_buffer = lax.dynamic_update_slice_in_dim(
            value_buffer, value_part.reshape(row_count, frames, model_width), key_start, 1
        )
        table_grad = table_grad + jnp.einsum(
            "hqk,qkb->hb",
            jnp.sum(score_low.astype(jnp.float32), axis=0),
            onehot,
            precision=lax.Precision.HIGHEST,
        )
        return (query_grad, key_buffer, value_buffer, table_grad)

    empty_buffer = jnp.zeros((row_count, blocks * frames, model_width), jnp.float32)
    start_state = (
        jnp.zeros((row_count, frames, H, HD), jnp.float32),
        empty_buffer,
        empty_buffer,
        jnp.zeros((H, NBUCKET), jnp.float32),
    )
    query_grad, key_buffer, value_buffer, table_grad = lax.fori_loop(
        0, blocks, grad_step, start_state
    )
    key_total, value_total = (
        lax.psum_scatter(
            key_buffer.astype(jnp.bfloat16), "blk", scatter_dimension=1, tiled=True
        ).astype(jnp.float32),
        lax.psum_scatter(
            value_buffer.astype(jnp.bfloat16), "blk", scatter_dimension=1, tiled=True
        ).astype(jnp.float32),
    )
    query_grad_low = (
        (query_grad * scale).reshape(row_count, frames, model_width).astype(jnp.bfloat16)
    )
    key_grad_low = key_total.astype(jnp.bfloat16)
    value_grad_low = value_total.astype(jnp.bfloat16)
    w_query_grad = weight_product(normed_low, query_grad_low)
    w_key_grad = weight_product(normed_low, key_grad_low)
    w_value_grad = weight_product(normed_low, value_grad_low)
    normed_grad = (
        project_back(query_grad_low, w_query)
        + project_back(key_grad_low, w_key)
        + project_back(value_grad_low, w_value)
    )
    input_grad, gain_grad = norm_backward(normed_grad, norm_gain, norm_stored)
    return (
        stream_grad + input_grad,
        (gain_grad, w_query_grad, w_key_grad, w_value_grad, w_output_grad, table_grad),
    )


def conv_forward(values, segment, live_mask, norm_gain, w_pw1, w_depth, bn_gain, w_pw2):
    row_count, frames, model_width = values.shape
    normed, norm_stored = norm_forward(values, norm_gain)
    normed_low = normed.astype(jnp.bfloat16)
    gate_pair = project(normed_low, w_pw1)
    first_half = gate_pair[..., :model_width]
    logistic = jax.nn.sigmoid(gate_pair[..., model_width:])
    live_frames = live_mask.astype(jnp.float32)[..., None]
    gated_low = (first_half * logistic * live_frames).astype(jnp.bfloat16)
    wide_units, wide_segment = (
        padded(gated_low, (("blk", 1),), KERNEL // 2),
        padded(segment.astype(jnp.bfloat16), (("blk", 1),), KERNEL // 2),
    )
    segment_float = segment.astype(jnp.float32)
    depth_sum = jnp.zeros((row_count, frames, model_width), jnp.float32)
    for kernel_tap in range(KERNEL):
        same_segment = (
            wide_segment[:, kernel_tap : kernel_tap + frames].astype(jnp.float32) == segment_float
        ).astype(jnp.float32)
        depth_sum = (
            depth_sum
            + w_depth[kernel_tap].astype(jnp.float32)
            * wide_units[:, kernel_tap : kernel_tap + frames].astype(jnp.float32)
            * same_segment[..., None]
        )
    norm_totals = lax.psum(
        (
            jnp.sum(depth_sum * live_frames, axis=(0, 1)),
            jnp.sum(depth_sum * depth_sum * live_frames, axis=(0, 1)),
            jnp.sum(live_frames),
        ),
        ("blk", "rows"),
    )
    frame_count = norm_totals[2]
    center = norm_totals[0] / frame_count
    spread = norm_totals[1] / frame_count - center * center
    inverse = lax.rsqrt(spread + epsilon)
    standard = (depth_sum - center) * inverse
    pre_act = standard * bn_gain
    act_low = jax.nn.silu(pre_act).astype(jnp.bfloat16)
    stored = (
        norm_stored,
        normed_low,
        first_half,
        logistic,
        live_frames,
        wide_units,
        wide_segment,
        frame_count,
        inverse,
        standard,
        pre_act,
        act_low,
    )
    return (project(act_low, w_pw2), stored)


def conv_backward(stream_grad, segment, norm_gain, w_pw1, w_depth, bn_gain, w_pw2, stored):
    (
        norm_stored,
        normed_low,
        first_half,
        logistic,
        live_frames,
        wide_units,
        wide_segment,
        frame_count,
        inverse,
        standard,
        pre_act,
        act_low,
    ) = stored
    row_count, frames, model_width = stream_grad.shape
    grad_low = stream_grad.astype(jnp.bfloat16)
    w_pw2_grad = weight_product(act_low, grad_low)
    act_grad = project_back(grad_low, w_pw2) * silu_slope(pre_act)
    hat_grad = act_grad * bn_gain
    grad_sums = lax.psum(
        (jnp.sum(hat_grad, axis=(0, 1)), jnp.sum(act_grad * standard, axis=(0, 1))), ("blk", "rows")
    )
    hat_total, bn_gain_grad = grad_sums
    frame_share = live_frames / frame_count
    depth_low = (
        inverse
        * (hat_grad - frame_share * hat_total - frame_share * standard * bn_gain * bn_gain_grad)
    ).astype(jnp.bfloat16)
    wide_grad = padded(depth_low, (("blk", 1),), KERNEL // 2)
    segment_float = segment.astype(jnp.float32)
    depth_float = depth_low.astype(jnp.float32)
    unit_grad = jnp.zeros((row_count, frames, model_width), jnp.float32)
    tap_grads = []
    for kernel_tap in range(KERNEL):
        forward_same = (
            wide_segment[:, kernel_tap : kernel_tap + frames].astype(jnp.float32) == segment_float
        ).astype(jnp.float32)[..., None]
        tap_grads.append(
            jnp.sum(
                depth_float
                * wide_units[:, kernel_tap : kernel_tap + frames].astype(jnp.float32)
                * forward_same,
                axis=(0, 1),
            )
        )
        mirror = KERNEL - 1 - kernel_tap
        backward_same = (
            wide_segment[:, mirror : mirror + frames].astype(jnp.float32) == segment_float
        ).astype(jnp.float32)[..., None]
        unit_grad = (
            unit_grad
            + w_depth[kernel_tap].astype(jnp.float32)
            * wide_grad[:, mirror : mirror + frames].astype(jnp.float32)
            * backward_same
        )
    unit_grad = unit_grad * live_frames
    pair_low = jnp.concatenate(
        [unit_grad * logistic, unit_grad * first_half * logistic * (1.0 - logistic)], axis=-1
    ).astype(jnp.bfloat16)
    w_pw1_grad = weight_product(normed_low, pair_low)
    input_grad, gain_grad = norm_backward(project_back(pair_low, w_pw1), norm_gain, norm_stored)
    return (
        stream_grad + input_grad,
        (gain_grad, w_pw1_grad, jnp.stack(tap_grads), bn_gain_grad, w_pw2_grad),
    )


def per_device(
    tokens,
    seg_ids,
    frame_mask,
    cotangent,
    g_ff1,
    w_ff1_in,
    w_ff1_out,
    g_att,
    w_query,
    w_key,
    w_value,
    w_output,
    rel_table,
    g_conv,
    w_pw1,
    w_depth,
    bn_gain,
    w_pw2,
    g_ff2,
    w_ff2_in,
    w_ff2_out,
    g_out,
):
    start_stream = tokens.astype(jnp.float32)
    ffn_one, ffn_one_stored = ffn_forward(start_stream, g_ff1, w_ff1_in, w_ff1_out)
    after_ffn = start_stream + 0.5 * ffn_one
    code_low = jnp.where(frame_mask == 1, seg_ids, -1).astype(jnp.bfloat16)
    attended, attend_stored = attend_forward(
        after_ffn, seg_ids, code_low, g_att, w_query, w_key, w_value, w_output, rel_table
    )
    after_att = after_ffn + attended
    conv_out, conv_stored = conv_forward(
        after_att, seg_ids, frame_mask, g_conv, w_pw1, w_depth, bn_gain, w_pw2
    )
    after_conv = after_att + conv_out
    ffn_two, ffn_two_stored = ffn_forward(after_conv, g_ff2, w_ff2_in, w_ff2_out)
    after_two = after_conv + 0.5 * ffn_two
    final_norm, final_stored = norm_forward(after_two, g_out)
    stream_grad, g_out_grad = norm_backward(cotangent.astype(jnp.float32), g_out, final_stored)
    stream_grad, ffn_two_grads = ffn_backward(
        stream_grad, g_ff2, w_ff2_in, w_ff2_out, ffn_two_stored
    )
    stream_grad, conv_grads = conv_backward(
        stream_grad, seg_ids, g_conv, w_pw1, w_depth, bn_gain, w_pw2, conv_stored
    )
    stream_grad, attend_grads = attend_backward(
        stream_grad, g_att, w_query, w_key, w_value, w_output, rel_table, attend_stored
    )
    stream_grad, ffn_one_grads = ffn_backward(
        stream_grad, g_ff1, w_ff1_in, w_ff1_out, ffn_one_stored
    )
    summed = lax.psum(
        (
            ffn_one_grads[0],
            ffn_one_grads[1],
            ffn_one_grads[2],
            attend_grads[0],
            attend_grads[1],
            attend_grads[2],
            attend_grads[3],
            attend_grads[4],
            attend_grads[5],
            conv_grads[0],
            conv_grads[1],
            conv_grads[2],
            conv_grads[4],
            ffn_two_grads[0],
            ffn_two_grads[1],
            ffn_two_grads[2],
            g_out_grad,
        ),
        ("blk", "rows"),
    )
    return (
        final_norm.astype(jnp.bfloat16),
        stream_grad,
        summed[0],
        summed[1],
        summed[2],
        summed[3],
        summed[4],
        summed[5],
        summed[6],
        summed[7],
        summed[8],
        summed[9],
        summed[10],
        summed[11],
        conv_grads[3],
        summed[12],
        summed[13],
        summed[14],
        summed[15],
        summed[16],
    )


def solution(mesh):
    blocks, groups = mesh.shape["blk"], mesh.shape["rows"]

    def device(tokens, *rest):
        rows, frames, _ = tokens.shape
        whole_rows = rows == blocks == 4 and groups == 8 and (rows * frames) % QT == 0
        return (row_device if whole_rows else per_device)(tokens, *rest)

    return jax.shard_map(
        device,
        mesh=mesh,
        in_specs=(
            P("rows", "blk", None),
            P("rows", "blk"),
            P("rows", "blk"),
            P("rows", "blk", None),
        )
        + (P(),) * 18,
        out_specs=(P("rows", "blk", None),) * 2 + (P(),) * 18,
        check_vma=False,
    )
```
